32 devices in a mesh: dp: 4 (over y, x), fsdp: 8 (over z, core).
Axes of the slice: x: 2, y: 2, z: 4, core: 2. Of those that a mesh axis runs over, the one named last changes fastest.
Arguments:
- tokens: bfloat16 [8, 2048, 768], P('dp', 'fsdp'), may hold values from -6 to 6
- doc_ids: int32 [8, 16], P('dp'), may hold values from 0 to 2, never falling along the last dimension, each value on 1 to 12 neighbouring positions
- pos_embed: bfloat16 [16, 768], P(None, ('dp', 'fsdp')), may hold values from -3 to 3
- w_qkv: bfloat16 [2, 768, 2304], P(None, ('dp', 'fsdp')), may hold values from -0.21875 to 0.21875
- w_out: bfloat16 [2, 768, 768], P(None, ('dp', 'fsdp')), may hold values from -1.25 to 1.25
- w_in: bfloat16 [2, 768, 3072], P(None, ('dp', 'fsdp')), may hold values from -0.21875 to 0.21875
- w_back: bfloat16 [2, 3072, 768], P(None, None, ('dp', 'fsdp')), may hold values from -0.109375 to 0.109375
- norm_gain: bfloat16 [2, 2, 768], P(None, None, ('dp', 'fsdp')), may hold values from 0.099609375 to 1.8984375
- norm_bias: bfloat16 [2, 2, 768], P(None, None, ('dp', 'fsdp')), may hold values from -1.796875 to 1.796875
- cotangent: bfloat16 [8, 2048, 768], P('dp', 'fsdp'), may hold values from -40 to 40
Outputs:
- output: bfloat16 [8, 2048, 768], P('dp', 'fsdp')
- grad_tokens: bfloat16 [8, 2048, 768], P('dp', 'fsdp')
- grad_pos: float32 [16, 768], P(None, ('dp', 'fsdp'))
- grad_qkv: float32 [2, 768, 2304], P(None, ('dp', 'fsdp'))
- grad_out: float32 [2, 768, 768], P(None, ('dp', 'fsdp'))
- grad_in: float32 [2, 768, 3072], P(None, ('dp', 'fsdp'))
- grad_back: float32 [2, 3072, 768], P(None, None, ('dp', 'fsdp'))
- grad_gain: float32 [2, 2, 768], P(None, None, ('dp', 'fsdp'))
- grad_bias: float32 [2, 2, 768], P(None, None, ('dp', 'fsdp'))
The draws below stay inside these ranges and needn't reach their ends.
Inputs may be any that keep to these rules, and one draw needn't show every extreme that they name: `doc_ids`: within a row, document numbers never fall from one segment to the next.
All inputs are finite; a program needn't handle non-finite values.
Results may differ from the reference program's by a relative error of at most 0.024.
Values may be sent and summed in bfloat16 or wider, within the bound.
A program may use at most 256 MiB of HBM per device.

```python
import math
import jax
import jax.numpy as jnp
import numpy as np
from jax import lax

D = 768
HEADS = 12
FF = 3072
SEG_LEN = 128
ROWS_DEV = 2
SEGS = 16
LENGTH = 2048
ROWS = 8


def draw_cotangent(key, part):
    noise_key = jax.random.fold_in(key, 11)
    pair_key = jax.random.fold_in(key, 23)
    noise = jnp.clip(jax.random.normal(noise_key, (ROWS, LENGTH, D), jnp.float32), -4.0, 4.0)
    position = lax.broadcasted_iota(jnp.int32, (1, LENGTH, 1), 1)
    leading = jnp.where(position % SEG_LEN == 0, 4.0, 1.0)
    blocks = ROWS // ROWS_DEV
    block_width = max(D // blocks, 1)
    target = jax.random.randint(pair_key, (blocks,), 0, blocks)
    row_block = lax.broadcasted_iota(jnp.int32, (ROWS, 1, 1), 0) // ROWS_DEV
    col_block = lax.broadcasted_iota(jnp.int32, (1, 1, D), 2) // block_width
    marked = col_block == target[row_block]
    spike = jnp.where(marked, 2.5, 1.0)
    return (noise * leading * spike).astype(jnp.bfloat16)


def levels(own_key, dims, shards, low, high):
    gain = 1.0
    for dim, shards_of in shards:
        draws = jax.random.uniform(jax.random.fold_in(jax.random.fold_in(own_key, 6), dim), (shards_of,), jnp.float32, low / len(shards), high / len(shards))
        gain = gain * jnp.repeat(jnp.exp(draws), dims[dim] // shards_of).reshape((-1,) + (1,) * (len(dims) - 1 - dim))
    return gain


def split_up(number_of, total, bound, skew):
    loads = [(1 << 20) // math.isqrt(grade ** skew) + 1 for grade in range(2, number_of + 1)]
    spare, holding = total - bound - (number_of - 1), [1] * (number_of - 1)
    while spare > 0:
        candidates = [i for i in range(number_of - 1) if holding[i] < bound]
        pool, remaining = sum([loads[i] for i in candidates]), spare
        for i in candidates:
            more = min(bound - holding[i], max(1, remaining * loads[i] // pool), spare)
            holding[i] = holding[i] + more
            spare = spare - more
    return np.array([bound] + holding)


def ragged(stream_key, number_of, total, bound, lean):
    if number_of == 2:
        one = jax.random.randint(stream_key, (), max(1, total - bound), min(bound, total - 1) + 1)
        return jnp.stack([one, total - one])
    lengths = jnp.asarray(split_up(number_of, total, bound, lean), jnp.int32)
    pairs = (number_of - 1) // 2
    giver, taker = lengths[1:1 + 2 * pairs:2], lengths[2:2 + 2 * pairs:2]
    room = jnp.minimum(giver - 1, bound - taker)
    moved = jax.random.randint(jax.random.fold_in(stream_key, 1), (pairs,), 0, 1 << 20) % (room + 1)
    lengths = lengths.at[1:1 + 2 * pairs:2].set(giver - moved).at[2:2 + 2 * pairs:2].set(taker + moved)
    return lengths[jax.random.permutation(jax.random.fold_in(stream_key, 2), number_of)]


def scatter_about(stream_key, extent, width, reach, pieces=(), kind=jnp.bfloat16):
    result = width * jax.random.normal(stream_key, extent, jnp.float32)
    if pieces:
        result = result * levels(stream_key, extent, pieces, -0.22, 0.18)
    return jnp.clip(result, -reach, reach).astype(kind)


def setup_inputs(seed: int = 0) -> dict:
    key_list = jax.random.split(jax.random.key(seed), 11)
    tokens = scatter_about(key_list[0], (ROWS, LENGTH, D), 1.0, 6.0, ((0, 4), (1, 8)))
    doc_ids = jax.vmap(lambda own: jnp.searchsorted(jnp.cumsum(ragged(own, 3, SEGS, 3 * SEGS // 4, 0)), jnp.arange(SEGS), side="right"))(jax.random.split(key_list[1], ROWS)).reshape((ROWS, SEGS)).astype(jnp.int32)
    pos_embed = scatter_about(key_list[2], (SEGS, D), 0.5, 3.0, ((1, 32),))
    w_qkv = scatter_about(key_list[3], (2, D, 3 * D), D ** -0.5, 0.21875, ((1, 32),))
    w_out = scatter_about(key_list[4], (2, D, D), (D // 32) ** -0.5, 1.25, ((1, 32),))
    w_in = scatter_about(key_list[5], (2, D, FF), D ** -0.5, 0.21875, ((1, 32),))
    w_back = scatter_about(key_list[6], (2, FF, D), FF ** -0.5, 0.109375, ((2, 32),))
    norm_gain = jnp.clip(1.0 + 0.18 * jax.random.normal(key_list[7], (2, 2, D), jnp.float32), 0.099609375, 1.8984375).astype(jnp.bfloat16)
    norm_bias = scatter_about(key_list[8], (2, 2, D), 0.3, 1.796875, ((2, 32),))
    cotangent = draw_cotangent(jax.random.fold_in(key_list[10], 71), 0)
    return {"tokens": tokens, "doc_ids": doc_ids, "pos_embed": pos_embed, "w_qkv": w_qkv, "w_out": w_out, "w_in": w_in, "w_back": w_back, "norm_gain": norm_gain, "norm_bias": norm_bias, "cotangent": cotangent}


epsilon = 1e-05
highest = lax.Precision.HIGHEST

@jax.custom_vjp
def low(v):
    return lax.optimization_barrier(v.astype(jnp.bfloat16)).astype(jnp.float32)

@jax.custom_vjp
def low_back(v):
    return v

def low_keep(v):
    return (low(v), None)

def low_pass(kept, grad):
    return (grad,)

def back_keep(v):
    return (v, None)

def back_low(kept, grad):
    return (low(grad),)
low.defvjp(low_keep, low_pass)
low_back.defvjp(back_keep, back_low)

def layer_norm(summed, norm_gains, norm_biases):
    average = lax.optimization_barrier(jnp.mean(summed, axis=-1, keepdims=True))
    centred = summed - average
    variance = lax.optimization_barrier(jnp.mean(centred * centred, axis=-1, keepdims=True))
    return centred * lax.rsqrt(variance + epsilon) * norm_gains + norm_biases

def post_block(states, allowed, w_qkv, w_out, w_in, w_back, norm_gains, norm_biases):
    groups, length, model_width = states.shape
    head_size = model_width // HEADS
    packed = low(low_back(jnp.einsum('gld,de->gle', low(states), w_qkv, precision=highest)))
    query_part = packed[..., :model_width].reshape(groups, length, HEADS, head_size)
    key_part = packed[..., model_width:2 * model_width].reshape(groups, length, HEADS, head_size)
    value_part = packed[..., 2 * model_width:].reshape(groups, length, HEADS, head_size)
    scores = low_back(jnp.einsum('glhe,gmhe->ghlm', query_part, key_part, precision=highest) * head_size ** (-0.5))
    scores = jnp.where(allowed[:, None], scores, -1e+30)
    attention = jax.nn.softmax(scores, axis=-1)
    context = low(low_back(jnp.einsum('ghlm,gmhe->glhe', low(attention), value_part, precision=highest)))
    context = context.reshape(groups, length, model_width)
    branch = low_back(jnp.einsum('gld,de->gle', context, w_out, precision=highest))
    normed = layer_norm(states + branch, norm_gains[0], norm_biases[0])
    hidden = low_back(jnp.einsum('gld,df->glf', low(normed), w_in, precision=highest))
    active = low(jax.nn.gelu(hidden, approximate=False))
    feed_out = low_back(jnp.einsum('glf,fd->gld', active, w_back, precision=highest))
    return layer_norm(normed + feed_out, norm_gains[1], norm_biases[1])

def one_row(states, documents, pos_f, qkv_f, out_f, in_f, back_f, gain_f, bias_f):
    segments = states.reshape(SEGS, SEG_LEN, D)
    every = jnp.ones((SEGS, SEG_LEN, SEG_LEN), dtype=jnp.bool_)
    segment_out = post_block(segments, every, qkv_f[0], out_f[0], in_f[0], back_f[0], gain_f[0], bias_f[0])
    leaders = segment_out[:, 0, :] + pos_f
    same_doc = documents[:, None] == documents[None, :]
    cross_out = post_block(leaders[None], same_doc[None], qkv_f[1], out_f[1], in_f[1], back_f[1], gain_f[1], bias_f[1])[0]
    joined = jnp.concatenate([cross_out[:, None, :], segment_out[:, 1:, :]], axis=1)
    return joined.reshape(LENGTH, D)

def reference(tokens, doc_ids, pos_embed, w_qkv, w_out, w_in, w_back, norm_gain, norm_bias, cotangent):

    def forward(states, pos_f, qkv_f, out_f, in_f, back_f, gain_f, bias_f):
        row_step = jax.checkpoint(lambda row_pair: one_row(row_pair[0], row_pair[1], pos_f, qkv_f, out_f, in_f, back_f, gain_f, bias_f))
        return lax.map(row_step, (states, doc_ids))
    output, pullback = jax.vjp(forward, tokens.astype(jnp.float32), pos_embed.astype(jnp.float32), w_qkv.astype(jnp.float32), w_out.astype(jnp.float32), w_in.astype(jnp.float32), w_back.astype(jnp.float32), norm_gain.astype(jnp.float32), norm_bias.astype(jnp.float32))
    grads = pullback(cotangent.astype(jnp.float32))
    return (output.astype(jnp.bfloat16), grads[0].astype(jnp.bfloat16), grads[1], grads[2], grads[3], grads[4], grads[5], grads[6], grads[7])
```

```python
from functools import partial

import jax
import jax.numpy as jnp
from jax import lax
from jax.experimental import pallas as pl
from jax.experimental.pallas import tpu as pltpu
from jax.sharding import PartitionSpec as P

HEADS = 12
SEG_LEN = 128


epsilon = 1e-05
root_half = 0.7071067811865476
inv_root_tau = 0.3989422804014327

bf16 = jnp.bfloat16
f32 = jnp.float32
MESH = pl.DeviceIdType.MESH
VM = pltpu.VMEM
MIB = 1024 * 1024
ROWS = 48
LANES = 128


class Place:
    def __init__(self):
        self.dp = lax.axis_index("dp")
        self.fsdp = lax.axis_index("fsdp")
        self.y, self.x = self.dp // 2, self.dp % 2
        self.z, self.core = self.fsdp // 2, self.fsdp % 2

    def at(self, dp, z, core):
        return (dp, z * 2 + core)

    @property
    def sib(self):
        return (self.dp, self.z * 2 + 1 - self.core)

    @property
    def xdp(self):
        return self.y * 2 + 1 - self.x

    @property
    def ydp(self):
        return (1 - self.y) * 2 + self.x

    @property
    def xnbr(self):
        return (self.xdp, self.fsdp)

    @property
    def ynbr(self):
        return (self.ydp, self.fsdp)


def greet(devices):
    barrier = pltpu.get_barrier_semaphore()
    for device in devices:
        pl.semaphore_signal(barrier, inc=1, device_id=device, device_id_type=MESH)
    pl.semaphore_wait(barrier, len(devices))


def remote(src, dst, send, recv, device):
    return pltpu.make_async_remote_copy(
        src_ref=src, dst_ref=dst, send_sem=send, recv_sem=recv, device_id=device, device_id_type=MESH
    )


def lanes(start, size):
    if isinstance(start, int):
        return pl.ds(start, size)
    return pl.ds(pl.multiple_of(start, LANES), size)


def rows_at(start, size, unit):
    return pl.ds(pl.multiple_of(start, unit), size)


class Gather:
    def __init__(self, place, out, block, start, width, index, sems, height2, slabs=False):
        self.p, self.out, self.block, self.start, self.width = place, out, block, start, width
        self.m, self.sems, self.h2, self.slabs = index, sems, height2, slabs
        self.half = width // 2
        tiles = self.half // LANES
        self.a = (tiles + 1) // 2 * LANES
        self.b = self.half - self.a
        self.sent = []

    def col(self, core, part):
        base = core * self.half
        if part == "A":
            return base, self.a
        if part == "B":
            return base + self.a, self.b
        return base, self.half

    def dst(self, dp, z, core, part, count=1):
        base, size = self.col(core, part)
        return self.out.at[rows_at((dp * 4 + z) * self.h2, self.h2 * count, 16), lanes(base, size)]

    def own(self, part, z=None):
        base, size = self.col(self.p.core, part)
        start = self.start + base
        if self.slabs:
            start = start + (self.p.z if z is None else z) * self.width
        return self.block.at[:, lanes(start, size)]

    def go(self, src, dst, slot, device, link=True):
        send, recv = (self.sems[0], self.sems[1]) if link else (self.sems[2], self.sems[3])
        copy = remote(src, dst, send.at[self.m, slot], recv.at[self.m, slot], device)
        copy.start()
        self.sent.append(copy)

    def arrived(self, dst, slot, link=True):
        send, recv = (self.sems[0], self.sems[1]) if link else (self.sems[2], self.sems[3])
        remote(dst, dst, send.at[self.m, slot], recv.at[self.m, slot], self.p.sib).wait_recv()

    def spread(self, src_of, z, d):
        p = self.p
        core = p.core
        self.go(src_of("A"), self.dst(p.dp, z, core, "A"), 3 + d, p.xnbr)
        if self.b:
            self.go(src_of("B"), self.dst(p.dp, z, core, "B"), 15 + d, p.ynbr)
        self.go(src_of("A"), self.dst(p.dp, z, core, "A"), 7 + d, p.ynbr)
        if self.b:
            self.go(src_of("B"), self.dst(p.dp, z, core, "B"), 19 + d, p.xnbr)

    def send_own(self):
        p = self.p
        for d in (1, 3, 2):
            z = (p.z + d) % 4
            self.go(self.own("AB", z), self.dst(p.dp, p.z, p.core, "AB"), d - 1, p.at(p.dp, z, p.core))
        self.spread(self.own, p.z, 0)

    def pass_line(self):
        p = self.p
        for d in (1, 3, 2):
            z = (p.z + 4 - d) % 4
            self.arrived(self.dst(p.dp, z, p.core, "AB"), d - 1)
            self.spread(lambda part: self.dst(p.dp, z, p.core, part), z, d)
        line = self.dst(p.dp, 0, p.core, "AB", 4)
        for d in (1, 2, 3):
            z = (p.z + 4 - d) % 4
            block = self.dst(p.dp, z, p.core, "AB")
            self.go(block, block, 4 + d, p.sib, link=False)

    def pass_plane(self):
        p = self.p
        for d in (0, 1, 3, 2):
            z = (p.z + 4 - d) % 4
            block = self.dst(p.xdp, z, p.core, "A")
            self.arrived(block, 3 + d)
            self.go(block, block, 11 + d, p.ynbr)
            if self.b:
                block = self.dst(p.ydp, z, p.core, "B")
                self.arrived(block, 15 + d)
                self.go(block, block, 23 + d, p.xnbr)
        block = self.dst(p.xdp, 0, p.core, "A", 4)
        self.go(block, block, 0, p.sib, link=False)
        if self.b:
            block = self.dst(p.ydp, 0, p.core, "B", 4)
            self.go(block, block, 1, p.sib, link=False)

    def last(self):
        p = self.p
        core, other = p.core, 1 - p.core
        far = (1 - p.y) * 2 + 1 - p.x
        for d in range(4):
            z = (p.z + 4 - d) % 4
            self.arrived(self.dst(p.ydp, z, core, "A"), 7 + d)
            if self.b:
                self.arrived(self.dst(p.xdp, z, core, "B"), 19 + d)
        block = self.dst(p.ydp, 0, core, "A", 4)
        self.go(block, block, 2, p.sib, link=False)
        if self.b:
            block = self.dst(p.xdp, 0, core, "B", 4)
            self.go(block, block, 3, p.sib, link=False)
        for d in range(4):
            z = (p.z + 4 - d) % 4
            self.arrived(self.dst(far, z, core, "A"), 11 + d)
            if self.b:
                self.arrived(self.dst(far, z, core, "B"), 23 + d)
        block = self.dst(far, 0, core, "AB" if self.b else "A", 4)
        self.go(block, block, 4, p.sib, link=False)

    def drain(self):
        p = self.p
        other = 1 - p.core
        far = (1 - p.y) * 2 + 1 - p.x
        for d in (1, 2, 3):
            z = (p.z + 4 - d) % 4
            self.arrived(self.dst(p.dp, z, other, "AB"), 4 + d, link=False)
        self.arrived(self.dst(p.xdp, 0, other, "A", 4), 0, link=False)
        if self.b:
            self.arrived(self.dst(p.ydp, 0, other, "B", 4), 1, link=False)
        self.arrived(self.dst(p.ydp, 0, other, "A", 4), 2, link=False)
        if self.b:
            self.arrived(self.dst(p.xdp, 0, other, "B", 4), 3, link=False)
        self.arrived(self.dst(far, 0, other, "AB" if self.b else "A", 4), 4, link=False)

    def finish(self):
        for copy in self.sent:
            copy.wait_send()


def run_gathers(gathers):
    n = len(gathers)
    for step in range(n + 3):
        if step < n:
            gathers[step].send_own()
        if 0 <= step - 1 < n:
            gathers[step - 1].pass_line()
            gathers[step - 1].pass_plane()
        if 0 <= step - 2 < n:
            gathers[step - 2].last()
        if 0 <= step - 3 < n:
            gathers[step - 3].drain()
    for g in gathers:
        g.finish()


def gather_peers(p):
    peers = [p.sib, p.xnbr, p.ynbr]
    for d in (1, 2, 3):
        peers.append(p.at(p.dp, (p.z + d) % 4, p.core))
    return peers


def everyone(p):
    return [
        (lax.rem(p.dp + i, 4), lax.rem(p.fsdp + j, 8)) for i in range(4) for j in range(8) if i or j
    ]


GATHER_SEMS = lambda n: [
    pltpu.SemaphoreType.DMA((n, 27)),
    pltpu.SemaphoreType.DMA((n, 27)),
    pltpu.SemaphoreType.DMA((n, 8)),
    pltpu.SemaphoreType.DMA((n, 8)),
]


def pair_rows(p, own_ref, sib_ref, block_ref, send, recv):
    copy = remote(own_ref, sib_ref, send, recv, p.sib)
    copy.start()
    copy.wait()
    height, width = block_ref.shape[0] // 2, own_ref.shape[1]
    step = 1024
    first = p.core == 0

    def chunk(at, size):
        mine = own_ref[:, lanes(at, size)].astype(f32)[:height]
        theirs = sib_ref[:, lanes(at, size)].astype(f32)[:height]
        both = jnp.concatenate(
            [jnp.where(first, mine, theirs), jnp.where(first, theirs, mine)], axis=0
        )
        block_ref[:, lanes(at, size)] = both.astype(bf16)

    @pl.loop(0, width // step)
    def _(i):
        chunk(i * step, step)

    if width % step:
        chunk(width // step * step, width % step)


def weights_kernel(widths, pack_ref, *refs):
    n = len(widths)
    outs, cross_out, wo_out = refs[:n], refs[n], refs[n + 1]
    sib_buf, block, s0, s1, s2, s3, pair_send, pair_recv, wo_send, wo_recv, local = refs[n + 2 :]
    p = Place()
    greet(everyone(p))
    pair_rows(p, pack_ref, sib_buf, block, pair_send, pair_recv)
    sems = (s0, s1, s2, s3)
    gathers, copies, at = [], [], 0
    key = rows_at((p.dp * 4 + p.z) * ROWS, ROWS, 16)
    for i, width in enumerate(widths):
        gathers.append(Gather(p, outs[i], block, at, width, i, sems, ROWS))
        copies.append((block.at[:, lanes(at, width)], outs[i].at[key]))
        at += width
    cw = cross_out.shape[1]
    gathers.append(Gather(p, cross_out, block, at, cw, n, sems, ROWS, slabs=True))
    copies.append((block.at[:, lanes(at + p.z * cw, cw)], cross_out.at[key]))
    at += 4 * cw
    for i, (src, dst) in enumerate(copies):
        pltpu.make_async_copy(src, dst, local.at[i]).start()
    width = wo_out.shape[1]
    half = width // 2
    wo_src = block.at[:, lanes(at + p.core * half, half)]
    wo_dst = wo_out.at[rows_at(p.z * ROWS, ROWS, 16), lanes(p.core * half, half)]
    for i in range(4):
        copy = remote(wo_src, wo_dst, wo_send.at[i], wo_recv.at[p.z], p.at(i, p.dp, p.core))
        here = jnp.logical_and(p.dp == i, p.dp == p.z)

        @pl.when(jnp.logical_not(here))
        def _():
            copy.start()

        @pl.when(here)
        def _():
            mine = pltpu.make_async_copy(wo_src, wo_dst, local.at[n + 1])
            mine.start()
            mine.wait()

    run_gathers(gathers)
    for i in range(4):
        piece = wo_out.at[pl.ds(i * ROWS, ROWS), lanes(p.core * half, half)]
        here = jnp.logical_and(p.z == p.dp, p.z == i)

        @pl.when(jnp.logical_not(here))
        def _():
            remote(piece, piece, wo_send.at[i], wo_recv.at[i], p.sib).wait_recv()

    mine = wo_out.at[:, lanes(p.core * half, half)]
    theirs = wo_out.at[:, lanes((1 - p.core) * half, half)]
    copy = remote(mine, mine, wo_send.at[4], wo_recv.at[4], p.sib)
    copy.start()
    remote(theirs, theirs, wo_send.at[4], wo_recv.at[4], p.sib).wait_recv()
    copy.wait_send()
    for i in range(4):
        here = jnp.logical_and(p.dp == i, p.dp == p.z)

        @pl.when(jnp.logical_not(here))
        def _():
            remote(wo_src, wo_dst, wo_send.at[i], wo_recv.at[p.z], p.at(i, p.dp, p.core)).wait_send()

    for i, (src, dst) in enumerate(copies):
        pltpu.make_async_copy(src, dst, local.at[i]).wait()


def gather_weights(pack, widths, cross_width, wo_width):
    n = len(widths)
    rows = 16 * ROWS
    outs = [jax.ShapeDtypeStruct((rows, w), bf16) for w in widths]
    outs += [jax.ShapeDtypeStruct((rows, cross_width), bf16), jax.ShapeDtypeStruct((192, wo_width), bf16)]
    height, total = pack.shape
    return pl.pallas_call(
        partial(weights_kernel, widths),
        out_shape=outs,
        in_specs=[pl.BlockSpec(memory_space=VM)],
        out_specs=[pl.BlockSpec(memory_space=pl.ANY)] * len(outs),
        scratch_shapes=[pltpu.VMEM((height, total), bf16), pltpu.VMEM((ROWS, total), bf16)]
        + GATHER_SEMS(n + 1)
        + [
            pltpu.SemaphoreType.DMA,
            pltpu.SemaphoreType.DMA,
            pltpu.SemaphoreType.DMA((5,)),
            pltpu.SemaphoreType.DMA((5,)),
            pltpu.SemaphoreType.DMA((n + 2,)),
        ],
        compiler_params=pltpu.CompilerParams(
            collective_id=0, has_side_effects=True, vmem_limit_bytes=32 * MIB
        ),
    )(pack)


class Scatter:
    def __init__(self, place, grad, out, index, sems, acc, pair, r1a, r1b, r2a, r2b, r3, give):
        self.p, self.grad, self.out, self.m = place, grad, out, index
        self.send, self.recv, self.local = sems
        self.acc, self.pair, self.r1a, self.r1b = acc, pair, r1a, r1b
        self.r2a, self.r2b, self.r3, self.give = r2a, r2b, r3, give
        self.half = grad.shape[1] // 2
        tiles = self.half // LANES
        self.a = (tiles + 1) // 2 * LANES
        self.b = self.half - self.a
        self.sent = []
        p = place
        far = (1 - p.y) * 2 + 1 - p.x
        self.groups = (far, p.ydp, p.xdp, p.dp)

    def group(self, ref, dp):
        return ref.at[rows_at(dp * 4 * ROWS, 4 * ROWS, 16)]

    def go(self, src, dst, slot, device):
        copy = remote(src, dst, self.send.at[self.m, slot], self.recv.at[self.m, slot], device)
        copy.start()
        self.sent.append(copy)

    def arrived(self, dst, slot):
        remote(dst, dst, self.send.at[self.m, slot], self.recv.at[self.m, slot], self.p.sib).wait_recv()

    def load(self, i):
        p = self.p
        mine = self.group(self.grad, self.groups[i]).at[:, lanes(p.core * self.half, self.half)]
        return pltpu.make_async_copy(mine, self.group(self.acc, self.groups[i]), self.local.at[self.m, i])

    def start(self):
        p = self.p
        for i, dp in enumerate(self.groups):
            theirs = self.group(self.grad, dp).at[:, lanes((1 - p.core) * self.half, self.half)]
            self.go(theirs, self.group(self.pair, dp), i, p.sib)
            self.load(i).start()

    def add(self, dp, part, other, other_row=0):
        at, size = {"A": (0, self.a), "B": (self.a, self.b), "AB": (0, self.half)}[part]
        base = dp * 4 * ROWS

        @pl.loop(0, 4)
        def _(i):
            key = (rows_at(base + i * ROWS, ROWS, 16), pl.ds(at, size))
            more = other[rows_at(other_row + i * ROWS, ROWS, 16), :]
            self.acc[key] = (self.acc[key].astype(f32) + more.astype(f32)).astype(bf16)

    def side(self, dp, part):
        at, size = (0, self.a) if part == "A" else (self.a, self.b)
        return self.group(self.acc, dp).at[:, pl.ds(at, size)]

    def one(self):
        p = self.p
        for i, dp in enumerate(self.groups):
            self.arrived(self.group(self.pair, dp), i)
            self.load(i).wait()
            self.add(dp, "AB", self.pair, dp * 4 * ROWS)
            if i == 0:
                self.go(self.side(dp, "A"), self.r1a.at[pl.ds(0, 4 * ROWS)], 4, p.ynbr)
                if self.b:
                    self.go(self.side(dp, "B"), self.r1b.at[pl.ds(0, 4 * ROWS)], 6, p.xnbr)
            if i == 1:
                self.go(self.side(dp, "A"), self.r1a.at[pl.ds(4 * ROWS, 4 * ROWS)], 5, p.ynbr)
            if i == 2 and self.b:
                self.go(self.side(dp, "B"), self.r1b.at[pl.ds(4 * ROWS, 4 * ROWS)], 7, p.xnbr)

    def two(self):
        p = self.p
        self.arrived(self.r1a.at[pl.ds(0, 4 * ROWS)], 4)
        self.add(p.xdp, "A", self.r1a)
        self.go(self.side(p.xdp, "A"), self.r2a, 8, p.xnbr)
        if self.b:
            self.arrived(self.r1b.at[pl.ds(0, 4 * ROWS)], 6)
            self.add(p.ydp, "B", self.r1b)
            self.go(self.side(p.ydp, "B"), self.r2b, 9, p.ynbr)
        self.arrived(self.r1a.at[pl.ds(4 * ROWS, 4 * ROWS)], 5)
        self.add(p.dp, "A", self.r1a, 4 * ROWS)
        if self.b:
            self.arrived(self.r1b.at[pl.ds(4 * ROWS, 4 * ROWS)], 7)
            self.add(p.dp, "B", self.r1b, 4 * ROWS)

    def three(self):
        p = self.p
        self.arrived(self.r2a, 8)
        self.add(p.dp, "A", self.r2a)
        if self.b:
            self.arrived(self.r2b, 9)
            self.add(p.dp, "B", self.r2b)
        for d in (1, 3, 2):
            z = (p.z + d) % 4
            src = self.acc.at[rows_at((p.dp * 4 + z) * ROWS, ROWS, 16)]
            self.go(src, self.r3.at[d - 1], 9 + d, p.at(p.dp, z, p.core))

    def four(self):
        p = self.p
        for d in (1, 3, 2):
            self.arrived(self.r3.at[d - 1], 9 + d)
        rows = rows_at((p.dp * 4 + p.z) * ROWS, ROWS, 16)
        step = self.a if self.b == self.a else self.half

        def chunk(at, size):
            cols = pl.ds(at, size)
            total = self.acc[rows, cols].astype(f32)
            for d in range(3):
                total = total + self.r3[d, :, cols].astype(f32)
            upper, lower = total[: ROWS // 2], total[ROWS // 2 :]
            first = p.core == 0
            self.give[:, cols] = jnp.where(first, lower, upper)
            self.out[:, lanes(p.core * self.half + at, size)] = jnp.where(first, upper, lower)

        for at in range(0, self.half, step):
            chunk(at, step)
        self.go(self.give, self.out.at[:, lanes(p.core * self.half, self.half)], 13, p.sib)

    def five(self):
        p = self.p
        self.arrived(self.out.at[:, lanes((1 - p.core) * self.half, self.half)], 13)

    def finish(self):
        for copy in self.sent:
            copy.wait_send()


def scatter_kernel(n, *refs):
    grads, outs = refs[:n], refs[n : 2 * n]
    scratch = refs[2 * n :]
    sems = scratch[:3]
    p = Place()
    greet(gather_peers(p))
    jobs = []
    for i in range(n):
        bufs = scratch[3 + 8 * i : 11 + 8 * i]
        jobs.append(Scatter(p, grads[i], outs[i], i, sems, *bufs))
    for job in jobs:
        job.start()
    for step in range(n + 4):
        for lag, name in enumerate(("one", "two", "three", "four", "five")):
            if 0 <= step - lag < n:
                getattr(jobs[step - lag], name)()
    for job in jobs:
        job.finish()


def scatter_grads(grads):
    n = len(grads)
    bufs = []
    for g in grads:
        half = g.shape[1] // 2
        tiles = half // LANES
        a = (tiles + 1) // 2 * LANES
        b = max(half - a, LANES)
        rows = g.shape[0]
        bufs += [
            pltpu.VMEM((rows, half), bf16),
            pltpu.VMEM((rows, half), bf16),
            pltpu.VMEM((8 * ROWS, a), bf16),
            pltpu.VMEM((8 * ROWS, b), bf16),
            pltpu.VMEM((4 * ROWS, a), bf16),
            pltpu.VMEM((4 * ROWS, b), bf16),
            pltpu.VMEM((3, ROWS, half), bf16),
            pltpu.VMEM((ROWS // 2, half), f32),
        ]
    return pl.pallas_call(
        partial(scatter_kernel, n),
        out_shape=[jax.ShapeDtypeStruct((ROWS // 2, g.shape[1]), f32) for g in grads],
        in_specs=[pl.BlockSpec(memory_space=pl.ANY)] * n,
        out_specs=[pl.BlockSpec(memory_space=VM)] * n,
        scratch_shapes=[
            pltpu.SemaphoreType.DMA((n, 14)),
            pltpu.SemaphoreType.DMA((n, 14)),
            pltpu.SemaphoreType.DMA((n, 4)),
        ]
        + bufs,
        compiler_params=pltpu.CompilerParams(
            collective_id=1, has_side_effects=True, vmem_limit_bytes=48 * MIB
        ),
    )(*grads)


NEG = -1e30


def mm(a, b, dims):
    return lax.dot_general(a, b, (dims, ((), ())), preferred_element_type=f32)


NN = ((1,), (0,))
NT = ((1,), (1,))
TN = ((0,), (0,))


def norm_rows(summed, gain, bias):
    centred = summed - jnp.mean(summed, axis=-1, keepdims=True)
    variance = jnp.mean(centred * centred, axis=-1, keepdims=True)
    inverse = lax.rsqrt(variance + epsilon)
    scaled = centred * inverse
    return scaled * gain + bias, scaled, inverse


def norm_rows_back(grad, scaled, inverse, gain):
    g = grad * gain
    first = jnp.mean(g, axis=-1, keepdims=True)
    second = jnp.mean(g * scaled, axis=-1, keepdims=True)
    return inverse * (g - first - scaled * second)


def gelu_parts(u):
    cumulative = 0.5 * (1.0 + lax.erf(u * root_half))
    return cumulative, cumulative + u * inv_root_tau * jnp.exp(-0.5 * u * u)


def cross_kernel(
    lead_ref, mask_ref, norm_ref, w_ref, wo_ref, home_ref, fac_ref, small_ref,
    gbuf, lead, xbuf, ybuf, dpack, g_send, g_recv, x_send, x_recv, h_send, h_recv, local,
):
    p = Place()
    group = [(p.dp, lax.rem(p.fsdp + j, 8)) for j in range(1, 8)]
    greet(group)
    width = lead_ref.shape[2] // 2
    slab = width // 4
    head = width // HEADS
    heads = HEADS // 4

    def lead_copy(z, j):
        i = 2 * z + j
        return remote(lead_ref.at[j], gbuf.at[p.fsdp], g_send.at[i], g_recv.at[p.fsdp], (p.dp, i))

    for d in range(4):
        z = (p.z + d) % 4
        for j in range(2):
            here = jnp.logical_and(p.z == z, p.core == j) if d == 0 else None
            if d:
                lead_copy(z, j).start()
            else:

                @pl.when(p.core != j)
                def _():
                    lead_copy(z, j).start()

                @pl.when(p.core == j)
                def _():
                    mine = pltpu.make_async_copy(lead_ref.at[j], gbuf.at[p.fsdp], local)
                    mine.start()
                    mine.wait()

    for d in range(1, 8):
        i = lax.rem(p.fsdp + d, 8)
        remote(gbuf.at[i], gbuf.at[i], g_send.at[i], g_recv.at[i], p.sib).wait_recv()
    for i in range(8):
        lead[2 * i : 2 * i + 2, :] = gbuf[i]
    states = lead[:, :width]
    cot = lead[:, width:]

    def sum_z(e, partial_sum):
        xbuf[e, p.z] = partial_sum.astype(bf16)
        copies = []
        for d in (1, 3, 2):
            z = (p.z + d) % 4
            copy = remote(
                xbuf.at[e, p.z], xbuf.at[e, p.z], x_send.at[e, d - 1], x_recv.at[e, p.z],
                p.at(p.dp, z, p.core),
            )
            copy.start()
            copies.append(copy)
        for d in (1, 3, 2):
            z = (p.z + d) % 4
            piece = xbuf.at[e, z]
            remote(piece, piece, x_send.at[e, d - 1], x_recv.at[e, z], p.sib).wait_recv()
        for copy in copies:
            copy.wait_send()
        return sum(xbuf[e, z].astype(f32) for z in range(4))

    gain0, gain1 = norm_ref[0:1, :], norm_ref[1:2, :]
    bias0, bias1 = norm_ref[2:3, :], norm_ref[3:4, :]
    in_cols, back_cols = pl.ds(3 * slab, width), pl.ds(3 * slab + width, width)
    qkv_cols = pl.ds(0, 3 * slab)
    factor = head ** (-0.5)
    allowed = mask_ref[...] > 0.5

    xl = states.astype(bf16)
    packed = mm(xl, w_ref[:, qkv_cols], NN).astype(bf16)
    q = [packed[:, i * head : (i + 1) * head] for i in range(heads)]
    k = [packed[:, slab + i * head : slab + (i + 1) * head] for i in range(heads)]
    v = [packed[:, 2 * slab + i * head : 2 * slab + (i + 1) * head] for i in range(heads)]
    att, context = [], []
    for i in range(heads):
        scores = jnp.where(allowed, mm(q[i], k[i], NT) * factor, NEG)
        top = jnp.max(scores, axis=-1, keepdims=True)
        terms = jnp.exp(scores - top)
        a = terms / jnp.sum(terms, axis=-1, keepdims=True)
        att.append(a)
        context.append(mm(a.astype(bf16), v[i], NN))
    context = jnp.concatenate(context, axis=1).astype(bf16)
    branch = sum_z(0, mm(context, wo_ref[...], NN))
    normed, z_one, r_one = norm_rows(states + branch, gain0, bias0)
    nl = normed.astype(bf16)
    hidden = mm(nl, w_ref[:, in_cols], NN)
    phi, slope = gelu_parts(hidden)
    active = (hidden * phi).astype(bf16)
    feed = sum_z(1, mm(active, w_ref[:, back_cols], NT))
    result, z_two, r_two = norm_rows(normed + feed, gain1, bias1)
    d_two = norm_rows_back(cot, z_two, r_two, gain1)
    df = d_two.astype(bf16)
    du = (mm(df, w_ref[:, back_cols], NN) * slope).astype(bf16)
    d_normed = d_two + sum_z(2, mm(du, w_ref[:, in_cols], NT))
    d_one = norm_rows_back(d_normed, z_one, r_one, gain0)
    db = d_one.astype(bf16)
    dc = mm(db, wo_ref[...], NT).astype(bf16)
    for i in range(heads):
        a = att[i]
        dci = dc[:, i * head : (i + 1) * head]
        da = mm(dci, v[i], NT)
        dv = mm(a.astype(bf16), dci, TN)
        ds = (a * (da - jnp.sum(a * da, axis=-1, keepdims=True))).astype(bf16)
        dq = mm(ds, k[i], NN) * factor
        dk = mm(ds, q[i], TN) * factor
        for j, piece in enumerate((dq, dk, dv)):
            dpack[:, j * slab + i * head : j * slab + (i + 1) * head] = piece
    dp = dpack[...].astype(bf16)
    dx = d_one + sum_z(3, mm(dp, w_ref[:, qkv_cols], NT))
    for i in range(8):
        ybuf[i, :, :width] = result[2 * i : 2 * i + 2]
        ybuf[i, :, width:] = dx[2 * i : 2 * i + 2]
    home = remote(
        ybuf.at[2 * p.z + 1 - p.core], home_ref.at[p.core], h_send, h_recv, p.sib
    )
    home.start()
    home_ref[p.core] = ybuf[2 * p.z + p.core]

    def part(full):
        pieces = [full[:, i * slab : (i + 1) * slab] for i in range(4)]
        out = pieces[0]
        for i in range(1, 4):
            out = jnp.where(p.z == i, pieces[i], out)
        return out.astype(bf16)

    fac_ref[:, :width] = active
    fac_ref[:, width : 2 * width] = du
    fac_ref[:, 2 * width :] = jnp.concatenate(
        [dp, part(d_one), part(states), part(normed), part(d_two), context], axis=1
    )
    once = jnp.where(p.z == 0, 1.0, 0.0)
    sums = [d_normed * z_one, cot * z_two, d_normed, cot]
    small_ref[...] = jnp.zeros_like(small_ref)
    for i, s in enumerate(sums):
        small_ref[i : i + 1, :] = once * jnp.sum(s, axis=0, keepdims=True)
    theirs = home_ref.at[1 - p.core]
    remote(theirs, theirs, h_send, h_recv, p.sib).wait_recv()
    home.wait_send()
    for d in range(4):
        z = (p.z + d) % 4
        for j in range(2):
            if d:
                lead_copy(z, j).wait_send()
            else:

                @pl.when(p.core != j)
                def _():
                    lead_copy(z, j).wait_send()


def cross_block(lead, mask, norms, weights, wo):
    width = wo.shape[1]
    segs = mask.shape[0]
    return pl.pallas_call(
        cross_kernel,
        out_shape=[
            jax.ShapeDtypeStruct((2, 2, 2 * width), f32),
            jax.ShapeDtypeStruct((segs, 4 * width), bf16),
            jax.ShapeDtypeStruct((8, width), f32),
        ],
        in_specs=[pl.BlockSpec(memory_space=VM)] * 5,
        out_specs=[pl.BlockSpec(memory_space=VM)] * 3,
        scratch_shapes=[
            pltpu.VMEM((8, 2, 2 * width), f32),
            pltpu.VMEM((segs, 2 * width), f32),
            pltpu.VMEM((4, 4, segs, width), bf16),
            pltpu.VMEM((8, 2, 2 * width), f32),
            pltpu.VMEM((segs, 3 * width // 4), f32),
            pltpu.SemaphoreType.DMA((8,)),
            pltpu.SemaphoreType.DMA((8,)),
            pltpu.SemaphoreType.DMA((4, 3)),
            pltpu.SemaphoreType.DMA((4, 4)),
            pltpu.SemaphoreType.DMA,
            pltpu.SemaphoreType.DMA,
            pltpu.SemaphoreType.DMA,
        ],
        compiler_params=pltpu.CompilerParams(
            collective_id=2, has_side_effects=True, vmem_limit_bytes=32 * MIB
        ),
    )(lead, mask, norms, weights, wo)


def factor_kernel(fac_ref, qkv_ref, out_ref, in_ref, back_ref, sib_buf, block, full, tmp, *sems):
    p = Place()
    greet(gather_peers(p))
    lead2 = block.shape[0]
    lead = lead2 // 2
    copy = remote(fac_ref, sib_buf, sems[4], sems[5], p.sib)
    copy.start()
    copy.wait()
    block[rows_at(p.core * lead, lead, 16), :] = fac_ref[...]
    block[rows_at((1 - p.core) * lead, lead, 16), :] = sib_buf[...]
    width = full.shape[1]
    model = width // 4
    slab = model // 4
    key = rows_at((p.dp * 4 + p.z) * lead2, lead2, 16)
    mine = pltpu.make_async_copy(block, full.at[key], sems[6])
    mine.start()
    run_gathers([Gather(p, full, block, 0, width, 0, sems[:4], lead2)])
    mine.wait()

    def rows_of(z, at, size):
        return jnp.concatenate(
            [full[rows_at((i * 4 + z) * lead2, lead2, 16), pl.ds(at, size)] for i in range(4)], axis=0
        )

    base = 2 * model + 3 * slab
    mid = p.dp
    xl = rows_of(mid, base + slab, slab)
    nl = rows_of(mid, base + 2 * slab, slab)
    df = rows_of(mid, base + 3 * slab, slab)
    ctx = rows_of(mid, base + 4 * slab, slab)
    own = rows_at(p.fsdp * (ROWS // 2), ROWS // 2, 8)
    for z in range(4):
        tmp[:, :model] = mm(df, rows_of(z, 0, model), TN)
        back_ref[:, z * model : (z + 1) * model] = tmp[own, :model]
        tmp[:, :model] = mm(nl, rows_of(z, model, model), TN)
        in_ref[:, z * model : (z + 1) * model] = tmp[own, :model]
        tmp[:, : 3 * slab] = mm(xl, rows_of(z, 2 * model, 3 * slab), TN)
        got = tmp[own, : 3 * slab]
        for j in range(3):
            at = j * model + z * slab
            qkv_ref[:, at : at + slab] = got[:, j * slab : (j + 1) * slab]
        tmp[:, :slab] = mm(ctx, rows_of(z, base, slab), TN)
        out_ref[:, z * slab : (z + 1) * slab] = tmp[own, :slab]


def factor_grads(fac):
    lead, width = fac.shape
    model = width // 4
    half = ROWS // 2
    return pl.pallas_call(
        factor_kernel,
        out_shape=[
            jax.ShapeDtypeStruct((half, 3 * model), f32),
            jax.ShapeDtypeStruct((half, model), f32),
            jax.ShapeDtypeStruct((half, width), f32),
            jax.ShapeDtypeStruct((half, width), f32),
        ],
        in_specs=[pl.BlockSpec(memory_space=VM)],
        out_specs=[pl.BlockSpec(memory_space=VM)] * 4,
        scratch_shapes=[
            pltpu.VMEM((lead, width), bf16),
            pltpu.VMEM((2 * lead, width), bf16),
            pltpu.VMEM((32 * lead, width), bf16),
            pltpu.VMEM((model // 4, model), f32),
        ]
        + GATHER_SEMS(1)
        + [pltpu.SemaphoreType.DMA, pltpu.SemaphoreType.DMA, pltpu.SemaphoreType.DMA],
        compiler_params=pltpu.CompilerParams(
            collective_id=3, has_side_effects=True, vmem_limit_bytes=32 * MIB
        ),
    )(fac)


def matmul(left, right, form):
    return jnp.einsum(form, left, right, preferred_element_type=jnp.float32)


def norm_forward(summed, gains, biases):
    average = jnp.mean(summed, axis=-1, keepdims=True)
    centred = summed - average
    variance = jnp.mean(centred * centred, axis=-1, keepdims=True)
    inverse = lax.rsqrt(variance + epsilon)
    scaled = centred * inverse
    return (scaled * gains + biases, scaled, inverse)


def norm_backward(grad_result, scaled, inverse, gains):
    grad_scaled = grad_result * gains
    first_mean = jnp.mean(grad_scaled, axis=-1, keepdims=True)
    second_mean = jnp.mean(grad_scaled * scaled, axis=-1, keepdims=True)
    grad_sum = inverse * (grad_scaled - first_mean - scaled * second_mean)
    return (grad_sum, jnp.sum(grad_result * scaled, axis=(0, 1)), jnp.sum(grad_result, axis=(0, 1)))


def split_heads(packed):
    groups, length, model_width = packed.shape
    return packed.reshape(groups, length, HEADS, model_width // HEADS)


def join_heads(split_part):
    groups, length, heads_count, head_size = split_part.shape
    return split_part.reshape(groups, length, heads_count * head_size)


def attend_forward(query_part, key_part, value_part, allowed):
    head_size = query_part.shape[-1]
    scores = matmul(query_part, key_part, "glhe,gmhe->ghlm") * head_size ** (-0.5)
    scores = jnp.where(allowed[:, None], scores, -1e30)
    row_max = jnp.max(scores, axis=-1, keepdims=True)
    exp_terms = jnp.exp(scores - row_max)
    row_total = jnp.sum(exp_terms, axis=-1, keepdims=True)
    attention = exp_terms / row_total
    context = matmul(attention.astype(jnp.bfloat16), value_part, "ghlm,gmhe->glhe")
    return (join_heads(context).astype(jnp.bfloat16), row_max + jnp.log(row_total))


def attend_backward(query_part, key_part, value_part, allowed, log_total, grad_context):
    head_size = query_part.shape[-1]
    factor = head_size ** (-0.5)
    scores = matmul(query_part, key_part, "glhe,gmhe->ghlm") * factor
    scores = jnp.where(allowed[:, None], scores, -1e30)
    attention = jnp.exp(scores - log_total)
    grad_attention = matmul(grad_context, value_part, "glhe,gmhe->ghlm")
    grad_value = matmul(attention.astype(jnp.bfloat16), grad_context, "ghlm,glhe->gmhe")
    inner = jnp.sum(attention * grad_attention, axis=-1, keepdims=True)
    grad_scores = (attention * (grad_attention - inner)).astype(jnp.bfloat16)
    grad_query = matmul(grad_scores, key_part, "ghlm,gmhe->glhe") * factor
    grad_key = matmul(grad_scores, query_part, "ghlm,glhe->gmhe") * factor
    return (join_heads(grad_query), join_heads(grad_key), join_heads(grad_value))


def segment_attend(packed):
    groups, length, total_width = packed.shape
    model_width = total_width // 3
    allowed = jnp.ones((groups, length, length), dtype=jnp.bool_)
    context, log_total = attend_forward(
        split_heads(packed[..., :model_width]),
        split_heads(packed[..., model_width : 2 * model_width]),
        split_heads(packed[..., 2 * model_width :]),
        allowed,
    )
    return (context, log_total)


def segment_attend_back(packed, log_total, grad_context):
    groups, length, total_width = packed.shape
    model_width = total_width // 3
    allowed = jnp.ones((groups, length, length), dtype=jnp.bool_)
    grad_query, grad_key, grad_value = attend_backward(
        split_heads(packed[..., :model_width]),
        split_heads(packed[..., model_width : 2 * model_width]),
        split_heads(packed[..., 2 * model_width :]),
        allowed,
        log_total,
        split_heads(grad_context),
    )
    return jnp.concatenate([grad_query, grad_key, grad_value], axis=-1)


def cross_attend(packed, allowed):
    model_width = packed.shape[-1] // 3
    remote = lax.all_gather(packed[..., model_width:], "fsdp", axis=1, tiled=True)
    context, log_total = attend_forward(
        split_heads(packed[..., :model_width]),
        split_heads(remote[..., :model_width]),
        split_heads(remote[..., model_width:]),
        allowed,
    )
    return (context, (remote, log_total))


def cross_attend_back(packed, saved, grad_context, allowed):
    remote, log_total = saved
    model_width = packed.shape[-1] // 3
    grad_query, grad_key, grad_value = attend_backward(
        split_heads(packed[..., :model_width]),
        split_heads(remote[..., :model_width]),
        split_heads(remote[..., model_width:]),
        allowed,
        log_total,
        split_heads(grad_context),
    )
    shared = jnp.concatenate([grad_key, grad_value], axis=-1)
    own_part = lax.psum_scatter(
        shared.astype(jnp.bfloat16), "fsdp", scatter_dimension=1, tiled=True
    ).astype(jnp.float32)
    return jnp.concatenate([grad_query, own_part], axis=-1)


def block_forward(states, weights, attend):
    w_qkv, w_out, w_in, w_back, gains, biases = weights
    gains = gains.astype(jnp.float32)
    biases = biases.astype(jnp.float32)
    states_low = states.astype(jnp.bfloat16)
    packed = matmul(states_low, w_qkv, "gld,de->gle").astype(jnp.bfloat16)
    context, saved = attend(packed)
    branch = matmul(context, w_out, "gld,de->gle")
    normed, scaled_one, inverse_one = norm_forward(states + branch, gains[0], biases[0])
    normed_low = normed.astype(jnp.bfloat16)
    hidden = matmul(normed_low, w_in, "gld,df->glf")
    active_low = jax.nn.gelu(hidden, approximate=False).astype(jnp.bfloat16)
    feed_out = matmul(active_low, w_back, "glf,fd->gld")
    result, scaled_two, inverse_two = norm_forward(normed + feed_out, gains[1], biases[1])
    kept = (
        states_low,
        packed,
        context,
        saved,
        scaled_one,
        inverse_one,
        normed_low,
        hidden,
        active_low,
        scaled_two,
        inverse_two,
    )
    return (result, kept)


def block_backward(grad_result, kept, weights, attend_back):
    w_qkv, w_out, w_in, w_back, gains, biases = weights
    gains = gains.astype(jnp.float32)
    (
        states_low,
        packed,
        context,
        saved,
        scaled_one,
        inverse_one,
        normed_low,
        hidden,
        active_low,
        scaled_two,
        inverse_two,
    ) = kept
    grad_sum_two, gain_two, bias_two = norm_backward(grad_result, scaled_two, inverse_two, gains[1])
    grad_feed = grad_sum_two.astype(jnp.bfloat16)
    grad_active = matmul(grad_feed, w_back, "gld,fd->glf")
    cumulative = 0.5 * (1.0 + lax.erf(hidden * root_half))
    slope = cumulative + hidden * inv_root_tau * jnp.exp(-0.5 * hidden * hidden)
    grad_hidden = (grad_active * slope).astype(jnp.bfloat16)
    grad_normed = grad_sum_two + matmul(grad_hidden, w_in, "glf,df->gld")
    grad_sum_one, gain_one, bias_one = norm_backward(grad_normed, scaled_one, inverse_one, gains[0])
    grad_branch = grad_sum_one.astype(jnp.bfloat16)
    grad_context = matmul(grad_branch, w_out, "gle,de->gld").astype(jnp.bfloat16)
    grad_packed = attend_back(packed, saved, grad_context).astype(jnp.bfloat16)
    grad_states = grad_sum_one + matmul(grad_packed, w_qkv, "gle,de->gld")
    factors = (
        states_low,
        grad_packed,
        context,
        grad_branch,
        normed_low,
        grad_hidden,
        grad_feed,
        active_low,
    )
    smalls = (jnp.stack([gain_one, gain_two]), jnp.stack([bias_one, bias_two]))
    return (grad_states, factors, smalls)


def weight_terms(factors):
    (
        states_low,
        grad_packed,
        context,
        grad_branch,
        normed_low,
        grad_hidden,
        grad_feed,
        active_low,
    ) = factors
    term_qkv = matmul(states_low, grad_packed, "gld,gle->de")
    term_out = matmul(context, grad_branch, "gld,gle->de")
    term_in = matmul(normed_low, grad_hidden, "gld,glf->df")
    term_back = matmul(grad_feed, active_low, "gld,glf->df")
    return jnp.concatenate([term_qkv, term_out, term_in, term_back], axis=1)


def gather_segment(w_qkv, w_out, w_in, w_back, norm_gain, norm_bias):
    return (
        lax.all_gather(w_qkv[0], ("dp", "fsdp"), axis=0, tiled=True),
        lax.all_gather(w_out[0], ("dp", "fsdp"), axis=0, tiled=True),
        lax.all_gather(w_in[0], ("dp", "fsdp"), axis=0, tiled=True),
        lax.all_gather(w_back[0], ("dp", "fsdp"), axis=1, tiled=True),
        lax.all_gather(norm_gain[0], ("dp", "fsdp"), axis=1, tiled=True),
        lax.all_gather(norm_bias[0], ("dp", "fsdp"), axis=1, tiled=True),
    )


def gather_cross(pos_embed, w_qkv, w_out, w_in, w_back, norm_gain, norm_bias):
    gathered = (
        lax.all_gather(w_qkv[1], ("dp", "fsdp"), axis=0, tiled=True),
        lax.all_gather(w_out[1], ("dp", "fsdp"), axis=0, tiled=True),
        lax.all_gather(w_in[1], ("dp", "fsdp"), axis=0, tiled=True),
        lax.all_gather(w_back[1], ("dp", "fsdp"), axis=1, tiled=True),
        lax.all_gather(norm_gain[1], ("dp", "fsdp"), axis=1, tiled=True),
        lax.all_gather(norm_bias[1], ("dp", "fsdp"), axis=1, tiled=True),
        lax.all_gather(pos_embed, ("dp", "fsdp"), axis=1, tiled=True),
    )
    return (gathered[:6], gathered[6])


def layer_forward(tokens, doc_ids, seg_weights, cross_weights, pos_full):
    rows, local_len, model_width = tokens.shape
    seg_count = local_len // SEG_LEN
    segments = tokens.reshape(rows * seg_count, SEG_LEN, model_width).astype(jnp.float32)
    seg_out, seg_kept = block_forward(segments, seg_weights, segment_attend)
    start = lax.axis_index("fsdp") * seg_count
    pos_local = lax.dynamic_slice_in_dim(pos_full, start, seg_count, 0).astype(jnp.float32)
    leaders = seg_out[:, 0, :].reshape(rows, seg_count, model_width) + pos_local
    own_docs = lax.dynamic_slice_in_dim(doc_ids, start, seg_count, 1)
    allowed = own_docs[:, :, None] == doc_ids[:, None, :]
    cross_out, cross_kept = block_forward(
        leaders, cross_weights, partial(cross_attend, allowed=allowed)
    )
    joined = jnp.concatenate(
        [cross_out.reshape(rows * seg_count, 1, model_width), seg_out[:, 1:, :]], axis=1
    )
    output = joined.reshape(rows, local_len, model_width).astype(jnp.bfloat16)
    return (output, (seg_kept, cross_kept, allowed))


def layer_backward(cotangent, doc_ids, kept, seg_weights, cross_weights):
    seg_kept, cross_kept, allowed = kept
    rows, local_len, model_width = cotangent.shape
    seg_count = local_len // SEG_LEN
    grad_all = cotangent.reshape(rows * seg_count, SEG_LEN, model_width).astype(jnp.float32)
    grad_cross = grad_all[:, 0, :].reshape(rows, seg_count, model_width)
    grad_leaders, cross_factors, cross_smalls = block_backward(
        grad_cross, cross_kept, cross_weights, partial(cross_attend_back, allowed=allowed)
    )
    start = lax.axis_index("fsdp") * seg_count
    empty_pos = jnp.zeros((doc_ids.shape[1], model_width), jnp.float32)
    grad_pos = lax.dynamic_update_slice_in_dim(empty_pos, jnp.sum(grad_leaders, axis=0), start, 0)
    grad_seg = jnp.concatenate(
        [grad_leaders.reshape(rows * seg_count, 1, model_width), grad_all[:, 1:, :]], axis=1
    )
    grad_states, seg_factors, seg_smalls = block_backward(
        grad_seg, seg_kept, seg_weights, segment_attend_back
    )
    grad_tokens = grad_states.reshape(rows, local_len, model_width).astype(jnp.bfloat16)
    return (grad_tokens, seg_factors, cross_factors, seg_smalls, cross_smalls, grad_pos)


def body(tokens, doc_ids, pos_embed, w_qkv, w_out, w_in, w_back, norm_gain, norm_bias, cotangent):
    seg_weights = gather_segment(w_qkv, w_out, w_in, w_back, norm_gain, norm_bias)
    cross_weights, pos_full = gather_cross(
        pos_embed, w_qkv, w_out, w_in, w_back, norm_gain, norm_bias
    )
    output, kept = layer_forward(tokens, doc_ids, seg_weights, cross_weights, pos_full)
    grad_tokens, seg_factors, cross_factors, seg_smalls, cross_smalls, grad_pos = layer_backward(
        cotangent, doc_ids, kept, seg_weights, cross_weights
    )
    model_width = tokens.shape[2]
    hidden_width = w_in.shape[2]
    seg_term = lax.psum_scatter(
        weight_terms(seg_factors), ("dp", "fsdp"), scatter_dimension=0, tiled=True
    )
    cross_term = lax.psum_scatter(
        weight_terms(cross_factors), ("dp", "fsdp"), scatter_dimension=0, tiled=True
    )
    stacked = jnp.stack([seg_term, cross_term])
    grad_qkv = stacked[:, :, : 3 * model_width]
    grad_out = stacked[:, :, 3 * model_width : 4 * model_width]
    grad_in = stacked[:, :, 4 * model_width : 4 * model_width + hidden_width]
    grad_back = jnp.transpose(stacked[:, :, 4 * model_width + hidden_width :], (0, 2, 1))
    gain_all = jnp.stack([seg_smalls[0], cross_smalls[0]])
    bias_all = jnp.stack([seg_smalls[1], cross_smalls[1]])
    grad_gain, grad_bias, pos_shard = (
        lax.psum_scatter(gain_all, ("dp", "fsdp"), scatter_dimension=2, tiled=True),
        lax.psum_scatter(bias_all, ("dp", "fsdp"), scatter_dimension=2, tiled=True),
        lax.psum_scatter(grad_pos, ("dp", "fsdp"), scatter_dimension=1, tiled=True),
    )
    return (
        output,
        grad_tokens,
        pos_shard,
        grad_qkv,
        grad_out,
        grad_in,
        grad_back,
        grad_gain,
        grad_bias,
    )


def block_backward_terms(factors):
    (
        states_low,
        grad_packed,
        context,
        grad_branch,
        normed_low,
        grad_hidden,
        grad_feed,
        active_low,
    ) = factors
    return (
        matmul(grad_feed, active_low, "gld,glf->df").astype(bf16),
        matmul(normed_low, grad_hidden, "gld,glf->df").astype(bf16),
        matmul(context, grad_branch, "gld,gle->de").astype(bf16),
        matmul(states_low, grad_packed, "gld,gle->de").astype(bf16),
    )


def make_pack(pos_embed, w_qkv, w_out, w_in, w_back, norm_gain, norm_bias):
    own, width = w_out.shape[1:]
    slab = width // 4
    items = jnp.concatenate([norm_gain[0], norm_bias[0], norm_gain[1], norm_bias[1], pos_embed], axis=0)
    small = jnp.pad(items.T, ((0, 0), (0, 256 - items.shape[0])))
    cross = jnp.concatenate(
        [
            w_qkv[1].reshape(own, 3, 4, slab).transpose(0, 2, 1, 3).reshape(own, 4, 3 * slab),
            w_in[1].reshape(own, 4, width),
            w_back[1].T.reshape(own, 4, width),
            jnp.zeros((own, 4, slab), bf16),
        ],
        axis=2,
    ).reshape(own, 12 * width)
    pack = jnp.concatenate(
        [w_qkv[0], small, w_out[0], w_in[0], w_back[0].T, cross, w_out[1]], axis=1
    )
    return jnp.pad(pack, ((0, 32 - own), (0, 0)))


def fast_body(tokens, doc_ids, pos_embed, w_qkv, w_out, w_in, w_back, norm_gain, norm_bias, cotangent):
    rows, local_len, width = tokens.shape
    seg_count = local_len // SEG_LEN
    hidden = w_in.shape[2]
    pack = make_pack(pos_embed, w_qkv, w_out, w_in, w_back, norm_gain, norm_bias)
    seg_qkv, small, seg_out_w, seg_in, seg_back, cross_w, cross_wo = gather_weights(
        pack, (3 * width, 256, width, hidden, hidden), 3 * width, width
    )
    items = small.T.astype(f32)
    seg_weights = (seg_qkv, seg_out_w, seg_in, seg_back.T, items[0:2], items[2:4])
    cross_norms = jnp.concatenate([items[4:8], jnp.zeros((4, width), f32)], axis=0)
    pos_full = items[8 : 8 + doc_ids.shape[1]]

    segments = tokens.reshape(rows * seg_count, SEG_LEN, width).astype(f32)
    seg_out, seg_kept = block_forward(segments, seg_weights, segment_attend)
    start = lax.axis_index("fsdp") * seg_count
    pos_local = lax.dynamic_slice_in_dim(pos_full, start, seg_count, 0)
    leaders = seg_out[:, 0, :].reshape(rows, seg_count, width) + pos_local
    grad_all = cotangent.reshape(rows * seg_count, SEG_LEN, width).astype(f32)
    grad_cross = grad_all[:, 0, :].reshape(rows, seg_count, width)
    own_row = lax.dynamic_index_in_dim(doc_ids, lax.axis_index("fsdp") % 2, 0, keepdims=False)
    mask = (own_row[:, None] == own_row[None, :]).astype(f32)
    home, fac, cross_small = cross_block(
        jnp.concatenate([leaders, grad_cross], axis=2), mask, cross_norms, cross_w, cross_wo
    )
    cross_out, grad_leaders = home[..., :width], home[..., width:]
    joined = jnp.concatenate(
        [cross_out.reshape(rows * seg_count, 1, width), seg_out[:, 1:, :]], axis=1
    )
    output = joined.reshape(rows, local_len, width).astype(bf16)
    crs_qkv, crs_out, crs_in, crs_back = factor_grads(fac)

    empty_pos = jnp.zeros((doc_ids.shape[1], width), f32)
    grad_pos = lax.dynamic_update_slice_in_dim(empty_pos, jnp.sum(grad_leaders, axis=0), start, 0)
    grad_seg = jnp.concatenate(
        [grad_leaders.reshape(rows * seg_count, 1, width), grad_all[:, 1:, :]], axis=1
    )
    grad_states, factors, smalls = block_backward(
        grad_seg, seg_kept, seg_weights, segment_attend_back
    )
    grad_tokens = grad_states.reshape(rows, local_len, width).astype(bf16)
    small_rows = jnp.concatenate([smalls[0], smalls[1], cross_small[:4], grad_pos], axis=0)
    small_grads = jnp.pad(small_rows.astype(bf16), ((0, 256 - small_rows.shape[0]), (0, 0))).T
    terms = block_backward_terms(factors)
    t_back, t_in, t_out, t_qkv, t_small = scatter_grads((*terms, small_grads))
    s = t_small.T
    grad_gain = jnp.stack([s[0:2], s[4:6]])
    grad_bias = jnp.stack([s[2:4], s[6:8]])
    return (
        output,
        grad_tokens,
        s[8 : 8 + doc_ids.shape[1]],
        jnp.stack([t_qkv, crs_qkv]),
        jnp.stack([t_out, crs_out]),
        jnp.stack([t_in, crs_in]),
        jnp.stack([t_back.T, crs_back.T]),
        grad_gain,
        grad_bias,
    )


def solution(mesh):
    fast = dict(mesh.shape) == {"dp": 4, "fsdp": 8}
    return jax.shard_map(
        fast_body if fast else body,
        mesh=mesh,
        in_specs=(
            P("dp", "fsdp", None),
            P("dp", None),
            P(None, ("dp", "fsdp")),
            P(None, ("dp", "fsdp"), None),
            P(None, ("dp", "fsdp"), None),
            P(None, ("dp", "fsdp"), None),
            P(None, None, ("dp", "fsdp")),
            P(None, None, ("dp", "fsdp")),
            P(None, None, ("dp", "fsdp")),
            P("dp", "fsdp", None),
        ),
        out_specs=(
            P("dp", "fsdp", None),
            P("dp", "fsdp", None),
            P(None, ("dp", "fsdp")),
            P(None, ("dp", "fsdp"), None),
            P(None, ("dp", "fsdp"), None),
            P(None, ("dp", "fsdp"), None),
            P(None, None, ("dp", "fsdp")),
            P(None, None, ("dp", "fsdp")),
            P(None, None, ("dp", "fsdp")),
        ),
        check_vma=False,
    )
```

```python
from functools import partial

import jax
import jax.numpy as jnp
from jax import lax
from jax.experimental import pallas as pl
from jax.experimental.pallas import tpu as pltpu
from jax.sharding import PartitionSpec as P

HEADS = 12
SEG_LEN = 128


epsilon = 1e-05
root_half = 0.7071067811865476
inv_root_tau = 0.3989422804014327

bf16 = jnp.bfloat16
f32 = jnp.float32
MESH = pl.DeviceIdType.MESH
VM = pltpu.VMEM
MIB = 1024 * 1024
ROWS = 48
LANES = 128


class Place:
    def __init__(self):
        self.dp = lax.axis_index("dp")
        self.fsdp = lax.axis_index("fsdp")
        self.y, self.x = self.dp // 2, self.dp % 2
        self.z, self.core = self.fsdp // 2, self.fsdp % 2

    def at(self, dp, z, core):
        return (dp, z * 2 + core)

    @property
    def sib(self):
        return (self.dp, self.z * 2 + 1 - self.core)

    @property
    def xdp(self):
        return self.y * 2 + 1 - self.x

    @property
    def ydp(self):
        return (1 - self.y) * 2 + self.x

    @property
    def xnbr(self):
        return (self.xdp, self.fsdp)

    @property
    def ynbr(self):
        return (self.ydp, self.fsdp)


def greet(devices):
    barrier = pltpu.get_barrier_semaphore()
    for device in devices:
        pl.semaphore_signal(barrier, inc=1, device_id=device, device_id_type=MESH)
    pl.semaphore_wait(barrier, len(devices))


def remote(src, dst, send, recv, device):
    return pltpu.make_async_remote_copy(
        src_ref=src, dst_ref=dst, send_sem=send, recv_sem=recv, device_id=device, device_id_type=MESH
    )


def lanes(start, size):
    if isinstance(start, int):
        return pl.ds(start, size)
    return pl.ds(pl.multiple_of(start, LANES), size)


def rows_at(start, size, unit):
    return pl.ds(pl.multiple_of(start, unit), size)


class Gather:
    def __init__(self, place, out, block, start, width, index, sems, height2, slabs=False):
        self.p, self.out, self.block, self.start, self.width = place, out, block, start, width
        self.m, self.sems, self.h2, self.slabs = index, sems, height2, slabs
        self.half = width // 2
        tiles = self.half // LANES
        self.a = (tiles + 1) // 2 * LANES
        self.b = self.half - self.a
        self.sent = []

    def col(self, core, part):
        base = core * self.half
        if part == "A":
            return base, self.a
        if part == "B":
            return base + self.a, self.b
        return base, self.half

    def dst(self, dp, z, core, part, count=1):
        base, size = self.col(core, part)
        return self.out.at[rows_at((dp * 4 + z) * self.h2, self.h2 * count, 16), lanes(base, size)]

    def own(self, part, z=None):
        base, size = self.col(self.p.core, part)
        start = self.start + base
        if self.slabs:
            start = start + (self.p.z if z is None else z) * self.width
        return self.block.at[:, lanes(start, size)]

    def go(self, src, dst, slot, device, link=True):
        send, recv = (self.sems[0], self.sems[1]) if link else (self.sems[2], self.sems[3])
        copy = remote(src, dst, send.at[self.m, slot], recv.at[self.m, slot], device)
        copy.start()
        self.sent.append(copy)

    def arrived(self, dst, slot, link=True):
        send, recv = (self.sems[0], self.sems[1]) if link else (self.sems[2], self.sems[3])
        remote(dst, dst, send.at[self.m, slot], recv.at[self.m, slot], self.p.sib).wait_recv()

    def spread(self, src_of, z, d):
        p = self.p
        core = p.core
        self.go(src_of("A"), self.dst(p.dp, z, core, "A"), 3 + d, p.xnbr)
        if self.b:
            self.go(src_of("B"), self.dst(p.dp, z, core, "B"), 15 + d, p.ynbr)
        self.go(src_of("A"), self.dst(p.dp, z, core, "A"), 7 + d, p.ynbr)
        if self.b:
            self.go(src_of("B"), self.dst(p.dp, z, core, "B"), 19 + d, p.xnbr)

    def send_own(self):
        p = self.p
        for d in (1, 3, 2):
            z = (p.z + d) % 4
            self.go(self.own("AB", z), self.dst(p.dp, p.z, p.core, "AB"), d - 1, p.at(p.dp, z, p.core))
        self.spread(self.own, p.z, 0)

    def pass_line(self):
        p = self.p
        for d in (1, 3, 2):
            z = (p.z + 4 - d) % 4
            self.arrived(self.dst(p.dp, z, p.core, "AB"), d - 1)
            self.spread(lambda part: self.dst(p.dp, z, p.core, part), z, d)
        line = self.dst(p.dp, 0, p.core, "AB", 4)
        for d in (1, 2, 3):
            z = (p.z + 4 - d) % 4
            block = self.dst(p.dp, z, p.core, "AB")
            self.go(block, block, 4 + d, p.sib, link=False)

    def pass_plane(self):
        p = self.p
        for d in (0, 1, 3, 2):
            z = (p.z + 4 - d) % 4
            block = self.dst(p.xdp, z, p.core, "A")
            self.arrived(block, 3 + d)
            self.go(block, block, 11 + d, p.ynbr)
            if self.b:
                block = self.dst(p.ydp, z, p.core, "B")
                self.arrived(block, 15 + d)
                self.go(block, block, 23 + d, p.xnbr)
        block = self.dst(p.xdp, 0, p.core, "A", 4)
        self.go(block, block, 0, p.sib, link=False)
        if self.b:
            block = self.dst(p.ydp, 0, p.core, "B", 4)
            self.go(block, block, 1, p.sib, link=False)

    def last(self):
        p = self.p
        core, other = p.core, 1 - p.core
        far = (1 - p.y) * 2 + 1 - p.x
        for d in range(4):
            z = (p.z + 4 - d) % 4
            self.arrived(self.dst(p.ydp, z, core, "A"), 7 + d)
            if self.b:
                self.arrived(self.dst(p.xdp, z, core, "B"), 19 + d)
        block = self.dst(p.ydp, 0, core, "A", 4)
        self.go(block, block, 2, p.sib, link=False)
        if self.b:
            block = self.dst(p.xdp, 0, core, "B", 4)
            self.go(block, block, 3, p.sib, link=False)
        for d in range(4):
            z = (p.z + 4 - d) % 4
            self.arrived(self.dst(far, z, core, "A"), 11 + d)
            if self.b:
                self.arrived(self.dst(far, z, core, "B"), 23 + d)
        block = self.dst(far, 0, core, "AB" if self.b else "A", 4)
        self.go(block, block, 4, p.sib, link=False)

    def drain(self):
        p = self.p
        other = 1 - p.core
        far = (1 - p.y) * 2 + 1 - p.x
        for d in (1, 2, 3):
            z = (p.z + 4 - d) % 4
            self.arrived(self.dst(p.dp, z, other, "AB"), 4 + d, link=False)
        self.arrived(self.dst(p.xdp, 0, other, "A", 4), 0, link=False)
        if self.b:
            self.arrived(self.dst(p.ydp, 0, other, "B", 4), 1, link=False)
        self.arrived(self.dst(p.ydp, 0, other, "A", 4), 2, link=False)
        if self.b:
            self.arrived(self.dst(p.xdp, 0, other, "B", 4), 3, link=False)
        self.arrived(self.dst(far, 0, other, "AB" if self.b else "A", 4), 4, link=False)

    def finish(self):
        for copy in self.sent:
            copy.wait_send()


def run_gathers(gathers):
    n = len(gathers)
    for step in range(n + 3):
        if step < n:
            gathers[step].send_own()
        if 0 <= step - 1 < n:
            gathers[step - 1].pass_line()
            gathers[step - 1].pass_plane()
        if 0 <= step - 2 < n:
            gathers[step - 2].last()
        if 0 <= step - 3 < n:
            gathers[step - 3].drain()
    for g in gathers:
        g.finish()


def gather_peers(p):
    peers = [p.sib, p.xnbr, p.ynbr]
    for d in (1, 2, 3):
        peers.append(p.at(p.dp, (p.z + d) % 4, p.core))
    return peers


def everyone(p):
    return [
        (lax.rem(p.dp + i, 4), lax.rem(p.fsdp + j, 8)) for i in range(4) for j in range(8) if i or j
    ]


GATHER_SEMS = lambda n: [
    pltpu.SemaphoreType.DMA((n, 27)),
    pltpu.SemaphoreType.DMA((n, 27)),
    pltpu.SemaphoreType.DMA((n, 8)),
    pltpu.SemaphoreType.DMA((n, 8)),
]


NEG = -1e30


def mm(a, b, dims):
    return lax.dot_general(a, b, (dims, ((), ())), preferred_element_type=f32)


NN = ((1,), (0,))
NT = ((1,), (1,))
TN = ((0,), (0,))


def norm_rows(summed, gain, bias):
    centred = summed - jnp.mean(summed, axis=-1, keepdims=True)
    variance = jnp.mean(centred * centred, axis=-1, keepdims=True)
    inverse = lax.rsqrt(variance + epsilon)
    scaled = centred * inverse
    return scaled * gain + bias, scaled, inverse


def norm_rows_back(grad, scaled, inverse, gain):
    g = grad * gain
    first = jnp.mean(g, axis=-1, keepdims=True)
    second = jnp.mean(g * scaled, axis=-1, keepdims=True)
    return inverse * (g - first - scaled * second)


def gelu_parts(u):
    cumulative = 0.5 * (1.0 + lax.erf(u * root_half))
    return cumulative, cumulative + u * inv_root_tau * jnp.exp(-0.5 * u * u)


def cross_kernel(
    lead_ref, mask_ref, norm_ref, w_ref, wo_ref, home_ref, fac_ref, small_ref,
    gbuf, lead, xbuf, ybuf, dpack, g_send, g_recv, x_send, x_recv, h_send, h_recv, local,
):
    p = Place()
    group = [(p.dp, lax.rem(p.fsdp + j, 8)) for j in range(1, 8)]
    greet(group)
    width = lead_ref.shape[2] // 2
    slab = width // 4
    head = width // HEADS
    heads = HEADS // 4

    def lead_copy(z, j):
        i = 2 * z + j
        return remote(lead_ref.at[j], gbuf.at[p.fsdp], g_send.at[i], g_recv.at[p.fsdp], (p.dp, i))

    for d in range(4):
        z = (p.z + d) % 4
        for j in range(2):
            here = jnp.logical_and(p.z == z, p.core == j) if d == 0 else None
            if d:
                lead_copy(z, j).start()
            else:

                @pl.when(p.core != j)
                def _():
                    lead_copy(z, j).start()

                @pl.when(p.core == j)
                def _():
                    mine = pltpu.make_async_copy(lead_ref.at[j], gbuf.at[p.fsdp], local)
                    mine.start()
                    mine.wait()

    for d in range(1, 8):
        i = lax.rem(p.fsdp + d, 8)
        remote(gbuf.at[i], gbuf.at[i], g_send.at[i], g_recv.at[i], p.sib).wait_recv()
    for i in range(8):
        lead[2 * i : 2 * i + 2, :] = gbuf[i]
    states = lead[:, :width]
    cot = lead[:, width:]

    def sum_z(e, partial_sum):
        xbuf[e, p.z] = partial_sum.astype(bf16)
        copies = []
        for d in (1, 3, 2):
            z = (p.z + d) % 4
            copy = remote(
                xbuf.at[e, p.z], xbuf.at[e, p.z], x_send.at[e, d - 1], x_recv.at[e, p.z],
                p.at(p.dp, z, p.core),
            )
            copy.start()
            copies.append(copy)
        for d in (1, 3, 2):
            z = (p.z + d) % 4
            piece = xbuf.at[e, z]
            remote(piece, piece, x_send.at[e, d - 1], x_recv.at[e, z], p.sib).wait_recv()
        for copy in copies:
            copy.wait_send()
        return sum(xbuf[e, z].astype(f32) for z in range(4))

    gain0, gain1 = norm_ref[0:1, :], norm_ref[1:2, :]
    bias0, bias1 = norm_ref[2:3, :], norm_ref[3:4, :]
    in_cols, back_cols = pl.ds(3 * slab, width), pl.ds(3 * slab + width, width)
    qkv_cols = pl.ds(0, 3 * slab)
    factor = head ** (-0.5)
    allowed = mask_ref[...] > 0.5

    xl = states.astype(bf16)
    packed = mm(xl, w_ref[:, qkv_cols], NN).astype(bf16)
    q = [packed[:, i * head : (i + 1) * head] for i in range(heads)]
    k = [packed[:, slab + i * head : slab + (i + 1) * head] for i in range(heads)]
    v = [packed[:, 2 * slab + i * head : 2 * slab + (i + 1) * head] for i in range(heads)]
    att, context = [], []
    for i in range(heads):
        scores = jnp.where(allowed, mm(q[i], k[i], NT) * factor, NEG)
        top = jnp.max(scores, axis=-1, keepdims=True)
        terms = jnp.exp(scores - top)
        a = terms / jnp.sum(terms, axis=-1, keepdims=True)
        att.append(a)
        context.append(mm(a.astype(bf16), v[i], NN))
    context = jnp.concatenate(context, axis=1).astype(bf16)
    branch = sum_z(0, mm(context, wo_ref[...], NN))
    normed, z_one, r_one = norm_rows(states + branch, gain0, bias0)
    nl = normed.astype(bf16)
    hidden = mm(nl, w_ref[:, in_cols], NN)
    phi, slope = gelu_parts(hidden)
    active = (hidden * phi).astype(bf16)
    feed = sum_z(1, mm(active, w_ref[:, back_cols], NT))
    result, z_two, r_two = norm_rows(normed + feed, gain1, bias1)
    d_two = norm_rows_back(cot, z_two, r_two, gain1)
    df = d_two.astype(bf16)
    du = (mm(df, w_ref[:, back_cols], NN) * slope).astype(bf16)
    d_normed = d_two + sum_z(2, mm(du, w_ref[:, in_cols], NT))
    d_one = norm_rows_back(d_normed, z_one, r_one, gain0)
    db = d_one.astype(bf16)
    dc = mm(db, wo_ref[...], NT).astype(bf16)
    for i in range(heads):
        a = att[i]
        dci = dc[:, i * head : (i + 1) * head]
        da = mm(dci, v[i], NT)
        dv = mm(a.astype(bf16), dci, TN)
        ds = (a * (da - jnp.sum(a * da, axis=-1, keepdims=True))).astype(bf16)
        dq = mm(ds, k[i], NN) * factor
        dk = mm(ds, q[i], TN) * factor
        for j, piece in enumerate((dq, dk, dv)):
            dpack[:, j * slab + i * head : j * slab + (i + 1) * head] = piece
    dp = dpack[...].astype(bf16)
    dx = d_one + sum_z(3, mm(dp, w_ref[:, qkv_cols], NT))
    for i in range(8):
        ybuf[i, :, :width] = result[2 * i : 2 * i + 2]
        ybuf[i, :, width:] = dx[2 * i : 2 * i + 2]
    home = remote(
        ybuf.at[2 * p.z + 1 - p.core], home_ref.at[p.core], h_send, h_recv, p.sib
    )
    home.start()
    home_ref[p.core] = ybuf[2 * p.z + p.core]

    def part(full):
        pieces = [full[:, i * slab : (i + 1) * slab] for i in range(4)]
        out = pieces[0]
        for i in range(1, 4):
            out = jnp.where(p.z == i, pieces[i], out)
        return out.astype(bf16)

    fac_ref[:, :width] = active
    fac_ref[:, width : 2 * width] = du
    fac_ref[:, 2 * width :] = jnp.concatenate(
        [dp, part(d_one), part(states), part(normed), part(d_two), context], axis=1
    )
    once = jnp.where(p.z == 0, 1.0, 0.0)
    sums = [d_normed * z_one, cot * z_two, d_normed, cot]
    small_ref[...] = jnp.zeros_like(small_ref)
    for i, s in enumerate(sums):
        small_ref[i : i + 1, :] = once * jnp.sum(s, axis=0, keepdims=True)
    theirs = home_ref.at[1 - p.core]
    remote(theirs, theirs, h_send, h_recv, p.sib).wait_recv()
    home.wait_send()
    for d in range(4):
        z = (p.z + d) % 4
        for j in range(2):
            if d:
                lead_copy(z, j).wait_send()
            else:

                @pl.when(p.core != j)
                def _():
                    lead_copy(z, j).wait_send()


def cross_block(lead, mask, norms, weights, wo):
    width = wo.shape[1]
    segs = mask.shape[0]
    return pl.pallas_call(
        cross_kernel,
        out_shape=[
            jax.ShapeDtypeStruct((2, 2, 2 * width), f32),
            jax.ShapeDtypeStruct((segs, 4 * width), bf16),
            jax.ShapeDtypeStruct((8, width), f32),
        ],
        in_specs=[pl.BlockSpec(memory_space=VM)] * 5,
        out_specs=[pl.BlockSpec(memory_space=VM)] * 3,
        scratch_shapes=[
            pltpu.VMEM((8, 2, 2 * width), f32),
            pltpu.VMEM((segs, 2 * width), f32),
            pltpu.VMEM((4, 4, segs, width), bf16),
            pltpu.VMEM((8, 2, 2 * width), f32),
            pltpu.VMEM((segs, 3 * width // 4), f32),
            pltpu.SemaphoreType.DMA((8,)),
            pltpu.SemaphoreType.DMA((8,)),
            pltpu.SemaphoreType.DMA((4, 3)),
            pltpu.SemaphoreType.DMA((4, 4)),
            pltpu.SemaphoreType.DMA,
            pltpu.SemaphoreType.DMA,
            pltpu.SemaphoreType.DMA,
        ],
        compiler_params=pltpu.CompilerParams(
            collective_id=2, has_side_effects=True, vmem_limit_bytes=32 * MIB
        ),
    )(lead, mask, norms, weights, wo)


def lane_halves(v):
    low = lax.broadcasted_iota(jnp.int32, v.shape, 1) < LANES // 2
    zero = jnp.zeros_like(v)
    return jnp.where(low, v, zero), jnp.where(low, zero, v)


def forward_kernel(widths, *refs):
    n = len(widths)
    pack_ref, x_ref, cot_ref = refs[:3]
    (
        w_hbm, i_hbm, o_hbm, b_hbm, cross_out, wo_out,
        p_hbm, a_hbm, c_hbm, nl_hbm, g_hbm, sl_hbm, z1_hbm, z2_hbm,
        y_ref, lead_ref, par_ref, r1_ref, r2_ref,
    ) = refs[3:22]
    (
        sw, ow, qw, iw, bw,
        pk, at, cx, h, nl, g, sl, z1, z2,
        sib_buf, block, s0, s1, s2, s3, pair_send, pair_recv, wo_send, wo_recv, local, out_sem,
    ) = refs[22:]
    p = Place()
    rows, width = x_ref.shape
    segs = rows // SEG_LEN
    hidden = iw.shape[1]
    pairs = width // LANES
    dests = (sw, qw, ow, iw, bw, cross_out)
    cw = cross_out.shape[1]
    sems = (s0, s1, s2, s3)
    starts, spot = [], 0
    for w in list(widths) + [4 * cw, wo_out.shape[1]]:
        starts.append((spot, w))
        spot += w
    greet(everyone(p))

    def pair(i):
        cols = pl.ds(*starts[i])
        return remote(
            pack_ref.at[:, cols], sib_buf.at[:, cols], pair_send.at[i], pair_recv.at[i], p.sib
        )

    for i in range(n + 2):
        pair(i).start()

    def join(i):
        pair(i).wait_recv()
        start, size = starts[i]
        first = p.core == 0
        half = ROWS // 2

        def chunk(spot, count):
            cols = lanes(spot, count)
            mine = pack_ref[:, cols].astype(f32)[:half]
            theirs = sib_buf[:, cols].astype(f32)[:half]
            both = [jnp.where(first, mine, theirs), jnp.where(first, theirs, mine)]
            block[:, cols] = jnp.concatenate(both, axis=0).astype(bf16)

        step = 768 if size % 768 == 0 else size

        @pl.loop(0, size // step)
        def _(k):
            chunk(start + k * step, step)

    gathers = []
    for i, w in enumerate(widths):
        gathers.append(Gather(p, dests[i], block, starts[i][0], w, i, sems, ROWS))
    gathers.append(Gather(p, cross_out, block, starts[n][0], cw, n, sems, ROWS, slabs=True))
    key = rows_at((p.dp * 4 + p.z) * ROWS, ROWS, 16)

    def own_copy(i):
        start = starts[i][0] + (p.z * cw if i == n else 0)
        return pltpu.make_async_copy(block.at[:, lanes(start, gathers[i].width)], dests[i].at[key], local.at[i])

    def own(i):
        join(i)
        own_copy(i).start()
        gathers[i].send_own()

    line = lambda i: gathers[i].pass_line()
    plane = lambda i: gathers[i].pass_plane()
    last = lambda i: gathers[i].last()

    def drain(i):
        gathers[i].drain()
        own_copy(i).wait()

    half_wo = wo_out.shape[1] // 2
    wo_src = block.at[:, lanes(starts[n + 1][0] + p.core * half_wo, half_wo)]
    wo_dst = wo_out.at[rows_at(p.z * ROWS, ROWS, 16), lanes(p.core * half_wo, half_wo)]

    def wo_copy(i):
        return remote(wo_src, wo_dst, wo_send.at[i], wo_recv.at[p.z], p.at(i, p.dp, p.core))

    def wo_start():
        join(n + 1)
        for i in range(4):
            here = jnp.logical_and(p.dp == i, p.dp == p.z)

            @pl.when(jnp.logical_not(here))
            def _():
                wo_copy(i).start()

            @pl.when(here)
            def _():
                mine = pltpu.make_async_copy(wo_src, wo_dst, local.at[n + 1])
                mine.start()
                mine.wait()

    def wo_finish():
        for i in range(4):
            piece = wo_out.at[pl.ds(i * ROWS, ROWS), lanes(p.core * half_wo, half_wo)]

            @pl.when(jnp.logical_not(jnp.logical_and(p.z == p.dp, p.z == i)))
            def _():
                remote(piece, piece, wo_send.at[i], wo_recv.at[i], p.sib).wait_recv()

        mine = wo_out.at[:, lanes(p.core * half_wo, half_wo)]
        theirs = wo_out.at[:, lanes((1 - p.core) * half_wo, half_wo)]
        copy = remote(mine, mine, wo_send.at[4], wo_recv.at[4], p.sib)
        copy.start()
        remote(theirs, theirs, wo_send.at[4], wo_recv.at[4], p.sib).wait_recv()
        copy.wait_send()
        for i in range(4):

            @pl.when(jnp.logical_not(jnp.logical_and(p.dp == i, p.dp == p.z)))
            def _():
                wo_copy(i).wait_send()

    kept = []

    def keep(src, dst):
        copy = pltpu.make_async_copy(src, dst, out_sem.at[len(kept)])
        copy.start()
        kept.append(copy)

    tile = 256

    def params():
        par_ref[...] = sw[...].astype(f32).T[: par_ref.shape[0]]

    def project():
        @pl.loop(0, 3 * width // tile)
        def _(i):
            cols = lanes(i * tile, tile)
            pk[:, cols] = mm(x_ref[...], qw[:, cols], NN).astype(bf16)

    def attend(s):
        key = pl.ds(s * SEG_LEN, SEG_LEN)

        @pl.loop(0, pairs)
        def _(j):
            q2 = pk[key, lanes(j * LANES, LANES)]
            k2 = pk[key, lanes(width + j * LANES, LANES)]
            v2 = pk[key, lanes(2 * width + j * LANES, LANES)]
            scores = mm(jnp.concatenate(lane_halves(q2), axis=0), k2, NT) * (LANES // 2) ** (-0.5)
            top = jnp.max(scores, axis=-1, keepdims=True)
            terms = jnp.exp(scores - top)
            a = (terms / jnp.sum(terms, axis=-1, keepdims=True)).astype(bf16)
            at[rows_at((s * pairs + j) * 2 * SEG_LEN, 2 * SEG_LEN, 16), :] = a
            both = jnp.concatenate([a[:SEG_LEN], a[SEG_LEN:]], axis=1)
            c2 = mm(both, jnp.concatenate(lane_halves(v2), axis=0), NN)
            cx[key, lanes(j * LANES, LANES)] = c2.astype(bf16)

    block_rows = 64

    def branch():
        @pl.loop(0, width // tile)
        def _(i):
            cols = lanes(i * tile, tile)
            h[:, cols] = x_ref[:, cols].astype(f32) + mm(cx[...], ow[:, cols], NN)

        @pl.loop(0, rows // block_rows)
        def _(i):
            key = rows_at(i * block_rows, block_rows, 16)
            normed, scaled, inverse = norm_rows(h[key, :], par_ref[0:1, :], par_ref[2:3, :])
            h[key, :] = normed
            nl[key, :] = normed.astype(bf16)
            z1[key, :] = scaled.astype(bf16)
            r1_ref[key, :] = jnp.broadcast_to(inverse, (block_rows, LANES))

    def feed_in(first, count):
        @pl.loop(first, first + count)
        def _(i):
            cols = lanes(i * tile, tile)
            u = mm(nl[...], iw[:, cols], NN)
            phi, slope = gelu_parts(u)
            g[:, cols] = (u * phi).astype(bf16)
            sl[:, cols] = slope.astype(bf16)

    def feed_back():
        @pl.loop(0, width // tile)
        def _(i):
            cols = lanes(i * tile, tile)
            h[:, cols] += mm(g[...], bw[rows_at(i * tile, tile, 16), :], NT)

        @pl.loop(0, rows // block_rows)
        def _(i):
            key = rows_at(i * block_rows, block_rows, 16)
            result, scaled, inverse = norm_rows(h[key, :], par_ref[1:2, :], par_ref[3:4, :])
            h[key, :] = result
            y_ref[key, :] = result.astype(bf16)
            z2[key, :] = scaled.astype(bf16)
            r2_ref[key, :] = jnp.broadcast_to(inverse, (block_rows, LANES))

        for s in range(segs):
            pos = par_ref[pl.ds(8 + p.fsdp * 2 + s % 2, 1), :]
            lead_ref[s // 2, s % 2 : s % 2 + 1, :width] = h[s * SEG_LEN : s * SEG_LEN + 1, :] + pos
            lead_ref[s // 2, s % 2 : s % 2 + 1, width:] = cot_ref[s * SEG_LEN : s * SEG_LEN + 16, :].astype(f32)[:1]

    chunks = hidden // tile
    own(0)
    own(1)
    own(2)
    line(0), plane(0)
    line(1), plane(1)
    own(3)
    line(2), plane(2)
    last(0), last(1), drain(0), drain(1)
    params()
    line(3)
    own(4)
    project()
    keep(qw, w_hbm), keep(pk, p_hbm)
    plane(3)
    attend(0)
    last(2), drain(2)
    line(4)
    attend(1)
    own(5)
    plane(4)
    attend(2)
    wo_start()
    line(5)
    attend(3)
    last(3)
    plane(5)
    keep(at, a_hbm), keep(cx, c_hbm)
    branch()
    keep(ow, o_hbm), keep(nl, nl_hbm), keep(z1, z1_hbm)
    drain(3)
    feed_in(0, chunks // 2)
    last(4)
    feed_in(chunks // 2, chunks - chunks // 2)
    keep(iw, i_hbm), keep(g, g_hbm), keep(sl, sl_hbm)
    drain(4)
    feed_back()
    keep(bw, b_hbm), keep(z2, z2_hbm)
    last(5)
    drain(5)
    wo_finish()
    for gather in gathers:
        gather.finish()
    for i in range(n + 2):
        pair(i).wait_send()
    for copy in kept:
        copy.wait()


def segment_forward(pack, x, cot, widths, cross_width, wo_width):
    n = len(widths)
    wrows = 16 * ROWS
    height, total = pack.shape
    rows, width = x.shape
    segs = rows // SEG_LEN
    hidden = widths[3]
    hbm, vm = pl.BlockSpec(memory_space=pl.ANY), pl.BlockSpec(memory_space=VM)
    arr = jax.ShapeDtypeStruct
    att_rows = segs * HEADS * SEG_LEN
    big = [
        arr((wrows, 3 * width), bf16), arr((wrows, hidden), bf16), arr((wrows, width), bf16),
        arr((wrows, hidden), bf16), arr((wrows, cross_width), bf16), arr((192, wo_width), bf16),
        arr((rows, 3 * width), bf16), arr((att_rows, SEG_LEN), bf16), arr((rows, width), bf16),
        arr((rows, width), bf16), arr((rows, hidden), bf16), arr((rows, hidden), bf16),
        arr((rows, width), bf16), arr((rows, width), bf16),
    ]
    near = [
        arr((rows, width), bf16), arr((2, 2, 2 * width), f32), arr((24, width), f32),
        arr((rows, LANES), f32), arr((rows, LANES), f32),
    ]
    return pl.pallas_call(
        partial(forward_kernel, widths),
        out_shape=big + near,
        in_specs=[vm] * 3,
        out_specs=[hbm] * len(big) + [vm] * len(near),
        scratch_shapes=[
            VM((wrows, 256), bf16), VM((wrows, width), bf16), VM((wrows, 3 * width), bf16),
            VM((wrows, hidden), bf16), VM((wrows, hidden), bf16),
            VM((rows, 3 * width), bf16), VM((att_rows, SEG_LEN), bf16), VM((rows, width), bf16),
            VM((rows, width), f32), VM((rows, width), bf16), VM((rows, hidden), bf16),
            VM((rows, hidden), bf16), VM((rows, width), bf16), VM((rows, width), bf16),
            VM((height, total), bf16), VM((ROWS, total), bf16),
        ]
        + GATHER_SEMS(n + 1)
        + [
            pltpu.SemaphoreType.DMA((n + 2,)),
            pltpu.SemaphoreType.DMA((n + 2,)),
            pltpu.SemaphoreType.DMA((5,)),
            pltpu.SemaphoreType.DMA((5,)),
            pltpu.SemaphoreType.DMA((n + 2,)),
            pltpu.SemaphoreType.DMA((12,)),
        ],
        compiler_params=pltpu.CompilerParams(
            collective_id=0, has_side_effects=True, vmem_limit_bytes=60 * MIB
        ),
    )(pack, x, cot)


class Scatter:
    def __init__(self, place, grad, out, index, sems, pair, r1a, r1b, r2a, r2b, r3, give):
        self.p, self.grad, self.out, self.m = place, grad, out, index
        self.send, self.recv = sems
        self.pair, self.r1a, self.r1b = pair, r1a, r1b
        self.r2a, self.r2b, self.r3, self.give = r2a, r2b, r3, give
        self.half = grad.shape[1] // 2
        tiles = self.half // LANES
        self.a = (tiles + 1) // 2 * LANES
        self.b = self.half - self.a
        self.sent = []
        p = place
        far = (1 - p.y) * 2 + 1 - p.x
        self.groups = (far, p.ydp, p.xdp, p.dp)

    def go(self, src, dst, slot, device):
        copy = remote(src, dst, self.send.at[self.m, slot], self.recv.at[self.m, slot], device)
        copy.start()
        self.sent.append(copy)

    def arrived(self, dst, slot):
        remote(dst, dst, self.send.at[self.m, slot], self.recv.at[self.m, slot], self.p.sib).wait_recv()

    def cols(self, at, size, core=None):
        core = self.p.core if core is None else core
        return lanes(core * self.half + at, size)

    def group(self, dp):
        return rows_at(dp * 4 * ROWS, 4 * ROWS, 16)

    def start(self):
        p = self.p
        for i, dp in enumerate(self.groups):
            theirs = self.grad.at[self.group(dp), self.cols(0, self.half, 1 - p.core)]
            self.go(theirs, self.pair.at[self.group(dp)], i, p.sib)

    def add(self, dp, part, other, other_row=0):
        at, size = {"A": (0, self.a), "B": (self.a, self.b), "AB": (0, self.half)}[part]
        base = dp * 4 * ROWS

        @pl.loop(0, 4)
        def _(i):
            key = (rows_at(base + i * ROWS, ROWS, 16), self.cols(at, size))
            more = other[rows_at(other_row + i * ROWS, ROWS, 16), :]
            self.grad[key] = (self.grad[key].astype(f32) + more.astype(f32)).astype(bf16)

    def side(self, dp, part):
        at, size = (0, self.a) if part == "A" else (self.a, self.b)
        return self.grad.at[self.group(dp), self.cols(at, size)]

    def one(self):
        p = self.p
        near, farther = pl.ds(0, 4 * ROWS), pl.ds(4 * ROWS, 4 * ROWS)
        for i, dp in enumerate(self.groups):
            self.arrived(self.pair.at[self.group(dp)], i)
            self.add(dp, "AB", self.pair, dp * 4 * ROWS)
            if i == 0:
                self.go(self.side(dp, "A"), self.r1a.at[near], 4, p.ynbr)
                if self.b:
                    self.go(self.side(dp, "B"), self.r1b.at[near], 6, p.xnbr)
            if i == 1:
                self.go(self.side(dp, "A"), self.r1a.at[farther], 5, p.ynbr)
            if i == 2 and self.b:
                self.go(self.side(dp, "B"), self.r1b.at[farther], 7, p.xnbr)

    def two(self):
        p = self.p
        near, farther = pl.ds(0, 4 * ROWS), pl.ds(4 * ROWS, 4 * ROWS)
        self.arrived(self.r1a.at[near], 4)
        self.add(p.xdp, "A", self.r1a)
        self.go(self.side(p.xdp, "A"), self.r2a, 8, p.xnbr)
        if self.b:
            self.arrived(self.r1b.at[near], 6)
            self.add(p.ydp, "B", self.r1b)
            self.go(self.side(p.ydp, "B"), self.r2b, 9, p.ynbr)
        self.arrived(self.r1a.at[farther], 5)
        self.add(p.dp, "A", self.r1a, 4 * ROWS)
        if self.b:
            self.arrived(self.r1b.at[farther], 7)
            self.add(p.dp, "B", self.r1b, 4 * ROWS)

    def three(self):
        p = self.p
        self.arrived(self.r2a, 8)
        self.add(p.dp, "A", self.r2a)
        if self.b:
            self.arrived(self.r2b, 9)
            self.add(p.dp, "B", self.r2b)
        for d in (1, 3, 2):
            z = (p.z + d) % 4
            src = self.grad.at[rows_at((p.dp * 4 + z) * ROWS, ROWS, 16), self.cols(0, self.half)]
            self.go(src, self.r3.at[d - 1], 9 + d, p.at(p.dp, z, p.core))

    def four(self):
        p = self.p
        for d in (1, 3, 2):
            self.arrived(self.r3.at[d - 1], 9 + d)
        rows = rows_at((p.dp * 4 + p.z) * ROWS, ROWS, 16)
        first = p.core == 0
        step = 384 if self.half % 384 == 0 else LANES

        @pl.loop(0, self.half // step)
        def _(i):
            cols = lanes(i * step, step)
            total = self.grad[rows, self.cols(i * step, step)].astype(f32)
            for d in range(3):
                total = total + self.r3[d, :, cols].astype(f32)
            upper, lower = total[: ROWS // 2], total[ROWS // 2 :]
            self.give[:, cols] = jnp.where(first, lower, upper)
            self.out[:, self.cols(i * step, step)] = jnp.where(first, upper, lower)

        self.go(self.give, self.out.at[:, self.cols(0, self.half)], 13, p.sib)

    def five(self):
        p = self.p
        self.arrived(self.out.at[:, self.cols(0, self.half, 1 - p.core)], 13)

    def finish(self):
        for copy in self.sent:
            copy.wait_send()


def scatter_buffers(width):
    half = width // 2
    tiles = half // LANES
    a = (tiles + 1) // 2 * LANES
    b = max(half - a, LANES)
    b_rows = 1 if half > a else 0
    return [
        VM((16 * ROWS, half), bf16),
        VM((8 * ROWS, a), bf16),
        VM((8 * ROWS if b_rows else 16, b), bf16),
        VM((4 * ROWS, a), bf16),
        VM((4 * ROWS if b_rows else 16, b), bf16),
        VM((3, ROWS, half), bf16),
        VM((ROWS // 2, half), f32),
    ]


def backward_kernel(*refs):
    (
        cot_ref, x_ref, home_ref, par_ref, r1_ref, r2_ref, z2_ref, fac_ref, csmall_ref,
        p_hbm, a_hbm, c_hbm, nl_hbm, g_hbm, sl_hbm, z1_hbm, w_hbm, o_hbm, i_hbm, b_hbm,
    ) = refs[:20]
    gt_ref, gq_ref, go_ref, gi_ref, gb_ref, gs_ref = refs[20:26]
    (
        pk, at, cx, nl, g, sl, z1, qw, ow, fw,
        h, df, tr, dwb, dwi, dwo, dwq, dws, small,
        sib_buf, block, full, tmp,
        s0, s1, s2, s3, pair_send, pair_recv, local, load, rs_send, rs_recv,
    ) = refs[26:59]
    bufs = refs[59:]
    p = Place()
    rows, width = x_ref.shape
    segs = rows // SEG_LEN
    hidden = g.shape[1]
    pairs = width // LANES
    tile = 256
    chunks = hidden // tile

    loads = {}
    order = [
        ("g", g_hbm, g), ("b", b_hbm, fw), ("sl", sl_hbm, sl), ("nl", nl_hbm, nl), ("z1", z1_hbm, z1),
        ("c", c_hbm, cx), ("o", o_hbm, ow), ("p", p_hbm, pk), ("a", a_hbm, at), ("w", w_hbm, qw),
        ("i", i_hbm, fw),
    ]
    for i, (name, src, dst) in enumerate(order):
        loads[name] = pltpu.make_async_copy(src, dst, load.at[i])
    for name, _, _ in order[:-1]:
        loads[name].start()
    greet(gather_peers(p))

    lead2 = block.shape[0]
    lead = lead2 // 2
    key_f = rows_at((p.dp * 4 + p.z) * lead2, lead2, 16)
    swap = remote(fac_ref, sib_buf, pair_send, pair_recv, p.sib)
    swap.start()
    mine = pltpu.make_async_copy(block, full.at[key_f], local)
    factors = Gather(p, full, block, 0, 4 * width, 0, (s0, s1, s2, s3), lead2)

    def factor_own():
        swap.wait_recv()
        block[rows_at(p.core * lead, lead, 16), :] = fac_ref[...]
        block[rows_at((1 - p.core) * lead, lead, 16), :] = sib_buf[...]
        mine.start()
        factors.send_own()

    def factor_grads():
        slab = width // 4

        def rows_of(z, at_col, size):
            return jnp.concatenate(
                [full[rows_at((i * 4 + z) * lead2, lead2, 16), pl.ds(at_col, size)] for i in range(4)],
                axis=0,
            )

        base = 2 * width + 3 * slab
        own = rows_at(p.fsdp * (ROWS // 2), ROWS // 2, 8)
        xl = rows_of(p.dp, base + slab, slab)
        nlf = rows_of(p.dp, base + 2 * slab, slab)
        dff = rows_of(p.dp, base + 3 * slab, slab)
        ctx = rows_of(p.dp, base + 4 * slab, slab)
        for z in range(4):
            tmp[:, :width] = mm(dff, rows_of(z, 0, width), TN)
            gb_ref[1, :, z * width : (z + 1) * width] = tmp[own, :width]
            tmp[:, :width] = mm(nlf, rows_of(z, width, width), TN)
            gi_ref[1, :, z * width : (z + 1) * width] = tmp[own, :width]
            tmp[:, : 3 * slab] = mm(xl, rows_of(z, 2 * width, 3 * slab), TN)
            got = tmp[own, : 3 * slab]
            for j in range(3):
                spot = j * width + z * slab
                gq_ref[1, :, spot : spot + slab] = got[:, j * slab : (j + 1) * slab]
            tmp[:, :slab] = mm(ctx, rows_of(z, base, slab), TN)
            go_ref[1, :, z * slab : (z + 1) * slab] = tmp[own, :slab]

    jobs = []
    for i, (grad, out) in enumerate(
        ((dwb, gb_ref.at[0]), (dwi, gi_ref.at[0]), (dwo, go_ref.at[0]), (dws, gs_ref), (dwq, gq_ref.at[0]))
    ):
        jobs.append(Scatter(p, grad, out, i, (rs_send, rs_recv), *bufs[7 * i : 7 * i + 7]))
    back, inn, out, sml, qkv = jobs

    block_rows = 64

    def norm_back(z_ref, r_ref, gain_row, low_ref, sums):
        def step(i, acc):
            key = rows_at(i * block_rows, block_rows, 16)
            dy = h[key, :]
            z = z_ref[key, :].astype(f32)
            r = jnp.concatenate([r_ref[key, :]] * (width // LANES), axis=1)
            e = dy * par_ref[gain_row : gain_row + 1, :]
            first = jnp.mean(e, axis=-1, keepdims=True)
            second = jnp.mean(e * z, axis=-1, keepdims=True)
            d = r * (e - first - z * second)
            h[key, :] = d
            low_ref[key, :] = d.astype(bf16)
            fold = lambda v: jnp.sum(v.reshape(block_rows // 8, 8, width), axis=0)
            return acc[0] + fold(dy * z), acc[1] + fold(dy)

        zero = jnp.zeros((8, width), f32)
        gain, bias = lax.fori_loop(0, rows // block_rows, step, (zero, zero))
        small[sums : sums + 1, :] = jnp.sum(gain, axis=0, keepdims=True)
        small[sums + 2 : sums + 3, :] = jnp.sum(bias, axis=0, keepdims=True)

    def turn(ref):
        @pl.loop(0, width // tile)
        def _(i):
            tr[rows_at(i * tile, tile, 16), :] = ref[:, lanes(i * tile, tile)].T

    def outer(dst, src, first, count):
        @pl.loop(first, first + count)
        def _(i):
            cols = lanes(i * tile, tile)
            dst[:, cols] = mm(tr[...], src[:, cols], NN).astype(bf16)

    def norm_two():
        @pl.loop(0, rows // block_rows)
        def _(i):
            key = rows_at(i * block_rows, block_rows, 16)
            h[key, :] = cot_ref[key, :].astype(f32)

        for s in range(segs):
            h[s * SEG_LEN : s * SEG_LEN + 1, :] = home_ref[s // 2, s % 2 : s % 2 + 1, width:]
        small[...] = jnp.zeros_like(small)
        small[4:8, :] = csmall_ref[0:4, :]
        for s in range(2):
            row = home_ref[0, s : s + 1, width:] + home_ref[1, s : s + 1, width:]
            small[pl.ds(8 + p.fsdp * 2 + s, 1), :] = row
        norm_back(z2_ref, r2_ref, 1, df, 1)
        turn(df)

    def active_back(first, count):
        @pl.loop(first, first + count)
        def _(i):
            cols = lanes(i * tile, tile)
            d = mm(df[...], fw[:, cols], NN) * sl[:, cols].astype(f32)
            sl[:, cols] = d.astype(bf16)

    def add_back(src, weight):
        @pl.loop(0, width // tile)
        def _(i):
            h[:, lanes(i * tile, tile)] += mm(src[...], weight[rows_at(i * tile, tile, 16), :], NT)

    def context_back():
        @pl.loop(0, width // tile)
        def _(i):
            d = mm(df[...], ow[rows_at(i * tile, tile, 16), :], NT)
            cx[:, lanes(i * tile, tile)] = d.astype(bf16)

    def attend_back(s):
        key = pl.ds(s * SEG_LEN, SEG_LEN)
        factor = (LANES // 2) ** (-0.5)

        @pl.loop(0, pairs)
        def _(j):
            a = at[rows_at((s * pairs + j) * 2 * SEG_LEN, 2 * SEG_LEN, 16), :]
            q_cols = lanes(j * LANES, LANES)
            k_cols = lanes(width + j * LANES, LANES)
            v_cols = lanes(2 * width + j * LANES, LANES)
            qs = jnp.concatenate(lane_halves(pk[key, q_cols]), axis=0)
            ks = jnp.concatenate(lane_halves(pk[key, k_cols]), axis=0)
            ds_in = jnp.concatenate(lane_halves(cx[key, q_cols]), axis=0)
            da = mm(ds_in, pk[key, v_cols], NT)
            af = a.astype(f32)
            ds = (af * (da - jnp.sum(af * da, axis=-1, keepdims=True))).astype(bf16)
            dv = mm(a, ds_in, TN)
            both = jnp.concatenate([ds[:SEG_LEN], ds[SEG_LEN:]], axis=1)
            dq = mm(both, ks, NN) * factor
            dk = mm(ds, qs, TN) * factor
            pk[key, q_cols] = dq.astype(bf16)
            pk[key, k_cols] = dk.astype(bf16)
            pk[key, v_cols] = dv.astype(bf16)

    def result():
        @pl.loop(0, width // tile)
        def _(i):
            cols = lanes(i * tile, tile)
            d = h[:, cols] + mm(pk[...], qw[rows_at(i * tile, tile, 16), :], NT)
            gt_ref[:, cols] = d.astype(bf16)

    def smalls():
        dws[:, :LANES] = small[...].T.astype(bf16)
        dws[:, LANES:] = jnp.zeros((dws.shape[0], LANES), bf16)

    factor_own()
    norm_two()
    factors.pass_line()
    loads["g"].wait()
    outer(dwb, g, 0, chunks)
    back.start()
    factors.pass_plane()
    loads["b"].wait()
    loads["sl"].wait()
    active_back(0, chunks // 2)
    back.one()
    active_back(chunks // 2, chunks - chunks // 2)
    loads["i"].start()
    loads["nl"].wait()
    turn(nl)
    factors.last()
    outer(dwi, sl, 0, chunks)
    inn.start()
    back.two()
    loads["i"].wait()
    add_back(sl, fw)
    inn.one()
    loads["z1"].wait()
    norm_back(z1, r1_ref, 0, df, 0)
    smalls()
    sml.start()
    back.three()
    loads["c"].wait()
    turn(cx)
    outer(dwo, df, 0, width // tile)
    out.start()
    factors.drain()
    mine.wait()
    loads["o"].wait()
    context_back()
    inn.two()
    out.one()
    loads["p"].wait()
    loads["a"].wait()
    attend_back(0)
    sml.one()
    back.four()
    attend_back(1)
    inn.three()
    out.two()
    attend_back(2)
    sml.two()
    inn.four()
    attend_back(3)
    turn(x_ref)
    outer(dwq, pk, 0, 3 * width // tile)
    qkv.start()
    out.three()
    sml.three()
    back.five()
    qkv.one()
    loads["w"].wait()
    result()
    qkv.two()
    inn.five()
    out.four()
    sml.four()
    factor_grads()
    qkv.three()
    out.five()
    sml.five()
    qkv.four()
    qkv.five()
    swap.wait_send()
    factors.finish()
    for job in jobs:
        job.finish()


def segment_backward(near, far):
    cot, x = near[0], near[1]
    rows, width = x.shape
    packed, att, context, nl, g = far[:5]
    hidden = g.shape[1]
    hbm, vm = pl.BlockSpec(memory_space=pl.ANY), pl.BlockSpec(memory_space=VM)
    arr = jax.ShapeDtypeStruct
    own = ROWS // 2
    lead = near[7].shape[0]
    like = lambda v: VM(v.shape, v.dtype)
    wrows = 16 * ROWS
    widths = (hidden, hidden, width, 256, 3 * width)
    bufs = []
    for w in widths:
        bufs += scatter_buffers(w)
    DMA = pltpu.SemaphoreType.DMA
    return pl.pallas_call(
        backward_kernel,
        out_shape=[
            arr((rows, width), bf16),
            arr((2, own, 3 * width), f32),
            arr((2, own, width), f32),
            arr((2, own, hidden), f32),
            arr((2, own, hidden), f32),
            arr((own, 256), f32),
        ],
        in_specs=[vm] * len(near) + [hbm] * len(far),
        out_specs=[vm] * 6,
        scratch_shapes=[
            like(packed), like(att), like(context), like(nl), like(g), like(g), like(nl),
            VM((wrows, 3 * width), bf16), VM((wrows, width), bf16), VM((wrows, hidden), bf16),
            VM((rows, width), f32), VM((rows, width), bf16), VM((width, rows), bf16),
            VM((wrows, hidden), bf16), VM((wrows, hidden), bf16), VM((wrows, width), bf16),
            VM((wrows, 3 * width), bf16), VM((wrows, 256), bf16), VM((LANES, width), f32),
            VM((lead, 4 * width), bf16), VM((2 * lead, 4 * width), bf16), VM((32 * lead, 4 * width), bf16),
            VM((width // 4, width), f32),
        ]
        + GATHER_SEMS(1)
        + [DMA, DMA, DMA, DMA((11,)), DMA((5, 14)), DMA((5, 14))]
        + bufs,
        compiler_params=pltpu.CompilerParams(
            collective_id=1, has_side_effects=True, vmem_limit_bytes=63 * MIB
        ),
    )(*near, *far)


def matmul(left, right, form):
    return jnp.einsum(form, left, right, preferred_element_type=jnp.float32)


def norm_forward(summed, gains, biases):
    average = jnp.mean(summed, axis=-1, keepdims=True)
    centred = summed - average
    variance = jnp.mean(centred * centred, axis=-1, keepdims=True)
    inverse = lax.rsqrt(variance + epsilon)
    scaled = centred * inverse
    return (scaled * gains + biases, scaled, inverse)


def norm_backward(grad_result, scaled, inverse, gains):
    grad_scaled = grad_result * gains
    first_mean = jnp.mean(grad_scaled, axis=-1, keepdims=True)
    second_mean = jnp.mean(grad_scaled * scaled, axis=-1, keepdims=True)
    grad_sum = inverse * (grad_scaled - first_mean - scaled * second_mean)
    return (grad_sum, jnp.sum(grad_result * scaled, axis=(0, 1)), jnp.sum(grad_result, axis=(0, 1)))


def split_heads(packed):
    groups, length, model_width = packed.shape
    return packed.reshape(groups, length, HEADS, model_width // HEADS)


def join_heads(split_part):
    groups, length, heads_count, head_size = split_part.shape
    return split_part.reshape(groups, length, heads_count * head_size)


def attend_forward(query_part, key_part, value_part, allowed):
    head_size = query_part.shape[-1]
    scores = matmul(query_part, key_part, "glhe,gmhe->ghlm") * head_size ** (-0.5)
    scores = jnp.where(allowed[:, None], scores, -1e30)
    row_max = jnp.max(scores, axis=-1, keepdims=True)
    exp_terms = jnp.exp(scores - row_max)
    row_total = jnp.sum(exp_terms, axis=-1, keepdims=True)
    attention = exp_terms / row_total
    context = matmul(attention.astype(jnp.bfloat16), value_part, "ghlm,gmhe->glhe")
    return (join_heads(context).astype(jnp.bfloat16), row_max + jnp.log(row_total))


def attend_backward(query_part, key_part, value_part, allowed, log_total, grad_context):
    head_size = query_part.shape[-1]
    factor = head_size ** (-0.5)
    scores = matmul(query_part, key_part, "glhe,gmhe->ghlm") * factor
    scores = jnp.where(allowed[:, None], scores, -1e30)
    attention = jnp.exp(scores - log_total)
    grad_attention = matmul(grad_context, value_part, "glhe,gmhe->ghlm")
    grad_value = matmul(attention.astype(jnp.bfloat16), grad_context, "ghlm,glhe->gmhe")
    inner = jnp.sum(attention * grad_attention, axis=-1, keepdims=True)
    grad_scores = (attention * (grad_attention - inner)).astype(jnp.bfloat16)
    grad_query = matmul(grad_scores, key_part, "ghlm,gmhe->glhe") * factor
    grad_key = matmul(grad_scores, query_part, "ghlm,glhe->gmhe") * factor
    return (join_heads(grad_query), join_heads(grad_key), join_heads(grad_value))


def segment_attend(packed):
    groups, length, total_width = packed.shape
    model_width = total_width // 3
    allowed = jnp.ones((groups, length, length), dtype=jnp.bool_)
    context, log_total = attend_forward(
        split_heads(packed[..., :model_width]),
        split_heads(packed[..., model_width : 2 * model_width]),
        split_heads(packed[..., 2 * model_width :]),
        allowed,
    )
    return (context, log_total)


def segment_attend_back(packed, log_total, grad_context):
    groups, length, total_width = packed.shape
    model_width = total_width // 3
    allowed = jnp.ones((groups, length, length), dtype=jnp.bool_)
    grad_query, grad_key, grad_value = attend_backward(
        split_heads(packed[..., :model_width]),
        split_heads(packed[..., model_width : 2 * model_width]),
        split_heads(packed[..., 2 * model_width :]),
        allowed,
        log_total,
        split_heads(grad_context),
    )
    return jnp.concatenate([grad_query, grad_key, grad_value], axis=-1)


def cross_attend(packed, allowed):
    model_width = packed.shape[-1] // 3
    remote = lax.all_gather(packed[..., model_width:], "fsdp", axis=1, tiled=True)
    context, log_total = attend_forward(
        split_heads(packed[..., :model_width]),
        split_heads(remote[..., :model_width]),
        split_heads(remote[..., model_width:]),
        allowed,
    )
    return (context, (remote, log_total))


def cross_attend_back(packed, saved, grad_context, allowed):
    remote, log_total = saved
    model_width = packed.shape[-1] // 3
    grad_query, grad_key, grad_value = attend_backward(
        split_heads(packed[..., :model_width]),
        split_heads(remote[..., :model_width]),
        split_heads(remote[..., model_width:]),
        allowed,
        log_total,
        split_heads(grad_context),
    )
    shared = jnp.concatenate([grad_key, grad_value], axis=-1)
    own_part = lax.psum_scatter(
        shared.astype(jnp.bfloat16), "fsdp", scatter_dimension=1, tiled=True
    ).astype(jnp.float32)
    return jnp.concatenate([grad_query, own_part], axis=-1)


def block_forward(states, weights, attend):
    w_qkv, w_out, w_in, w_back, gains, biases = weights
    gains = gains.astype(jnp.float32)
    biases = biases.astype(jnp.float32)
    states_low = states.astype(jnp.bfloat16)
    packed = matmul(states_low, w_qkv, "gld,de->gle").astype(jnp.bfloat16)
    context, saved = attend(packed)
    branch = matmul(context, w_out, "gld,de->gle")
    normed, scaled_one, inverse_one = norm_forward(states + branch, gains[0], biases[0])
    normed_low = normed.astype(jnp.bfloat16)
    hidden = matmul(normed_low, w_in, "gld,df->glf")
    active_low = jax.nn.gelu(hidden, approximate=False).astype(jnp.bfloat16)
    feed_out = matmul(active_low, w_back, "glf,fd->gld")
    result, scaled_two, inverse_two = norm_forward(normed + feed_out, gains[1], biases[1])
    kept = (
        states_low,
        packed,
        context,
        saved,
        scaled_one,
        inverse_one,
        normed_low,
        hidden,
        active_low,
        scaled_two,
        inverse_two,
    )
    return (result, kept)


def block_backward(grad_result, kept, weights, attend_back):
    w_qkv, w_out, w_in, w_back, gains, biases = weights
    gains = gains.astype(jnp.float32)
    (
        states_low,
        packed,
        context,
        saved,
        scaled_one,
        inverse_one,
        normed_low,
        hidden,
        active_low,
        scaled_two,
        inverse_two,
    ) = kept
    grad_sum_two, gain_two, bias_two = norm_backward(grad_result, scaled_two, inverse_two, gains[1])
    grad_feed = grad_sum_two.astype(jnp.bfloat16)
    grad_active = matmul(grad_feed, w_back, "gld,fd->glf")
    cumulative = 0.5 * (1.0 + lax.erf(hidden * root_half))
    slope = cumulative + hidden * inv_root_tau * jnp.exp(-0.5 * hidden * hidden)
    grad_hidden = (grad_active * slope).astype(jnp.bfloat16)
    grad_normed = grad_sum_two + matmul(grad_hidden, w_in, "glf,df->gld")
    grad_sum_one, gain_one, bias_one = norm_backward(grad_normed, scaled_one, inverse_one, gains[0])
    grad_branch = grad_sum_one.astype(jnp.bfloat16)
    grad_context = matmul(grad_branch, w_out, "gle,de->gld").astype(jnp.bfloat16)
    grad_packed = attend_back(packed, saved, grad_context).astype(jnp.bfloat16)
    grad_states = grad_sum_one + matmul(grad_packed, w_qkv, "gle,de->gld")
    factors = (
        states_low,
        grad_packed,
        context,
        grad_branch,
        normed_low,
        grad_hidden,
        grad_feed,
        active_low,
    )
    smalls = (jnp.stack([gain_one, gain_two]), jnp.stack([bias_one, bias_two]))
    return (grad_states, factors, smalls)


def weight_terms(factors):
    (
        states_low,
        grad_packed,
        context,
        grad_branch,
        normed_low,
        grad_hidden,
        grad_feed,
        active_low,
    ) = factors
    term_qkv = matmul(states_low, grad_packed, "gld,gle->de")
    term_out = matmul(context, grad_branch, "gld,gle->de")
    term_in = matmul(normed_low, grad_hidden, "gld,glf->df")
    term_back = matmul(grad_feed, active_low, "gld,glf->df")
    return jnp.concatenate([term_qkv, term_out, term_in, term_back], axis=1)


def gather_segment(w_qkv, w_out, w_in, w_back, norm_gain, norm_bias):
    return (
        lax.all_gather(w_qkv[0], ("dp", "fsdp"), axis=0, tiled=True),
        lax.all_gather(w_out[0], ("dp", "fsdp"), axis=0, tiled=True),
        lax.all_gather(w_in[0], ("dp", "fsdp"), axis=0, tiled=True),
        lax.all_gather(w_back[0], ("dp", "fsdp"), axis=1, tiled=True),
        lax.all_gather(norm_gain[0], ("dp", "fsdp"), axis=1, tiled=True),
        lax.all_gather(norm_bias[0], ("dp", "fsdp"), axis=1, tiled=True),
    )


def gather_cross(pos_embed, w_qkv, w_out, w_in, w_back, norm_gain, norm_bias):
    gathered = (
        lax.all_gather(w_qkv[1], ("dp", "fsdp"), axis=0, tiled=True),
        lax.all_gather(w_out[1], ("dp", "fsdp"), axis=0, tiled=True),
        lax.all_gather(w_in[1], ("dp", "fsdp"), axis=0, tiled=True),
        lax.all_gather(w_back[1], ("dp", "fsdp"), axis=1, tiled=True),
        lax.all_gather(norm_gain[1], ("dp", "fsdp"), axis=1, tiled=True),
        lax.all_gather(norm_bias[1], ("dp", "fsdp"), axis=1, tiled=True),
        lax.all_gather(pos_embed, ("dp", "fsdp"), axis=1, tiled=True),
    )
    return (gathered[:6], gathered[6])


def layer_forward(tokens, doc_ids, seg_weights, cross_weights, pos_full):
    rows, local_len, model_width = tokens.shape
    seg_count = local_len // SEG_LEN
    segments = tokens.reshape(rows * seg_count, SEG_LEN, model_width).astype(jnp.float32)
    seg_out, seg_kept = block_forward(segments, seg_weights, segment_attend)
    start = lax.axis_index("fsdp") * seg_count
    pos_local = lax.dynamic_slice_in_dim(pos_full, start, seg_count, 0).astype(jnp.float32)
    leaders = seg_out[:, 0, :].reshape(rows, seg_count, model_width) + pos_local
    own_docs = lax.dynamic_slice_in_dim(doc_ids, start, seg_count, 1)
    allowed = own_docs[:, :, None] == doc_ids[:, None, :]
    cross_out, cross_kept = block_forward(
        leaders, cross_weights, partial(cross_attend, allowed=allowed)
    )
    joined = jnp.concatenate(
        [cross_out.reshape(rows * seg_count, 1, model_width), seg_out[:, 1:, :]], axis=1
    )
    output = joined.reshape(rows, local_len, model_width).astype(jnp.bfloat16)
    return (output, (seg_kept, cross_kept, allowed))


def layer_backward(cotangent, doc_ids, kept, seg_weights, cross_weights):
    seg_kept, cross_kept, allowed = kept
    rows, local_len, model_width = cotangent.shape
    seg_count = local_len // SEG_LEN
    grad_all = cotangent.reshape(rows * seg_count, SEG_LEN, model_width).astype(jnp.float32)
    grad_cross = grad_all[:, 0, :].reshape(rows, seg_count, model_width)
    grad_leaders, cross_factors, cross_smalls = block_backward(
        grad_cross, cross_kept, cross_weights, partial(cross_attend_back, allowed=allowed)
    )
    start = lax.axis_index("fsdp") * seg_count
    empty_pos = jnp.zeros((doc_ids.shape[1], model_width), jnp.float32)
    grad_pos = lax.dynamic_update_slice_in_dim(empty_pos, jnp.sum(grad_leaders, axis=0), start, 0)
    grad_seg = jnp.concatenate(
        [grad_leaders.reshape(rows * seg_count, 1, model_width), grad_all[:, 1:, :]], axis=1
    )
    grad_states, seg_factors, seg_smalls = block_backward(
        grad_seg, seg_kept, seg_weights, segment_attend_back
    )
    grad_tokens = grad_states.reshape(rows, local_len, model_width).astype(jnp.bfloat16)
    return (grad_tokens, seg_factors, cross_factors, seg_smalls, cross_smalls, grad_pos)


def body(tokens, doc_ids, pos_embed, w_qkv, w_out, w_in, w_back, norm_gain, norm_bias, cotangent):
    seg_weights = gather_segment(w_qkv, w_out, w_in, w_back, norm_gain, norm_bias)
    cross_weights, pos_full = gather_cross(
        pos_embed, w_qkv, w_out, w_in, w_back, norm_gain, norm_bias
    )
    output, kept = layer_forward(tokens, doc_ids, seg_weights, cross_weights, pos_full)
    grad_tokens, seg_factors, cross_factors, seg_smalls, cross_smalls, grad_pos = layer_backward(
        cotangent, doc_ids, kept, seg_weights, cross_weights
    )
    model_width = tokens.shape[2]
    hidden_width = w_in.shape[2]
    seg_term = lax.psum_scatter(
        weight_terms(seg_factors), ("dp", "fsdp"), scatter_dimension=0, tiled=True
    )
    cross_term = lax.psum_scatter(
        weight_terms(cross_factors), ("dp", "fsdp"), scatter_dimension=0, tiled=True
    )
    stacked = jnp.stack([seg_term, cross_term])
    grad_qkv = stacked[:, :, : 3 * model_width]
    grad_out = stacked[:, :, 3 * model_width : 4 * model_width]
    grad_in = stacked[:, :, 4 * model_width : 4 * model_width + hidden_width]
    grad_back = jnp.transpose(stacked[:, :, 4 * model_width + hidden_width :], (0, 2, 1))
    gain_all = jnp.stack([seg_smalls[0], cross_smalls[0]])
    bias_all = jnp.stack([seg_smalls[1], cross_smalls[1]])
    grad_gain, grad_bias, pos_shard = (
        lax.psum_scatter(gain_all, ("dp", "fsdp"), scatter_dimension=2, tiled=True),
        lax.psum_scatter(bias_all, ("dp", "fsdp"), scatter_dimension=2, tiled=True),
        lax.psum_scatter(grad_pos, ("dp", "fsdp"), scatter_dimension=1, tiled=True),
    )
    return (
        output,
        grad_tokens,
        pos_shard,
        grad_qkv,
        grad_out,
        grad_in,
        grad_back,
        grad_gain,
        grad_bias,
    )


def make_pack(pos_embed, w_qkv, w_out, w_in, w_back, norm_gain, norm_bias):
    own, width = w_out.shape[1:]
    slab = width // 4
    items = jnp.concatenate([norm_gain[0], norm_bias[0], norm_gain[1], norm_bias[1], pos_embed], axis=0)
    small = jnp.pad(items.T, ((0, 0), (0, 256 - items.shape[0])))
    cross = jnp.concatenate(
        [
            w_qkv[1].reshape(own, 3, 4, slab).transpose(0, 2, 1, 3).reshape(own, 4, 3 * slab),
            w_in[1].reshape(own, 4, width),
            w_back[1].T.reshape(own, 4, width),
            jnp.zeros((own, 4, slab), bf16),
        ],
        axis=2,
    ).reshape(own, 12 * width)
    pack = jnp.concatenate(
        [small, w_qkv[0], w_out[0], w_in[0], w_back[0].T, cross, w_out[1]], axis=1
    )
    return jnp.pad(pack, ((0, 32 - own), (0, 0)))


def fast_body(tokens, doc_ids, pos_embed, w_qkv, w_out, w_in, w_back, norm_gain, norm_bias, cotangent):
    nrows, local_len, width = tokens.shape
    rows = nrows * local_len
    segs = rows // SEG_LEN
    hidden = w_in.shape[2]
    pack = make_pack(pos_embed, w_qkv, w_out, w_in, w_back, norm_gain, norm_bias)
    x = tokens.reshape(rows, width)
    cot = cotangent.reshape(rows, width)
    (
        s_qkv, s_in, s_out, s_back, cross_w, cross_wo,
        packed, att, context, nl, act, slope, z_one, z_two,
        y, lead, par, r_one, r_two,
    ) = segment_forward(pack, x, cot, (256, 3 * width, width, hidden, hidden), 3 * width, width)
    norms = par[4:8]
    own_row = lax.dynamic_index_in_dim(doc_ids, lax.axis_index("fsdp") % 2, 0, keepdims=False)
    mask = (own_row[:, None] == own_row[None, :]).astype(f32)
    home, fac, cross_small = cross_block(
        lead, mask, jnp.pad(norms, ((0, 4), (0, 0))), cross_w, cross_wo
    )
    cross_out = home[..., :width]
    output = y.reshape(segs, SEG_LEN, width).at[:, 0].set(cross_out.reshape(segs, width).astype(bf16))
    output = output.reshape(tokens.shape)
    grad_tokens, g_qkv, g_out, g_in, g_back, t_small = segment_backward(
        (cot, x, home, par, r_one, r_two, z_two, fac, cross_small),
        (packed, att, context, nl, act, slope, z_one, s_qkv, s_out, s_in, s_back),
    )
    s = t_small.T
    return (
        output,
        grad_tokens.reshape(tokens.shape),
        s[8 : 8 + doc_ids.shape[1]],
        g_qkv,
        g_out,
        g_in,
        jnp.swapaxes(g_back, 1, 2),
        jnp.stack([s[0:2], s[4:6]]),
        jnp.stack([s[2:4], s[6:8]]),
    )


def solution(mesh):
    fast = dict(mesh.shape) == {"dp": 4, "fsdp": 8}
    return jax.shard_map(
        fast_body if fast else body,
        mesh=mesh,
        in_specs=(
            P("dp", "fsdp", None),
            P("dp", None),
            P(None, ("dp", "fsdp")),
            P(None, ("dp", "fsdp"), None),
            P(None, ("dp", "fsdp"), None),
            P(None, ("dp", "fsdp"), None),
            P(None, None, ("dp", "fsdp")),
            P(None, None, ("dp", "fsdp")),
            P(None, None, ("dp", "fsdp")),
            P("dp", "fsdp", None),
        ),
        out_specs=(
            P("dp", "fsdp", None),
            P("dp", "fsdp", None),
            P(None, ("dp", "fsdp")),
            P(None, ("dp", "fsdp"), None),
            P(None, ("dp", "fsdp"), None),
            P(None, ("dp", "fsdp"), None),
            P(None, None, ("dp", "fsdp")),
            P(None, None, ("dp", "fsdp")),
            P(None, None, ("dp", "fsdp")),
        ),
        check_vma=False,
    )
```

```python
from functools import partial

import jax
import jax.numpy as jnp
from jax import lax
from jax.experimental import pallas as pl
from jax.experimental.pallas import tpu as pltpu
from jax.sharding import PartitionSpec as P

HEADS = 12
SEG_LEN = 128


epsilon = 1e-05
root_half = 0.7071067811865476
inv_root_tau = 0.3989422804014327

bf16 = jnp.bfloat16
f32 = jnp.float32
MESH = pl.DeviceIdType.MESH
VM = pltpu.VMEM
MIB = 1024 * 1024
ROWS = 48
LANES = 128


class Place:
    def __init__(self):
        self.dp = lax.axis_index("dp")
        self.fsdp = lax.axis_index("fsdp")
        self.y, self.x = self.dp // 2, self.dp % 2
        self.z, self.core = self.fsdp // 2, self.fsdp % 2

    def at(self, dp, z, core):
        return (dp, z * 2 + core)

    @property
    def sib(self):
        return (self.dp, self.z * 2 + 1 - self.core)

    @property
    def xdp(self):
        return self.y * 2 + 1 - self.x

    @property
    def ydp(self):
        return (1 - self.y) * 2 + self.x

    @property
    def xnbr(self):
        return (self.xdp, self.fsdp)

    @property
    def ynbr(self):
        return (self.ydp, self.fsdp)


def greet(devices):
    barrier = pltpu.get_barrier_semaphore()
    for device in devices:
        pl.semaphore_signal(barrier, inc=1, device_id=device, device_id_type=MESH)
    pl.semaphore_wait(barrier, len(devices))


def remote(src, dst, send, recv, device):
    return pltpu.make_async_remote_copy(
        src_ref=src, dst_ref=dst, send_sem=send, recv_sem=recv, device_id=device, device_id_type=MESH
    )


def lanes(start, size):
    if isinstance(start, int):
        return pl.ds(start, size)
    return pl.ds(pl.multiple_of(start, LANES), size)


def rows_at(start, size, unit):
    return pl.ds(pl.multiple_of(start, unit), size)


class Gather:
    def __init__(self, place, out, off, width, source, index, sems, height2, wide_a=True):
        self.p, self.out, self.off, self.source = place, out, off, source
        self.m, self.sems, self.h2 = index, sems, height2
        self.half = width // 2
        tiles = self.half // LANES
        self.a = ((tiles + 1) // 2 if wide_a else max(tiles // 2, 1)) * LANES
        self.b = self.half - self.a
        self.sent = []
        self.far = (1 - place.y) * 2 + 1 - place.x

    def cols(self, core, part="AB"):
        at, size = {"A": (0, self.a), "B": (self.a, self.b), "AB": (0, self.half)}[part]
        return lanes(self.off + core * self.half + at, size)

    def block(self, z, core):
        return self.out.at[rows_at((self.p.dp * 4 + z) * self.h2, self.h2, 16), self.cols(core)]

    def group(self, dp, core, part="AB"):
        return self.out.at[rows_at(dp * 4 * self.h2, self.h2 * 4, 16), self.cols(core, part)]

    def go(self, src, dst, slot, device):
        copy = remote(src, dst, self.sems[0].at[self.m, slot], self.sems[1].at[self.m, slot], device)
        copy.start()
        self.sent.append(copy)

    def hand(self, ref, slot):
        self.go(ref, ref, slot, self.p.sib)

    def arrived(self, dst, slot):
        remote(dst, dst, self.sems[0].at[self.m, slot], self.sems[1].at[self.m, slot], self.p.sib).wait_recv()

    def own(self):
        p = self.p
        for d in (1, 3, 2):
            z = (p.z + d) % 4
            self.go(self.source(z), self.block(p.z, p.core), d - 1, p.at(p.dp, z, p.core))

    def line(self):
        p = self.p
        for d in (1, 3, 2):
            self.arrived(self.block((p.z + 4 - d) % 4, p.core), d - 1)
        mine = self.group(p.dp, p.core)
        self.go(mine, mine, 3, p.xnbr)
        self.go(mine, mine, 4, p.ynbr)
        self.hand(mine, 7)

    def plane(self):
        p = self.p
        over_x, over_y = self.group(p.xdp, p.core), self.group(p.ydp, p.core)
        self.arrived(over_x, 3)
        part = self.group(p.xdp, p.core, "A")
        self.go(part, part, 5, p.ynbr)
        self.arrived(over_y, 4)
        if self.b:
            part = self.group(p.ydp, p.core, "B")
            self.go(part, part, 6, p.xnbr)
        self.hand(over_x, 8)
        self.hand(over_y, 9)

    def last(self):
        p = self.p
        self.arrived(self.group(self.far, p.core, "A"), 5)
        if self.b:
            self.arrived(self.group(self.far, p.core, "B"), 6)
        self.hand(self.group(self.far, p.core), 10)

    def drain(self):
        p = self.p
        for slot, dp in ((7, p.dp), (8, p.xdp), (9, p.ydp), (10, self.far)):
            self.arrived(self.group(dp, 1 - p.core), slot)

    def finish(self):
        for copy in self.sent:
            copy.wait_send()


class Staged:
    def __init__(self, units, order):
        self.units, self.order, self.at = units, order, 0

    def step(self, count=1):
        for name, i in self.order[self.at : self.at + count]:
            getattr(self.units[i], name)()
        self.at += count

    def upto(self, name, i):
        spot = self.order.index((name, i)) + 1
        if spot > self.at:
            self.step(spot - self.at)

    def finish(self):
        self.step(len(self.order) - self.at)
        for unit in self.units:
            unit.finish()


def staggered(count, lags, first=0):
    order = []
    for t in range(min(lags.values()), count + max(lags.values())):
        for name, lag in lags.items():
            if 0 <= t - lag < count and (t >= 0 or lag < 0):
                order.append((name, t - lag + first))
    return order


def gather_peers(p):
    peers = [p.sib, p.xnbr, p.ynbr]
    for d in (1, 2, 3):
        peers.append(p.at(p.dp, (p.z + d) % 4, p.core))
    return peers


def everyone(p):
    return [
        (lax.rem(p.dp + i, 4), lax.rem(p.fsdp + j, 8)) for i in range(4) for j in range(8) if i or j
    ]


NEG = -1e30


def mm(a, b, dims):
    return lax.dot_general(a, b, (dims, ((), ())), preferred_element_type=f32)


NN = ((1,), (0,))
NT = ((1,), (1,))
TN = ((0,), (0,))


def norm_rows(summed, gain, bias):
    centred = summed - jnp.mean(summed, axis=-1, keepdims=True)
    variance = jnp.mean(centred * centred, axis=-1, keepdims=True)
    inverse = lax.rsqrt(variance + epsilon)
    scaled = centred * inverse
    return scaled * gain + bias, scaled, inverse


def norm_rows_back(grad, scaled, inverse, gain):
    g = grad * gain
    first = jnp.mean(g, axis=-1, keepdims=True)
    second = jnp.mean(g * scaled, axis=-1, keepdims=True)
    return inverse * (g - first - scaled * second)


def gelu_parts(u):
    cumulative = 0.5 * (1.0 + lax.erf(u * root_half))
    return cumulative, cumulative + u * inv_root_tau * jnp.exp(-0.5 * u * u)


def lane_halves(v):
    low = lax.broadcasted_iota(jnp.int32, v.shape, 1) < LANES // 2
    zero = jnp.zeros_like(v)
    return jnp.where(low, v, zero), jnp.where(low, zero, v)


FORWARD_LAGS = {"own": -3, "line": 0, "plane": 1, "last": 2, "drain": 3}


def forward_order(n_seg, n_cross):
    n = n_seg + n_cross
    order = staggered(n, FORWARD_LAGS)
    stop = order.index(("line", n_seg))
    head, rest = order[:stop], order[stop:]
    head += [s for s in rest if s[0] == "own"]
    done = set(head)
    tail = [("plane", n_seg - 1), ("line", n_seg), ("line", n_seg + 1)]
    for u in range(n_seg - 3, n_seg):
        tail += [("last", u), ("drain", u)]
    tail += [("plane", n_seg), ("line", n_seg + 2)]
    for u in range(n_seg, n):
        tail += [("last", u), ("plane", u + 1), ("drain", u)]
    return head + [s for s in tail if s not in done and s[1] < n]


def forward_kernel(*refs):
    wq_ref, wo_ref, wi_ref, wb_ref, ws_ref, x_ref, cot_ref, mask_ref = refs[:8]
    (
        w_hbm, i_hbm, o_hbm, b_hbm,
        p_hbm, a_hbm, c_hbm, nl_hbm, g_hbm, sl_hbm, z1_hbm, z2_hbm,
        y_ref, par_ref, r1_ref, r2_ref, home_ref, fac_ref, small_ref,
    ) = refs[8:27]
    (
        sw, ow, qw, iw, bw, cw, cwo,
        pk, at, cx, h, nl, g, sl, z1, z2,
        own_buf, sib_buf, block,
        lead_out, gbuf, lead, xbuf, ybuf, dpack,
        s_send, s_recv, pair_send, pair_recv, wo_send, wo_recv, local, out_sem,
        g_send, g_recv, x_send, x_recv, h_send, h_recv, lead_sem,
    ) = refs[27:]
    p = Place()
    rows, width = x_ref.shape
    segs = rows // SEG_LEN
    hidden = iw.shape[1]
    pairs = width // LANES
    slab = width // 4
    cross_width = cw.shape[1]
    half_rows = ROWS // 2
    key_own = rows_at((p.dp * 4 + p.z) * ROWS, ROWS, 16)

    sizes = [ws_ref.shape[1]] + [width] * (3 + 1 + 2 * (hidden // width)) + [4 * cross_width, width]
    starts = [sum(sizes[:i]) for i in range(len(sizes))]
    n_seg = len(sizes) - 2
    part_cross, part_wo = n_seg, n_seg + 1

    def put(start, value):
        zero = jnp.zeros((own_buf.shape[0] - half_rows, value.shape[1]), f32)
        full = jnp.concatenate([value.astype(f32), zero], axis=0).astype(bf16)
        own_buf[:, pl.ds(start, value.shape[1])] = full

    def pair(i):
        cols = pl.ds(starts[i], sizes[i])
        return remote(
            own_buf.at[:, cols], sib_buf.at[:, cols], pair_send.at[i], pair_recv.at[i], p.sib
        )

    def stage(i):
        spot = starts[i]
        per = hidden // width
        if i == 0:
            put(spot, ws_ref[...])
        elif i < 4:
            put(spot, wq_ref[0, :, (i - 1) * width : i * width])
        elif i == 4:
            put(spot, wo_ref[0])
        elif i < 5 + per:
            put(spot, wi_ref[0, :, (i - 5) * width : (i - 4) * width])
        elif i < 5 + 2 * per:
            put(spot, wb_ref[0, :, (i - 5 - per) * width : (i - 4 - per) * width])
        elif i == part_cross:
            for z in range(4):
                heads = [wq_ref[1, :, j * width + z * slab : j * width + (z + 1) * slab] for j in range(3)]
                heads.append(heads[2])
                put(spot, jnp.concatenate([v.astype(f32) for v in heads], axis=1).astype(bf16))
                put(spot + width, wi_ref[1, :, z * width : (z + 1) * width])
                put(spot + 2 * width, wb_ref[1, :, z * width : (z + 1) * width])
                spot += cross_width
        else:
            put(spot, wo_ref[1])

    def joined(start, size):
        cols = lanes(start, size)
        first = p.core == 0
        mine = own_buf[:, cols].astype(f32)[:half_rows]
        theirs = sib_buf[:, cols].astype(f32)[:half_rows]
        both = [jnp.where(first, mine, theirs), jnp.where(first, theirs, mine)]
        return jnp.concatenate(both, axis=0).astype(bf16)

    ahead = 4

    def begin(i):
        if i < n_seg + 2:
            stage(i)
            pair(i).start()

    stage(0)
    greet(everyone(p))
    pair(0).start()
    for i in range(1, ahead):
        begin(i)

    sems = (s_send, s_recv)
    dests = [(sw, 0)] + [(qw, i * width) for i in range(3)] + [(ow, 0)]
    dests += [(iw, i * width) for i in range(hidden // width)]
    dests += [(bw, i * width) for i in range(hidden // width)]

    class SegUnit(Gather):
        def __init__(self, i):
            dst, off = dests[i]
            mine = lambda z: dst.at[key_own, self.cols(p.core)]
            super().__init__(p, dst, off, sizes[i], mine, i, sems, ROWS, i % 2 == 0)
            self.i = i

        def own(self):
            pair(self.i).wait_recv()
            self.out[key_own, self.cols(p.core)] = joined(
                starts[self.i] + p.core * self.half, self.half
            )
            super().own()
            begin(self.i + ahead)

    class CrossUnit(Gather):
        def __init__(self, i):
            start = i * width
            self.i = i

            def mine(z):
                spot = z * cross_width + start + p.core * self.half
                return block.at[:, lanes(spot, self.half)]

            super().__init__(p, cw, start, width, mine, n_seg + i, sems, ROWS, i % 2 == 0)

        def own(self):
            if self.i == 0:
                pair(part_cross).wait_recv()

                @pl.loop(0, 4 * cross_width // width)
                def _(k):
                    block[:, lanes(k * width, width)] = joined(starts[part_cross] + k * width, width)

            spot = p.z * cross_width + self.i * width + p.core * self.half
            self.out[key_own, self.cols(p.core)] = block[:, lanes(spot, self.half)]
            super().own()

    units = [SegUnit(i) for i in range(n_seg)] + [CrossUnit(i) for i in range(cross_width // width)]
    n_cross = len(units) - n_seg
    comm = Staged(units, forward_order(n_seg, n_cross))

    def need(i):
        comm.upto("drain", i)

    def pump():
        comm.step(5)

    half_wo = width // 2
    wo_block = block.at[:, pl.ds(4 * cross_width, width)]
    wo_src = block.at[:, lanes(4 * cross_width + p.core * half_wo, half_wo)]
    wo_dst = cwo.at[rows_at(p.z * ROWS, ROWS, 16), lanes(p.core * half_wo, half_wo)]

    def wo_copy(i):
        return remote(wo_src, wo_dst, wo_send.at[i], wo_recv.at[p.z], p.at(i, p.dp, p.core))

    def wo_start():
        pair(part_wo).wait_recv()
        wo_block[...] = joined(starts[part_wo], width)
        for i in range(4):
            here = jnp.logical_and(p.dp == i, p.dp == p.z)

            @pl.when(jnp.logical_not(here))
            def _():
                wo_copy(i).start()

            @pl.when(here)
            def _():
                mine = pltpu.make_async_copy(wo_src, wo_dst, local)
                mine.start()
                mine.wait()

    wo_mine = cwo.at[:, lanes(p.core * half_wo, half_wo)]
    wo_theirs = cwo.at[:, lanes((1 - p.core) * half_wo, half_wo)]
    wo_hand = remote(wo_mine, wo_mine, wo_send.at[4], wo_recv.at[4], p.sib)

    def wo_middle():
        for i in range(4):
            piece = cwo.at[pl.ds(i * ROWS, ROWS), lanes(p.core * half_wo, half_wo)]

            @pl.when(jnp.logical_not(jnp.logical_and(p.z == p.dp, p.z == i)))
            def _():
                remote(piece, piece, wo_send.at[i], wo_recv.at[i], p.sib).wait_recv()

        wo_hand.start()

    def wo_finish():
        remote(wo_theirs, wo_theirs, wo_send.at[4], wo_recv.at[4], p.sib).wait_recv()
        wo_hand.wait_send()
        for i in range(4):

            @pl.when(jnp.logical_not(jnp.logical_and(p.dp == i, p.dp == p.z)))
            def _():
                wo_copy(i).wait_send()

    kept = []

    def keep(src, dst):
        copy = pltpu.make_async_copy(src, dst, out_sem.at[len(kept)])
        copy.start()
        kept.append(copy)

    tile = 256

    def params():
        par_ref[...] = sw[...].astype(f32).T[: par_ref.shape[0]]

    def project(first, count):
        @pl.loop(first, first + count)
        def _(i):
            cols = lanes(i * tile, tile)
            pk[:, cols] = mm(x_ref[...], qw[:, cols], NN).astype(bf16)

    def attend(s):
        key = pl.ds(s * SEG_LEN, SEG_LEN)

        @pl.loop(0, pairs)
        def _(j):
            q2 = pk[key, lanes(j * LANES, LANES)]
            k2 = pk[key, lanes(width + j * LANES, LANES)]
            v2 = pk[key, lanes(2 * width + j * LANES, LANES)]
            scores = mm(jnp.concatenate(lane_halves(q2), axis=0), k2, NT) * (LANES // 2) ** (-0.5)
            top = jnp.max(scores, axis=-1, keepdims=True)
            terms = jnp.exp(scores - top)
            a = (terms / jnp.sum(terms, axis=-1, keepdims=True)).astype(bf16)
            at[rows_at((s * pairs + j) * 2 * SEG_LEN, 2 * SEG_LEN, 16), :] = a
            both = jnp.concatenate([a[:SEG_LEN], a[SEG_LEN:]], axis=1)
            c2 = mm(both, jnp.concatenate(lane_halves(v2), axis=0), NN)
            cx[key, lanes(j * LANES, LANES)] = c2.astype(bf16)

    block_rows = 64

    def branch():
        @pl.loop(0, width // tile)
        def _(i):
            cols = lanes(i * tile, tile)
            h[:, cols] = x_ref[:, cols].astype(f32) + mm(cx[...], ow[:, cols], NN)

        @pl.loop(0, rows // block_rows)
        def _(i):
            key = rows_at(i * block_rows, block_rows, 16)
            normed, scaled, inverse = norm_rows(h[key, :], par_ref[0:1, :], par_ref[2:3, :])
            h[key, :] = normed
            nl[key, :] = normed.astype(bf16)
            z1[key, :] = scaled.astype(bf16)
            r1_ref[key, :] = jnp.broadcast_to(inverse, (block_rows, LANES))

    def feed_in(first, count):
        @pl.loop(first, first + count)
        def _(i):
            cols = lanes(i * tile, tile)
            u = mm(nl[...], iw[:, cols], NN)
            phi, slope = gelu_parts(u)
            g[:, cols] = (u * phi).astype(bf16)
            sl[:, cols] = slope.astype(bf16)

    def feed_back(part):
        inner = pl.ds(part * width, width)

        @pl.loop(0, width // tile)
        def _(i):
            cols = lanes(i * tile, tile)
            h[:, cols] += mm(g[:, inner], bw[rows_at(i * tile, tile, 16), inner], NT)

    def finish_block():
        @pl.loop(0, rows // block_rows)
        def _(i):
            key = rows_at(i * block_rows, block_rows, 16)
            result, scaled, inverse = norm_rows(h[key, :], par_ref[1:2, :], par_ref[3:4, :])
            h[key, :] = result
            y_ref[key, :] = result.astype(bf16)
            z2[key, :] = scaled.astype(bf16)
            r2_ref[key, :] = jnp.broadcast_to(inverse, (block_rows, LANES))

    def leaders():
        for s in range(segs):
            pos = par_ref[pl.ds(8 + p.fsdp * 2 + s % 2, 1), :]
            lead_out[s // 2, s % 2 : s % 2 + 1, :width] = h[s * SEG_LEN : s * SEG_LEN + 1, :] + pos
            lead_out[s // 2, s % 2 : s % 2 + 1, width:] = cot_ref[s * SEG_LEN : s * SEG_LEN + 16, :].astype(f32)[:1]

    def lead_copy(z, j):
        i = 2 * z + j
        return remote(lead_out.at[j], gbuf.at[p.fsdp], g_send.at[i], g_recv.at[p.fsdp], (p.dp, i))

    per = hidden // width
    head = width // HEADS
    heads = HEADS // 4
    n_tiles = width // tile
    need(0)
    params()
    for i in range(3):
        need(1 + i)
        project(i * n_tiles, n_tiles)
    for s in range(segs):
        attend(s)
        comm.upto("drain", 4 + s)
    keep(qw, w_hbm), keep(pk, p_hbm), keep(at, a_hbm), keep(cx, c_hbm)
    branch()
    keep(ow, o_hbm), keep(nl, nl_hbm), keep(z1, z1_hbm)
    for i in range(per):
        need(8 + i)
        feed_in(i * n_tiles, n_tiles)
    wo_start()
    keep(iw, i_hbm), keep(g, g_hbm), keep(sl, sl_hbm)
    for i in range(per):
        need(5 + per + i)
        feed_back(i)
    finish_block()
    keep(bw, b_hbm), keep(z2, z2_hbm)
    leaders()
    for d in range(4):
        z = (p.z + d) % 4
        for j in range(2):
            if d:
                lead_copy(z, j).start()
            else:

                @pl.when(p.core != j)
                def _():
                    lead_copy(z, j).start()

                @pl.when(p.core == j)
                def _():
                    mine = pltpu.make_async_copy(lead_out.at[j], gbuf.at[p.fsdp], lead_sem)
                    mine.start()
                    mine.wait()

    need(n_seg)
    wo_middle()
    for d in range(1, 8):
        i = lax.rem(p.fsdp + d, 8)
        remote(gbuf.at[i], gbuf.at[i], g_send.at[i], g_recv.at[i], p.sib).wait_recv()
    for i in range(8):
        lead[2 * i : 2 * i + 2, :] = gbuf[i]
    states = lead[:, :width]
    cot = lead[:, width:]

    def sum_z(e, partial_sum):
        xbuf[e, p.z] = partial_sum.astype(bf16)
        copies = []
        for d in (1, 3, 2):
            z = (p.z + d) % 4
            copy = remote(
                xbuf.at[e, p.z], xbuf.at[e, p.z], x_send.at[e, d - 1], x_recv.at[e, p.z],
                p.at(p.dp, z, p.core),
            )
            copy.start()
            copies.append(copy)
        for d in (1, 3, 2):
            z = (p.z + d) % 4
            piece = xbuf.at[e, z]
            remote(piece, piece, x_send.at[e, d - 1], x_recv.at[e, z], p.sib).wait_recv()
        for copy in copies:
            copy.wait_send()
        return sum(xbuf[e, z].astype(f32) for z in range(4))

    gain0, gain1 = par_ref[4:5, :], par_ref[5:6, :]
    bias0, bias1 = par_ref[6:7, :], par_ref[7:8, :]
    in_cols, back_cols = pl.ds(width, width), pl.ds(2 * width, width)
    qkv_cols = pl.ds(0, 3 * slab)
    factor = head ** (-0.5)
    allowed = mask_ref[...] > 0.5

    xl = states.astype(bf16)
    packed = mm(xl, cw[:, qkv_cols], NN).astype(bf16)
    q = [packed[:, i * head : (i + 1) * head] for i in range(heads)]
    k = [packed[:, slab + i * head : slab + (i + 1) * head] for i in range(heads)]
    v = [packed[:, 2 * slab + i * head : 2 * slab + (i + 1) * head] for i in range(heads)]
    att, context = [], []
    for i in range(heads):
        scores = jnp.where(allowed, mm(q[i], k[i], NT) * factor, NEG)
        top = jnp.max(scores, axis=-1, keepdims=True)
        terms = jnp.exp(scores - top)
        a = terms / jnp.sum(terms, axis=-1, keepdims=True)
        att.append(a)
        context.append(mm(a.astype(bf16), v[i], NN))
    context = jnp.concatenate(context, axis=1).astype(bf16)
    wo_finish()
    branch = sum_z(0, mm(context, cwo[...], NN))
    normed, z_one, r_one = norm_rows(states + branch, gain0, bias0)
    nl = normed.astype(bf16)
    need(n_seg + 1)
    hidden = mm(nl, cw[:, in_cols], NN)
    phi, slope = gelu_parts(hidden)
    active = (hidden * phi).astype(bf16)
    need(n_seg + 2)
    feed = sum_z(1, mm(active, cw[:, back_cols], NT))
    result, z_two, r_two = norm_rows(normed + feed, gain1, bias1)
    d_two = norm_rows_back(cot, z_two, r_two, gain1)
    df = d_two.astype(bf16)
    du = (mm(df, cw[:, back_cols], NN) * slope).astype(bf16)
    d_normed = d_two + sum_z(2, mm(du, cw[:, in_cols], NT))
    d_one = norm_rows_back(d_normed, z_one, r_one, gain0)
    db = d_one.astype(bf16)
    dc = mm(db, cwo[...], NT).astype(bf16)
    for i in range(heads):
        a = att[i]
        dci = dc[:, i * head : (i + 1) * head]
        da = mm(dci, v[i], NT)
        dv = mm(a.astype(bf16), dci, TN)
        ds = (a * (da - jnp.sum(a * da, axis=-1, keepdims=True))).astype(bf16)
        dq = mm(ds, k[i], NN) * factor
        dk = mm(ds, q[i], TN) * factor
        for j, piece in enumerate((dq, dk, dv)):
            dpack[:, j * slab + i * head : j * slab + (i + 1) * head] = piece
    dp = dpack[...].astype(bf16)
    dx = d_one + sum_z(3, mm(dp, cw[:, qkv_cols], NT))
    for i in range(8):
        ybuf[i, :, :width] = result[2 * i : 2 * i + 2]
        ybuf[i, :, width:] = dx[2 * i : 2 * i + 2]
    home = remote(
        ybuf.at[2 * p.z + 1 - p.core], home_ref.at[p.core], h_send, h_recv, p.sib
    )
    home.start()
    home_ref[p.core] = ybuf[2 * p.z + p.core]

    def part(full):
        pieces = [full[:, i * slab : (i + 1) * slab] for i in range(4)]
        out = pieces[0]
        for i in range(1, 4):
            out = jnp.where(p.z == i, pieces[i], out)
        return out.astype(bf16)

    fac_ref[:, :width] = active
    fac_ref[:, width : 2 * width] = du
    fac_ref[:, 2 * width :] = jnp.concatenate(
        [dp, part(d_one), part(states), part(normed), part(d_two), context], axis=1
    )
    once = jnp.where(p.z == 0, 1.0, 0.0)
    sums = [d_normed * z_one, cot * z_two, d_normed, cot]
    small_ref[...] = jnp.zeros_like(small_ref)
    for i, s in enumerate(sums):
        small_ref[i : i + 1, :] = once * jnp.sum(s, axis=0, keepdims=True)
    theirs = home_ref.at[1 - p.core]
    remote(theirs, theirs, h_send, h_recv, p.sib).wait_recv()
    home.wait_send()
    for d in range(4):
        z = (p.z + d) % 4
        for j in range(2):
            if d:
                lead_copy(z, j).wait_send()
            else:

                @pl.when(p.core != j)
                def _():
                    lead_copy(z, j).wait_send()
    comm.finish()
    for i in range(n_seg + 2):
        pair(i).wait_send()
    for s in range(segs):
        spot = pl.ds(s * SEG_LEN, 16)
        old = y_ref[spot, :].astype(f32)
        new = jnp.broadcast_to(home_ref[s // 2, s % 2 : s % 2 + 1, :width], old.shape)
        top = lax.broadcasted_iota(jnp.int32, old.shape, 0) == 0
        y_ref[spot, :] = jnp.where(top, new, old).astype(bf16)
    for copy in kept:
        copy.wait()


def segment_forward(ws, wq, wo, wi, wb, x, cot, mask):
    wrows = 16 * ROWS
    rows, width = x.shape
    segs = rows // SEG_LEN
    leads = mask.shape[0]
    hidden = wi.shape[2]
    cross_width = 3 * width
    total = ws.shape[1] + 3 * width + width + 2 * hidden + 4 * cross_width + width
    parts = 5 + 2 * hidden // width + 2
    n_units = parts - 2 + 3
    hbm, vm = pl.BlockSpec(memory_space=pl.ANY), pl.BlockSpec(memory_space=VM)
    arr = jax.ShapeDtypeStruct
    DMA = pltpu.SemaphoreType.DMA
    att_rows = segs * HEADS * SEG_LEN
    big = [
        arr((wrows, 3 * width), bf16), arr((wrows, hidden), bf16), arr((wrows, width), bf16),
        arr((wrows, hidden), bf16),
        arr((rows, 3 * width), bf16), arr((att_rows, SEG_LEN), bf16), arr((rows, width), bf16),
        arr((rows, width), bf16), arr((rows, hidden), bf16), arr((rows, hidden), bf16),
        arr((rows, width), bf16), arr((rows, width), bf16),
    ]
    near = [
        arr((rows, width), bf16), arr((24, width), f32),
        arr((rows, LANES), f32), arr((rows, LANES), f32),
        arr((2, 2, 2 * width), f32), arr((leads, 4 * width), bf16), arr((8, width), f32),
    ]
    return pl.pallas_call(
        forward_kernel,
        out_shape=big + near,
        in_specs=[vm] * 8,
        out_specs=[hbm] * len(big) + [vm] * len(near),
        scratch_shapes=[
            VM((wrows, ws.shape[1]), bf16), VM((wrows, width), bf16), VM((wrows, 3 * width), bf16),
            VM((wrows, hidden), bf16), VM((wrows, hidden), bf16),
            VM((wrows, cross_width), bf16), VM((wrows // 4, width), bf16),
            VM((rows, 3 * width), bf16), VM((att_rows, SEG_LEN), bf16), VM((rows, width), bf16),
            VM((rows, width), f32), VM((rows, width), bf16), VM((rows, hidden), bf16),
            VM((rows, hidden), bf16), VM((rows, width), bf16), VM((rows, width), bf16),
            VM((32, total), bf16), VM((32, total), bf16), VM((ROWS, 4 * cross_width + width), bf16),
            VM((2, 2, 2 * width), f32), VM((8, 2, 2 * width), f32), VM((leads, 2 * width), f32),
            VM((4, 4, leads, width), bf16), VM((8, 2, 2 * width), f32), VM((leads, 3 * width // 4), f32),
            DMA((n_units, 11)), DMA((n_units, 11)), DMA((parts,)), DMA((parts,)),
            DMA((5,)), DMA((5,)), DMA, DMA((12,)),
            DMA((8,)), DMA((8,)), DMA((4, 3)), DMA((4, 4)), DMA, DMA, DMA,
        ],
        compiler_params=pltpu.CompilerParams(
            collective_id=0, has_side_effects=True, vmem_limit_bytes=60 * MIB
        ),
    )(wq, wo, wi, wb, ws, x, cot, mask)


class Scatter:
    def __init__(self, place, grad, off, width, out, index, sems, bufs, wide_a=True):
        self.p, self.grad, self.off, self.out, self.m = place, grad, off, out, index
        self.send, self.recv = sems
        self.pair, self.r1a, self.r1b, self.rx, self.ry, self.r3, self.give = bufs
        self.half = width // 2
        self.a = split_half(width, wide_a)
        self.b = self.half - self.a
        self.sent = []
        p = place
        self.far = (1 - p.y) * 2 + 1 - p.x
        self.groups = (self.far, p.xdp, p.ydp, p.dp)

    def go(self, src, dst, slot, device):
        copy = remote(src, dst, self.send.at[self.m, slot], self.recv.at[self.m, slot], device)
        copy.start()
        self.sent.append(copy)

    def arrived(self, dst, slot):
        remote(dst, dst, self.send.at[self.m, slot], self.recv.at[self.m, slot], self.p.sib).wait_recv()

    def cols(self, part="AB", core=None):
        at, size = {"A": (0, self.a), "B": (self.a, self.b), "AB": (0, self.half)}[part]
        core = self.p.core if core is None else core
        return lanes(self.off + core * self.half + at, size)

    def group(self, dp):
        return rows_at(dp * 4 * ROWS, 4 * ROWS, 16)

    def side(self, dp, part="AB"):
        return self.grad.at[self.group(dp), self.cols(part)]

    def start(self):
        p = self.p
        for i, dp in enumerate(self.groups):
            theirs = self.grad.at[self.group(dp), self.cols("AB", 1 - p.core)]
            self.go(theirs, self.pair.at[self.group(dp)], i, p.sib)

    def add(self, dp, part, other, other_row=0):
        @pl.loop(0, 4)
        def _(i):
            key = (rows_at(dp * 4 * ROWS + i * ROWS, ROWS, 16), self.cols(part))
            self.grad[key] = self.grad[key] + other[rows_at(other_row + i * ROWS, ROWS, 16), :]

    def one(self):
        p = self.p
        for i, dp in enumerate(self.groups):
            self.arrived(self.pair.at[self.group(dp)], i)
            self.add(dp, "AB", self.pair, dp * 4 * ROWS)
            if i == 0:
                self.go(self.side(dp, "A"), self.r1a, 4, p.ynbr)
                if self.b:
                    self.go(self.side(dp, "B"), self.r1b, 5, p.xnbr)

    def two(self):
        p = self.p
        self.arrived(self.r1a, 4)
        self.add(p.xdp, "A", self.r1a)
        self.go(self.side(p.xdp), self.rx, 6, p.xnbr)
        if self.b:
            self.arrived(self.r1b, 5)
            self.add(p.ydp, "B", self.r1b)
        self.go(self.side(p.ydp), self.ry, 7, p.ynbr)

    def three(self):
        p = self.p
        self.arrived(self.rx, 6)
        self.arrived(self.ry, 7)

        @pl.loop(0, 4)
        def _(i):
            key = (rows_at(p.dp * 4 * ROWS + i * ROWS, ROWS, 16), self.cols())
            own = rows_at(i * ROWS, ROWS, 16)
            self.grad[key] = self.grad[key] + (self.rx[own, :] + self.ry[own, :])

        for d in (1, 3, 2):
            z = (p.z + d) % 4
            src = self.grad.at[rows_at((p.dp * 4 + z) * ROWS, ROWS, 16), self.cols()]
            self.go(src, self.r3.at[d - 1], 7 + d, p.at(p.dp, z, p.core))

    def four(self):
        p = self.p
        for d in (1, 3, 2):
            self.arrived(self.r3.at[d - 1], 7 + d)
        rows = rows_at((p.dp * 4 + p.z) * ROWS, ROWS, 16)
        total = self.grad[rows, self.cols()].astype(f32)
        for d in range(3):
            total = total + self.r3[d].astype(f32)
        upper, lower = total[: ROWS // 2], total[ROWS // 2 :]
        first = p.core == 0
        self.give[...] = jnp.where(first, lower, upper)
        self.out[:, self.cols()] = jnp.where(first, upper, lower)
        self.go(self.give, self.out.at[:, self.cols()], 11, p.sib)

    def five(self):
        self.arrived(self.out.at[:, self.cols("AB", 1 - self.p.core)], 11)

    def finish(self):
        for copy in self.sent:
            copy.wait_send()


def split_half(width, wide_a):
    tiles = width // 2 // LANES
    return ((tiles + 1) // 2 if wide_a else max(tiles // 2, 1)) * LANES


def scatter_buffers(width, wide_a):
    half = width // 2
    a = split_half(width, wide_a)
    b = half - a
    return [
        VM((16 * ROWS, half), bf16),
        VM((4 * ROWS, a), bf16),
        VM((4 * ROWS if b else 16, max(b, LANES)), bf16),
        VM((4 * ROWS, half), bf16),
        VM((4 * ROWS, half), bf16),
        VM((3, ROWS, half), bf16),
        VM((ROWS // 2, half), f32),
    ]


SCATTER_LAGS = {"start": 0, "one": 1, "two": 2, "three": 3, "four": 4, "five": 5}
FACTOR_LAGS = {"own": -2, "line": 0, "plane": 1, "last": 2, "drain": 3}


def scatter_step(sums, jobs):
    begun = len([s for s in sums.order[: sums.at] if s[0] == "start"])
    follow = [i for i, s in enumerate(sums.order) if s == ("start", begun + 1)]
    if begun < len(jobs):
        sums.step((follow[0] if follow else sums.order.index(("start", begun)) + 1) - sums.at)


def backward_kernel(*refs):
    (
        cot_ref, x_ref, home_ref, par_ref, r1_ref, r2_ref, z2_ref, fac_ref, csmall_ref,
        p_hbm, a_hbm, c_hbm, nl_hbm, g_hbm, sl_hbm, z1_hbm, w_hbm, o_hbm, i_hbm, b_hbm,
    ) = refs[:20]
    gt_ref, gq_ref, go_ref, gi_ref, gb_ref, gs_ref = refs[20:26]
    (
        pk, at, cx, nl, g, sl, z1, qw, ow, fw,
        h, df, tr, tr2, dwb, dwi, dwo, dwq, dws, small,
        sib_buf, full, tmp,
        f_send, f_recv, pair_send, pair_recv, load, rs_send, rs_recv,
    ) = refs[26:56]
    bufs = refs[56:]
    p = Place()
    rows, width = x_ref.shape
    segs = rows // SEG_LEN
    hidden = g.shape[1]
    pairs = width // LANES
    tile = 256
    chunks = hidden // tile

    loads = {}
    order = [
        ("g", g_hbm, g), ("b", b_hbm, fw), ("sl", sl_hbm, sl), ("nl", nl_hbm, nl), ("z1", z1_hbm, z1),
        ("c", c_hbm, cx), ("o", o_hbm, ow), ("p", p_hbm, pk), ("a", a_hbm, at), ("w", w_hbm, qw),
        ("i", i_hbm, fw),
    ]
    for i, (name, src, dst) in enumerate(order):
        loads[name] = pltpu.make_async_copy(src, dst, load.at[i])
    for name, _, _ in order[:-1]:
        loads[name].start()
    greet(gather_peers(p))

    lead = fac_ref.shape[0]
    lead2 = 2 * lead
    key_f = rows_at((p.dp * 4 + p.z) * lead2, lead2, 16)
    swap = remote(fac_ref, sib_buf, pair_send, pair_recv, p.sib)
    swap.start()

    class Factor(Gather):
        def __init__(self, i):
            mine = lambda z: full.at[key_f, self.cols(p.core)]
            super().__init__(p, full, i * width, width, mine, i, (f_send, f_recv), lead2, i % 2 == 0)

    factors = Staged([Factor(i) for i in range(4)], staggered(4, FACTOR_LAGS))

    def factor_own():
        swap.wait_recv()
        base = (p.dp * 4 + p.z) * lead2
        for i in range(4):
            cols = lanes(i * width + p.core * (width // 2), width // 2)
            full[rows_at(base + p.core * lead, lead, 16), cols] = fac_ref[:, cols]
            full[rows_at(base + (1 - p.core) * lead, lead, 16), cols] = sib_buf[:, cols]

    def factor_grads():
        slab = width // 4

        def rows_of(z, at_col, size):
            return jnp.concatenate(
                [full[rows_at((i * 4 + z) * lead2, lead2, 16), pl.ds(at_col, size)] for i in range(4)],
                axis=0,
            )

        base = 2 * width + 3 * slab
        own = rows_at(p.fsdp * (ROWS // 2), ROWS // 2, 8)
        xl = rows_of(p.dp, base + slab, slab)
        nlf = rows_of(p.dp, base + 2 * slab, slab)
        dff = rows_of(p.dp, base + 3 * slab, slab)
        ctx = rows_of(p.dp, base + 4 * slab, slab)
        for z in range(4):
            tmp[:, :width] = mm(dff, rows_of(z, 0, width), TN)
            gb_ref[1, :, z * width : (z + 1) * width] = tmp[own, :width]
            tmp[:, :width] = mm(nlf, rows_of(z, width, width), TN)
            gi_ref[1, :, z * width : (z + 1) * width] = tmp[own, :width]
            tmp[:, : 3 * slab] = mm(xl, rows_of(z, 2 * width, 3 * slab), TN)
            got = tmp[own, : 3 * slab]
            for j in range(3):
                spot = j * width + z * slab
                gq_ref[1, :, spot : spot + slab] = got[:, j * slab : (j + 1) * slab]
            tmp[:, :slab] = mm(ctx, rows_of(z, base, slab), TN)
            go_ref[1, :, z * slab : (z + 1) * slab] = tmp[own, :slab]

    jobs = []
    for i, (grad, off, size, dst) in enumerate(
        [(dwb, i * width, width, gb_ref.at[0]) for i in range(hidden // width)]
        + [(dwi, i * width, width, gi_ref.at[0]) for i in range(hidden // width)]
        + [(dwo, 0, width, go_ref.at[0]), (dws, 0, dws.shape[1], gs_ref)]
        + [(dwq, i * width, width, gq_ref.at[0]) for i in range(3)]
    ):
        jobs.append(
            Scatter(p, grad, off, size, dst, i, (rs_send, rs_recv), bufs[7 * i : 7 * i + 7], i % 2 == 0)
        )
    sums = Staged(jobs, staggered(len(jobs), SCATTER_LAGS))

    block_rows = 64

    def norm_back(z_ref, r_ref, gain_row, low_ref, sums):
        def step(i, acc):
            key = rows_at(i * block_rows, block_rows, 16)
            dy = h[key, :]
            z = z_ref[key, :].astype(f32)
            r = jnp.concatenate([r_ref[key, :]] * (width // LANES), axis=1)
            e = dy * par_ref[gain_row : gain_row + 1, :]
            first = jnp.mean(e, axis=-1, keepdims=True)
            second = jnp.mean(e * z, axis=-1, keepdims=True)
            d = r * (e - first - z * second)
            h[key, :] = d
            low_ref[key, :] = d.astype(bf16)
            fold = lambda v: jnp.sum(v.reshape(block_rows // 8, 8, width), axis=0)
            return acc[0] + fold(dy * z), acc[1] + fold(dy)

        zero = jnp.zeros((8, width), f32)
        gain, bias = lax.fori_loop(0, rows // block_rows, step, (zero, zero))
        small[sums : sums + 1, :] = jnp.sum(gain, axis=0, keepdims=True)
        small[sums + 2 : sums + 3, :] = jnp.sum(bias, axis=0, keepdims=True)

    def turn(tr, ref):
        @pl.loop(0, width // tile)
        def _(i):
            tr[rows_at(i * tile, tile, 16), :] = ref[:, lanes(i * tile, tile)].T

    def outer(dst, tr, src, part):
        @pl.loop(part * (width // tile), (part + 1) * (width // tile))
        def _(i):
            cols = lanes(i * tile, tile)
            dst[:, cols] = mm(tr[...], src[:, cols], NN).astype(bf16)

    def norm_two():
        @pl.loop(0, rows // block_rows)
        def _(i):
            key = rows_at(i * block_rows, block_rows, 16)
            h[key, :] = cot_ref[key, :].astype(f32)

        for s in range(segs):
            h[s * SEG_LEN : s * SEG_LEN + 1, :] = home_ref[s // 2, s % 2 : s % 2 + 1, width:]
        small[...] = jnp.zeros_like(small)
        small[4:8, :] = csmall_ref[0:4, :]
        for s in range(2):
            row = home_ref[0, s : s + 1, width:] + home_ref[1, s : s + 1, width:]
            small[pl.ds(8 + p.fsdp * 2 + s, 1), :] = row
        norm_back(z2_ref, r2_ref, 1, df, 1)
        turn(tr, df)

    def active_back(first, count):
        @pl.loop(first, first + count)
        def _(i):
            cols = lanes(i * tile, tile)
            d = mm(df[...], fw[:, cols], NN) * sl[:, cols].astype(f32)
            sl[:, cols] = d.astype(bf16)

    def add_back(src, weight):
        @pl.loop(0, width // tile)
        def _(i):
            h[:, lanes(i * tile, tile)] += mm(src[...], weight[rows_at(i * tile, tile, 16), :], NT)

    def context_back():
        @pl.loop(0, width // tile)
        def _(i):
            d = mm(df[...], ow[rows_at(i * tile, tile, 16), :], NT)
            cx[:, lanes(i * tile, tile)] = d.astype(bf16)

    def attend_back(s):
        key = pl.ds(s * SEG_LEN, SEG_LEN)
        factor = (LANES // 2) ** (-0.5)

        @pl.loop(0, pairs)
        def _(j):
            a = at[rows_at((s * pairs + j) * 2 * SEG_LEN, 2 * SEG_LEN, 16), :]
            q_cols = lanes(j * LANES, LANES)
            k_cols = lanes(width + j * LANES, LANES)
            v_cols = lanes(2 * width + j * LANES, LANES)
            qs = jnp.concatenate(lane_halves(pk[key, q_cols]), axis=0)
            ks = jnp.concatenate(lane_halves(pk[key, k_cols]), axis=0)
            ds_in = jnp.concatenate(lane_halves(cx[key, q_cols]), axis=0)
            da = mm(ds_in, pk[key, v_cols], NT)
            af = a.astype(f32)
            ds = (af * (da - jnp.sum(af * da, axis=-1, keepdims=True))).astype(bf16)
            dv = mm(a, ds_in, TN)
            both = jnp.concatenate([ds[:SEG_LEN], ds[SEG_LEN:]], axis=1)
            dq = mm(both, ks, NN) * factor
            dk = mm(ds, qs, TN) * factor
            pk[key, q_cols] = dq.astype(bf16)
            pk[key, k_cols] = dk.astype(bf16)
            pk[key, v_cols] = dv.astype(bf16)

    def result():
        @pl.loop(0, width // tile)
        def _(i):
            cols = lanes(i * tile, tile)
            d = h[:, cols] + mm(pk[...], qw[rows_at(i * tile, tile, 16), :], NT)
            gt_ref[:, cols] = d.astype(bf16)

    def smalls():
        dws[:, :LANES] = small[...].T.astype(bf16)
        dws[:, LANES:] = jnp.zeros((dws.shape[0], LANES), bf16)

    per = hidden // width
    factor_own()
    factors.step(3)
    norm_two()
    factors.step(3)
    loads["g"].wait()
    for i in range(per):
        outer(dwb, tr, g, i)
        scatter_step(sums, jobs)
        factors.step(3)
    loads["b"].wait()
    loads["sl"].wait()
    active_back(0, chunks // 2)
    factors.step(3)
    active_back(chunks // 2, chunks - chunks // 2)
    loads["i"].start()
    loads["nl"].wait()
    turn(tr, nl)
    outer(dwi, tr, sl, 0)
    scatter_step(sums, jobs)
    loads["i"].wait()
    add_back(sl, fw)
    outer(dwi, tr, sl, 1)
    scatter_step(sums, jobs)
    loads["z1"].wait()
    norm_back(z1, r1_ref, 0, df, 0)
    smalls()
    for i in range(2, per - 1):
        outer(dwi, tr, sl, i)
        scatter_step(sums, jobs)
    loads["c"].wait()
    turn(tr2, cx)
    loads["o"].wait()
    outer(dwo, tr2, df, 0)
    context_back()
    loads["p"].wait()
    loads["a"].wait()
    attend_back(0)
    outer(dwi, tr, sl, per - 1)
    scatter_step(sums, jobs)
    attend_back(1)
    scatter_step(sums, jobs)
    attend_back(2)
    scatter_step(sums, jobs)
    attend_back(3)
    turn(tr2, x_ref)
    for i in range(3):
        outer(dwq, tr2, pk, i)
        scatter_step(sums, jobs)
    loads["w"].wait()
    result()
    factors.finish()
    factor_grads()
    sums.finish()
    swap.wait_send()


def segment_backward(near, far):
    cot, x = near[0], near[1]
    rows, width = x.shape
    packed, att, context, nl, g = far[:5]
    hidden = g.shape[1]
    hbm, vm = pl.BlockSpec(memory_space=pl.ANY), pl.BlockSpec(memory_space=VM)
    arr = jax.ShapeDtypeStruct
    own = ROWS // 2
    lead = near[7].shape[0]
    like = lambda v: VM(v.shape, v.dtype)
    wrows = 16 * ROWS
    widths = [width] * (2 * (hidden // width) + 1) + [256] + [width] * 3
    bufs = []
    for i, w in enumerate(widths):
        bufs += scatter_buffers(w, i % 2 == 0)
    DMA = pltpu.SemaphoreType.DMA
    return pl.pallas_call(
        backward_kernel,
        out_shape=[
            arr((rows, width), bf16),
            arr((2, own, 3 * width), f32),
            arr((2, own, width), f32),
            arr((2, own, hidden), f32),
            arr((2, own, hidden), f32),
            arr((own, 256), f32),
        ],
        in_specs=[vm] * len(near) + [hbm] * len(far),
        out_specs=[vm] * 6,
        scratch_shapes=[
            like(packed), like(att), like(context), like(nl), like(g), like(g), like(nl),
            VM((wrows, 3 * width), bf16), VM((wrows, width), bf16), VM((wrows, hidden), bf16),
            VM((rows, width), f32), VM((rows, width), bf16), VM((width, rows), bf16), VM((width, rows), bf16),
            VM((wrows, hidden), bf16), VM((wrows, hidden), bf16), VM((wrows, width), bf16),
            VM((wrows, 3 * width), bf16), VM((wrows, 256), bf16), VM((LANES, width), f32),
            VM((lead, 4 * width), bf16), VM((32 * lead, 4 * width), bf16), VM((width // 4, width), f32),
            DMA((4, 11)), DMA((4, 11)), DMA, DMA, DMA((11,)), DMA((len(widths), 12)), DMA((len(widths), 12)),
        ]
        + bufs,
        compiler_params=pltpu.CompilerParams(
            collective_id=1, has_side_effects=True, vmem_limit_bytes=63 * MIB
        ),
    )(*near, *far)


def matmul(left, right, form):
    return jnp.einsum(form, left, right, preferred_element_type=jnp.float32)


def norm_forward(summed, gains, biases):
    average = jnp.mean(summed, axis=-1, keepdims=True)
    centred = summed - average
    variance = jnp.mean(centred * centred, axis=-1, keepdims=True)
    inverse = lax.rsqrt(variance + epsilon)
    scaled = centred * inverse
    return (scaled * gains + biases, scaled, inverse)


def norm_backward(grad_result, scaled, inverse, gains):
    grad_scaled = grad_result * gains
    first_mean = jnp.mean(grad_scaled, axis=-1, keepdims=True)
    second_mean = jnp.mean(grad_scaled * scaled, axis=-1, keepdims=True)
    grad_sum = inverse * (grad_scaled - first_mean - scaled * second_mean)
    return (grad_sum, jnp.sum(grad_result * scaled, axis=(0, 1)), jnp.sum(grad_result, axis=(0, 1)))


def split_heads(packed):
    groups, length, model_width = packed.shape
    return packed.reshape(groups, length, HEADS, model_width // HEADS)


def join_heads(split_part):
    groups, length, heads_count, head_size = split_part.shape
    return split_part.reshape(groups, length, heads_count * head_size)


def attend_forward(query_part, key_part, value_part, allowed):
    head_size = query_part.shape[-1]
    scores = matmul(query_part, key_part, "glhe,gmhe->ghlm") * head_size ** (-0.5)
    scores = jnp.where(allowed[:, None], scores, -1e30)
    row_max = jnp.max(scores, axis=-1, keepdims=True)
    exp_terms = jnp.exp(scores - row_max)
    row_total = jnp.sum(exp_terms, axis=-1, keepdims=True)
    attention = exp_terms / row_total
    context = matmul(attention.astype(jnp.bfloat16), value_part, "ghlm,gmhe->glhe")
    return (join_heads(context).astype(jnp.bfloat16), row_max + jnp.log(row_total))


def attend_backward(query_part, key_part, value_part, allowed, log_total, grad_context):
    head_size = query_part.shape[-1]
    factor = head_size ** (-0.5)
    scores = matmul(query_part, key_part, "glhe,gmhe->ghlm") * factor
    scores = jnp.where(allowed[:, None], scores, -1e30)
    attention = jnp.exp(scores - log_total)
    grad_attention = matmul(grad_context, value_part, "glhe,gmhe->ghlm")
    grad_value = matmul(attention.astype(jnp.bfloat16), grad_context, "ghlm,glhe->gmhe")
    inner = jnp.sum(attention * grad_attention, axis=-1, keepdims=True)
    grad_scores = (attention * (grad_attention - inner)).astype(jnp.bfloat16)
    grad_query = matmul(grad_scores, key_part, "ghlm,gmhe->glhe") * factor
    grad_key = matmul(grad_scores, query_part, "ghlm,glhe->gmhe") * factor
    return (join_heads(grad_query), join_heads(grad_key), join_heads(grad_value))


def segment_attend(packed):
    groups, length, total_width = packed.shape
    model_width = total_width // 3
    allowed = jnp.ones((groups, length, length), dtype=jnp.bool_)
    context, log_total = attend_forward(
        split_heads(packed[..., :model_width]),
        split_heads(packed[..., model_width : 2 * model_width]),
        split_heads(packed[..., 2 * model_width :]),
        allowed,
    )
    return (context, log_total)


def segment_attend_back(packed, log_total, grad_context):
    groups, length, total_width = packed.shape
    model_width = total_width // 3
    allowed = jnp.ones((groups, length, length), dtype=jnp.bool_)
    grad_query, grad_key, grad_value = attend_backward(
        split_heads(packed[..., :model_width]),
        split_heads(packed[..., model_width : 2 * model_width]),
        split_heads(packed[..., 2 * model_width :]),
        allowed,
        log_total,
        split_heads(grad_context),
    )
    return jnp.concatenate([grad_query, grad_key, grad_value], axis=-1)


def cross_attend(packed, allowed):
    model_width = packed.shape[-1] // 3
    remote = lax.all_gather(packed[..., model_width:], "fsdp", axis=1, tiled=True)
    context, log_total = attend_forward(
        split_heads(packed[..., :model_width]),
        split_heads(remote[..., :model_width]),
        split_heads(remote[..., model_width:]),
        allowed,
    )
    return (context, (remote, log_total))


def cross_attend_back(packed, saved, grad_context, allowed):
    remote, log_total = saved
    model_width = packed.shape[-1] // 3
    grad_query, grad_key, grad_value = attend_backward(
        split_heads(packed[..., :model_width]),
        split_heads(remote[..., :model_width]),
        split_heads(remote[..., model_width:]),
        allowed,
        log_total,
        split_heads(grad_context),
    )
    shared = jnp.concatenate([grad_key, grad_value], axis=-1)
    own_part = lax.psum_scatter(
        shared.astype(jnp.bfloat16), "fsdp", scatter_dimension=1, tiled=True
    ).astype(jnp.float32)
    return jnp.concatenate([grad_query, own_part], axis=-1)


def block_forward(states, weights, attend):
    w_qkv, w_out, w_in, w_back, gains, biases = weights
    gains = gains.astype(jnp.float32)
    biases = biases.astype(jnp.float32)
    states_low = states.astype(jnp.bfloat16)
    packed = matmul(states_low, w_qkv, "gld,de->gle").astype(jnp.bfloat16)
    context, saved = attend(packed)
    branch = matmul(context, w_out, "gld,de->gle")
    normed, scaled_one, inverse_one = norm_forward(states + branch, gains[0], biases[0])
    normed_low = normed.astype(jnp.bfloat16)
    hidden = matmul(normed_low, w_in, "gld,df->glf")
    active_low = jax.nn.gelu(hidden, approximate=False).astype(jnp.bfloat16)
    feed_out = matmul(active_low, w_back, "glf,fd->gld")
    result, scaled_two, inverse_two = norm_forward(normed + feed_out, gains[1], biases[1])
    kept = (
        states_low,
        packed,
        context,
        saved,
        scaled_one,
        inverse_one,
        normed_low,
        hidden,
        active_low,
        scaled_two,
        inverse_two,
    )
    return (result, kept)


def block_backward(grad_result, kept, weights, attend_back):
    w_qkv, w_out, w_in, w_back, gains, biases = weights
    gains = gains.astype(jnp.float32)
    (
        states_low,
        packed,
        context,
        saved,
        scaled_one,
        inverse_one,
        normed_low,
        hidden,
        active_low,
        scaled_two,
        inverse_two,
    ) = kept
    grad_sum_two, gain_two, bias_two = norm_backward(grad_result, scaled_two, inverse_two, gains[1])
    grad_feed = grad_sum_two.astype(jnp.bfloat16)
    grad_active = matmul(grad_feed, w_back, "gld,fd->glf")
    cumulative = 0.5 * (1.0 + lax.erf(hidden * root_half))
    slope = cumulative + hidden * inv_root_tau * jnp.exp(-0.5 * hidden * hidden)
    grad_hidden = (grad_active * slope).astype(jnp.bfloat16)
    grad_normed = grad_sum_two + matmul(grad_hidden, w_in, "glf,df->gld")
    grad_sum_one, gain_one, bias_one = norm_backward(grad_normed, scaled_one, inverse_one, gains[0])
    grad_branch = grad_sum_one.astype(jnp.bfloat16)
    grad_context = matmul(grad_branch, w_out, "gle,de->gld").astype(jnp.bfloat16)
    grad_packed = attend_back(packed, saved, grad_context).astype(jnp.bfloat16)
    grad_states = grad_sum_one + matmul(grad_packed, w_qkv, "gle,de->gld")
    factors = (
        states_low,
        grad_packed,
        context,
        grad_branch,
        normed_low,
        grad_hidden,
        grad_feed,
        active_low,
    )
    smalls = (jnp.stack([gain_one, gain_two]), jnp.stack([bias_one, bias_two]))
    return (grad_states, factors, smalls)


def weight_terms(factors):
    (
        states_low,
        grad_packed,
        context,
        grad_branch,
        normed_low,
        grad_hidden,
        grad_feed,
        active_low,
    ) = factors
    term_qkv = matmul(states_low, grad_packed, "gld,gle->de")
    term_out = matmul(context, grad_branch, "gld,gle->de")
    term_in = matmul(normed_low, grad_hidden, "gld,glf->df")
    term_back = matmul(grad_feed, active_low, "gld,glf->df")
    return jnp.concatenate([term_qkv, term_out, term_in, term_back], axis=1)


def gather_segment(w_qkv, w_out, w_in, w_back, norm_gain, norm_bias):
    return (
        lax.all_gather(w_qkv[0], ("dp", "fsdp"), axis=0, tiled=True),
        lax.all_gather(w_out[0], ("dp", "fsdp"), axis=0, tiled=True),
        lax.all_gather(w_in[0], ("dp", "fsdp"), axis=0, tiled=True),
        lax.all_gather(w_back[0], ("dp", "fsdp"), axis=1, tiled=True),
        lax.all_gather(norm_gain[0], ("dp", "fsdp"), axis=1, tiled=True),
        lax.all_gather(norm_bias[0], ("dp", "fsdp"), axis=1, tiled=True),
    )


def gather_cross(pos_embed, w_qkv, w_out, w_in, w_back, norm_gain, norm_bias):
    gathered = (
        lax.all_gather(w_qkv[1], ("dp", "fsdp"), axis=0, tiled=True),
        lax.all_gather(w_out[1], ("dp", "fsdp"), axis=0, tiled=True),
        lax.all_gather(w_in[1], ("dp", "fsdp"), axis=0, tiled=True),
        lax.all_gather(w_back[1], ("dp", "fsdp"), axis=1, tiled=True),
        lax.all_gather(norm_gain[1], ("dp", "fsdp"), axis=1, tiled=True),
        lax.all_gather(norm_bias[1], ("dp", "fsdp"), axis=1, tiled=True),
        lax.all_gather(pos_embed, ("dp", "fsdp"), axis=1, tiled=True),
    )
    return (gathered[:6], gathered[6])


def layer_forward(tokens, doc_ids, seg_weights, cross_weights, pos_full):
    rows, local_len, model_width = tokens.shape
    seg_count = local_len // SEG_LEN
    segments = tokens.reshape(rows * seg_count, SEG_LEN, model_width).astype(jnp.float32)
    seg_out, seg_kept = block_forward(segments, seg_weights, segment_attend)
    start = lax.axis_index("fsdp") * seg_count
    pos_local = lax.dynamic_slice_in_dim(pos_full, start, seg_count, 0).astype(jnp.float32)
    leaders = seg_out[:, 0, :].reshape(rows, seg_count, model_width) + pos_local
    own_docs = lax.dynamic_slice_in_dim(doc_ids, start, seg_count, 1)
    allowed = own_docs[:, :, None] == doc_ids[:, None, :]
    cross_out, cross_kept = block_forward(
        leaders, cross_weights, partial(cross_attend, allowed=allowed)
    )
    joined = jnp.concatenate(
        [cross_out.reshape(rows * seg_count, 1, model_width), seg_out[:, 1:, :]], axis=1
    )
    output = joined.reshape(rows, local_len, model_width).astype(jnp.bfloat16)
    return (output, (seg_kept, cross_kept, allowed))


def layer_backward(cotangent, doc_ids, kept, seg_weights, cross_weights):
    seg_kept, cross_kept, allowed = kept
    rows, local_len, model_width = cotangent.shape
    seg_count = local_len // SEG_LEN
    grad_all = cotangent.reshape(rows * seg_count, SEG_LEN, model_width).astype(jnp.float32)
    grad_cross = grad_all[:, 0, :].reshape(rows, seg_count, model_width)
    grad_leaders, cross_factors, cross_smalls = block_backward(
        grad_cross, cross_kept, cross_weights, partial(cross_attend_back, allowed=allowed)
    )
    start = lax.axis_index("fsdp") * seg_count
    empty_pos = jnp.zeros((doc_ids.shape[1], model_width), jnp.float32)
    grad_pos = lax.dynamic_update_slice_in_dim(empty_pos, jnp.sum(grad_leaders, axis=0), start, 0)
    grad_seg = jnp.concatenate(
        [grad_leaders.reshape(rows * seg_count, 1, model_width), grad_all[:, 1:, :]], axis=1
    )
    grad_states, seg_factors, seg_smalls = block_backward(
        grad_seg, seg_kept, seg_weights, segment_attend_back
    )
    grad_tokens = grad_states.reshape(rows, local_len, model_width).astype(jnp.bfloat16)
    return (grad_tokens, seg_factors, cross_factors, seg_smalls, cross_smalls, grad_pos)


def body(tokens, doc_ids, pos_embed, w_qkv, w_out, w_in, w_back, norm_gain, norm_bias, cotangent):
    seg_weights = gather_segment(w_qkv, w_out, w_in, w_back, norm_gain, norm_bias)
    cross_weights, pos_full = gather_cross(
        pos_embed, w_qkv, w_out, w_in, w_back, norm_gain, norm_bias
    )
    output, kept = layer_forward(tokens, doc_ids, seg_weights, cross_weights, pos_full)
    grad_tokens, seg_factors, cross_factors, seg_smalls, cross_smalls, grad_pos = layer_backward(
        cotangent, doc_ids, kept, seg_weights, cross_weights
    )
    model_width = tokens.shape[2]
    hidden_width = w_in.shape[2]
    seg_term = lax.psum_scatter(
        weight_terms(seg_factors), ("dp", "fsdp"), scatter_dimension=0, tiled=True
    )
    cross_term = lax.psum_scatter(
        weight_terms(cross_factors), ("dp", "fsdp"), scatter_dimension=0, tiled=True
    )
    stacked = jnp.stack([seg_term, cross_term])
    grad_qkv = stacked[:, :, : 3 * model_width]
    grad_out = stacked[:, :, 3 * model_width : 4 * model_width]
    grad_in = stacked[:, :, 4 * model_width : 4 * model_width + hidden_width]
    grad_back = jnp.transpose(stacked[:, :, 4 * model_width + hidden_width :], (0, 2, 1))
    gain_all = jnp.stack([seg_smalls[0], cross_smalls[0]])
    bias_all = jnp.stack([seg_smalls[1], cross_smalls[1]])
    grad_gain, grad_bias, pos_shard = (
        lax.psum_scatter(gain_all, ("dp", "fsdp"), scatter_dimension=2, tiled=True),
        lax.psum_scatter(bias_all, ("dp", "fsdp"), scatter_dimension=2, tiled=True),
        lax.psum_scatter(grad_pos, ("dp", "fsdp"), scatter_dimension=1, tiled=True),
    )
    return (
        output,
        grad_tokens,
        pos_shard,
        grad_qkv,
        grad_out,
        grad_in,
        grad_back,
        grad_gain,
        grad_bias,
    )


def fast_body(tokens, doc_ids, pos_embed, w_qkv, w_out, w_in, w_back, norm_gain, norm_bias, cotangent):
    nrows, local_len, width = tokens.shape
    rows = nrows * local_len
    segs = rows // SEG_LEN
    hidden = w_in.shape[2]
    items = jnp.concatenate([norm_gain[0], norm_bias[0], norm_gain[1], norm_bias[1], pos_embed], axis=0)
    small = jnp.pad(items.T, ((0, 0), (0, 256 - items.shape[0])))
    x = tokens.reshape(rows, width)
    cot = cotangent.reshape(rows, width)
    own_row = lax.dynamic_index_in_dim(doc_ids, lax.axis_index("fsdp") % 2, 0, keepdims=False)
    mask = (own_row[:, None] == own_row[None, :]).astype(f32)
    (
        s_qkv, s_in, s_out, s_back,
        packed, att, context, nl, act, slope, z_one, z_two,
        output, par, r_one, r_two, home, fac, cross_small,
    ) = segment_forward(small, w_qkv, w_out, w_in, jnp.swapaxes(w_back, 1, 2), x, cot, mask)
    grad_tokens, g_qkv, g_out, g_in, g_back, t_small = segment_backward(
        (cot, x, home, par, r_one, r_two, z_two, fac, cross_small),
        (packed, att, context, nl, act, slope, z_one, s_qkv, s_out, s_in, s_back),
    )
    s = t_small.T
    return (
        output.reshape(tokens.shape),
        grad_tokens.reshape(tokens.shape),
        s[8 : 8 + doc_ids.shape[1]],
        g_qkv,
        g_out,
        g_in,
        jnp.swapaxes(g_back, 1, 2),
        jnp.stack([s[0:2], s[4:6]]),
        jnp.stack([s[2:4], s[6:8]]),
    )


def solution(mesh):
    fast = dict(mesh.shape) == {"dp": 4, "fsdp": 8}
    return jax.shard_map(
        fast_body if fast else body,
        mesh=mesh,
        in_specs=(
            P("dp", "fsdp", None),
            P("dp", None),
            P(None, ("dp", "fsdp")),
            P(None, ("dp", "fsdp"), None),
            P(None, ("dp", "fsdp"), None),
            P(None, ("dp", "fsdp"), None),
            P(None, None, ("dp", "fsdp")),
            P(None, None, ("dp", "fsdp")),
            P(None, None, ("dp", "fsdp")),
            P("dp", "fsdp", None),
        ),
        out_specs=(
            P("dp", "fsdp", None),
            P("dp", "fsdp", None),
            P(None, ("dp", "fsdp")),
            P(None, ("dp", "fsdp"), None),
            P(None, ("dp", "fsdp"), None),
            P(None, ("dp", "fsdp"), None),
            P(None, None, ("dp", "fsdp")),
            P(None, None, ("dp", "fsdp")),
            P(None, None, ("dp", "fsdp")),
        ),
        check_vma=False,
    )
```

```python
from functools import partial

import jax
import jax.numpy as jnp
from jax import lax
from jax.experimental import pallas as pl
from jax.experimental.pallas import tpu as pltpu
from jax.sharding import PartitionSpec as P

HEADS = 12
SEG_LEN = 128


epsilon = 1e-05
root_half = 0.7071067811865476
inv_root_tau = 0.3989422804014327

bf16 = jnp.bfloat16
f32 = jnp.float32
MESH = pl.DeviceIdType.MESH
VM = pltpu.VMEM
MIB = 1024 * 1024
ROWS = 48
LANES = 128


class Place:
    def __init__(self):
        self.dp = lax.axis_index("dp")
        self.fsdp = lax.axis_index("fsdp")
        self.y, self.x = self.dp // 2, self.dp % 2
        self.z, self.core = self.fsdp // 2, self.fsdp % 2

    def at(self, dp, z, core):
        return (dp, z * 2 + core)

    @property
    def sib(self):
        return (self.dp, self.z * 2 + 1 - self.core)

    @property
    def xdp(self):
        return self.y * 2 + 1 - self.x

    @property
    def ydp(self):
        return (1 - self.y) * 2 + self.x

    @property
    def xnbr(self):
        return (self.xdp, self.fsdp)

    @property
    def ynbr(self):
        return (self.ydp, self.fsdp)


def greet(devices):
    barrier = pltpu.get_barrier_semaphore()
    for device in devices:
        pl.semaphore_signal(barrier, inc=1, device_id=device, device_id_type=MESH)
    pl.semaphore_wait(barrier, len(devices))


def remote(src, dst, send, recv, device):
    return pltpu.make_async_remote_copy(
        src_ref=src, dst_ref=dst, send_sem=send, recv_sem=recv, device_id=device, device_id_type=MESH
    )


def lanes(start, size):
    if isinstance(start, int):
        return pl.ds(start, size)
    return pl.ds(pl.multiple_of(start, LANES), size)


def rows_at(start, size, unit):
    return pl.ds(pl.multiple_of(start, unit), size)


class Gather:
    def __init__(self, place, out, off, width, source, index, sems, height2, wide_a=True):
        self.p, self.out, self.off, self.source = place, out, off, source
        self.m, self.sems, self.h2 = index, sems, height2
        self.half = width // 2
        tiles = self.half // LANES
        self.a = ((tiles + 1) // 2 if wide_a else max(tiles // 2, 1)) * LANES
        self.b = self.half - self.a
        self.sent = []
        self.far = (1 - place.y) * 2 + 1 - place.x

    def cols(self, core, part="AB"):
        at, size = {"A": (0, self.a), "B": (self.a, self.b), "AB": (0, self.half)}[part]
        return lanes(self.off + core * self.half + at, size)

    def block(self, z, core):
        return self.out.at[rows_at((self.p.dp * 4 + z) * self.h2, self.h2, 16), self.cols(core)]

    def group(self, dp, core, part="AB"):
        return self.out.at[rows_at(dp * 4 * self.h2, self.h2 * 4, 16), self.cols(core, part)]

    def go(self, src, dst, slot, device):
        copy = remote(src, dst, self.sems[0].at[self.m, slot], self.sems[1].at[self.m, slot], device)
        copy.start()
        self.sent.append(copy)

    def hand(self, ref, slot):
        self.go(ref, ref, slot, self.p.sib)

    def arrived(self, dst, slot):
        remote(dst, dst, self.sems[0].at[self.m, slot], self.sems[1].at[self.m, slot], self.p.sib).wait_recv()

    def own(self):
        p = self.p
        for d in (1, 3, 2):
            z = (p.z + d) % 4
            self.go(self.source(z), self.block(p.z, p.core), d - 1, p.at(p.dp, z, p.core))

    def line(self):
        p = self.p
        for d in (1, 3, 2):
            self.arrived(self.block((p.z + 4 - d) % 4, p.core), d - 1)
        mine = self.group(p.dp, p.core)
        self.go(mine, mine, 3, p.xnbr)
        self.go(mine, mine, 4, p.ynbr)
        self.hand(mine, 7)

    def plane(self):
        p = self.p
        over_x, over_y = self.group(p.xdp, p.core), self.group(p.ydp, p.core)
        self.arrived(over_x, 3)
        part = self.group(p.xdp, p.core, "A")
        self.go(part, part, 5, p.ynbr)
        self.arrived(over_y, 4)
        if self.b:
            part = self.group(p.ydp, p.core, "B")
            self.go(part, part, 6, p.xnbr)
        self.hand(over_x, 8)
        self.hand(over_y, 9)

    def last(self):
        p = self.p
        self.arrived(self.group(self.far, p.core, "A"), 5)
        if self.b:
            self.arrived(self.group(self.far, p.core, "B"), 6)
        self.hand(self.group(self.far, p.core), 10)

    def drain(self):
        p = self.p
        for slot, dp in ((7, p.dp), (8, p.xdp), (9, p.ydp), (10, self.far)):
            self.arrived(self.group(dp, 1 - p.core), slot)

    def finish(self):
        for copy in self.sent:
            copy.wait_send()


class Staged:
    def __init__(self, units, order):
        self.units, self.order, self.at = units, order, 0

    def step(self, count=1):
        for name, i in self.order[self.at : self.at + count]:
            getattr(self.units[i], name)()
        self.at += count

    def upto(self, name, i):
        spot = self.order.index((name, i)) + 1
        if spot > self.at:
            self.step(spot - self.at)

    def finish(self):
        self.step(len(self.order) - self.at)
        for unit in self.units:
            unit.finish()


def staggered(count, lags, first=0):
    order = []
    for t in range(min(lags.values()), count + max(lags.values())):
        for name, lag in lags.items():
            if 0 <= t - lag < count and (t >= 0 or lag < 0):
                order.append((name, t - lag + first))
    return order


def gather_peers(p):
    peers = [p.sib, p.xnbr, p.ynbr]
    for d in (1, 2, 3):
        peers.append(p.at(p.dp, (p.z + d) % 4, p.core))
    return peers


def everyone(p):
    return [
        (lax.rem(p.dp + i, 4), lax.rem(p.fsdp + j, 8)) for i in range(4) for j in range(8) if i or j
    ]


NEG = -1e30


def mm(a, b, dims):
    return lax.dot_general(a, b, (dims, ((), ())), preferred_element_type=f32)


NN = ((1,), (0,))
NT = ((1,), (1,))
TN = ((0,), (0,))


def norm_rows(summed, gain, bias):
    centred = summed - jnp.mean(summed, axis=-1, keepdims=True)
    variance = jnp.mean(centred * centred, axis=-1, keepdims=True)
    inverse = lax.rsqrt(variance + epsilon)
    scaled = centred * inverse
    return scaled * gain + bias, scaled, inverse


def norm_rows_back(grad, scaled, inverse, gain):
    g = grad * gain
    first = jnp.mean(g, axis=-1, keepdims=True)
    second = jnp.mean(g * scaled, axis=-1, keepdims=True)
    return inverse * (g - first - scaled * second)


def gelu_parts(u):
    cumulative = 0.5 * (1.0 + lax.erf(u * root_half))
    return cumulative, cumulative + u * inv_root_tau * jnp.exp(-0.5 * u * u)


def lane_halves(v):
    low = lax.broadcasted_iota(jnp.int32, v.shape, 1) < LANES // 2
    zero = jnp.zeros_like(v)
    return jnp.where(low, v, zero), jnp.where(low, zero, v)


FORWARD_LAGS = {"own": -3, "line": 0, "plane": 1, "last": 2, "drain": 3}


def forward_order(n_seg, n_cross):
    n = n_seg + n_cross
    order = staggered(n, FORWARD_LAGS)
    stop = order.index(("line", n_seg))
    head, rest = order[:stop], order[stop:]
    head += [s for s in rest if s[0] == "own"]
    done = set(head)
    tail = [("plane", n_seg - 1), ("line", n_seg), ("line", n_seg + 1)]
    for u in range(n_seg - 3, n_seg):
        tail += [("last", u), ("drain", u)]
    tail += [("plane", n_seg), ("line", n_seg + 2)]
    for u in range(n_seg, n):
        tail += [("last", u), ("plane", u + 1), ("drain", u)]
    return head + [s for s in tail if s not in done and s[1] < n]


class Scatter:
    def __init__(self, place, grad, off, width, out, index, sems, bufs, wide_a=True):
        self.p, self.grad, self.off, self.out, self.m = place, grad, off, out, index
        self.send, self.recv = sems
        self.pair, self.r1a, self.r1b, self.rx, self.ry, self.r3, self.give = bufs
        self.half = width // 2
        self.a = split_half(width, wide_a)
        self.b = self.half - self.a
        self.sent = []
        self.free, self.waits, self.frees = None, False, False
        p = place
        self.far = (1 - p.y) * 2 + 1 - p.x
        self.groups = (self.far, p.xdp, p.ydp, p.dp)

    def go(self, src, dst, slot, device):
        copy = remote(src, dst, self.send.at[self.m, slot], self.recv.at[self.m, slot], device)
        copy.start()
        self.sent.append(copy)

    def arrived(self, dst, slot):
        remote(dst, dst, self.send.at[self.m, slot], self.recv.at[self.m, slot], self.p.sib).wait_recv()

    def cols(self, part="AB", core=None):
        at, size = {"A": (0, self.a), "B": (self.a, self.b), "AB": (0, self.half)}[part]
        core = self.p.core if core is None else core
        return lanes(self.off + core * self.half + at, size)

    def group(self, dp):
        return rows_at(dp * 4 * ROWS, 4 * ROWS, 16)

    def side(self, dp, part="AB"):
        return self.grad.at[self.group(dp), self.cols(part)]

    def start(self):
        p = self.p
        if self.waits:
            pl.semaphore_wait(self.free, 1)
        for i, dp in enumerate(self.groups):
            theirs = self.grad.at[self.group(dp), self.cols("AB", 1 - p.core)]
            self.go(theirs, self.pair.at[self.group(dp)], i, p.sib)

    def add(self, dp, part, other, other_row=0):
        @pl.loop(0, 4)
        def _(i):
            key = (rows_at(dp * 4 * ROWS + i * ROWS, ROWS, 16), self.cols(part))
            self.grad[key] = self.grad[key] + other[rows_at(other_row + i * ROWS, ROWS, 16), :]

    def one(self):
        p = self.p
        for i, dp in enumerate(self.groups):
            self.arrived(self.pair.at[self.group(dp)], i)
            self.add(dp, "AB", self.pair, dp * 4 * ROWS)
            if i == 0:
                self.go(self.side(dp, "A"), self.r1a, 4, p.ynbr)
                if self.b:
                    self.go(self.side(dp, "B"), self.r1b, 5, p.xnbr)
        if self.frees:
            pl.semaphore_signal(self.free, inc=1, device_id=p.sib, device_id_type=MESH)

    def two(self):
        p = self.p
        self.arrived(self.r1a, 4)
        self.add(p.xdp, "A", self.r1a)
        self.go(self.side(p.xdp), self.rx, 6, p.xnbr)
        if self.b:
            self.arrived(self.r1b, 5)
            self.add(p.ydp, "B", self.r1b)
        self.go(self.side(p.ydp), self.ry, 7, p.ynbr)

    def three(self):
        p = self.p
        self.arrived(self.rx, 6)
        self.arrived(self.ry, 7)

        @pl.loop(0, 4)
        def _(i):
            key = (rows_at(p.dp * 4 * ROWS + i * ROWS, ROWS, 16), self.cols())
            own = rows_at(i * ROWS, ROWS, 16)
            self.grad[key] = self.grad[key] + (self.rx[own, :] + self.ry[own, :])

        for d in (1, 3, 2):
            z = (p.z + d) % 4
            src = self.grad.at[rows_at((p.dp * 4 + z) * ROWS, ROWS, 16), self.cols()]
            self.go(src, self.r3.at[d - 1], 7 + d, p.at(p.dp, z, p.core))

    def four(self):
        p = self.p
        for d in (1, 3, 2):
            self.arrived(self.r3.at[d - 1], 7 + d)
        rows = rows_at((p.dp * 4 + p.z) * ROWS, ROWS, 16)
        total = self.grad[rows, self.cols()].astype(f32)
        for d in range(3):
            total = total + self.r3[d].astype(f32)
        upper, lower = total[: ROWS // 2], total[ROWS // 2 :]
        first = p.core == 0
        self.give[...] = jnp.where(first, lower, upper)
        self.out[:, self.cols()] = jnp.where(first, upper, lower)
        self.go(self.give, self.out.at[:, self.cols()], 11, p.sib)

    def five(self):
        self.arrived(self.out.at[:, self.cols("AB", 1 - self.p.core)], 11)

    def finish(self):
        for copy in self.sent:
            copy.wait_send()


def split_half(width, wide_a):
    tiles = width // 2 // LANES
    return ((tiles + 1) // 2 if wide_a else max(tiles // 2, 1)) * LANES


def scatter_buffers(width, wide_a):
    half = width // 2
    a = split_half(width, wide_a)
    b = half - a
    return [
        VM((4 * ROWS, a), bf16),
        VM((4 * ROWS if b else 16, max(b, LANES)), bf16),
        VM((4 * ROWS, half), bf16),
        VM((4 * ROWS, half), bf16),
        VM((3, ROWS, half), bf16),
        VM((ROWS // 2, half), f32),
    ]


SCATTER_LAGS = {"start": 0, "one": 1, "two": 2, "three": 3, "four": 4, "five": 5}
PAIR_SLOTS = 4


def tail_units(width):
    return [(0, width), (width, width), (2 * width, width - 256), (3 * width - 256, 256)]


def scatter_step(sums, jobs):
    begun = len([s for s in sums.order[: sums.at] if s[0] == "start"])
    follow = [i for i, s in enumerate(sums.order) if s == ("start", begun + 1)]
    if begun < len(jobs):
        sums.step((follow[0] if follow else sums.order.index(("start", begun)) + 1) - sums.at)


def layer_kernel(*refs):
    wq_ref, wo_ref, wi_ref, wb_ref, ws_ref, x_ref, cot_ref, mask_ref = refs[:8]
    y_ref, gt_ref, gq_ref, go_ref, gi_ref, gb_ref, gs_ref = refs[8:15]
    (
        sw, ow, qw, iw, bw, cw, cwo,
        pk, at, cx, h, nl, g, sl, z1, z2, r1_ref, r2_ref, par_ref,
        own_buf, sib_buf, block,
        lead_out, gbuf, lead, xbuf, ybuf, dpack, home_ref, fac, fac_sib, csmall,
        df, tr, tr2, dws, small, full, tmp, ring, pair_wide, pair_small,
        s_send, s_recv, pair_send, pair_recv, wo_send, wo_recv, local,
        g_send, g_recv, x_send, x_recv, h_send, h_recv, lead_sem,
        f_send, f_recv, swap_send, swap_recv, rs_send, rs_recv, free,
    ) = refs[15:78]
    bufs = refs[78:]
    p = Place()
    rows, width = x_ref.shape
    segs = rows // SEG_LEN
    hidden = iw.shape[1]
    pairs = width // LANES
    slab = width // 4
    cross_width = cw.shape[1]
    half_rows = ROWS // 2
    key_own = rows_at((p.dp * 4 + p.z) * ROWS, ROWS, 16)

    sizes = [ws_ref.shape[1]] + [width] * (3 + 1 + 2 * (hidden // width)) + [4 * cross_width, width]
    starts = [sum(sizes[:i]) for i in range(len(sizes))]
    n_seg = len(sizes) - 2
    part_cross, part_wo = n_seg, n_seg + 1

    def put(start, value):
        zero = jnp.zeros((own_buf.shape[0] - half_rows, value.shape[1]), f32)
        full = jnp.concatenate([value.astype(f32), zero], axis=0).astype(bf16)
        own_buf[:, pl.ds(start, value.shape[1])] = full

    def pair(i):
        cols = pl.ds(starts[i], sizes[i])
        return remote(
            own_buf.at[:, cols], sib_buf.at[:, cols], pair_send.at[i], pair_recv.at[i], p.sib
        )

    def stage(i):
        spot = starts[i]
        per = hidden // width
        if i == 0:
            put(spot, ws_ref[...])
        elif i < 4:
            put(spot, wq_ref[0, :, (i - 1) * width : i * width])
        elif i == 4:
            put(spot, wo_ref[0])
        elif i < 5 + per:
            put(spot, wi_ref[0, :, (i - 5) * width : (i - 4) * width])
        elif i < 5 + 2 * per:
            put(spot, wb_ref[0, :, (i - 5 - per) * width : (i - 4 - per) * width])
        elif i == part_cross:
            for z in range(4):
                heads = [wq_ref[1, :, j * width + z * slab : j * width + (z + 1) * slab] for j in range(3)]
                heads.append(heads[2])
                put(spot, jnp.concatenate([v.astype(f32) for v in heads], axis=1).astype(bf16))
                put(spot + width, wi_ref[1, :, z * width : (z + 1) * width])
                put(spot + 2 * width, wb_ref[1, :, z * width : (z + 1) * width])
                spot += cross_width
        else:
            put(spot, wo_ref[1])

    def joined(start, size):
        cols = lanes(start, size)
        first = p.core == 0
        mine = own_buf[:, cols].astype(f32)[:half_rows]
        theirs = sib_buf[:, cols].astype(f32)[:half_rows]
        both = [jnp.where(first, mine, theirs), jnp.where(first, theirs, mine)]
        return jnp.concatenate(both, axis=0).astype(bf16)

    ahead = 4

    def begin(i):
        if i < n_seg + 2:
            stage(i)
            pair(i).start()

    stage(0)
    greet(everyone(p))
    pair(0).start()
    for i in range(1, ahead):
        begin(i)

    sems = (s_send, s_recv)
    dests = [(sw, 0)] + [(qw, i * width) for i in range(3)] + [(ow, 0)]
    dests += [(iw, i * width) for i in range(hidden // width)]
    dests += [(bw, i * width) for i in range(hidden // width)]

    class SegUnit(Gather):
        def __init__(self, i):
            dst, off = dests[i]
            mine = lambda z: dst.at[key_own, self.cols(p.core)]
            super().__init__(p, dst, off, sizes[i], mine, i, sems, ROWS, i % 2 == 0)
            self.i = i

        def own(self):
            pair(self.i).wait_recv()
            self.out[key_own, self.cols(p.core)] = joined(
                starts[self.i] + p.core * self.half, self.half
            )
            super().own()
            begin(self.i + ahead)

    class CrossUnit(Gather):
        def __init__(self, i):
            start = i * width
            self.i = i

            def mine(z):
                spot = z * cross_width + start + p.core * self.half
                return block.at[:, lanes(spot, self.half)]

            super().__init__(p, cw, start, width, mine, n_seg + i, sems, ROWS, i % 2 == 0)

        def own(self):
            if self.i == 0:
                pair(part_cross).wait_recv()

                @pl.loop(0, 4 * cross_width // width)
                def _(k):
                    block[:, lanes(k * width, width)] = joined(starts[part_cross] + k * width, width)

            spot = p.z * cross_width + self.i * width + p.core * self.half
            self.out[key_own, self.cols(p.core)] = block[:, lanes(spot, self.half)]
            super().own()

    units = [SegUnit(i) for i in range(n_seg)] + [CrossUnit(i) for i in range(cross_width // width)]
    n_cross = len(units) - n_seg
    comm = Staged(units, forward_order(n_seg, n_cross))

    def need(i):
        comm.upto("drain", i)

    def pump():
        comm.step(5)

    half_wo = width // 2
    wo_block = block.at[:, pl.ds(4 * cross_width, width)]
    wo_src = block.at[:, lanes(4 * cross_width + p.core * half_wo, half_wo)]
    wo_dst = cwo.at[rows_at(p.z * ROWS, ROWS, 16), lanes(p.core * half_wo, half_wo)]

    def wo_copy(i):
        return remote(wo_src, wo_dst, wo_send.at[i], wo_recv.at[p.z], p.at(i, p.dp, p.core))

    def wo_start():
        pair(part_wo).wait_recv()
        wo_block[...] = joined(starts[part_wo], width)
        for i in range(4):
            here = jnp.logical_and(p.dp == i, p.dp == p.z)

            @pl.when(jnp.logical_not(here))
            def _():
                wo_copy(i).start()

            @pl.when(here)
            def _():
                mine = pltpu.make_async_copy(wo_src, wo_dst, local)
                mine.start()
                mine.wait()

    wo_mine = cwo.at[:, lanes(p.core * half_wo, half_wo)]
    wo_theirs = cwo.at[:, lanes((1 - p.core) * half_wo, half_wo)]
    wo_hand = remote(wo_mine, wo_mine, wo_send.at[4], wo_recv.at[4], p.sib)

    def wo_middle():
        for i in range(4):
            piece = cwo.at[pl.ds(i * ROWS, ROWS), lanes(p.core * half_wo, half_wo)]

            @pl.when(jnp.logical_not(jnp.logical_and(p.z == p.dp, p.z == i)))
            def _():
                remote(piece, piece, wo_send.at[i], wo_recv.at[i], p.sib).wait_recv()

        wo_hand.start()

    def wo_finish():
        remote(wo_theirs, wo_theirs, wo_send.at[4], wo_recv.at[4], p.sib).wait_recv()
        wo_hand.wait_send()
        for i in range(4):

            @pl.when(jnp.logical_not(jnp.logical_and(p.dp == i, p.dp == p.z)))
            def _():
                wo_copy(i).wait_send()

    tile = 256

    def params():
        par_ref[...] = sw[...].astype(f32).T[: par_ref.shape[0]]

    def project(first, count):
        @pl.loop(first, first + count)
        def _(i):
            cols = lanes(i * tile, tile)
            pk[:, cols] = mm(x_ref[...], qw[:, cols], NN).astype(bf16)

    def attend(s):
        key = pl.ds(s * SEG_LEN, SEG_LEN)

        @pl.loop(0, pairs)
        def _(j):
            q2 = pk[key, lanes(j * LANES, LANES)]
            k2 = pk[key, lanes(width + j * LANES, LANES)]
            v2 = pk[key, lanes(2 * width + j * LANES, LANES)]
            scores = mm(jnp.concatenate(lane_halves(q2), axis=0), k2, NT) * (LANES // 2) ** (-0.5)
            top = jnp.max(scores, axis=-1, keepdims=True)
            terms = jnp.exp(scores - top)
            a = (terms / jnp.sum(terms, axis=-1, keepdims=True)).astype(bf16)
            at[rows_at((s * pairs + j) * 2 * SEG_LEN, 2 * SEG_LEN, 16), :] = a
            both = jnp.concatenate([a[:SEG_LEN], a[SEG_LEN:]], axis=1)
            c2 = mm(both, jnp.concatenate(lane_halves(v2), axis=0), NN)
            cx[key, lanes(j * LANES, LANES)] = c2.astype(bf16)

    block_rows = 64

    def branch():
        @pl.loop(0, width // tile)
        def _(i):
            cols = lanes(i * tile, tile)
            h[:, cols] = x_ref[:, cols].astype(f32) + mm(cx[...], ow[:, cols], NN)

        @pl.loop(0, rows // block_rows)
        def _(i):
            key = rows_at(i * block_rows, block_rows, 16)
            normed, scaled, inverse = norm_rows(h[key, :], par_ref[0:1, :], par_ref[2:3, :])
            h[key, :] = normed
            nl[key, :] = normed.astype(bf16)
            z1[key, :] = scaled.astype(bf16)
            r1_ref[key, :] = jnp.broadcast_to(inverse, (block_rows, LANES))

    def feed_in(first, count):
        @pl.loop(first, first + count)
        def _(i):
            cols = lanes(i * tile, tile)
            u = mm(nl[...], iw[:, cols], NN)
            phi, slope = gelu_parts(u)
            g[:, cols] = (u * phi).astype(bf16)
            sl[:, cols] = slope.astype(bf16)

    def feed_back(part):
        inner = pl.ds(part * width, width)

        @pl.loop(0, width // tile)
        def _(i):
            cols = lanes(i * tile, tile)
            h[:, cols] += mm(g[:, inner], bw[rows_at(i * tile, tile, 16), inner], NT)

    def finish_block():
        @pl.loop(0, rows // block_rows)
        def _(i):
            key = rows_at(i * block_rows, block_rows, 16)
            result, scaled, inverse = norm_rows(h[key, :], par_ref[1:2, :], par_ref[3:4, :])
            h[key, :] = result
            y_ref[key, :] = result.astype(bf16)
            z2[key, :] = scaled.astype(bf16)
            r2_ref[key, :] = jnp.broadcast_to(inverse, (block_rows, LANES))

    def leaders():
        for s in range(segs):
            pos = par_ref[pl.ds(8 + p.fsdp * 2 + s % 2, 1), :]
            lead_out[s // 2, s % 2 : s % 2 + 1, :width] = h[s * SEG_LEN : s * SEG_LEN + 1, :] + pos
            lead_out[s // 2, s % 2 : s % 2 + 1, width:] = cot_ref[s * SEG_LEN : s * SEG_LEN + 16, :].astype(f32)[:1]

    def lead_copy(z, j):
        i = 2 * z + j
        return remote(lead_out.at[j], gbuf.at[p.fsdp], g_send.at[i], g_recv.at[p.fsdp], (p.dp, i))


    leads = fac.shape[0]
    lead2 = 2 * leads
    key_f = rows_at((p.dp * 4 + p.z) * lead2, lead2, 16)

    def swap(i):
        cols = pl.ds(i * width, width)
        return remote(fac.at[:, cols], fac_sib.at[:, cols], swap_send.at[i], swap_recv.at[i], p.sib)

    def give_factor(i, value):
        fac[:, i * width : (i + 1) * width] = value
        swap(i).start()

    class Factor(Gather):
        def __init__(self, i):
            mine = lambda z: full.at[key_f, self.cols(p.core)]
            super().__init__(p, full, i * width, width, mine, i, (f_send, f_recv), lead2, i % 2 == 0)
            self.i = i

        def own(self):
            swap(self.i).wait_recv()
            base = (p.dp * 4 + p.z) * lead2
            cols = lanes(self.i * width + p.core * (width // 2), width // 2)
            full[rows_at(base + p.core * leads, leads, 16), cols] = fac[:, cols]
            full[rows_at(base + (1 - p.core) * leads, leads, 16), cols] = fac_sib[:, cols]
            super().own()

    factors = [Factor(i) for i in range(4)]

    def factor_grads():
        def rows_of(z, at_col, size):
            return jnp.concatenate(
                [full[rows_at((i * 4 + z) * lead2, lead2, 16), pl.ds(at_col, size)] for i in range(4)],
                axis=0,
            )

        base = 2 * width
        own = rows_at(p.fsdp * (ROWS // 2), ROWS // 2, 8)
        xl = rows_of(p.dp, base, slab)
        nlf = rows_of(p.dp, base + slab, slab)
        dff = rows_of(p.dp, base + 2 * slab, slab)
        ctx = rows_of(p.dp, base + 3 * slab, slab)
        for z in range(4):
            tmp[:, :width] = mm(dff, rows_of(z, 0, width), TN)
            gb_ref[1, :, z * width : (z + 1) * width] = tmp[own, :width]
            tmp[:, :width] = mm(nlf, rows_of(z, width, width), TN)
            gi_ref[1, :, z * width : (z + 1) * width] = tmp[own, :width]
            tmp[:, : 3 * slab] = mm(xl, rows_of(z, 3 * width, 3 * slab), TN)
            got = tmp[own, : 3 * slab]
            for j in range(3):
                spot = j * width + z * slab
                gq_ref[1, :, spot : spot + slab] = got[:, j * slab : (j + 1) * slab]
            tmp[:, :slab] = mm(ctx, rows_of(z, 3 * width + 3 * slab, slab), TN)
            go_ref[1, :, z * slab : (z + 1) * slab] = tmp[own, :slab]


    n_tiles = width // tile
    head = width // HEADS
    heads = HEADS // 4

    def cross():
        for d in range(4):
            z = (p.z + d) % 4
            for j in range(2):
                if d:
                    lead_copy(z, j).start()
                else:

                    @pl.when(p.core != j)
                    def _():
                        lead_copy(z, j).start()

                    @pl.when(p.core == j)
                    def _():
                        mine = pltpu.make_async_copy(lead_out.at[j], gbuf.at[p.fsdp], lead_sem)
                        mine.start()
                        mine.wait()

        need(n_seg)
        wo_middle()
        for d in range(1, 8):
            i = lax.rem(p.fsdp + d, 8)
            remote(gbuf.at[i], gbuf.at[i], g_send.at[i], g_recv.at[i], p.sib).wait_recv()
        for i in range(8):
            lead[2 * i : 2 * i + 2, :] = gbuf[i]
        states = lead[:, :width]
        cot_rows = lead[:, width:]

        def sum_z(e, partial_sum, between):
            xbuf[e, p.z] = partial_sum.astype(bf16)
            copies = []
            for d in (1, 3, 2):
                z = (p.z + d) % 4
                copy = remote(
                    xbuf.at[e, p.z], xbuf.at[e, p.z], x_send.at[e, d - 1], x_recv.at[e, p.z],
                    p.at(p.dp, z, p.core),
                )
                copy.start()
                copies.append(copy)
            between()
            for d in (1, 3, 2):
                z = (p.z + d) % 4
                piece = xbuf.at[e, z]
                remote(piece, piece, x_send.at[e, d - 1], x_recv.at[e, z], p.sib).wait_recv()
            for copy in copies:
                copy.wait_send()
            return sum(xbuf[e, z].astype(f32) for z in range(4))

        gain0, gain1 = par_ref[4:5, :], par_ref[5:6, :]
        bias0, bias1 = par_ref[6:7, :], par_ref[7:8, :]
        in_cols, back_cols = pl.ds(width, width), pl.ds(2 * width, width)
        qkv_cols = pl.ds(0, 3 * slab)
        factor = head ** (-0.5)
        allowed = mask_ref[...] > 0.5

        def part(full):
            pieces = [full[:, i * slab : (i + 1) * slab] for i in range(4)]
            out = pieces[0]
            for i in range(1, 4):
                out = jnp.where(p.z == i, pieces[i], out)
            return out.astype(bf16)

        xl = states.astype(bf16)
        packed = mm(xl, cw[:, qkv_cols], NN).astype(bf16)
        q = [packed[:, i * head : (i + 1) * head] for i in range(heads)]
        k = [packed[:, slab + i * head : slab + (i + 1) * head] for i in range(heads)]
        v = [packed[:, 2 * slab + i * head : 2 * slab + (i + 1) * head] for i in range(heads)]
        att, context = [], []
        for i in range(heads):
            scores = jnp.where(allowed, mm(q[i], k[i], NT) * factor, NEG)
            top = jnp.max(scores, axis=-1, keepdims=True)
            terms = jnp.exp(scores - top)
            a = terms / jnp.sum(terms, axis=-1, keepdims=True)
            att.append(a)
            context.append(mm(a.astype(bf16), v[i], NN))
        context = jnp.concatenate(context, axis=1).astype(bf16)
        wo_finish()
        branch = sum_z(0, mm(context, cwo[...], NN), lambda: None)
        normed, z_one, r_one = norm_rows(states + branch, gain0, bias0)
        nl = normed.astype(bf16)
        need(n_seg + 1)
        hidden = mm(nl, cw[:, in_cols], NN)
        phi, slope = gelu_parts(hidden)
        active = (hidden * phi).astype(bf16)
        give_factor(0, active)
        need(n_seg + 2)

        def during_one():
            factors[0].own()

        feed = sum_z(1, mm(active, cw[:, back_cols], NT), during_one)
        result, z_two, r_two = norm_rows(normed + feed, gain1, bias1)
        d_two = norm_rows_back(cot_rows, z_two, r_two, gain1)
        df = d_two.astype(bf16)
        du = (mm(df, cw[:, back_cols], NN) * slope).astype(bf16)
        give_factor(1, du)
        give_factor(2, jnp.concatenate([part(states), part(normed), part(d_two), context], axis=1))

        def during_two():
            factors[0].line()
            factors[1].own()
            factors[2].own()

        d_normed = d_two + sum_z(2, mm(du, cw[:, in_cols], NT), during_two)
        d_one = norm_rows_back(d_normed, z_one, r_one, gain0)
        db = d_one.astype(bf16)
        dc = mm(db, cwo[...], NT).astype(bf16)
        for i in range(heads):
            a = att[i]
            dci = dc[:, i * head : (i + 1) * head]
            da = mm(dci, v[i], NT)
            dv = mm(a.astype(bf16), dci, TN)
            ds = (a * (da - jnp.sum(a * da, axis=-1, keepdims=True))).astype(bf16)
            dq = mm(ds, k[i], NN) * factor
            dk = mm(ds, q[i], TN) * factor
            for j, piece in enumerate((dq, dk, dv)):
                dpack[:, j * slab + i * head : j * slab + (i + 1) * head] = piece
        dp = dpack[...].astype(bf16)
        give_factor(3, jnp.concatenate([dp, part(d_one)], axis=1))

        def during_three():
            factors[0].plane()
            factors[1].line()
            factors[3].own()
            factors[2].line()

        dx = d_one + sum_z(3, mm(dp, cw[:, qkv_cols], NT), during_three)
        for i in range(8):
            ybuf[i, :, :width] = result[2 * i : 2 * i + 2]
            ybuf[i, :, width:] = dx[2 * i : 2 * i + 2]
        home = remote(
            ybuf.at[2 * p.z + 1 - p.core], home_ref.at[p.core], h_send, h_recv, p.sib
        )
        home.start()
        home_ref[p.core] = ybuf[2 * p.z + p.core]

        once = jnp.where(p.z == 0, 1.0, 0.0)
        sums_of = [d_normed * z_one, cot_rows * z_two, d_normed, cot_rows]
        csmall[...] = jnp.zeros_like(csmall)
        for i, s in enumerate(sums_of):
            csmall[i : i + 1, :] = once * jnp.sum(s, axis=0, keepdims=True)
        theirs = home_ref.at[1 - p.core]
        remote(theirs, theirs, h_send, h_recv, p.sib).wait_recv()
        home.wait_send()

    def wait_leads():
        for d in range(4):
            z = (p.z + d) % 4
            for j in range(2):
                if d:
                    lead_copy(z, j).wait_send()
                else:

                    @pl.when(p.core != j)
                    def _():
                        lead_copy(z, j).wait_send()


    def patch():
        for s in range(segs):
            spot = pl.ds(s * SEG_LEN, 16)
            old = y_ref[spot, :].astype(f32)
            new = jnp.broadcast_to(home_ref[s // 2, s % 2 : s % 2 + 1, :width], old.shape)
            top = lax.broadcasted_iota(jnp.int32, old.shape, 0) == 0
            y_ref[spot, :] = jnp.where(top, new, old).astype(bf16)
    per = hidden // width
    parts = [(bw, i * width, width, gb_ref.at[0]) for i in range(per)]
    parts += [(iw, i * width, width, gi_ref.at[0]) for i in range(per)]
    parts += [(ow, 0, width, go_ref.at[0]), (dws, 0, dws.shape[1], gs_ref)]
    parts += [(qw, at_col, size, gq_ref.at[0]) for at_col, size in tail_units(width)]
    jobs, shared = [], []
    for i, (grad, off, size, dst) in enumerate(parts):
        job_bufs = list(bufs[6 * i : 6 * i + 6])
        if size == width:
            slot = len(shared) % PAIR_SLOTS
            job = Scatter(p, grad, off, size, dst, i, (rs_send, rs_recv), [ring.at[slot]] + job_bufs, i % 2 == 0)
            job.free = free.at[slot]
            if len(shared) >= PAIR_SLOTS:
                job.waits = True
                shared[len(shared) - PAIR_SLOTS].frees = True
            shared.append(job)
        else:
            own_pair = pair_wide if size > 256 else pair_small.at[len([j for j in jobs if j.half == LANES])]
            job = Scatter(p, grad, off, size, dst, i, (rs_send, rs_recv), [own_pair] + job_bufs, i % 2 == 0)
        jobs.append(job)
    sums = Staged(jobs, staggered(len(jobs), SCATTER_LAGS))


    def norm_back(z_ref, r_ref, gain_row, low_ref, sums):
        def step(i, acc):
            key = rows_at(i * block_rows, block_rows, 16)
            dy = h[key, :]
            z = z_ref[key, :].astype(f32)
            r = jnp.concatenate([r_ref[key, :]] * (width // LANES), axis=1)
            e = dy * par_ref[gain_row : gain_row + 1, :]
            first = jnp.mean(e, axis=-1, keepdims=True)
            second = jnp.mean(e * z, axis=-1, keepdims=True)
            d = r * (e - first - z * second)
            h[key, :] = d
            low_ref[key, :] = d.astype(bf16)
            fold = lambda v: jnp.sum(v.reshape(block_rows // 8, 8, width), axis=0)
            return acc[0] + fold(dy * z), acc[1] + fold(dy)

        zero = jnp.zeros((8, width), f32)
        gain, bias = lax.fori_loop(0, rows // block_rows, step, (zero, zero))
        small[sums : sums + 1, :] = jnp.sum(gain, axis=0, keepdims=True)
        small[sums + 2 : sums + 3, :] = jnp.sum(bias, axis=0, keepdims=True)

    def turn(tr, ref):
        @pl.loop(0, width // tile)
        def _(i):
            tr[rows_at(i * tile, tile, 16), :] = ref[:, lanes(i * tile, tile)].T

    def outer(dst, tr, src, first, size):
        @pl.loop(first // tile, (first + size) // tile)
        def _(i):
            cols = lanes(i * tile, tile)
            dst[:, cols] = mm(tr[...], src[:, cols], NN).astype(bf16)

    def norm_two():
        @pl.loop(0, rows // block_rows)
        def _(i):
            key = rows_at(i * block_rows, block_rows, 16)
            h[key, :] = cot_ref[key, :].astype(f32)

        for s in range(segs):
            h[s * SEG_LEN : s * SEG_LEN + 1, :] = home_ref[s // 2, s % 2 : s % 2 + 1, width:]
        small[...] = jnp.zeros_like(small)
        small[4:8, :] = csmall[0:4, :]
        for s in range(2):
            row = home_ref[0, s : s + 1, width:] + home_ref[1, s : s + 1, width:]
            small[pl.ds(8 + p.fsdp * 2 + s, 1), :] = row
        norm_back(z2, r2_ref, 1, df, 1)
        turn(tr, df)

    def active_back(part):
        @pl.loop(part * n_tiles, (part + 1) * n_tiles)
        def _(i):
            cols = lanes(i * tile, tile)
            d = mm(df[...], bw[:, cols], NN) * sl[:, cols].astype(f32)
            sl[:, cols] = d.astype(bf16)

    def add_back(src, weight, first, size):
        inner = pl.ds(first, size)

        @pl.loop(0, n_tiles)
        def _(i):
            cols = lanes(i * tile, tile)
            h[:, cols] += mm(src[:, inner], weight[rows_at(i * tile, tile, 16), inner], NT)

    def context_back():
        @pl.loop(0, width // tile)
        def _(i):
            d = mm(df[...], ow[rows_at(i * tile, tile, 16), :], NT)
            cx[:, lanes(i * tile, tile)] = d.astype(bf16)

    def attend_back(s):
        key = pl.ds(s * SEG_LEN, SEG_LEN)
        factor = (LANES // 2) ** (-0.5)

        @pl.loop(0, pairs)
        def _(j):
            a = at[rows_at((s * pairs + j) * 2 * SEG_LEN, 2 * SEG_LEN, 16), :]
            q_cols = lanes(j * LANES, LANES)
            k_cols = lanes(width + j * LANES, LANES)
            v_cols = lanes(2 * width + j * LANES, LANES)
            qs = jnp.concatenate(lane_halves(pk[key, q_cols]), axis=0)
            ks = jnp.concatenate(lane_halves(pk[key, k_cols]), axis=0)
            ds_in = jnp.concatenate(lane_halves(cx[key, q_cols]), axis=0)
            da = mm(ds_in, pk[key, v_cols], NT)
            af = a.astype(f32)
            ds = (af * (da - jnp.sum(af * da, axis=-1, keepdims=True))).astype(bf16)
            dv = mm(a, ds_in, TN)
            both = jnp.concatenate([ds[:SEG_LEN], ds[SEG_LEN:]], axis=1)
            dq = mm(both, ks, NN) * factor
            dk = mm(ds, qs, TN) * factor
            pk[key, q_cols] = dq.astype(bf16)
            pk[key, k_cols] = dk.astype(bf16)
            pk[key, v_cols] = dv.astype(bf16)

    def result():
        @pl.loop(0, rows // block_rows)
        def _(i):
            key = rows_at(i * block_rows, block_rows, 16)
            gt_ref[key, :] = h[key, :].astype(bf16)

    def smalls():
        dws[:, :LANES] = small[...].T.astype(bf16)
        dws[:, LANES:] = jnp.zeros((dws.shape[0], LANES), bf16)

    need(0)
    params()
    for i in range(3):
        need(1 + i)
        project(i * n_tiles, n_tiles)
    for s in range(segs):
        attend(s)
        comm.upto("drain", 4 + s)
    branch()
    for i in range(per):
        need(8 + i)
        feed_in(i * n_tiles, n_tiles)
    wo_start()
    for i in range(per):
        need(5 + per + i)
        feed_back(i)
    finish_block()
    leaders()
    cross()
    comm.finish()
    for i in range(n_seg + 2):
        pair(i).wait_send()
    patch()
    sum_step = lambda: scatter_step(sums, jobs)
    norm_two()
    factors[1].plane()
    factors[2].plane()
    factors[0].last()
    for i in range(per):
        active_back(i)
        outer(bw, tr, g, i * width, width)
        sum_step()
        if i == 0:
            factors[3].line()
            factors[1].last()
        if i == 1:
            factors[2].last()
            factors[3].plane()
        if i == 2:
            factors[3].last()
    turn(tr, nl)
    add_back(sl, iw, 0, 2 * width)
    add_back(sl, iw, 2 * width, hidden - 2 * width)
    outer(iw, tr, sl, 0, width)
    sum_step()
    norm_back(z1, r1_ref, 0, df, 0)
    outer(iw, tr, sl, width, width)
    sum_step()
    smalls()
    turn(tr2, cx)
    context_back()
    attend_back(0)
    for i in range(2, per - 1):
        outer(iw, tr, sl, i * width, width)
        sum_step()
    attend_back(1)
    outer(iw, tr, sl, (per - 1) * width, width)
    sum_step()
    attend_back(2)
    outer(ow, tr2, df, 0, width)
    sum_step()
    attend_back(3)
    sum_step()
    turn(tr2, x_ref)
    for at_col, size in tail_units(width):
        add_back(pk, qw, at_col, size)
        outer(qw, tr2, pk, at_col, size)
        sum_step()
    result()
    for unit in factors:
        unit.drain()
    factor_grads()
    sums.finish()
    for unit in factors:
        unit.finish()
    for i in range(4):
        swap(i).wait_send()
    wait_leads()


def layer(ws, wq, wo, wi, wb, x, cot, mask):
    wrows = 16 * ROWS
    rows, width = x.shape
    segs = rows // SEG_LEN
    leads = mask.shape[0]
    hidden = wi.shape[2]
    own = ROWS // 2
    cross_width = 3 * width
    total = ws.shape[1] + 3 * width + width + 2 * hidden + 4 * cross_width + width
    parts = 5 + 2 * hidden // width + 2
    n_units = parts - 2 + 3
    vm = pl.BlockSpec(memory_space=VM)
    arr = jax.ShapeDtypeStruct
    DMA = pltpu.SemaphoreType.DMA
    att_rows = segs * HEADS * SEG_LEN
    wide = lambda v, kind=bf16: VM((rows, v), kind)
    weight = lambda v: VM((wrows, v), bf16)
    widths = [width] * (2 * (hidden // width) + 1) + [256] + [size for _, size in tail_units(width)]
    bufs = []
    for i, w in enumerate(widths):
        bufs += scatter_buffers(w, i % 2 == 0)
    small_units = len([w for w in widths if w == 256])
    return pl.pallas_call(
        layer_kernel,
        out_shape=[
            arr((rows, width), bf16),
            arr((rows, width), bf16),
            arr((2, own, 3 * width), f32),
            arr((2, own, width), f32),
            arr((2, own, hidden), f32),
            arr((2, own, hidden), f32),
            arr((own, 256), f32),
        ],
        in_specs=[vm] * 8,
        out_specs=[vm] * 7,
        scratch_shapes=[
            weight(ws.shape[1]), weight(width), weight(3 * width), weight(hidden), weight(hidden),
            weight(cross_width), VM((wrows // 4, width), bf16),
            wide(3 * width), VM((att_rows, SEG_LEN), bf16), wide(width), wide(width, f32), wide(width),
            wide(hidden), wide(hidden), wide(width), wide(width),
            wide(LANES, f32), wide(LANES, f32), VM((24, width), f32),
            VM((32, total), bf16), VM((32, total), bf16), VM((ROWS, 4 * cross_width + width), bf16),
            VM((2, 2, 2 * width), f32), VM((8, 2, 2 * width), f32), VM((leads, 2 * width), f32),
            VM((4, 4, leads, width), bf16), VM((8, 2, 2 * width), f32), VM((leads, 3 * width // 4), f32),
            VM((2, 2, 2 * width), f32), VM((leads, 4 * width), bf16), VM((leads, 4 * width), bf16),
            VM((8, width), f32),
            wide(width), VM((width, rows), bf16), VM((width, rows), bf16), weight(256),
            VM((LANES, width), f32), VM((32 * leads, 4 * width), bf16), VM((width // 4, width), f32),
            VM((PAIR_SLOTS, wrows, width // 2), bf16), weight((width - 256) // 2),
            VM((small_units, wrows, LANES), bf16),
            DMA((n_units, 11)), DMA((n_units, 11)), DMA((parts,)), DMA((parts,)),
            DMA((5,)), DMA((5,)), DMA,
            DMA((8,)), DMA((8,)), DMA((4, 3)), DMA((4, 4)), DMA, DMA, DMA,
            DMA((4, 11)), DMA((4, 11)), DMA((4,)), DMA((4,)),
            DMA((len(widths), 12)), DMA((len(widths), 12)), pltpu.SemaphoreType.REGULAR((PAIR_SLOTS,)),
        ]
        + bufs,
        compiler_params=pltpu.CompilerParams(
            collective_id=0, has_side_effects=True, vmem_limit_bytes=63 * MIB
        ),
    )(wq, wo, wi, wb, ws, x, cot, mask)


def matmul(left, right, form):
    return jnp.einsum(form, left, right, preferred_element_type=jnp.float32)


def norm_forward(summed, gains, biases):
    average = jnp.mean(summed, axis=-1, keepdims=True)
    centred = summed - average
    variance = jnp.mean(centred * centred, axis=-1, keepdims=True)
    inverse = lax.rsqrt(variance + epsilon)
    scaled = centred * inverse
    return (scaled * gains + biases, scaled, inverse)


def norm_backward(grad_result, scaled, inverse, gains):
    grad_scaled = grad_result * gains
    first_mean = jnp.mean(grad_scaled, axis=-1, keepdims=True)
    second_mean = jnp.mean(grad_scaled * scaled, axis=-1, keepdims=True)
    grad_sum = inverse * (grad_scaled - first_mean - scaled * second_mean)
    return (grad_sum, jnp.sum(grad_result * scaled, axis=(0, 1)), jnp.sum(grad_result, axis=(0, 1)))


def split_heads(packed):
    groups, length, model_width = packed.shape
    return packed.reshape(groups, length, HEADS, model_width // HEADS)


def join_heads(split_part):
    groups, length, heads_count, head_size = split_part.shape
    return split_part.reshape(groups, length, heads_count * head_size)


def attend_forward(query_part, key_part, value_part, allowed):
    head_size = query_part.shape[-1]
    scores = matmul(query_part, key_part, "glhe,gmhe->ghlm") * head_size ** (-0.5)
    scores = jnp.where(allowed[:, None], scores, -1e30)
    row_max = jnp.max(scores, axis=-1, keepdims=True)
    exp_terms = jnp.exp(scores - row_max)
    row_total = jnp.sum(exp_terms, axis=-1, keepdims=True)
    attention = exp_terms / row_total
    context = matmul(attention.astype(jnp.bfloat16), value_part, "ghlm,gmhe->glhe")
    return (join_heads(context).astype(jnp.bfloat16), row_max + jnp.log(row_total))


def attend_backward(query_part, key_part, value_part, allowed, log_total, grad_context):
    head_size = query_part.shape[-1]
    factor = head_size ** (-0.5)
    scores = matmul(query_part, key_part, "glhe,gmhe->ghlm") * factor
    scores = jnp.where(allowed[:, None], scores, -1e30)
    attention = jnp.exp(scores - log_total)
    grad_attention = matmul(grad_context, value_part, "glhe,gmhe->ghlm")
    grad_value = matmul(attention.astype(jnp.bfloat16), grad_context, "ghlm,glhe->gmhe")
    inner = jnp.sum(attention * grad_attention, axis=-1, keepdims=True)
    grad_scores = (attention * (grad_attention - inner)).astype(jnp.bfloat16)
    grad_query = matmul(grad_scores, key_part, "ghlm,gmhe->glhe") * factor
    grad_key = matmul(grad_scores, query_part, "ghlm,glhe->gmhe") * factor
    return (join_heads(grad_query), join_heads(grad_key), join_heads(grad_value))


def segment_attend(packed):
    groups, length, total_width = packed.shape
    model_width = total_width // 3
    allowed = jnp.ones((groups, length, length), dtype=jnp.bool_)
    context, log_total = attend_forward(
        split_heads(packed[..., :model_width]),
        split_heads(packed[..., model_width : 2 * model_width]),
        split_heads(packed[..., 2 * model_width :]),
        allowed,
    )
    return (context, log_total)


def segment_attend_back(packed, log_total, grad_context):
    groups, length, total_width = packed.shape
    model_width = total_width // 3
    allowed = jnp.ones((groups, length, length), dtype=jnp.bool_)
    grad_query, grad_key, grad_value = attend_backward(
        split_heads(packed[..., :model_width]),
        split_heads(packed[..., model_width : 2 * model_width]),
        split_heads(packed[..., 2 * model_width :]),
        allowed,
        log_total,
        split_heads(grad_context),
    )
    return jnp.concatenate([grad_query, grad_key, grad_value], axis=-1)


def cross_attend(packed, allowed):
    model_width = packed.shape[-1] // 3
    remote = lax.all_gather(packed[..., model_width:], "fsdp", axis=1, tiled=True)
    context, log_total = attend_forward(
        split_heads(packed[..., :model_width]),
        split_heads(remote[..., :model_width]),
        split_heads(remote[..., model_width:]),
        allowed,
    )
    return (context, (remote, log_total))


def cross_attend_back(packed, saved, grad_context, allowed):
    remote, log_total = saved
    model_width = packed.shape[-1] // 3
    grad_query, grad_key, grad_value = attend_backward(
        split_heads(packed[..., :model_width]),
        split_heads(remote[..., :model_width]),
        split_heads(remote[..., model_width:]),
        allowed,
        log_total,
        split_heads(grad_context),
    )
    shared = jnp.concatenate([grad_key, grad_value], axis=-1)
    own_part = lax.psum_scatter(
        shared.astype(jnp.bfloat16), "fsdp", scatter_dimension=1, tiled=True
    ).astype(jnp.float32)
    return jnp.concatenate([grad_query, own_part], axis=-1)


def block_forward(states, weights, attend):
    w_qkv, w_out, w_in, w_back, gains, biases = weights
    gains = gains.astype(jnp.float32)
    biases = biases.astype(jnp.float32)
    states_low = states.astype(jnp.bfloat16)
    packed = matmul(states_low, w_qkv, "gld,de->gle").astype(jnp.bfloat16)
    context, saved = attend(packed)
    branch = matmul(context, w_out, "gld,de->gle")
    normed, scaled_one, inverse_one = norm_forward(states + branch, gains[0], biases[0])
    normed_low = normed.astype(jnp.bfloat16)
    hidden = matmul(normed_low, w_in, "gld,df->glf")
    active_low = jax.nn.gelu(hidden, approximate=False).astype(jnp.bfloat16)
    feed_out = matmul(active_low, w_back, "glf,fd->gld")
    result, scaled_two, inverse_two = norm_forward(normed + feed_out, gains[1], biases[1])
    kept = (
        states_low,
        packed,
        context,
        saved,
        scaled_one,
        inverse_one,
        normed_low,
        hidden,
        active_low,
        scaled_two,
        inverse_two,
    )
    return (result, kept)


def block_backward(grad_result, kept, weights, attend_back):
    w_qkv, w_out, w_in, w_back, gains, biases = weights
    gains = gains.astype(jnp.float32)
    (
        states_low,
        packed,
        context,
        saved,
        scaled_one,
        inverse_one,
        normed_low,
        hidden,
        active_low,
        scaled_two,
        inverse_two,
    ) = kept
    grad_sum_two, gain_two, bias_two = norm_backward(grad_result, scaled_two, inverse_two, gains[1])
    grad_feed = grad_sum_two.astype(jnp.bfloat16)
    grad_active = matmul(grad_feed, w_back, "gld,fd->glf")
    cumulative = 0.5 * (1.0 + lax.erf(hidden * root_half))
    slope = cumulative + hidden * inv_root_tau * jnp.exp(-0.5 * hidden * hidden)
    grad_hidden = (grad_active * slope).astype(jnp.bfloat16)
    grad_normed = grad_sum_two + matmul(grad_hidden, w_in, "glf,df->gld")
    grad_sum_one, gain_one, bias_one = norm_backward(grad_normed, scaled_one, inverse_one, gains[0])
    grad_branch = grad_sum_one.astype(jnp.bfloat16)
    grad_context = matmul(grad_branch, w_out, "gle,de->gld").astype(jnp.bfloat16)
    grad_packed = attend_back(packed, saved, grad_context).astype(jnp.bfloat16)
    grad_states = grad_sum_one + matmul(grad_packed, w_qkv, "gle,de->gld")
    factors = (
        states_low,
        grad_packed,
        context,
        grad_branch,
        normed_low,
        grad_hidden,
        grad_feed,
        active_low,
    )
    smalls = (jnp.stack([gain_one, gain_two]), jnp.stack([bias_one, bias_two]))
    return (grad_states, factors, smalls)


def weight_terms(factors):
    (
        states_low,
        grad_packed,
        context,
        grad_branch,
        normed_low,
        grad_hidden,
        grad_feed,
        active_low,
    ) = factors
    term_qkv = matmul(states_low, grad_packed, "gld,gle->de")
    term_out = matmul(context, grad_branch, "gld,gle->de")
    term_in = matmul(normed_low, grad_hidden, "gld,glf->df")
    term_back = matmul(grad_feed, active_low, "gld,glf->df")
    return jnp.concatenate([term_qkv, term_out, term_in, term_back], axis=1)


def gather_segment(w_qkv, w_out, w_in, w_back, norm_gain, norm_bias):
    return (
        lax.all_gather(w_qkv[0], ("dp", "fsdp"), axis=0, tiled=True),
        lax.all_gather(w_out[0], ("dp", "fsdp"), axis=0, tiled=True),
        lax.all_gather(w_in[0], ("dp", "fsdp"), axis=0, tiled=True),
        lax.all_gather(w_back[0], ("dp", "fsdp"), axis=1, tiled=True),
        lax.all_gather(norm_gain[0], ("dp", "fsdp"), axis=1, tiled=True),
        lax.all_gather(norm_bias[0], ("dp", "fsdp"), axis=1, tiled=True),
    )


def gather_cross(pos_embed, w_qkv, w_out, w_in, w_back, norm_gain, norm_bias):
    gathered = (
        lax.all_gather(w_qkv[1], ("dp", "fsdp"), axis=0, tiled=True),
        lax.all_gather(w_out[1], ("dp", "fsdp"), axis=0, tiled=True),
        lax.all_gather(w_in[1], ("dp", "fsdp"), axis=0, tiled=True),
        lax.all_gather(w_back[1], ("dp", "fsdp"), axis=1, tiled=True),
        lax.all_gather(norm_gain[1], ("dp", "fsdp"), axis=1, tiled=True),
        lax.all_gather(norm_bias[1], ("dp", "fsdp"), axis=1, tiled=True),
        lax.all_gather(pos_embed, ("dp", "fsdp"), axis=1, tiled=True),
    )
    return (gathered[:6], gathered[6])


def layer_forward(tokens, doc_ids, seg_weights, cross_weights, pos_full):
    rows, local_len, model_width = tokens.shape
    seg_count = local_len // SEG_LEN
    segments = tokens.reshape(rows * seg_count, SEG_LEN, model_width).astype(jnp.float32)
    seg_out, seg_kept = block_forward(segments, seg_weights, segment_attend)
    start = lax.axis_index("fsdp") * seg_count
    pos_local = lax.dynamic_slice_in_dim(pos_full, start, seg_count, 0).astype(jnp.float32)
    leaders = seg_out[:, 0, :].reshape(rows, seg_count, model_width) + pos_local
    own_docs = lax.dynamic_slice_in_dim(doc_ids, start, seg_count, 1)
    allowed = own_docs[:, :, None] == doc_ids[:, None, :]
    cross_out, cross_kept = block_forward(
        leaders, cross_weights, partial(cross_attend, allowed=allowed)
    )
    joined = jnp.concatenate(
        [cross_out.reshape(rows * seg_count, 1, model_width), seg_out[:, 1:, :]], axis=1
    )
    output = joined.reshape(rows, local_len, model_width).astype(jnp.bfloat16)
    return (output, (seg_kept, cross_kept, allowed))


def layer_backward(cotangent, doc_ids, kept, seg_weights, cross_weights):
    seg_kept, cross_kept, allowed = kept
    rows, local_len, model_width = cotangent.shape
    seg_count = local_len // SEG_LEN
    grad_all = cotangent.reshape(rows * seg_count, SEG_LEN, model_width).astype(jnp.float32)
    grad_cross = grad_all[:, 0, :].reshape(rows, seg_count, model_width)
    grad_leaders, cross_factors, cross_smalls = block_backward(
        grad_cross, cross_kept, cross_weights, partial(cross_attend_back, allowed=allowed)
    )
    start = lax.axis_index("fsdp") * seg_count
    empty_pos = jnp.zeros((doc_ids.shape[1], model_width), jnp.float32)
    grad_pos = lax.dynamic_update_slice_in_dim(empty_pos, jnp.sum(grad_leaders, axis=0), start, 0)
    grad_seg = jnp.concatenate(
        [grad_leaders.reshape(rows * seg_count, 1, model_width), grad_all[:, 1:, :]], axis=1
    )
    grad_states, seg_factors, seg_smalls = block_backward(
        grad_seg, seg_kept, seg_weights, segment_attend_back
    )
    grad_tokens = grad_states.reshape(rows, local_len, model_width).astype(jnp.bfloat16)
    return (grad_tokens, seg_factors, cross_factors, seg_smalls, cross_smalls, grad_pos)


def body(tokens, doc_ids, pos_embed, w_qkv, w_out, w_in, w_back, norm_gain, norm_bias, cotangent):
    seg_weights = gather_segment(w_qkv, w_out, w_in, w_back, norm_gain, norm_bias)
    cross_weights, pos_full = gather_cross(
        pos_embed, w_qkv, w_out, w_in, w_back, norm_gain, norm_bias
    )
    output, kept = layer_forward(tokens, doc_ids, seg_weights, cross_weights, pos_full)
    grad_tokens, seg_factors, cross_factors, seg_smalls, cross_smalls, grad_pos = layer_backward(
        cotangent, doc_ids, kept, seg_weights, cross_weights
    )
    model_width = tokens.shape[2]
    hidden_width = w_in.shape[2]
    seg_term = lax.psum_scatter(
        weight_terms(seg_factors), ("dp", "fsdp"), scatter_dimension=0, tiled=True
    )
    cross_term = lax.psum_scatter(
        weight_terms(cross_factors), ("dp", "fsdp"), scatter_dimension=0, tiled=True
    )
    stacked = jnp.stack([seg_term, cross_term])
    grad_qkv = stacked[:, :, : 3 * model_width]
    grad_out = stacked[:, :, 3 * model_width : 4 * model_width]
    grad_in = stacked[:, :, 4 * model_width : 4 * model_width + hidden_width]
    grad_back = jnp.transpose(stacked[:, :, 4 * model_width + hidden_width :], (0, 2, 1))
    gain_all = jnp.stack([seg_smalls[0], cross_smalls[0]])
    bias_all = jnp.stack([seg_smalls[1], cross_smalls[1]])
    grad_gain, grad_bias, pos_shard = (
        lax.psum_scatter(gain_all, ("dp", "fsdp"), scatter_dimension=2, tiled=True),
        lax.psum_scatter(bias_all, ("dp", "fsdp"), scatter_dimension=2, tiled=True),
        lax.psum_scatter(grad_pos, ("dp", "fsdp"), scatter_dimension=1, tiled=True),
    )
    return (
        output,
        grad_tokens,
        pos_shard,
        grad_qkv,
        grad_out,
        grad_in,
        grad_back,
        grad_gain,
        grad_bias,
    )


def fast_body(tokens, doc_ids, pos_embed, w_qkv, w_out, w_in, w_back, norm_gain, norm_bias, cotangent):
    nrows, local_len, width = tokens.shape
    rows = nrows * local_len
    segs = rows // SEG_LEN
    hidden = w_in.shape[2]
    items = jnp.concatenate([norm_gain[0], norm_bias[0], norm_gain[1], norm_bias[1], pos_embed], axis=0)
    small = jnp.pad(items.T, ((0, 0), (0, 256 - items.shape[0])))
    x = tokens.reshape(rows, width)
    cot = cotangent.reshape(rows, width)
    own_row = lax.dynamic_index_in_dim(doc_ids, lax.axis_index("fsdp") % 2, 0, keepdims=False)
    mask = (own_row[:, None] == own_row[None, :]).astype(f32)
    output, grad_tokens, g_qkv, g_out, g_in, g_back, t_small = layer(
        small, w_qkv, w_out, w_in, jnp.swapaxes(w_back, 1, 2), x, cot, mask
    )
    s = t_small.T
    return (
        output.reshape(tokens.shape),
        grad_tokens.reshape(tokens.shape),
        s[8 : 8 + doc_ids.shape[1]],
        g_qkv,
        g_out,
        g_in,
        jnp.swapaxes(g_back, 1, 2),
        jnp.stack([s[0:2], s[4:6]]),
        jnp.stack([s[2:4], s[6:8]]),
    )


def solution(mesh):
    fast = dict(mesh.shape) == {"dp": 4, "fsdp": 8}
    return jax.shard_map(
        fast_body if fast else body,
        mesh=mesh,
        in_specs=(
            P("dp", "fsdp", None),
            P("dp", None),
            P(None, ("dp", "fsdp")),
            P(None, ("dp", "fsdp"), None),
            P(None, ("dp", "fsdp"), None),
            P(None, ("dp", "fsdp"), None),
            P(None, None, ("dp", "fsdp")),
            P(None, None, ("dp", "fsdp")),
            P(None, None, ("dp", "fsdp")),
            P("dp", "fsdp", None),
        ),
        out_specs=(
            P("dp", "fsdp", None),
            P("dp", "fsdp", None),
            P(None, ("dp", "fsdp")),
            P(None, ("dp", "fsdp"), None),
            P(None, ("dp", "fsdp"), None),
            P(None, ("dp", "fsdp"), None),
            P(None, None, ("dp", "fsdp")),
            P(None, None, ("dp", "fsdp")),
            P(None, None, ("dp", "fsdp")),
        ),
        check_vma=False,
    )
```

```python
from functools import partial

import jax
import jax.numpy as jnp
from jax import lax
from jax.experimental import pallas as pl
from jax.experimental.pallas import tpu as pltpu
from jax.sharding import PartitionSpec as P

HEADS = 12
SEG_LEN = 128


epsilon = 1e-05
root_half = 0.7071067811865476
inv_root_tau = 0.3989422804014327

bf16 = jnp.bfloat16
f32 = jnp.float32
MESH = pl.DeviceIdType.MESH
VM = pltpu.VMEM
MIB = 1024 * 1024
ROWS = 48
LANES = 128


class Place:
    def __init__(self):
        self.dp = lax.axis_index("dp")
        self.fsdp = lax.axis_index("fsdp")
        self.y, self.x = self.dp // 2, self.dp % 2
        self.z, self.core = self.fsdp // 2, self.fsdp % 2

    def at(self, dp, z, core):
        return (dp, z * 2 + core)

    @property
    def sib(self):
        return (self.dp, self.z * 2 + 1 - self.core)

    @property
    def xdp(self):
        return self.y * 2 + 1 - self.x

    @property
    def ydp(self):
        return (1 - self.y) * 2 + self.x

    @property
    def xnbr(self):
        return (self.xdp, self.fsdp)

    @property
    def ynbr(self):
        return (self.ydp, self.fsdp)


def greet(devices):
    barrier = pltpu.get_barrier_semaphore()
    for device in devices:
        pl.semaphore_signal(barrier, inc=1, device_id=device, device_id_type=MESH)
    pl.semaphore_wait(barrier, len(devices))


def remote(src, dst, send, recv, device):
    return pltpu.make_async_remote_copy(
        src_ref=src, dst_ref=dst, send_sem=send, recv_sem=recv, device_id=device, device_id_type=MESH
    )


def lanes(start, size):
    if isinstance(start, int):
        return pl.ds(start, size)
    return pl.ds(pl.multiple_of(start, LANES), size)


def rows_at(start, size, unit):
    return pl.ds(pl.multiple_of(start, unit), size)


class Gather:
    def __init__(self, place, out, off, width, source, index, sems, height2, wide_a=True):
        self.p, self.out, self.off, self.source = place, out, off, source
        self.m, self.sems, self.h2 = index, sems, height2
        self.half = width // 2
        tiles = self.half // LANES
        self.a = ((tiles + 1) // 2 if wide_a else max(tiles // 2, 1)) * LANES
        self.b = self.half - self.a
        self.sent = []
        self.far = (1 - place.y) * 2 + 1 - place.x

    def cols(self, core, part="AB"):
        at, size = {"A": (0, self.a), "B": (self.a, self.b), "AB": (0, self.half)}[part]
        return lanes(self.off + core * self.half + at, size)

    def block(self, z, core):
        return self.out.at[rows_at((self.p.dp * 4 + z) * self.h2, self.h2, 16), self.cols(core)]

    def group(self, dp, core, part="AB"):
        return self.out.at[rows_at(dp * 4 * self.h2, self.h2 * 4, 16), self.cols(core, part)]

    def go(self, src, dst, slot, device):
        copy = remote(src, dst, self.sems[0].at[self.m, slot], self.sems[1].at[self.m, slot], device)
        copy.start()
        self.sent.append(copy)

    def hand(self, ref, slot):
        self.go(ref, ref, slot, self.p.sib)

    def arrived(self, dst, slot):
        remote(dst, dst, self.sems[0].at[self.m, slot], self.sems[1].at[self.m, slot], self.p.sib).wait_recv()

    def own(self):
        p = self.p
        for d in (1, 3, 2):
            z = (p.z + d) % 4
            self.go(self.source(z), self.block(p.z, p.core), d - 1, p.at(p.dp, z, p.core))

    def line(self):
        p = self.p
        for d in (1, 3, 2):
            self.arrived(self.block((p.z + 4 - d) % 4, p.core), d - 1)
        mine = self.group(p.dp, p.core)
        self.go(mine, mine, 3, p.xnbr)
        self.go(mine, mine, 4, p.ynbr)
        self.hand(mine, 7)

    def plane(self):
        p = self.p
        over_x, over_y = self.group(p.xdp, p.core), self.group(p.ydp, p.core)
        self.arrived(over_x, 3)
        part = self.group(p.xdp, p.core, "A")
        self.go(part, part, 5, p.ynbr)
        self.arrived(over_y, 4)
        if self.b:
            part = self.group(p.ydp, p.core, "B")
            self.go(part, part, 6, p.xnbr)
        self.hand(over_x, 8)
        self.hand(over_y, 9)

    def last(self):
        p = self.p
        self.arrived(self.group(self.far, p.core, "A"), 5)
        if self.b:
            self.arrived(self.group(self.far, p.core, "B"), 6)
        self.hand(self.group(self.far, p.core), 10)

    def drain(self):
        p = self.p
        for slot, dp in ((7, p.dp), (8, p.xdp), (9, p.ydp), (10, self.far)):
            self.arrived(self.group(dp, 1 - p.core), slot)

    def finish(self):
        for copy in self.sent:
            copy.wait_send()


class Staged:
    def __init__(self, units, order):
        self.units, self.order, self.at = units, order, 0

    def step(self, count=1):
        for name, i in self.order[self.at : self.at + count]:
            getattr(self.units[i], name)()
        self.at += count

    def upto(self, name, i):
        spot = self.order.index((name, i)) + 1
        if spot > self.at:
            self.step(spot - self.at)

    def finish(self):
        self.step(len(self.order) - self.at)
        for unit in self.units:
            unit.finish()


def staggered(count, lags, first=0):
    order = []
    for t in range(min(lags.values()), count + max(lags.values())):
        for name, lag in lags.items():
            if 0 <= t - lag < count and (t >= 0 or lag < 0):
                order.append((name, t - lag + first))
    return order


def gather_peers(p):
    peers = [p.sib, p.xnbr, p.ynbr]
    for d in (1, 2, 3):
        peers.append(p.at(p.dp, (p.z + d) % 4, p.core))
    return peers


def everyone(p):
    return [
        (lax.rem(p.dp + i, 4), lax.rem(p.fsdp + j, 8)) for i in range(4) for j in range(8) if i or j
    ]


NEG = -1e30


def mm(a, b, dims):
    return lax.dot_general(a, b, (dims, ((), ())), preferred_element_type=f32)


NN = ((1,), (0,))
NT = ((1,), (1,))
TN = ((0,), (0,))


def norm_rows(summed, gain, bias):
    centred = summed - jnp.mean(summed, axis=-1, keepdims=True)
    variance = jnp.mean(centred * centred, axis=-1, keepdims=True)
    inverse = lax.rsqrt(variance + epsilon)
    scaled = centred * inverse
    return scaled * gain + bias, scaled, inverse


def norm_rows_back(grad, scaled, inverse, gain):
    g = grad * gain
    first = jnp.mean(g, axis=-1, keepdims=True)
    second = jnp.mean(g * scaled, axis=-1, keepdims=True)
    return inverse * (g - first - scaled * second)


def gelu_parts(u):
    cumulative = 0.5 * (1.0 + lax.erf(u * root_half))
    return cumulative, cumulative + u * inv_root_tau * jnp.exp(-0.5 * u * u)


def lane_halves(v):
    low = lax.broadcasted_iota(jnp.int32, v.shape, 1) < LANES // 2
    zero = jnp.zeros_like(v)
    return jnp.where(low, v, zero), jnp.where(low, zero, v)


FORWARD_LAGS = {"own": -3, "line": 0, "plane": 1, "last": 2, "drain": 3}


def forward_order(n_seg, n_cross):
    n = n_seg + n_cross
    order = staggered(n, FORWARD_LAGS)
    stop = order.index(("line", n_seg))
    head, rest = order[:stop], order[stop:]
    head += [s for s in rest if s[0] == "own"]
    done = set(head)
    tail = [("plane", n_seg - 1), ("line", n_seg), ("line", n_seg + 1)]
    for u in range(n_seg - 3, n_seg):
        tail += [("last", u), ("drain", u)]
    tail += [("plane", n_seg), ("line", n_seg + 2)]
    for u in range(n_seg, n):
        tail += [("last", u), ("plane", u + 1), ("drain", u)]
    return head + [s for s in tail if s not in done and s[1] < n]


class Scatter:
    def __init__(self, place, grad, off, width, out, index, sems, bufs, wide_a=True):
        self.p, self.grad, self.off, self.out, self.m = place, grad, off, out, index
        self.send, self.recv = sems
        self.pair, self.r1a, self.r1b, self.rx, self.ry, self.r3, self.give = bufs
        self.half = width // 2
        self.a = split_half(width, wide_a)
        self.b = self.half - self.a
        self.sent = []
        self.free, self.waits, self.frees = None, False, False
        p = place
        self.far = (1 - p.y) * 2 + 1 - p.x
        self.groups = (self.far, p.xdp, p.ydp, p.dp)

    def go(self, src, dst, slot, device):
        copy = remote(src, dst, self.send.at[self.m, slot], self.recv.at[self.m, slot], device)
        copy.start()
        self.sent.append(copy)

    def arrived(self, dst, slot):
        remote(dst, dst, self.send.at[self.m, slot], self.recv.at[self.m, slot], self.p.sib).wait_recv()

    def cols(self, part="AB", core=None):
        at, size = {"A": (0, self.a), "B": (self.a, self.b), "AB": (0, self.half)}[part]
        core = self.p.core if core is None else core
        return lanes(self.off + core * self.half + at, size)

    def group(self, dp):
        return rows_at(dp * 4 * ROWS, 4 * ROWS, 16)

    def side(self, dp, part="AB"):
        return self.grad.at[self.group(dp), self.cols(part)]

    def start(self):
        p = self.p
        if self.waits:
            pl.semaphore_wait(self.free, 1)
        for i, dp in enumerate(self.groups):
            theirs = self.grad.at[self.group(dp), self.cols("AB", 1 - p.core)]
            self.go(theirs, self.pair.at[self.group(dp)], i, p.sib)

    def add(self, dp, part, other, other_row=0):
        @pl.loop(0, 4)
        def _(i):
            key = (rows_at(dp * 4 * ROWS + i * ROWS, ROWS, 16), self.cols(part))
            self.grad[key] = self.grad[key] + other[rows_at(other_row + i * ROWS, ROWS, 16), :]

    def one(self):
        p = self.p
        for i, dp in enumerate(self.groups):
            self.arrived(self.pair.at[self.group(dp)], i)
            self.add(dp, "AB", self.pair, dp * 4 * ROWS)
            if i == 0:
                self.go(self.side(dp, "A"), self.r1a, 4, p.ynbr)
                if self.b:
                    self.go(self.side(dp, "B"), self.r1b, 5, p.xnbr)
        if self.frees:
            pl.semaphore_signal(self.free, inc=1, device_id=p.sib, device_id_type=MESH)

    def two(self):
        p = self.p
        self.arrived(self.r1a, 4)
        self.add(p.xdp, "A", self.r1a)
        self.go(self.side(p.xdp), self.rx, 6, p.xnbr)
        if self.b:
            self.arrived(self.r1b, 5)
            self.add(p.ydp, "B", self.r1b)
        self.go(self.side(p.ydp), self.ry, 7, p.ynbr)

    def three(self):
        p = self.p
        self.arrived(self.rx, 6)
        self.arrived(self.ry, 7)

        @pl.loop(0, 4)
        def _(i):
            key = (rows_at(p.dp * 4 * ROWS + i * ROWS, ROWS, 16), self.cols())
            own = rows_at(i * ROWS, ROWS, 16)
            self.grad[key] = self.grad[key] + (self.rx[own, :] + self.ry[own, :])

        for d in (1, 3, 2):
            z = (p.z + d) % 4
            src = self.grad.at[rows_at((p.dp * 4 + z) * ROWS, ROWS, 16), self.cols()]
            self.go(src, self.r3.at[d - 1], 7 + d, p.at(p.dp, z, p.core))

    def four(self):
        p = self.p
        for d in (1, 3, 2):
            self.arrived(self.r3.at[d - 1], 7 + d)
        rows = rows_at((p.dp * 4 + p.z) * ROWS, ROWS, 16)
        total = self.grad[rows, self.cols()].astype(f32)
        for d in range(3):
            total = total + self.r3[d].astype(f32)
        upper, lower = total[: ROWS // 2], total[ROWS // 2 :]
        first = p.core == 0
        self.give[...] = jnp.where(first, lower, upper)
        self.out[:, self.cols()] = jnp.where(first, upper, lower)
        self.go(self.give, self.out.at[:, self.cols()], 11, p.sib)

    def five(self):
        self.arrived(self.out.at[:, self.cols("AB", 1 - self.p.core)], 11)

    def finish(self):
        for copy in self.sent:
            copy.wait_send()


def split_half(width, wide_a):
    tiles = width // 2 // LANES
    return ((tiles + 1) // 2 if wide_a else max(tiles // 2, 1)) * LANES


def scatter_buffers(width, wide_a):
    half = width // 2
    a = split_half(width, wide_a)
    b = half - a
    return [
        VM((4 * ROWS, a), bf16),
        VM((4 * ROWS if b else 16, max(b, LANES)), bf16),
        VM((4 * ROWS, half), bf16),
        VM((4 * ROWS, half), bf16),
        VM((3, ROWS, half), bf16),
        VM((ROWS // 2, half), f32),
    ]


SCATTER_LAGS = {"start": 0, "one": 1, "two": 2, "three": 3, "four": 4, "five": 5}
PAIR_SLOTS = 4


def tail_units(width):
    return [(0, width), (width, width), (2 * width, width - 256), (3 * width - 256, 256)]


def scatter_step(sums, jobs):
    begun = len([s for s in sums.order[: sums.at] if s[0] == "start"])
    follow = [i for i, s in enumerate(sums.order) if s == ("start", begun + 1)]
    if begun < len(jobs):
        sums.step((follow[0] if follow else sums.order.index(("start", begun)) + 1) - sums.at)


def layer_kernel(*refs):
    wq_ref, wo_ref, wi_ref, wb_ref, gain_ref, bias_ref, pos_ref, docs_ref, x_ref, cot_ref = refs[:10]
    y_ref, gt_ref, gq_ref, go_ref, gi_ref, gb_ref, gs_ref = refs[10:17]
    (
        sw, ow, qw, iw, bw, cw, cwo,
        pk, at, cx, h, nl, g, sl, z1, z2, r1_ref, r2_ref, par_ref,
        own_buf, sib_buf, block, square,
        lead_out, gbuf, lead, xbuf, ybuf, dpack, home_ref, fac, fac_sib, csmall,
        df, tr, tr2, dws, small, full, tmp, ring, pair_wide, pair_small,
        s_send, s_recv, pair_send, pair_recv, wo_send, wo_recv, local,
        g_send, g_recv, x_send, x_recv, h_send, h_recv, lead_sem,
        f_send, f_recv, swap_send, swap_recv, rs_send, rs_recv, free,
    ) = refs[17:81]
    bufs = refs[81:]
    p = Place()
    rows, width = x_ref.shape
    segs = rows // SEG_LEN
    hidden = iw.shape[1]
    pairs = width // LANES
    slab = width // 4
    cross_width = cw.shape[1]
    half_rows = ROWS // 2
    key_own = rows_at((p.dp * 4 + p.z) * ROWS, ROWS, 16)

    sizes = [sw.shape[1]] + [width] * (3 + 1 + 2 * (hidden // width)) + [4 * cross_width, width]
    starts = [sum(sizes[:i]) for i in range(len(sizes))]
    n_seg = len(sizes) - 2
    part_cross, part_wo = n_seg, n_seg + 1

    def put(start, value):
        zero = jnp.zeros((own_buf.shape[0] - half_rows, value.shape[1]), f32)
        full = jnp.concatenate([value.astype(f32), zero], axis=0).astype(bf16)
        own_buf[:, pl.ds(start, value.shape[1])] = full

    def pair(i):
        cols = pl.ds(starts[i], sizes[i])
        return remote(
            own_buf.at[:, cols], sib_buf.at[:, cols], pair_send.at[i], pair_recv.at[i], p.sib
        )

    def stage(i):
        spot = starts[i]
        per = hidden // width
        if i == 0:
            own = gain_ref.shape[2]
            square[...] = jnp.zeros_like(square)
            for b in range(2):
                square[4 * b : 4 * b + 2, :own] = gain_ref[b].astype(f32)
                square[4 * b + 2 : 4 * b + 4, :own] = bias_ref[b].astype(f32)
            square[8 : 8 + pos_ref.shape[0], :own] = pos_ref[...].astype(f32)
            turned = square[...].T[:half_rows]
            put(spot, jnp.concatenate([turned, jnp.zeros_like(turned)], axis=1))
        elif i < 4:
            put(spot, wq_ref[0, :, (i - 1) * width : i * width])
        elif i == 4:
            put(spot, wo_ref[0])
        elif i < 5 + per:
            put(spot, wi_ref[0, :, (i - 5) * width : (i - 4) * width])
        elif i < 5 + 2 * per:
            put(spot, wb_ref[0, :, (i - 5 - per) * width : (i - 4 - per) * width])
        elif i == part_cross:
            for z in range(4):
                heads = [wq_ref[1, :, j * width + z * slab : j * width + (z + 1) * slab] for j in range(3)]
                heads.append(heads[2])
                put(spot, jnp.concatenate([v.astype(f32) for v in heads], axis=1).astype(bf16))
                put(spot + width, wi_ref[1, :, z * width : (z + 1) * width])
                put(spot + 2 * width, wb_ref[1, :, z * width : (z + 1) * width])
                spot += cross_width
        else:
            put(spot, wo_ref[1])

    def joined(start, size):
        cols = lanes(start, size)
        first = p.core == 0
        mine = own_buf[:, cols].astype(f32)[:half_rows]
        theirs = sib_buf[:, cols].astype(f32)[:half_rows]
        both = [jnp.where(first, mine, theirs), jnp.where(first, theirs, mine)]
        return jnp.concatenate(both, axis=0).astype(bf16)

    ahead = 4

    def begin(i):
        if i < n_seg + 2:
            stage(i)
            pair(i).start()

    stage(0)
    greet(everyone(p))
    pair(0).start()
    for i in range(1, ahead):
        begin(i)

    sems = (s_send, s_recv)
    dests = [(sw, 0)] + [(qw, i * width) for i in range(3)] + [(ow, 0)]
    dests += [(iw, i * width) for i in range(hidden // width)]
    dests += [(bw, i * width) for i in range(hidden // width)]

    class SegUnit(Gather):
        def __init__(self, i):
            dst, off = dests[i]
            mine = lambda z: dst.at[key_own, self.cols(p.core)]
            super().__init__(p, dst, off, sizes[i], mine, i, sems, ROWS, i % 2 == 0)
            self.i = i

        def own(self):
            pair(self.i).wait_recv()
            self.out[key_own, self.cols(p.core)] = joined(
                starts[self.i] + p.core * self.half, self.half
            )
            super().own()
            begin(self.i + ahead)

    class CrossUnit(Gather):
        def __init__(self, i):
            start = i * width
            self.i = i

            def mine(z):
                spot = z * cross_width + start + p.core * self.half
                return block.at[:, lanes(spot, self.half)]

            super().__init__(p, cw, start, width, mine, n_seg + i, sems, ROWS, i % 2 == 0)

        def own(self):
            if self.i == 0:
                pair(part_cross).wait_recv()

                @pl.loop(0, 4 * cross_width // width)
                def _(k):
                    block[:, lanes(k * width, width)] = joined(starts[part_cross] + k * width, width)

            spot = p.z * cross_width + self.i * width + p.core * self.half
            self.out[key_own, self.cols(p.core)] = block[:, lanes(spot, self.half)]
            super().own()

    units = [SegUnit(i) for i in range(n_seg)] + [CrossUnit(i) for i in range(cross_width // width)]
    n_cross = len(units) - n_seg
    comm = Staged(units, forward_order(n_seg, n_cross))

    def need(i):
        comm.upto("drain", i)

    def pump():
        comm.step(5)

    half_wo = width // 2
    wo_block = block.at[:, pl.ds(4 * cross_width, width)]
    wo_src = block.at[:, lanes(4 * cross_width + p.core * half_wo, half_wo)]
    wo_dst = cwo.at[rows_at(p.z * ROWS, ROWS, 16), lanes(p.core * half_wo, half_wo)]

    def wo_copy(i):
        return remote(wo_src, wo_dst, wo_send.at[i], wo_recv.at[p.z], p.at(i, p.dp, p.core))

    def wo_start():
        pair(part_wo).wait_recv()
        wo_block[...] = joined(starts[part_wo], width)
        for i in range(4):
            here = jnp.logical_and(p.dp == i, p.dp == p.z)

            @pl.when(jnp.logical_not(here))
            def _():
                wo_copy(i).start()

            @pl.when(here)
            def _():
                mine = pltpu.make_async_copy(wo_src, wo_dst, local)
                mine.start()
                mine.wait()

    wo_mine = cwo.at[:, lanes(p.core * half_wo, half_wo)]
    wo_theirs = cwo.at[:, lanes((1 - p.core) * half_wo, half_wo)]
    wo_hand = remote(wo_mine, wo_mine, wo_send.at[4], wo_recv.at[4], p.sib)

    def wo_middle():
        for i in range(4):
            piece = cwo.at[pl.ds(i * ROWS, ROWS), lanes(p.core * half_wo, half_wo)]

            @pl.when(jnp.logical_not(jnp.logical_and(p.z == p.dp, p.z == i)))
            def _():
                remote(piece, piece, wo_send.at[i], wo_recv.at[i], p.sib).wait_recv()

        wo_hand.start()

    def wo_finish():
        remote(wo_theirs, wo_theirs, wo_send.at[4], wo_recv.at[4], p.sib).wait_recv()
        wo_hand.wait_send()
        for i in range(4):

            @pl.when(jnp.logical_not(jnp.logical_and(p.dp == i, p.dp == p.z)))
            def _():
                wo_copy(i).wait_send()

    tile = 256

    def params():
        par_ref[...] = sw[...].astype(f32).T[: par_ref.shape[0]]

    def project(first, count):
        @pl.loop(first, first + count)
        def _(i):
            cols = lanes(i * tile, tile)
            pk[:, cols] = mm(x_ref[...], qw[:, cols], NN).astype(bf16)

    def attend(s):
        key = pl.ds(s * SEG_LEN, SEG_LEN)

        @pl.loop(0, pairs, unroll=True)
        def _(j):
            q2 = pk[key, lanes(j * LANES, LANES)]
            k2 = pk[key, lanes(width + j * LANES, LANES)]
            v2 = pk[key, lanes(2 * width + j * LANES, LANES)]
            scores = mm(jnp.concatenate(lane_halves(q2), axis=0), k2, NT) * (LANES // 2) ** (-0.5)
            top = jnp.max(scores, axis=-1, keepdims=True)
            terms = jnp.exp(scores - top)
            a = (terms / jnp.sum(terms, axis=-1, keepdims=True)).astype(bf16)
            at[rows_at((s * pairs + j) * 2 * SEG_LEN, 2 * SEG_LEN, 16), :] = a
            both = jnp.concatenate([a[:SEG_LEN], a[SEG_LEN:]], axis=1)
            c2 = mm(both, jnp.concatenate(lane_halves(v2), axis=0), NN)
            cx[key, lanes(j * LANES, LANES)] = c2.astype(bf16)

    block_rows = 64

    def branch():
        @pl.loop(0, width // tile)
        def _(i):
            cols = lanes(i * tile, tile)
            h[:, cols] = x_ref[:, cols].astype(f32) + mm(cx[...], ow[:, cols], NN)

        @pl.loop(0, rows // block_rows, unroll=2)
        def _(i):
            key = rows_at(i * block_rows, block_rows, 16)
            normed, scaled, inverse = norm_rows(h[key, :], par_ref[0:1, :], par_ref[2:3, :])
            h[key, :] = normed
            nl[key, :] = normed.astype(bf16)
            z1[key, :] = scaled.astype(bf16)
            r1_ref[key, :] = jnp.broadcast_to(inverse, (block_rows, LANES))

    def feed_in(first, count):
        @pl.loop(first, first + count)
        def _(i):
            cols = lanes(i * tile, tile)
            u = mm(nl[...], iw[:, cols], NN)
            phi, slope = gelu_parts(u)
            g[:, cols] = (u * phi).astype(bf16)
            sl[:, cols] = slope.astype(bf16)

    def feed_back(part):
        inner = pl.ds(part * width, width)

        @pl.loop(0, width // tile)
        def _(i):
            cols = lanes(i * tile, tile)
            h[:, cols] += mm(g[:, inner], bw[rows_at(i * tile, tile, 16), inner], NT)

    def finish_block():
        @pl.loop(0, rows // block_rows, unroll=2)
        def _(i):
            key = rows_at(i * block_rows, block_rows, 16)
            result, scaled, inverse = norm_rows(h[key, :], par_ref[1:2, :], par_ref[3:4, :])
            h[key, :] = result
            y_ref[key, :] = result.astype(bf16)
            z2[key, :] = scaled.astype(bf16)
            r2_ref[key, :] = jnp.broadcast_to(inverse, (block_rows, LANES))

    def leaders():
        for s in range(segs):
            pos = par_ref[pl.ds(8 + p.fsdp * 2 + s % 2, 1), :]
            lead_out[s // 2, s % 2 : s % 2 + 1, :width] = h[s * SEG_LEN : s * SEG_LEN + 1, :] + pos
            lead_out[s // 2, s % 2 : s % 2 + 1, width:] = cot_ref[s * SEG_LEN : s * SEG_LEN + 16, :].astype(f32)[:1]

    def lead_copy(z, j):
        i = 2 * z + j
        return remote(lead_out.at[j], gbuf.at[p.fsdp], g_send.at[i], g_recv.at[p.fsdp], (p.dp, i))


    leads = fac.shape[0]
    lead2 = 2 * leads
    key_f = rows_at((p.dp * 4 + p.z) * lead2, lead2, 16)

    def swap(i):
        cols = pl.ds(i * width, width)
        return remote(fac.at[:, cols], fac_sib.at[:, cols], swap_send.at[i], swap_recv.at[i], p.sib)

    def give_factor(i, value):
        fac[:, i * width : (i + 1) * width] = value
        swap(i).start()

    class Factor(Gather):
        def __init__(self, i):
            mine = lambda z: full.at[key_f, self.cols(p.core)]
            super().__init__(p, full, i * width, width, mine, i, (f_send, f_recv), lead2, i % 2 == 0)
            self.i = i

        def own(self):
            swap(self.i).wait_recv()
            base = (p.dp * 4 + p.z) * lead2
            cols = lanes(self.i * width + p.core * (width // 2), width // 2)
            full[rows_at(base + p.core * leads, leads, 16), cols] = fac[:, cols]
            full[rows_at(base + (1 - p.core) * leads, leads, 16), cols] = fac_sib[:, cols]
            super().own()

    factors = [Factor(i) for i in range(4)]

    def factor_grads():
        def rows_of(z, at_col, size):
            return jnp.concatenate(
                [full[rows_at((i * 4 + z) * lead2, lead2, 16), pl.ds(at_col, size)] for i in range(4)],
                axis=0,
            )

        base = 2 * width
        own = rows_at(p.fsdp * (ROWS // 2), ROWS // 2, 8)
        xl = rows_of(p.dp, base, slab)
        nlf = rows_of(p.dp, base + slab, slab)
        dff = rows_of(p.dp, base + 2 * slab, slab)
        ctx = rows_of(p.dp, base + 3 * slab, slab)
        for z in range(4):
            tmp[:, :width] = mm(dff, rows_of(z, 0, width), TN)
            gb_ref[1, :, z * width : (z + 1) * width] = tmp[own, :width]
            tmp[:, :width] = mm(nlf, rows_of(z, width, width), TN)
            gi_ref[1, :, z * width : (z + 1) * width] = tmp[own, :width]
            tmp[:, : 3 * slab] = mm(xl, rows_of(z, 3 * width, 3 * slab), TN)
            got = tmp[own, : 3 * slab]
            for j in range(3):
                spot = j * width + z * slab
                gq_ref[1, :, spot : spot + slab] = got[:, j * slab : (j + 1) * slab]
            tmp[:, :slab] = mm(ctx, rows_of(z, 3 * width + 3 * slab, slab), TN)
            go_ref[1, :, z * slab : (z + 1) * slab] = tmp[own, :slab]


    n_tiles = width // tile
    head = width // HEADS
    heads = HEADS // 4

    def cross():
        for d in range(4):
            z = (p.z + d) % 4
            for j in range(2):
                if d:
                    lead_copy(z, j).start()
                else:

                    @pl.when(p.core != j)
                    def _():
                        lead_copy(z, j).start()

                    @pl.when(p.core == j)
                    def _():
                        mine = pltpu.make_async_copy(lead_out.at[j], gbuf.at[p.fsdp], lead_sem)
                        mine.start()
                        mine.wait()

        need(n_seg)
        wo_middle()
        for d in range(1, 8):
            i = lax.rem(p.fsdp + d, 8)
            remote(gbuf.at[i], gbuf.at[i], g_send.at[i], g_recv.at[i], p.sib).wait_recv()
        for i in range(8):
            lead[2 * i : 2 * i + 2, :] = gbuf[i]
        states = lead[:, :width]
        cot_rows = lead[:, width:]

        def sum_z(e, partial_sum, between):
            xbuf[e, p.z] = partial_sum.astype(bf16)
            copies = []
            for d in (1, 3, 2):
                z = (p.z + d) % 4
                copy = remote(
                    xbuf.at[e, p.z], xbuf.at[e, p.z], x_send.at[e, d - 1], x_recv.at[e, p.z],
                    p.at(p.dp, z, p.core),
                )
                copy.start()
                copies.append(copy)
            between()
            for d in (1, 3, 2):
                z = (p.z + d) % 4
                piece = xbuf.at[e, z]
                remote(piece, piece, x_send.at[e, d - 1], x_recv.at[e, z], p.sib).wait_recv()
            for copy in copies:
                copy.wait_send()
            return sum(xbuf[e, z].astype(f32) for z in range(4))

        gain0, gain1 = par_ref[4:5, :], par_ref[5:6, :]
        bias0, bias1 = par_ref[6:7, :], par_ref[7:8, :]
        in_cols, back_cols = pl.ds(width, width), pl.ds(2 * width, width)
        qkv_cols = pl.ds(0, 3 * slab)
        factor = head ** (-0.5)
        docs = docs_ref[...].astype(f32)
        number = docs.shape[1]
        square[:number, :number] = jnp.broadcast_to(
            jnp.where(p.core == 0, docs[0:1], docs[1:2]), (number, number)
        )
        allowed = square[:number, :number] == square[...].T[:number, :number]

        def part(full):
            pieces = [full[:, i * slab : (i + 1) * slab] for i in range(4)]
            out = pieces[0]
            for i in range(1, 4):
                out = jnp.where(p.z == i, pieces[i], out)
            return out.astype(bf16)

        xl = states.astype(bf16)
        packed = mm(xl, cw[:, qkv_cols], NN).astype(bf16)
        q = [packed[:, i * head : (i + 1) * head] for i in range(heads)]
        k = [packed[:, slab + i * head : slab + (i + 1) * head] for i in range(heads)]
        v = [packed[:, 2 * slab + i * head : 2 * slab + (i + 1) * head] for i in range(heads)]
        att, context = [], []
        for i in range(heads):
            scores = jnp.where(allowed, mm(q[i], k[i], NT) * factor, NEG)
            top = jnp.max(scores, axis=-1, keepdims=True)
            terms = jnp.exp(scores - top)
            a = terms / jnp.sum(terms, axis=-1, keepdims=True)
            att.append(a)
            context.append(mm(a.astype(bf16), v[i], NN))
        context = jnp.concatenate(context, axis=1).astype(bf16)
        wo_finish()
        branch = sum_z(0, mm(context, cwo[...], NN), lambda: None)
        normed, z_one, r_one = norm_rows(states + branch, gain0, bias0)
        nl = normed.astype(bf16)
        need(n_seg + 1)
        hidden = mm(nl, cw[:, in_cols], NN)
        phi, slope = gelu_parts(hidden)
        active = (hidden * phi).astype(bf16)
        give_factor(0, active)
        need(n_seg + 2)

        def during_one():
            factors[0].own()

        feed = sum_z(1, mm(active, cw[:, back_cols], NT), during_one)
        result, z_two, r_two = norm_rows(normed + feed, gain1, bias1)
        d_two = norm_rows_back(cot_rows, z_two, r_two, gain1)
        df = d_two.astype(bf16)
        du = (mm(df, cw[:, back_cols], NN) * slope).astype(bf16)
        give_factor(1, du)
        give_factor(2, jnp.concatenate([part(states), part(normed), part(d_two), context], axis=1))

        def during_two():
            factors[0].line()
            factors[1].own()
            factors[2].own()

        d_normed = d_two + sum_z(2, mm(du, cw[:, in_cols], NT), during_two)
        d_one = norm_rows_back(d_normed, z_one, r_one, gain0)
        db = d_one.astype(bf16)
        dc = mm(db, cwo[...], NT).astype(bf16)
        for i in range(heads):
            a = att[i]
            dci = dc[:, i * head : (i + 1) * head]
            da = mm(dci, v[i], NT)
            dv = mm(a.astype(bf16), dci, TN)
            ds = (a * (da - jnp.sum(a * da, axis=-1, keepdims=True))).astype(bf16)
            dq = mm(ds, k[i], NN) * factor
            dk = mm(ds, q[i], TN) * factor
            for j, piece in enumerate((dq, dk, dv)):
                dpack[:, j * slab + i * head : j * slab + (i + 1) * head] = piece
        dp = dpack[...].astype(bf16)
        give_factor(3, jnp.concatenate([dp, part(d_one)], axis=1))

        def during_three():
            factors[0].plane()
            factors[1].line()
            factors[3].own()
            factors[2].line()

        dx = d_one + sum_z(3, mm(dp, cw[:, qkv_cols], NT), during_three)
        for i in range(8):
            ybuf[i, :, :width] = result[2 * i : 2 * i + 2]
            ybuf[i, :, width:] = dx[2 * i : 2 * i + 2]
        home = remote(
            ybuf.at[2 * p.z + 1 - p.core], home_ref.at[p.core], h_send, h_recv, p.sib
        )
        home.start()
        home_ref[p.core] = ybuf[2 * p.z + p.core]

        once = jnp.where(p.z == 0, 1.0, 0.0)
        sums_of = [d_normed * z_one, cot_rows * z_two, d_normed, cot_rows]
        csmall[...] = jnp.zeros_like(csmall)
        for i, s in enumerate(sums_of):
            csmall[i : i + 1, :] = once * jnp.sum(s, axis=0, keepdims=True)
        theirs = home_ref.at[1 - p.core]
        remote(theirs, theirs, h_send, h_recv, p.sib).wait_recv()
        home.wait_send()

    def wait_leads():
        for d in range(4):
            z = (p.z + d) % 4
            for j in range(2):
                if d:
                    lead_copy(z, j).wait_send()
                else:

                    @pl.when(p.core != j)
                    def _():
                        lead_copy(z, j).wait_send()


    def patch():
        for s in range(segs):
            spot = pl.ds(s * SEG_LEN, 16)
            old = y_ref[spot, :].astype(f32)
            new = jnp.broadcast_to(home_ref[s // 2, s % 2 : s % 2 + 1, :width], old.shape)
            top = lax.broadcasted_iota(jnp.int32, old.shape, 0) == 0
            y_ref[spot, :] = jnp.where(top, new, old).astype(bf16)
    per = hidden // width
    parts = [(bw, i * width, width, gb_ref.at[0]) for i in range(per)]
    parts += [(iw, i * width, width, gi_ref.at[0]) for i in range(per)]
    parts += [(ow, 0, width, go_ref.at[0]), (dws, 0, dws.shape[1], gs_ref)]
    parts += [(qw, at_col, size, gq_ref.at[0]) for at_col, size in tail_units(width)]
    jobs, shared = [], []
    for i, (grad, off, size, dst) in enumerate(parts):
        job_bufs = list(bufs[6 * i : 6 * i + 6])
        if size == width:
            slot = len(shared) % PAIR_SLOTS
            job = Scatter(p, grad, off, size, dst, i, (rs_send, rs_recv), [ring.at[slot]] + job_bufs, i % 2 == 0)
            job.free = free.at[slot]
            if len(shared) >= PAIR_SLOTS:
                job.waits = True
                shared[len(shared) - PAIR_SLOTS].frees = True
            shared.append(job)
        else:
            own_pair = pair_wide if size > 256 else pair_small.at[len([j for j in jobs if j.half == LANES])]
            job = Scatter(p, grad, off, size, dst, i, (rs_send, rs_recv), [own_pair] + job_bufs, i % 2 == 0)
        jobs.append(job)
    sums = Staged(jobs, staggered(len(jobs), SCATTER_LAGS))


    def norm_back(z_ref, r_ref, gain_row, low_ref, sums):
        def step(i, acc):
            key = rows_at(i * block_rows, block_rows, 16)
            dy = h[key, :]
            z = z_ref[key, :].astype(f32)
            r = jnp.concatenate([r_ref[key, :]] * (width // LANES), axis=1)
            e = dy * par_ref[gain_row : gain_row + 1, :]
            first = jnp.mean(e, axis=-1, keepdims=True)
            second = jnp.mean(e * z, axis=-1, keepdims=True)
            d = r * (e - first - z * second)
            h[key, :] = d
            low_ref[key, :] = d.astype(bf16)
            fold = lambda v: jnp.sum(v.reshape(block_rows // 8, 8, width), axis=0)
            return acc[0] + fold(dy * z), acc[1] + fold(dy)

        zero = jnp.zeros((8, width), f32)
        gain, bias = lax.fori_loop(0, rows // block_rows, step, (zero, zero), unroll=2)
        small[sums : sums + 1, :] = jnp.sum(gain, axis=0, keepdims=True)
        small[sums + 2 : sums + 3, :] = jnp.sum(bias, axis=0, keepdims=True)

    def turn(tr, ref):
        @pl.loop(0, width // tile)
        def _(i):
            tr[rows_at(i * tile, tile, 16), :] = ref[:, lanes(i * tile, tile)].T

    def outer(dst, tr, src, first, size):
        @pl.loop(first // tile, (first + size) // tile)
        def _(i):
            cols = lanes(i * tile, tile)
            dst[:, cols] = mm(tr[...], src[:, cols], NN).astype(bf16)

    def norm_two():
        @pl.loop(0, rows // block_rows, unroll=2)
        def _(i):
            key = rows_at(i * block_rows, block_rows, 16)
            h[key, :] = cot_ref[key, :].astype(f32)

        for s in range(segs):
            h[s * SEG_LEN : s * SEG_LEN + 1, :] = home_ref[s // 2, s % 2 : s % 2 + 1, width:]
        small[...] = jnp.zeros_like(small)
        small[4:8, :] = csmall[0:4, :]
        for s in range(2):
            row = home_ref[0, s : s + 1, width:] + home_ref[1, s : s + 1, width:]
            small[pl.ds(8 + p.fsdp * 2 + s, 1), :] = row
        norm_back(z2, r2_ref, 1, df, 1)
        turn(tr, df)

    def active_back(part):
        @pl.loop(part * n_tiles, (part + 1) * n_tiles)
        def _(i):
            cols = lanes(i * tile, tile)
            d = mm(df[...], bw[:, cols], NN) * sl[:, cols].astype(f32)
            sl[:, cols] = d.astype(bf16)

    def add_back(src, weight, first, size):
        inner = pl.ds(first, size)

        @pl.loop(0, n_tiles)
        def _(i):
            cols = lanes(i * tile, tile)
            h[:, cols] += mm(src[:, inner], weight[rows_at(i * tile, tile, 16), inner], NT)

    def context_back():
        @pl.loop(0, width // tile)
        def _(i):
            d = mm(df[...], ow[rows_at(i * tile, tile, 16), :], NT)
            cx[:, lanes(i * tile, tile)] = d.astype(bf16)

    def attend_back(s):
        key = pl.ds(s * SEG_LEN, SEG_LEN)
        factor = (LANES // 2) ** (-0.5)

        @pl.loop(0, pairs, unroll=True)
        def _(j):
            a = at[rows_at((s * pairs + j) * 2 * SEG_LEN, 2 * SEG_LEN, 16), :]
            q_cols = lanes(j * LANES, LANES)
            k_cols = lanes(width + j * LANES, LANES)
            v_cols = lanes(2 * width + j * LANES, LANES)
            qs = jnp.concatenate(lane_halves(pk[key, q_cols]), axis=0)
            ks = jnp.concatenate(lane_halves(pk[key, k_cols]), axis=0)
            ds_in = jnp.concatenate(lane_halves(cx[key, q_cols]), axis=0)
            da = mm(ds_in, pk[key, v_cols], NT)
            af = a.astype(f32)
            ds = (af * (da - jnp.sum(af * da, axis=-1, keepdims=True))).astype(bf16)
            dv = mm(a, ds_in, TN)
            both = jnp.concatenate([ds[:SEG_LEN], ds[SEG_LEN:]], axis=1)
            dq = mm(both, ks, NN) * factor
            dk = mm(ds, qs, TN) * factor
            pk[key, q_cols] = dq.astype(bf16)
            pk[key, k_cols] = dk.astype(bf16)
            pk[key, v_cols] = dv.astype(bf16)

    def result():
        @pl.loop(0, rows // block_rows, unroll=2)
        def _(i):
            key = rows_at(i * block_rows, block_rows, 16)
            gt_ref[key, :] = h[key, :].astype(bf16)

    def smalls():
        dws[:, :LANES] = small[...].T.astype(bf16)
        dws[:, LANES:] = jnp.zeros((dws.shape[0], LANES), bf16)

    need(0)
    params()
    for i in range(3):
        need(1 + i)
        project(i * n_tiles, n_tiles)
    for s in range(segs):
        attend(s)
        comm.upto("drain", 4 + s)
    branch()
    for i in range(per):
        need(4 + per + i)
        feed_in(i * n_tiles, n_tiles)
        if i:
            feed_back(i - 1)
    wo_start()
    need(4 + 2 * per)
    feed_back(per - 1)
    finish_block()
    leaders()
    cross()
    comm.finish()
    for i in range(n_seg + 2):
        pair(i).wait_send()
    patch()
    sum_step = lambda: scatter_step(sums, jobs)
    norm_two()
    factors[1].plane()
    factors[2].plane()
    factors[0].last()
    for i in range(per):
        active_back(i)
        outer(bw, tr, g, i * width, width)
        sum_step()
        if i == 0:
            factors[3].line()
            factors[1].last()
        if i == 1:
            factors[2].last()
            factors[3].plane()
        if i == 2:
            factors[3].last()
    turn(tr, nl)
    add_back(sl, iw, 0, 2 * width)
    add_back(sl, iw, 2 * width, hidden - 2 * width)
    outer(iw, tr, sl, 0, width)
    sum_step()
    norm_back(z1, r1_ref, 0, df, 0)
    outer(iw, tr, sl, width, width)
    sum_step()
    smalls()
    turn(tr2, cx)
    context_back()
    attend_back(0)
    for i in range(2, per - 1):
        outer(iw, tr, sl, i * width, width)
        sum_step()
    attend_back(1)
    outer(iw, tr, sl, (per - 1) * width, width)
    sum_step()
    attend_back(2)
    outer(ow, tr2, df, 0, width)
    sum_step()
    attend_back(3)
    sum_step()
    turn(tr2, x_ref)
    for at_col, size in tail_units(width):
        add_back(pk, qw, at_col, size)
        outer(qw, tr2, pk, at_col, size)
        sum_step()
    result()
    for unit in factors:
        unit.drain()
    factor_grads()
    sums.finish()
    for unit in factors:
        unit.finish()
    for i in range(4):
        swap(i).wait_send()
    wait_leads()


def layer(wq, wo, wi, wb, gain, bias, pos, docs, x, cot):
    wrows = 16 * ROWS
    rows, width = x.shape
    segs = rows // SEG_LEN
    leads = docs.shape[1]
    hidden = wi.shape[2]
    own = ROWS // 2
    cross_width = 3 * width
    total = 2 * LANES + 3 * width + width + 2 * hidden + 4 * cross_width + width
    parts = 5 + 2 * hidden // width + 2
    n_units = parts - 2 + 3
    vm = pl.BlockSpec(memory_space=VM)
    arr = jax.ShapeDtypeStruct
    DMA = pltpu.SemaphoreType.DMA
    att_rows = segs * HEADS * SEG_LEN
    wide = lambda v, kind=bf16: VM((rows, v), kind)
    weight = lambda v: VM((wrows, v), bf16)
    widths = [width] * (2 * (hidden // width) + 1) + [256] + [size for _, size in tail_units(width)]
    bufs = []
    for i, w in enumerate(widths):
        bufs += scatter_buffers(w, i % 2 == 0)
    small_units = len([w for w in widths if w == 256])
    return pl.pallas_call(
        layer_kernel,
        out_shape=[
            arr((rows, width), bf16),
            arr((rows, width), bf16),
            arr((2, own, 3 * width), f32),
            arr((2, own, width), f32),
            arr((2, own, hidden), f32),
            arr((2, own, hidden), f32),
            arr((own, 256), f32),
        ],
        in_specs=[vm] * 10,
        out_specs=[vm] * 7,
        scratch_shapes=[
            weight(2 * LANES), weight(width), weight(3 * width), weight(hidden), weight(hidden),
            weight(cross_width), VM((wrows // 4, width), bf16),
            wide(3 * width), VM((att_rows, SEG_LEN), bf16), wide(width), wide(width, f32), wide(width),
            wide(hidden), wide(hidden), wide(width), wide(width),
            wide(LANES, f32), wide(LANES, f32), VM((24, width), f32),
            VM((32, total), bf16), VM((32, total), bf16), VM((ROWS, 4 * cross_width + width), bf16),
            VM((LANES, LANES), f32),
            VM((2, 2, 2 * width), f32), VM((8, 2, 2 * width), f32), VM((leads, 2 * width), f32),
            VM((4, 4, leads, width), bf16), VM((8, 2, 2 * width), f32), VM((leads, 3 * width // 4), f32),
            VM((2, 2, 2 * width), f32), VM((leads, 4 * width), bf16), VM((leads, 4 * width), bf16),
            VM((8, width), f32),
            wide(width), VM((width, rows), bf16), VM((width, rows), bf16), weight(256),
            VM((LANES, width), f32), VM((32 * leads, 4 * width), bf16), VM((width // 4, width), f32),
            VM((PAIR_SLOTS, wrows, width // 2), bf16), weight((width - 256) // 2),
            VM((small_units, wrows, LANES), bf16),
            DMA((n_units, 11)), DMA((n_units, 11)), DMA((parts,)), DMA((parts,)),
            DMA((5,)), DMA((5,)), DMA,
            DMA((8,)), DMA((8,)), DMA((4, 3)), DMA((4, 4)), DMA, DMA, DMA,
            DMA((4, 11)), DMA((4, 11)), DMA((4,)), DMA((4,)),
            DMA((len(widths), 12)), DMA((len(widths), 12)), pltpu.SemaphoreType.REGULAR((PAIR_SLOTS,)),
        ]
        + bufs,
        compiler_params=pltpu.CompilerParams(
            collective_id=0, has_side_effects=True, vmem_limit_bytes=63 * MIB
        ),
    )(wq, wo, wi, wb, gain, bias, pos, docs, x, cot)


def matmul(left, right, form):
    return jnp.einsum(form, left, right, preferred_element_type=jnp.float32)


def norm_forward(summed, gains, biases):
    average = jnp.mean(summed, axis=-1, keepdims=True)
    centred = summed - average
    variance = jnp.mean(centred * centred, axis=-1, keepdims=True)
    inverse = lax.rsqrt(variance + epsilon)
    scaled = centred * inverse
    return (scaled * gains + biases, scaled, inverse)


def norm_backward(grad_result, scaled, inverse, gains):
    grad_scaled = grad_result * gains
    first_mean = jnp.mean(grad_scaled, axis=-1, keepdims=True)
    second_mean = jnp.mean(grad_scaled * scaled, axis=-1, keepdims=True)
    grad_sum = inverse * (grad_scaled - first_mean - scaled * second_mean)
    return (grad_sum, jnp.sum(grad_result * scaled, axis=(0, 1)), jnp.sum(grad_result, axis=(0, 1)))


def split_heads(packed):
    groups, length, model_width = packed.shape
    return packed.reshape(groups, length, HEADS, model_width // HEADS)


def join_heads(split_part):
    groups, length, heads_count, head_size = split_part.shape
    return split_part.reshape(groups, length, heads_count * head_size)


def attend_forward(query_part, key_part, value_part, allowed):
    head_size = query_part.shape[-1]
    scores = matmul(query_part, key_part, "glhe,gmhe->ghlm") * head_size ** (-0.5)
    scores = jnp.where(allowed[:, None], scores, -1e30)
    row_max = jnp.max(scores, axis=-1, keepdims=True)
    exp_terms = jnp.exp(scores - row_max)
    row_total = jnp.sum(exp_terms, axis=-1, keepdims=True)
    attention = exp_terms / row_total
    context = matmul(attention.astype(jnp.bfloat16), value_part, "ghlm,gmhe->glhe")
    return (join_heads(context).astype(jnp.bfloat16), row_max + jnp.log(row_total))


def attend_backward(query_part, key_part, value_part, allowed, log_total, grad_context):
    head_size = query_part.shape[-1]
    factor = head_size ** (-0.5)
    scores = matmul(query_part, key_part, "glhe,gmhe->ghlm") * factor
    scores = jnp.where(allowed[:, None], scores, -1e30)
    attention = jnp.exp(scores - log_total)
    grad_attention = matmul(grad_context, value_part, "glhe,gmhe->ghlm")
    grad_value = matmul(attention.astype(jnp.bfloat16), grad_context, "ghlm,glhe->gmhe")
    inner = jnp.sum(attention * grad_attention, axis=-1, keepdims=True)
    grad_scores = (attention * (grad_attention - inner)).astype(jnp.bfloat16)
    grad_query = matmul(grad_scores, key_part, "ghlm,gmhe->glhe") * factor
    grad_key = matmul(grad_scores, query_part, "ghlm,glhe->gmhe") * factor
    return (join_heads(grad_query), join_heads(grad_key), join_heads(grad_value))


def segment_attend(packed):
    groups, length, total_width = packed.shape
    model_width = total_width // 3
    allowed = jnp.ones((groups, length, length), dtype=jnp.bool_)
    context, log_total = attend_forward(
        split_heads(packed[..., :model_width]),
        split_heads(packed[..., model_width : 2 * model_width]),
        split_heads(packed[..., 2 * model_width :]),
        allowed,
    )
    return (context, log_total)


def segment_attend_back(packed, log_total, grad_context):
    groups, length, total_width = packed.shape
    model_width = total_width // 3
    allowed = jnp.ones((groups, length, length), dtype=jnp.bool_)
    grad_query, grad_key, grad_value = attend_backward(
        split_heads(packed[..., :model_width]),
        split_heads(packed[..., model_width : 2 * model_width]),
        split_heads(packed[..., 2 * model_width :]),
        allowed,
        log_total,
        split_heads(grad_context),
    )
    return jnp.concatenate([grad_query, grad_key, grad_value], axis=-1)


def cross_attend(packed, allowed):
    model_width = packed.shape[-1] // 3
    remote = lax.all_gather(packed[..., model_width:], "fsdp", axis=1, tiled=True)
    context, log_total = attend_forward(
        split_heads(packed[..., :model_width]),
        split_heads(remote[..., :model_width]),
        split_heads(remote[..., model_width:]),
        allowed,
    )
    return (context, (remote, log_total))


def cross_attend_back(packed, saved, grad_context, allowed):
    remote, log_total = saved
    model_width = packed.shape[-1] // 3
    grad_query, grad_key, grad_value = attend_backward(
        split_heads(packed[..., :model_width]),
        split_heads(remote[..., :model_width]),
        split_heads(remote[..., model_width:]),
        allowed,
        log_total,
        split_heads(grad_context),
    )
    shared = jnp.concatenate([grad_key, grad_value], axis=-1)
    own_part = lax.psum_scatter(
        shared.astype(jnp.bfloat16), "fsdp", scatter_dimension=1, tiled=True
    ).astype(jnp.float32)
    return jnp.concatenate([grad_query, own_part], axis=-1)


def block_forward(states, weights, attend):
    w_qkv, w_out, w_in, w_back, gains, biases = weights
    gains = gains.astype(jnp.float32)
    biases = biases.astype(jnp.float32)
    states_low = states.astype(jnp.bfloat16)
    packed = matmul(states_low, w_qkv, "gld,de->gle").astype(jnp.bfloat16)
    context, saved = attend(packed)
    branch = matmul(context, w_out, "gld,de->gle")
    normed, scaled_one, inverse_one = norm_forward(states + branch, gains[0], biases[0])
    normed_low = normed.astype(jnp.bfloat16)
    hidden = matmul(normed_low, w_in, "gld,df->glf")
    active_low = jax.nn.gelu(hidden, approximate=False).astype(jnp.bfloat16)
    feed_out = matmul(active_low, w_back, "glf,fd->gld")
    result, scaled_two, inverse_two = norm_forward(normed + feed_out, gains[1], biases[1])
    kept = (
        states_low,
        packed,
        context,
        saved,
        scaled_one,
        inverse_one,
        normed_low,
        hidden,
        active_low,
        scaled_two,
        inverse_two,
    )
    return (result, kept)


def block_backward(grad_result, kept, weights, attend_back):
    w_qkv, w_out, w_in, w_back, gains, biases = weights
    gains = gains.astype(jnp.float32)
    (
        states_low,
        packed,
        context,
        saved,
        scaled_one,
        inverse_one,
        normed_low,
        hidden,
        active_low,
        scaled_two,
        inverse_two,
    ) = kept
    grad_sum_two, gain_two, bias_two = norm_backward(grad_result, scaled_two, inverse_two, gains[1])
    grad_feed = grad_sum_two.astype(jnp.bfloat16)
    grad_active = matmul(grad_feed, w_back, "gld,fd->glf")
    cumulative = 0.5 * (1.0 + lax.erf(hidden * root_half))
    slope = cumulative + hidden * inv_root_tau * jnp.exp(-0.5 * hidden * hidden)
    grad_hidden = (grad_active * slope).astype(jnp.bfloat16)
    grad_normed = grad_sum_two + matmul(grad_hidden, w_in, "glf,df->gld")
    grad_sum_one, gain_one, bias_one = norm_backward(grad_normed, scaled_one, inverse_one, gains[0])
    grad_branch = grad_sum_one.astype(jnp.bfloat16)
    grad_context = matmul(grad_branch, w_out, "gle,de->gld").astype(jnp.bfloat16)
    grad_packed = attend_back(packed, saved, grad_context).astype(jnp.bfloat16)
    grad_states = grad_sum_one + matmul(grad_packed, w_qkv, "gle,de->gld")
    factors = (
        states_low,
        grad_packed,
        context,
        grad_branch,
        normed_low,
        grad_hidden,
        grad_feed,
        active_low,
    )
    smalls = (jnp.stack([gain_one, gain_two]), jnp.stack([bias_one, bias_two]))
    return (grad_states, factors, smalls)


def weight_terms(factors):
    (
        states_low,
        grad_packed,
        context,
        grad_branch,
        normed_low,
        grad_hidden,
        grad_feed,
        active_low,
    ) = factors
    term_qkv = matmul(states_low, grad_packed, "gld,gle->de")
    term_out = matmul(context, grad_branch, "gld,gle->de")
    term_in = matmul(normed_low, grad_hidden, "gld,glf->df")
    term_back = matmul(grad_feed, active_low, "gld,glf->df")
    return jnp.concatenate([term_qkv, term_out, term_in, term_back], axis=1)


def gather_segment(w_qkv, w_out, w_in, w_back, norm_gain, norm_bias):
    return (
        lax.all_gather(w_qkv[0], ("dp", "fsdp"), axis=0, tiled=True),
        lax.all_gather(w_out[0], ("dp", "fsdp"), axis=0, tiled=True),
        lax.all_gather(w_in[0], ("dp", "fsdp"), axis=0, tiled=True),
        lax.all_gather(w_back[0], ("dp", "fsdp"), axis=1, tiled=True),
        lax.all_gather(norm_gain[0], ("dp", "fsdp"), axis=1, tiled=True),
        lax.all_gather(norm_bias[0], ("dp", "fsdp"), axis=1, tiled=True),
    )


def gather_cross(pos_embed, w_qkv, w_out, w_in, w_back, norm_gain, norm_bias):
    gathered = (
        lax.all_gather(w_qkv[1], ("dp", "fsdp"), axis=0, tiled=True),
        lax.all_gather(w_out[1], ("dp", "fsdp"), axis=0, tiled=True),
        lax.all_gather(w_in[1], ("dp", "fsdp"), axis=0, tiled=True),
        lax.all_gather(w_back[1], ("dp", "fsdp"), axis=1, tiled=True),
        lax.all_gather(norm_gain[1], ("dp", "fsdp"), axis=1, tiled=True),
        lax.all_gather(norm_bias[1], ("dp", "fsdp"), axis=1, tiled=True),
        lax.all_gather(pos_embed, ("dp", "fsdp"), axis=1, tiled=True),
    )
    return (gathered[:6], gathered[6])


def layer_forward(tokens, doc_ids, seg_weights, cross_weights, pos_full):
    rows, local_len, model_width = tokens.shape
    seg_count = local_len // SEG_LEN
    segments = tokens.reshape(rows * seg_count, SEG_LEN, model_width).astype(jnp.float32)
    seg_out, seg_kept = block_forward(segments, seg_weights, segment_attend)
    start = lax.axis_index("fsdp") * seg_count
    pos_local = lax.dynamic_slice_in_dim(pos_full, start, seg_count, 0).astype(jnp.float32)
    leaders = seg_out[:, 0, :].reshape(rows, seg_count, model_width) + pos_local
    own_docs = lax.dynamic_slice_in_dim(doc_ids, start, seg_count, 1)
    allowed = own_docs[:, :, None] == doc_ids[:, None, :]
    cross_out, cross_kept = block_forward(
        leaders, cross_weights, partial(cross_attend, allowed=allowed)
    )
    joined = jnp.concatenate(
        [cross_out.reshape(rows * seg_count, 1, model_width), seg_out[:, 1:, :]], axis=1
    )
    output = joined.reshape(rows, local_len, model_width).astype(jnp.bfloat16)
    return (output, (seg_kept, cross_kept, allowed))


def layer_backward(cotangent, doc_ids, kept, seg_weights, cross_weights):
    seg_kept, cross_kept, allowed = kept
    rows, local_len, model_width = cotangent.shape
    seg_count = local_len // SEG_LEN
    grad_all = cotangent.reshape(rows * seg_count, SEG_LEN, model_width).astype(jnp.float32)
    grad_cross = grad_all[:, 0, :].reshape(rows, seg_count, model_width)
    grad_leaders, cross_factors, cross_smalls = block_backward(
        grad_cross, cross_kept, cross_weights, partial(cross_attend_back, allowed=allowed)
    )
    start = lax.axis_index("fsdp") * seg_count
    empty_pos = jnp.zeros((doc_ids.shape[1], model_width), jnp.float32)
    grad_pos = lax.dynamic_update_slice_in_dim(empty_pos, jnp.sum(grad_leaders, axis=0), start, 0)
    grad_seg = jnp.concatenate(
        [grad_leaders.reshape(rows * seg_count, 1, model_width), grad_all[:, 1:, :]], axis=1
    )
    grad_states, seg_factors, seg_smalls = block_backward(
        grad_seg, seg_kept, seg_weights, segment_attend_back
    )
    grad_tokens = grad_states.reshape(rows, local_len, model_width).astype(jnp.bfloat16)
    return (grad_tokens, seg_factors, cross_factors, seg_smalls, cross_smalls, grad_pos)


def body(tokens, doc_ids, pos_embed, w_qkv, w_out, w_in, w_back, norm_gain, norm_bias, cotangent):
    seg_weights = gather_segment(w_qkv, w_out, w_in, w_back, norm_gain, norm_bias)
    cross_weights, pos_full = gather_cross(
        pos_embed, w_qkv, w_out, w_in, w_back, norm_gain, norm_bias
    )
    output, kept = layer_forward(tokens, doc_ids, seg_weights, cross_weights, pos_full)
    grad_tokens, seg_factors, cross_factors, seg_smalls, cross_smalls, grad_pos = layer_backward(
        cotangent, doc_ids, kept, seg_weights, cross_weights
    )
    model_width = tokens.shape[2]
    hidden_width = w_in.shape[2]
    seg_term = lax.psum_scatter(
        weight_terms(seg_factors), ("dp", "fsdp"), scatter_dimension=0, tiled=True
    )
    cross_term = lax.psum_scatter(
        weight_terms(cross_factors), ("dp", "fsdp"), scatter_dimension=0, tiled=True
    )
    stacked = jnp.stack([seg_term, cross_term])
    grad_qkv = stacked[:, :, : 3 * model_width]
    grad_out = stacked[:, :, 3 * model_width : 4 * model_width]
    grad_in = stacked[:, :, 4 * model_width : 4 * model_width + hidden_width]
    grad_back = jnp.transpose(stacked[:, :, 4 * model_width + hidden_width :], (0, 2, 1))
    gain_all = jnp.stack([seg_smalls[0], cross_smalls[0]])
    bias_all = jnp.stack([seg_smalls[1], cross_smalls[1]])
    grad_gain, grad_bias, pos_shard = (
        lax.psum_scatter(gain_all, ("dp", "fsdp"), scatter_dimension=2, tiled=True),
        lax.psum_scatter(bias_all, ("dp", "fsdp"), scatter_dimension=2, tiled=True),
        lax.psum_scatter(grad_pos, ("dp", "fsdp"), scatter_dimension=1, tiled=True),
    )
    return (
        output,
        grad_tokens,
        pos_shard,
        grad_qkv,
        grad_out,
        grad_in,
        grad_back,
        grad_gain,
        grad_bias,
    )


def write_kernel(n, *refs):
    sources, smalls = refs[:n], refs[n]
    targets, pos_ref, gain_ref, bias_ref, sems = refs[n + 1 : 2 * n + 1], *refs[2 * n + 1 :]
    copies = [pltpu.make_async_copy(sources[i], targets[i], sems.at[i]) for i in range(n)]
    for copy in copies:
        copy.start()
    rows = smalls[:, :LANES].T[:, : smalls.shape[0]]
    pos_ref[...] = rows[8 : 8 + pos_ref.shape[0]]
    for b in range(2):
        gain_ref[b] = rows[4 * b : 4 * b + 2]
        bias_ref[b] = rows[4 * b + 2 : 4 * b + 4]
    for copy in copies:
        copy.wait()


def write_results(arrays, smalls, positions):
    n = len(arrays)
    own = smalls.shape[0]
    hbm, vm = pl.BlockSpec(memory_space=pl.ANY), pl.BlockSpec(memory_space=VM)
    like = [jax.ShapeDtypeStruct(v.shape, v.dtype) for v in arrays]
    shapes = [(positions, own), (2, 2, own), (2, 2, own)]
    return pl.pallas_call(
        partial(write_kernel, n),
        out_shape=like + [jax.ShapeDtypeStruct(v, f32) for v in shapes],
        in_specs=[vm] * (n + 1),
        out_specs=[hbm] * n + [vm] * 3,
        scratch_shapes=[pltpu.SemaphoreType.DMA((n,))],
    )(*arrays, smalls)


def fast_body(tokens, doc_ids, pos_embed, w_qkv, w_out, w_in, w_back, norm_gain, norm_bias, cotangent):
    nrows, local_len, width = tokens.shape
    rows = nrows * local_len
    x = tokens.reshape(rows, width)
    cot = cotangent.reshape(rows, width)
    output, grad_tokens, g_qkv, g_out, g_in, g_back, t_small = layer(
        w_qkv, w_out, w_in, jnp.swapaxes(w_back, 1, 2), norm_gain, norm_bias, pos_embed, doc_ids, x, cot
    )
    output, grad_tokens, g_qkv, g_out, g_in, g_back, grad_pos, grad_gain, grad_bias = write_results(
        (output, grad_tokens, g_qkv, g_out, g_in, g_back), t_small, doc_ids.shape[1]
    )
    return (
        output.reshape(tokens.shape),
        grad_tokens.reshape(tokens.shape),
        grad_pos,
        g_qkv,
        g_out,
        g_in,
        jnp.swapaxes(g_back, 1, 2),
        grad_gain,
        grad_bias,
    )


def solution(mesh):
    fast = dict(mesh.shape) == {"dp": 4, "fsdp": 8}
    return jax.shard_map(
        fast_body if fast else body,
        mesh=mesh,
        in_specs=(
            P("dp", "fsdp", None),
            P("dp", None),
            P(None, ("dp", "fsdp")),
            P(None, ("dp", "fsdp"), None),
            P(None, ("dp", "fsdp"), None),
            P(None, ("dp", "fsdp"), None),
            P(None, None, ("dp", "fsdp")),
            P(None, None, ("dp", "fsdp")),
            P(None, None, ("dp", "fsdp")),
            P("dp", "fsdp", None),
        ),
        out_specs=(
            P("dp", "fsdp", None),
            P("dp", "fsdp", None),
            P(None, ("dp", "fsdp")),
            P(None, ("dp", "fsdp"), None),
            P(None, ("dp", "fsdp"), None),
            P(None, ("dp", "fsdp"), None),
            P(None, None, ("dp", "fsdp")),
            P(None, None, ("dp", "fsdp")),
            P(None, None, ("dp", "fsdp")),
        ),
        check_vma=False,
    )
```

```python
from functools import partial

import jax
import jax.numpy as jnp
from jax import lax
from jax.experimental import pallas as pl
from jax.experimental.pallas import tpu as pltpu
from jax.sharding import PartitionSpec as P

HEADS = 12
SEG_LEN = 128


epsilon = 1e-05
root_half = 0.7071067811865476
inv_root_tau = 0.3989422804014327

bf16 = jnp.bfloat16
f32 = jnp.float32
MESH = pl.DeviceIdType.MESH
VM = pltpu.VMEM
MIB = 1024 * 1024
ROWS = 48
LANES = 128


class Place:
    def __init__(self):
        self.dp = lax.axis_index("dp")
        self.fsdp = lax.axis_index("fsdp")
        self.y, self.x = self.dp // 2, self.dp % 2
        self.z, self.core = self.fsdp // 2, self.fsdp % 2

    def at(self, dp, z, core):
        return (dp, z * 2 + core)

    @property
    def sib(self):
        return (self.dp, self.z * 2 + 1 - self.core)

    @property
    def xdp(self):
        return self.y * 2 + 1 - self.x

    @property
    def ydp(self):
        return (1 - self.y) * 2 + self.x

    @property
    def xnbr(self):
        return (self.xdp, self.fsdp)

    @property
    def ynbr(self):
        return (self.ydp, self.fsdp)


def greet(devices):
    barrier = pltpu.get_barrier_semaphore()
    for device in devices:
        pl.semaphore_signal(barrier, inc=1, device_id=device, device_id_type=MESH)
    pl.semaphore_wait(barrier, len(devices))


def remote(src, dst, send, recv, device):
    return pltpu.make_async_remote_copy(
        src_ref=src, dst_ref=dst, send_sem=send, recv_sem=recv, device_id=device, device_id_type=MESH
    )


def lanes(start, size):
    if isinstance(start, int):
        return pl.ds(start, size)
    return pl.ds(pl.multiple_of(start, LANES), size)


def rows_at(start, size, unit):
    return pl.ds(pl.multiple_of(start, unit), size)


class Gather:
    def __init__(self, place, out, off, width, source, index, sems, height2, wide_a=True):
        self.p, self.out, self.off, self.source = place, out, off, source
        self.m, self.sems, self.h2 = index, sems, height2
        self.half = width // 2
        tiles = self.half // LANES
        self.a = ((tiles + 1) // 2 if wide_a else max(tiles // 2, 1)) * LANES
        self.b = self.half - self.a
        self.sent = []
        self.far = (1 - place.y) * 2 + 1 - place.x

    def cols(self, core, part="AB"):
        at, size = {"A": (0, self.a), "B": (self.a, self.b), "AB": (0, self.half)}[part]
        return lanes(self.off + core * self.half + at, size)

    def block(self, z, core):
        return self.out.at[rows_at((self.p.dp * 4 + z) * self.h2, self.h2, 16), self.cols(core)]

    def group(self, dp, core, part="AB"):
        return self.out.at[rows_at(dp * 4 * self.h2, self.h2 * 4, 16), self.cols(core, part)]

    def go(self, src, dst, slot, device):
        copy = remote(src, dst, self.sems[0].at[self.m, slot], self.sems[1].at[self.m, slot], device)
        copy.start()
        self.sent.append(copy)

    def hand(self, ref, slot):
        self.go(ref, ref, slot, self.p.sib)

    def arrived(self, dst, slot):
        remote(dst, dst, self.sems[0].at[self.m, slot], self.sems[1].at[self.m, slot], self.p.sib).wait_recv()

    def own(self):
        p = self.p
        for d in (1, 3, 2):
            z = (p.z + d) % 4
            self.go(self.source(z), self.block(p.z, p.core), d - 1, p.at(p.dp, z, p.core))

    def line(self):
        p = self.p
        for d in (1, 3, 2):
            self.arrived(self.block((p.z + 4 - d) % 4, p.core), d - 1)
        mine = self.group(p.dp, p.core)
        self.go(mine, mine, 3, p.xnbr)
        self.go(mine, mine, 4, p.ynbr)
        self.hand(mine, 7)

    def plane(self):
        p = self.p
        over_x, over_y = self.group(p.xdp, p.core), self.group(p.ydp, p.core)
        self.arrived(over_x, 3)
        part = self.group(p.xdp, p.core, "A")
        self.go(part, part, 5, p.ynbr)
        self.arrived(over_y, 4)
        if self.b:
            part = self.group(p.ydp, p.core, "B")
            self.go(part, part, 6, p.xnbr)
        self.hand(over_x, 8)
        self.hand(over_y, 9)

    def last(self):
        p = self.p
        self.arrived(self.group(self.far, p.core, "A"), 5)
        if self.b:
            self.arrived(self.group(self.far, p.core, "B"), 6)
        self.hand(self.group(self.far, p.core), 10)

    def drain(self):
        p = self.p
        for slot, dp in ((7, p.dp), (8, p.xdp), (9, p.ydp), (10, self.far)):
            self.arrived(self.group(dp, 1 - p.core), slot)

    def finish(self):
        for copy in self.sent:
            copy.wait_send()


class Staged:
    def __init__(self, units, order):
        self.units, self.order, self.at = units, order, 0

    def step(self, count=1):
        for name, i in self.order[self.at : self.at + count]:
            getattr(self.units[i], name)()
        self.at += count

    def upto(self, name, i):
        spot = self.order.index((name, i)) + 1
        if spot > self.at:
            self.step(spot - self.at)

    def finish(self):
        self.step(len(self.order) - self.at)
        for unit in self.units:
            unit.finish()


def staggered(count, lags, first=0):
    order = []
    for t in range(min(lags.values()), count + max(lags.values())):
        for name, lag in lags.items():
            if 0 <= t - lag < count and (t >= 0 or lag < 0):
                order.append((name, t - lag + first))
    return order


def gather_peers(p):
    peers = [p.sib, p.xnbr, p.ynbr]
    for d in (1, 2, 3):
        peers.append(p.at(p.dp, (p.z + d) % 4, p.core))
    return peers


def everyone(p):
    return [
        (lax.rem(p.dp + i, 4), lax.rem(p.fsdp + j, 8)) for i in range(4) for j in range(8) if i or j
    ]


NEG = -1e30


def mm(a, b, dims):
    return lax.dot_general(a, b, (dims, ((), ())), preferred_element_type=f32)


NN = ((1,), (0,))
NT = ((1,), (1,))
TN = ((0,), (0,))


def norm_rows(summed, gain, bias):
    centred = summed - jnp.mean(summed, axis=-1, keepdims=True)
    variance = jnp.mean(centred * centred, axis=-1, keepdims=True)
    inverse = lax.rsqrt(variance + epsilon)
    scaled = centred * inverse
    return scaled * gain + bias, scaled, inverse


def norm_rows_back(grad, scaled, inverse, gain):
    g = grad * gain
    first = jnp.mean(g, axis=-1, keepdims=True)
    second = jnp.mean(g * scaled, axis=-1, keepdims=True)
    return inverse * (g - first - scaled * second)


def gelu_parts(u):
    cumulative = 0.5 * (1.0 + lax.erf(u * root_half))
    return cumulative, cumulative + u * inv_root_tau * jnp.exp(-0.5 * u * u)


def lane_halves(v):
    low = lax.broadcasted_iota(jnp.int32, v.shape, 1) < LANES // 2
    zero = jnp.zeros_like(v)
    return jnp.where(low, v, zero), jnp.where(low, zero, v)


FORWARD_LAGS = {"own": -3, "line": 0, "plane": 1, "last": 2, "drain": 3}


def forward_order(n_seg, n_cross):
    n = n_seg + n_cross
    order = staggered(n, FORWARD_LAGS)
    stop = order.index(("line", n_seg))
    head, rest = order[:stop], order[stop:]
    head += [s for s in rest if s[0] == "own"]
    done = set(head)
    tail = [("plane", n_seg - 1), ("line", n_seg), ("line", n_seg + 1)]
    for u in range(n_seg - 3, n_seg):
        tail += [("last", u), ("drain", u)]
    tail += [("plane", n_seg), ("line", n_seg + 2)]
    for u in range(n_seg, n):
        tail += [("last", u), ("plane", u + 1), ("drain", u)]
    return head + [s for s in tail if s not in done and s[1] < n]


class Scatter:
    def __init__(self, place, grad, off, width, out, index, sems, bufs, wide_a=True):
        self.p, self.grad, self.off, self.out, self.m = place, grad, off, out, index
        self.send, self.recv = sems
        self.pair, self.r1a, self.r1b, self.rx, self.ry, self.r3, self.give = bufs
        self.half = width // 2
        self.a = split_half(width, wide_a)
        self.b = self.half - self.a
        self.sent = []
        self.free, self.waits, self.frees = None, False, False
        p = place
        self.far = (1 - p.y) * 2 + 1 - p.x
        self.groups = (self.far, p.xdp, p.ydp, p.dp)

    def go(self, src, dst, slot, device):
        copy = remote(src, dst, self.send.at[self.m, slot], self.recv.at[self.m, slot], device)
        copy.start()
        self.sent.append(copy)

    def arrived(self, dst, slot):
        remote(dst, dst, self.send.at[self.m, slot], self.recv.at[self.m, slot], self.p.sib).wait_recv()

    def cols(self, part="AB", core=None):
        at, size = {"A": (0, self.a), "B": (self.a, self.b), "AB": (0, self.half)}[part]
        core = self.p.core if core is None else core
        return lanes(self.off + core * self.half + at, size)

    def group(self, dp):
        return rows_at(dp * 4 * ROWS, 4 * ROWS, 16)

    def side(self, dp, part="AB"):
        return self.grad.at[self.group(dp), self.cols(part)]

    def start(self):
        p = self.p
        if self.waits:
            pl.semaphore_wait(self.free, 1)
        for i, dp in enumerate(self.groups):
            theirs = self.grad.at[self.group(dp), self.cols("AB", 1 - p.core)]
            self.go(theirs, self.pair.at[self.group(dp)], i, p.sib)

    def add(self, dp, part, other, other_row=0):
        @pl.loop(0, 4)
        def _(i):
            key = (rows_at(dp * 4 * ROWS + i * ROWS, ROWS, 16), self.cols(part))
            self.grad[key] = self.grad[key] + other[rows_at(other_row + i * ROWS, ROWS, 16), :]

    def one(self):
        p = self.p
        for i, dp in enumerate(self.groups):
            self.arrived(self.pair.at[self.group(dp)], i)
            self.add(dp, "AB", self.pair, dp * 4 * ROWS)
            if i == 0:
                self.go(self.side(dp, "A"), self.r1a, 4, p.ynbr)
                if self.b:
                    self.go(self.side(dp, "B"), self.r1b, 5, p.xnbr)
        if self.frees:
            pl.semaphore_signal(self.free, inc=1, device_id=p.sib, device_id_type=MESH)

    def two(self):
        p = self.p
        self.arrived(self.r1a, 4)
        self.add(p.xdp, "A", self.r1a)
        self.go(self.side(p.xdp), self.rx, 6, p.xnbr)
        if self.b:
            self.arrived(self.r1b, 5)
            self.add(p.ydp, "B", self.r1b)
        self.go(self.side(p.ydp), self.ry, 7, p.ynbr)

    def three(self):
        p = self.p
        self.arrived(self.rx, 6)
        self.arrived(self.ry, 7)

        @pl.loop(0, 4)
        def _(i):
            key = (rows_at(p.dp * 4 * ROWS + i * ROWS, ROWS, 16), self.cols())
            own = rows_at(i * ROWS, ROWS, 16)
            self.grad[key] = self.grad[key] + (self.rx[own, :] + self.ry[own, :])

        for d in (1, 3, 2):
            z = (p.z + d) % 4
            src = self.grad.at[rows_at((p.dp * 4 + z) * ROWS, ROWS, 16), self.cols()]
            self.go(src, self.r3.at[d - 1], 7 + d, p.at(p.dp, z, p.core))

    def four(self):
        p = self.p
        for d in (1, 3, 2):
            self.arrived(self.r3.at[d - 1], 7 + d)
        rows = rows_at((p.dp * 4 + p.z) * ROWS, ROWS, 16)
        total = self.grad[rows, self.cols()].astype(f32)
        for d in range(3):
            total = total + self.r3[d].astype(f32)
        upper, lower = total[: ROWS // 2], total[ROWS // 2 :]
        first = p.core == 0
        self.give[...] = jnp.where(first, lower, upper)
        self.out[:, self.cols()] = jnp.where(first, upper, lower)
        self.go(self.give, self.out.at[:, self.cols()], 11, p.sib)

    def five(self):
        self.arrived(self.out.at[:, self.cols("AB", 1 - self.p.core)], 11)

    def finish(self):
        for copy in self.sent:
            copy.wait_send()


def split_half(width, wide_a):
    tiles = width // 2 // LANES
    return ((tiles + 1) // 2 if wide_a else max(tiles // 2, 1)) * LANES


def scatter_buffers(width, wide_a):
    half = width // 2
    a = split_half(width, wide_a)
    b = half - a
    return [
        VM((4 * ROWS, a), bf16),
        VM((4 * ROWS if b else 16, max(b, LANES)), bf16),
        VM((4 * ROWS, half), bf16),
        VM((4 * ROWS, half), bf16),
        VM((3, ROWS, half), bf16),
        VM((ROWS // 2, half), f32),
    ]


SCATTER_LAGS = {"start": 0, "one": 1, "two": 2, "three": 4, "four": 7, "five": 9}
PAIR_SLOTS = 4


def tail_units(width):
    return [(0, width), (width, width), (2 * width, width - 256), (3 * width - 256, 256)]


def scatter_step(sums, jobs):
    begun = len([s for s in sums.order[: sums.at] if s[0] == "start"])
    follow = [i for i, s in enumerate(sums.order) if s == ("start", begun + 1)]
    if begun < len(jobs):
        sums.step((follow[0] if follow else sums.order.index(("start", begun)) + 1) - sums.at)


def layer_kernel(*refs):
    wq_ref, wo_ref, wi_ref, wb_ref, gain_ref, bias_ref, pos_ref, docs_ref, x_ref, cot_ref = refs[:10]
    y_ref, gt_ref, gq_ref, go_ref, gi_ref, gb_ref, gs_ref = refs[10:17]
    (
        sw, ow, qw, iw, bw, cw, cwo,
        pk, at, cx, h, nl, g, sl, z1, z2, r1_ref, r2_ref, par_ref,
        own_buf, sib_buf, block, square,
        lead_out, gbuf, lead, xbuf, ybuf, dpack, home_y, home_dx, dbuf, dland, fac, fac_sib, csmall,
        df, tr, tr2, dws, small, full, tmp, ring, pair_wide, pair_small,
        s_send, s_recv, pair_send, pair_recv, wo_send, wo_recv, local,
        g_send, g_recv, x_send, x_recv, h_send, h_recv, lead_sem, d_send, d_recv,
        f_send, f_recv, swap_send, swap_recv, rs_send, rs_recv, free,
    ) = refs[17:86]
    bufs = refs[86:]
    p = Place()
    rows, width = x_ref.shape
    segs = rows // SEG_LEN
    hidden = iw.shape[1]
    pairs = width // LANES
    slab = width // 4
    cross_width = cw.shape[1]
    half_rows = ROWS // 2
    key_own = rows_at((p.dp * 4 + p.z) * ROWS, ROWS, 16)

    sizes = [sw.shape[1]] + [width] * (3 + 1 + 2 * (hidden // width)) + [4 * cross_width, width]
    starts = [sum(sizes[:i]) for i in range(len(sizes))]
    n_seg = len(sizes) - 2
    part_cross, part_wo = n_seg, n_seg + 1

    def put(start, value):
        zero = jnp.zeros((own_buf.shape[0] - half_rows, value.shape[1]), f32)
        full = jnp.concatenate([value.astype(f32), zero], axis=0).astype(bf16)
        own_buf[:, pl.ds(start, value.shape[1])] = full

    def pair(i):
        cols = pl.ds(starts[i], sizes[i])
        return remote(
            own_buf.at[:, cols], sib_buf.at[:, cols], pair_send.at[i], pair_recv.at[i], p.sib
        )

    def stage(i):
        spot = starts[i]
        per = hidden // width
        if i == 0:
            own = gain_ref.shape[2]
            square[...] = jnp.zeros_like(square)
            for b in range(2):
                square[4 * b : 4 * b + 2, :own] = gain_ref[b].astype(f32)
                square[4 * b + 2 : 4 * b + 4, :own] = bias_ref[b].astype(f32)
            square[8 : 8 + pos_ref.shape[0], :own] = pos_ref[...].astype(f32)
            turned = square[...].T[:half_rows]
            put(spot, jnp.concatenate([turned, jnp.zeros_like(turned)], axis=1))
        elif i < 4:
            put(spot, wq_ref[0, :, (i - 1) * width : i * width])
        elif i == 4:
            put(spot, wo_ref[0])
        elif i < 5 + per:
            put(spot, wi_ref[0, :, (i - 5) * width : (i - 4) * width])
        elif i < 5 + 2 * per:
            put(spot, wb_ref[0, :, (i - 5 - per) * width : (i - 4 - per) * width])
        elif i == part_cross:
            for z in range(4):
                heads = [wq_ref[1, :, j * width + z * slab : j * width + (z + 1) * slab] for j in range(3)]
                heads.append(heads[2])
                put(spot, jnp.concatenate([v.astype(f32) for v in heads], axis=1).astype(bf16))
                put(spot + width, wi_ref[1, :, z * width : (z + 1) * width])
                put(spot + 2 * width, wb_ref[1, :, z * width : (z + 1) * width])
                spot += cross_width
        else:
            put(spot, wo_ref[1])

    def joined(start, size):
        cols = lanes(start, size)
        first = p.core == 0
        mine = own_buf[:, cols].astype(f32)[:half_rows]
        theirs = sib_buf[:, cols].astype(f32)[:half_rows]
        both = [jnp.where(first, mine, theirs), jnp.where(first, theirs, mine)]
        return jnp.concatenate(both, axis=0).astype(bf16)

    ahead = 4

    def begin(i):
        if i < n_seg + 2:
            stage(i)
            pair(i).start()

    stage(0)
    greet(everyone(p))
    pair(0).start()
    for i in range(1, ahead):
        begin(i)

    sems = (s_send, s_recv)
    dests = [(sw, 0)] + [(qw, i * width) for i in range(3)] + [(ow, 0)]
    dests += [(iw, i * width) for i in range(hidden // width)]
    dests += [(bw, i * width) for i in range(hidden // width)]

    class SegUnit(Gather):
        def __init__(self, i):
            dst, off = dests[i]
            mine = lambda z: dst.at[key_own, self.cols(p.core)]
            super().__init__(p, dst, off, sizes[i], mine, i, sems, ROWS, i % 2 == 0)
            self.i = i

        def own(self):
            pair(self.i).wait_recv()
            self.out[key_own, self.cols(p.core)] = joined(
                starts[self.i] + p.core * self.half, self.half
            )
            super().own()
            begin(self.i + ahead)

    class CrossUnit(Gather):
        def __init__(self, i):
            start = i * width
            self.i = i

            def mine(z):
                spot = z * cross_width + start + p.core * self.half
                return block.at[:, lanes(spot, self.half)]

            super().__init__(p, cw, start, width, mine, n_seg + i, sems, ROWS, i % 2 == 0)

        def own(self):
            if self.i == 0:
                pair(part_cross).wait_recv()

                @pl.loop(0, 4 * cross_width // width)
                def _(k):
                    block[:, lanes(k * width, width)] = joined(starts[part_cross] + k * width, width)

            spot = p.z * cross_width + self.i * width + p.core * self.half
            self.out[key_own, self.cols(p.core)] = block[:, lanes(spot, self.half)]
            super().own()

    units = [SegUnit(i) for i in range(n_seg)] + [CrossUnit(i) for i in range(cross_width // width)]
    n_cross = len(units) - n_seg
    comm = Staged(units, forward_order(n_seg, n_cross))

    def need(i):
        comm.upto("drain", i)

    def pump():
        comm.step(5)

    half_wo = width // 2
    wo_block = block.at[:, pl.ds(4 * cross_width, width)]
    wo_src = block.at[:, lanes(4 * cross_width + p.core * half_wo, half_wo)]
    wo_dst = cwo.at[rows_at(p.z * ROWS, ROWS, 16), lanes(p.core * half_wo, half_wo)]

    def wo_copy(i):
        return remote(wo_src, wo_dst, wo_send.at[i], wo_recv.at[p.z], p.at(i, p.dp, p.core))

    def wo_start():
        pair(part_wo).wait_recv()
        wo_block[...] = joined(starts[part_wo], width)
        for i in range(4):
            here = jnp.logical_and(p.dp == i, p.dp == p.z)

            @pl.when(jnp.logical_not(here))
            def _():
                wo_copy(i).start()

            @pl.when(here)
            def _():
                mine = pltpu.make_async_copy(wo_src, wo_dst, local)
                mine.start()
                mine.wait()

    wo_mine = cwo.at[:, lanes(p.core * half_wo, half_wo)]
    wo_theirs = cwo.at[:, lanes((1 - p.core) * half_wo, half_wo)]
    wo_hand = remote(wo_mine, wo_mine, wo_send.at[4], wo_recv.at[4], p.sib)

    def wo_middle():
        for i in range(4):
            piece = cwo.at[pl.ds(i * ROWS, ROWS), lanes(p.core * half_wo, half_wo)]

            @pl.when(jnp.logical_not(jnp.logical_and(p.z == p.dp, p.z == i)))
            def _():
                remote(piece, piece, wo_send.at[i], wo_recv.at[i], p.sib).wait_recv()

        wo_hand.start()

    def wo_finish():
        remote(wo_theirs, wo_theirs, wo_send.at[4], wo_recv.at[4], p.sib).wait_recv()
        wo_hand.wait_send()
        for i in range(4):

            @pl.when(jnp.logical_not(jnp.logical_and(p.dp == i, p.dp == p.z)))
            def _():
                wo_copy(i).wait_send()

    tile = 256

    def params():
        par_ref[...] = sw[...].astype(f32).T[: par_ref.shape[0]]

    def project(first, count):
        @pl.loop(first, first + count)
        def _(i):
            cols = lanes(i * tile, tile)
            pk[:, cols] = mm(x_ref[...], qw[:, cols], NN).astype(bf16)

    def attend(s):
        key = pl.ds(s * SEG_LEN, SEG_LEN)

        @pl.loop(0, pairs, unroll=True)
        def _(j):
            q2 = pk[key, lanes(j * LANES, LANES)]
            k2 = pk[key, lanes(width + j * LANES, LANES)]
            v2 = pk[key, lanes(2 * width + j * LANES, LANES)]
            scores = mm(jnp.concatenate(lane_halves(q2), axis=0), k2, NT) * (LANES // 2) ** (-0.5)
            top = jnp.max(scores, axis=-1, keepdims=True)
            terms = jnp.exp(scores - top)
            a = (terms / jnp.sum(terms, axis=-1, keepdims=True)).astype(bf16)
            at[rows_at((s * pairs + j) * 2 * SEG_LEN, 2 * SEG_LEN, 16), :] = a
            both = jnp.concatenate([a[:SEG_LEN], a[SEG_LEN:]], axis=1)
            c2 = mm(both, jnp.concatenate(lane_halves(v2), axis=0), NN)
            cx[key, lanes(j * LANES, LANES)] = c2.astype(bf16)

    block_rows = 64

    def branch():
        @pl.loop(0, width // tile)
        def _(i):
            cols = lanes(i * tile, tile)
            h[:, cols] = x_ref[:, cols].astype(f32) + mm(cx[...], ow[:, cols], NN)

        @pl.loop(0, rows // block_rows, unroll=2)
        def _(i):
            key = rows_at(i * block_rows, block_rows, 16)
            normed, scaled, inverse = norm_rows(h[key, :], par_ref[0:1, :], par_ref[2:3, :])
            h[key, :] = normed
            nl[key, :] = normed.astype(bf16)
            z1[key, :] = scaled.astype(bf16)
            r1_ref[key, :] = jnp.broadcast_to(inverse, (block_rows, LANES))

    def feed_in(first, count):
        @pl.loop(first, first + count)
        def _(i):
            cols = lanes(i * tile, tile)
            u = mm(nl[...], iw[:, cols], NN)
            phi, slope = gelu_parts(u)
            g[:, cols] = (u * phi).astype(bf16)
            sl[:, cols] = slope.astype(bf16)

    def feed_back(part):
        inner = pl.ds(part * width, width)

        @pl.loop(0, width // tile)
        def _(i):
            cols = lanes(i * tile, tile)
            h[:, cols] += mm(g[:, inner], bw[rows_at(i * tile, tile, 16), inner], NT)

    def finish_block():
        @pl.loop(0, rows // block_rows, unroll=2)
        def _(i):
            key = rows_at(i * block_rows, block_rows, 16)
            result, scaled, inverse = norm_rows(h[key, :], par_ref[1:2, :], par_ref[3:4, :])
            h[key, :] = result
            y_ref[key, :] = result.astype(bf16)
            z2[key, :] = scaled.astype(bf16)
            r2_ref[key, :] = jnp.broadcast_to(inverse, (block_rows, LANES))

    def leaders():
        first = [h[s * SEG_LEN : s * SEG_LEN + 1, :] for s in range(segs)]
        result = norm_rows(jnp.concatenate(first, axis=0), par_ref[1:2, :], par_ref[3:4, :])[0]
        for s in range(segs):
            pos = par_ref[pl.ds(8 + p.fsdp * 2 + s % 2, 1), :]
            lead_out[s // 2, s % 2 : s % 2 + 1, :width] = result[s : s + 1] + pos
            lead_out[s // 2, s % 2 : s % 2 + 1, width:] = cot_ref[s * SEG_LEN : s * SEG_LEN + 16, :].astype(f32)[:1]

    def lead_copy(z, j):
        i = 2 * z + j
        return remote(lead_out.at[j], gbuf.at[p.fsdp], g_send.at[i], g_recv.at[p.fsdp], (p.dp, i))


    leads = fac.shape[0]
    lead2 = 2 * leads
    key_f = rows_at((p.dp * 4 + p.z) * lead2, lead2, 16)

    def swap(i):
        cols = pl.ds(i * width, width)
        return remote(fac.at[:, cols], fac_sib.at[:, cols], swap_send.at[i], swap_recv.at[i], p.sib)

    def give_factor(i, value):
        fac[:, i * width : (i + 1) * width] = value
        swap(i).start()

    class Factor(Gather):
        def __init__(self, i):
            mine = lambda z: full.at[key_f, self.cols(p.core)]
            super().__init__(p, full, i * width, width, mine, i, (f_send, f_recv), lead2, i % 2 == 0)
            self.i = i

        def own(self):
            swap(self.i).wait_recv()
            base = (p.dp * 4 + p.z) * lead2
            cols = lanes(self.i * width + p.core * (width // 2), width // 2)
            full[rows_at(base + p.core * leads, leads, 16), cols] = fac[:, cols]
            full[rows_at(base + (1 - p.core) * leads, leads, 16), cols] = fac_sib[:, cols]
            super().own()

    factors = [Factor(i) for i in range(4)]

    def factor_grads():
        def rows_of(z, at_col, size):
            return jnp.concatenate(
                [full[rows_at((i * 4 + z) * lead2, lead2, 16), pl.ds(at_col, size)] for i in range(4)],
                axis=0,
            )

        base = 2 * width
        own = rows_at(p.fsdp * (ROWS // 2), ROWS // 2, 8)
        xl = rows_of(p.dp, base, slab)
        nlf = rows_of(p.dp, base + slab, slab)
        dff = rows_of(p.dp, base + 2 * slab, slab)
        ctx = rows_of(p.dp, base + 3 * slab, slab)
        for z in range(4):
            tmp[:, :width] = mm(dff, rows_of(z, 0, width), TN)
            gb_ref[1, :, z * width : (z + 1) * width] = tmp[own, :width]
            tmp[:, :width] = mm(nlf, rows_of(z, width, width), TN)
            gi_ref[1, :, z * width : (z + 1) * width] = tmp[own, :width]
            tmp[:, : 3 * slab] = mm(xl, rows_of(z, 3 * width, 3 * slab), TN)
            got = tmp[own, : 3 * slab]
            for j in range(3):
                spot = j * width + z * slab
                gq_ref[1, :, spot : spot + slab] = got[:, j * slab : (j + 1) * slab]
            tmp[:, :slab] = mm(ctx, rows_of(z, 3 * width + 3 * slab, slab), TN)
            go_ref[1, :, z * slab : (z + 1) * slab] = tmp[own, :slab]


    n_tiles = width // tile
    head = width // HEADS
    heads = HEADS // 4

    def cross():
        for d in range(4):
            z = (p.z + d) % 4
            for j in range(2):
                if d:
                    lead_copy(z, j).start()
                else:

                    @pl.when(p.core != j)
                    def _():
                        lead_copy(z, j).start()

                    @pl.when(p.core == j)
                    def _():
                        mine = pltpu.make_async_copy(lead_out.at[j], gbuf.at[p.fsdp], lead_sem)
                        mine.start()
                        mine.wait()

        comm.upto("plane", n_seg)
        comm.upto("line", n_seg + 2)
        finish_block()
        need(n_seg)
        wo_middle()
        for d in range(1, 8):
            i = lax.rem(p.fsdp + d, 8)
            remote(gbuf.at[i], gbuf.at[i], g_send.at[i], g_recv.at[i], p.sib).wait_recv()
        for i in range(8):
            lead[2 * i : 2 * i + 2, :] = gbuf[i]
        states = lead[:, :width]
        cot_rows = lead[:, width:]

        def sum_z(e, partial_sum, between):
            xbuf[e, p.z] = partial_sum.astype(bf16)
            copies = []
            for d in (1, 3, 2):
                z = (p.z + d) % 4
                copy = remote(
                    xbuf.at[e, p.z], xbuf.at[e, p.z], x_send.at[e, d - 1], x_recv.at[e, p.z],
                    p.at(p.dp, z, p.core),
                )
                copy.start()
                copies.append(copy)
            between()
            for d in (1, 3, 2):
                z = (p.z + d) % 4
                piece = xbuf.at[e, z]
                remote(piece, piece, x_send.at[e, d - 1], x_recv.at[e, z], p.sib).wait_recv()
            for copy in copies:
                copy.wait_send()
            return sum(xbuf[e, z].astype(f32) for z in range(4))

        gain0, gain1 = par_ref[4:5, :], par_ref[5:6, :]
        bias0, bias1 = par_ref[6:7, :], par_ref[7:8, :]
        in_cols, back_cols = pl.ds(width, width), pl.ds(2 * width, width)
        qkv_cols = pl.ds(0, 3 * slab)
        factor = head ** (-0.5)
        docs = docs_ref[...].astype(f32)
        number = docs.shape[1]
        square[:number, :number] = jnp.broadcast_to(
            jnp.where(p.core == 0, docs[0:1], docs[1:2]), (number, number)
        )
        allowed = square[:number, :number] == square[...].T[:number, :number]

        def part(full):
            pieces = [full[:, i * slab : (i + 1) * slab] for i in range(4)]
            out = pieces[0]
            for i in range(1, 4):
                out = jnp.where(p.z == i, pieces[i], out)
            return out.astype(bf16)

        xl = states.astype(bf16)
        packed = mm(xl, cw[:, qkv_cols], NN).astype(bf16)
        q = [packed[:, i * head : (i + 1) * head] for i in range(heads)]
        k = [packed[:, slab + i * head : slab + (i + 1) * head] for i in range(heads)]
        v = [packed[:, 2 * slab + i * head : 2 * slab + (i + 1) * head] for i in range(heads)]
        att, context = [], []
        for i in range(heads):
            scores = jnp.where(allowed, mm(q[i], k[i], NT) * factor, NEG)
            top = jnp.max(scores, axis=-1, keepdims=True)
            terms = jnp.exp(scores - top)
            a = terms / jnp.sum(terms, axis=-1, keepdims=True)
            att.append(a)
            context.append(mm(a.astype(bf16), v[i], NN))
        context = jnp.concatenate(context, axis=1).astype(bf16)
        wo_finish()
        branch = sum_z(0, mm(context, cwo[...], NN), norm_two)
        normed, z_one, r_one = norm_rows(states + branch, gain0, bias0)
        nl = normed.astype(bf16)
        need(n_seg + 1)
        hidden = mm(nl, cw[:, in_cols], NN)
        phi, slope = gelu_parts(hidden)
        active = (hidden * phi).astype(bf16)
        give_factor(0, active)
        need(n_seg + 2)

        def during_one():
            factors[0].own()

        feed = sum_z(1, mm(active, cw[:, back_cols], NT), during_one)
        result, z_two, r_two = norm_rows(normed + feed, gain1, bias1)
        d_two = norm_rows_back(cot_rows, z_two, r_two, gain1)
        df = d_two.astype(bf16)
        du = (mm(df, cw[:, back_cols], NN) * slope).astype(bf16)
        give_factor(1, du)
        give_factor(2, jnp.concatenate([part(states), part(normed), part(d_two), context], axis=1))

        for i in range(8):
            ybuf[i] = result[2 * i : 2 * i + 2]
        home = remote(ybuf.at[2 * p.z + 1 - p.core], home_y.at[p.core], h_send, h_recv, p.sib)

        def during_two():
            home.start()
            home_y[p.core] = ybuf[2 * p.z + p.core]
            factors[0].line()
            factors[1].own()
            factors[2].own()

        d_normed = d_two + sum_z(2, mm(du, cw[:, in_cols], NT), during_two)
        d_one = norm_rows_back(d_normed, z_one, r_one, gain0)
        db = d_one.astype(bf16)
        dc = mm(db, cwo[...], NT).astype(bf16)
        for i in range(heads):
            a = att[i]
            dci = dc[:, i * head : (i + 1) * head]
            da = mm(dci, v[i], NT)
            dv = mm(a.astype(bf16), dci, TN)
            ds = (a * (da - jnp.sum(a * da, axis=-1, keepdims=True))).astype(bf16)
            dq = mm(ds, k[i], NN) * factor
            dk = mm(ds, q[i], TN) * factor
            for j, piece in enumerate((dq, dk, dv)):
                dpack[:, j * slab + i * head : j * slab + (i + 1) * head] = piece
        dp = dpack[...].astype(bf16)
        give_factor(3, jnp.concatenate([dp, part(d_one)], axis=1))

        def during_three():
            factors[0].plane()
            factors[1].line()
            factors[3].own()
            factors[2].line()

        partial_dx = mm(dp, cw[:, qkv_cols], NT)
        for i in range(8):
            mine = jnp.where(p.z == i // 2, 1.0, 0.0) * d_one[2 * i : 2 * i + 2]
            dbuf[i] = partial_dx[2 * i : 2 * i + 2] + mine
        sent = []
        for d in range(1, 8):
            i = lax.rem(p.fsdp + d, 8)
            copy = remote(dbuf.at[i], dland.at[p.fsdp], d_send.at[d], d_recv.at[p.fsdp], (p.dp, i))
            copy.start()
            sent.append(copy)
        during_three()
        dland[p.fsdp] = dbuf[p.fsdp]
        for d in range(1, 8):
            i = lax.rem(p.fsdp + d, 8)
            remote(dland.at[i], dland.at[i], d_send.at[d], d_recv.at[i], p.sib).wait_recv()
        for j in range(2):
            home_dx[j] = (dland[j] + dland[2 + j]) + (dland[4 + j] + dland[6 + j])
        for copy in sent:
            copy.wait_send()
        once = jnp.where(p.z == 0, 1.0, 0.0)
        sums_of = [d_normed * z_one, cot_rows * z_two, d_normed, cot_rows]
        csmall[...] = jnp.zeros_like(csmall)
        for i, s in enumerate(sums_of):
            csmall[i : i + 1, :] = once * jnp.sum(s, axis=0, keepdims=True)
        theirs = home_y.at[1 - p.core]
        remote(theirs, theirs, h_send, h_recv, p.sib).wait_recv()
        home.wait_send()

    def wait_leads():
        for d in range(4):
            z = (p.z + d) % 4
            for j in range(2):
                if d:
                    lead_copy(z, j).wait_send()
                else:

                    @pl.when(p.core != j)
                    def _():
                        lead_copy(z, j).wait_send()


    def patch():
        for s in range(segs):
            spot = pl.ds(s * SEG_LEN, 16)
            old = y_ref[spot, :].astype(f32)
            new = jnp.broadcast_to(home_y[s // 2, s % 2 : s % 2 + 1, :], old.shape)
            top = lax.broadcasted_iota(jnp.int32, old.shape, 0) == 0
            y_ref[spot, :] = jnp.where(top, new, old).astype(bf16)
    per = hidden // width
    parts = [(bw, i * width, width, gb_ref.at[0]) for i in range(per)]
    parts += [(iw, i * width, width, gi_ref.at[0]) for i in range(per)]
    parts += [(ow, 0, width, go_ref.at[0]), (dws, 0, dws.shape[1], gs_ref)]
    parts += [(qw, at_col, size, gq_ref.at[0]) for at_col, size in tail_units(width)]
    jobs, shared = [], []
    for i, (grad, off, size, dst) in enumerate(parts):
        job_bufs = list(bufs[6 * i : 6 * i + 6])
        if size == width:
            slot = len(shared) % PAIR_SLOTS
            job = Scatter(p, grad, off, size, dst, i, (rs_send, rs_recv), [ring.at[slot]] + job_bufs, i % 2 == 0)
            job.free = free.at[slot]
            if len(shared) >= PAIR_SLOTS:
                job.waits = True
                shared[len(shared) - PAIR_SLOTS].frees = True
            shared.append(job)
        else:
            own_pair = pair_wide if size > 256 else pair_small.at[len([j for j in jobs if j.half == LANES])]
            job = Scatter(p, grad, off, size, dst, i, (rs_send, rs_recv), [own_pair] + job_bufs, i % 2 == 0)
        jobs.append(job)
    sums = Staged(jobs, staggered(len(jobs), SCATTER_LAGS))


    def norm_back(z_ref, r_ref, gain_row, low_ref, sums):
        def step(i, acc):
            key = rows_at(i * block_rows, block_rows, 16)
            dy = h[key, :]
            z = z_ref[key, :].astype(f32)
            r = jnp.concatenate([r_ref[key, :]] * (width // LANES), axis=1)
            e = dy * par_ref[gain_row : gain_row + 1, :]
            first = jnp.mean(e, axis=-1, keepdims=True)
            second = jnp.mean(e * z, axis=-1, keepdims=True)
            d = r * (e - first - z * second)
            h[key, :] = d
            low_ref[key, :] = d.astype(bf16)
            fold = lambda v: jnp.sum(v.reshape(block_rows // 8, 8, width), axis=0)
            return acc[0] + fold(dy * z), acc[1] + fold(dy)

        zero = jnp.zeros((8, width), f32)
        gain, bias = lax.fori_loop(0, rows // block_rows, step, (zero, zero), unroll=2)
        small[sums : sums + 1, :] = jnp.sum(gain, axis=0, keepdims=True)
        small[sums + 2 : sums + 3, :] = jnp.sum(bias, axis=0, keepdims=True)

    def turn(tr, ref):
        @pl.loop(0, width // tile)
        def _(i):
            tr[rows_at(i * tile, tile, 16), :] = ref[:, lanes(i * tile, tile)].T

    def outer(dst, tr, src, first, size):
        @pl.loop(first // tile, (first + size) // tile)
        def _(i):
            cols = lanes(i * tile, tile)
            dst[:, cols] = mm(tr[...], src[:, cols], NN).astype(bf16)

    def norm_two():
        @pl.loop(0, rows // block_rows)
        def _(i):
            key = rows_at(i * block_rows, block_rows, 16)
            h[key, :] = cot_ref[key, :].astype(f32)

        for s in range(segs):
            h[s * SEG_LEN : s * SEG_LEN + 1, :] = jnp.zeros((1, width), f32)
        small[...] = jnp.zeros_like(small)
        norm_back(z2, r2_ref, 1, df, 1)

    def norm_leaders():
        pick = lambda take: jnp.concatenate([take(s * SEG_LEN) for s in range(segs)], axis=0)
        dy = jnp.concatenate([home_dx[s // 2, s % 2 : s % 2 + 1, :] for s in range(segs)], axis=0)
        z = pick(lambda row: z2[row : row + 16, :].astype(f32)[:1])
        r = pick(lambda row: jnp.concatenate([r2_ref[row : row + 1, :]] * (width // LANES), axis=1))
        d = norm_rows_back(dy, z, r, par_ref[1:2, :])
        for s in range(segs):
            h[s * SEG_LEN : s * SEG_LEN + 1, :] = d[s : s + 1]
            spot = pl.ds(s * SEG_LEN, 16)
            old = df[spot, :].astype(f32)
            top = lax.broadcasted_iota(jnp.int32, old.shape, 0) == 0
            df[spot, :] = jnp.where(top, jnp.broadcast_to(d[s : s + 1], old.shape), old).astype(bf16)
        small[1:2, :] += jnp.sum(dy * z, axis=0, keepdims=True)
        small[3:4, :] += jnp.sum(dy, axis=0, keepdims=True)
        small[4:8, :] = csmall[0:4, :]
        for s in range(2):
            row = home_dx[0, s : s + 1, :] + home_dx[1, s : s + 1, :]
            small[pl.ds(8 + p.fsdp * 2 + s, 1), :] = row
        turn(tr, df)

    def active_back(part):
        @pl.loop(part * n_tiles, (part + 1) * n_tiles)
        def _(i):
            cols = lanes(i * tile, tile)
            d = mm(df[...], bw[:, cols], NN) * sl[:, cols].astype(f32)
            sl[:, cols] = d.astype(bf16)

    def add_back(src, weight, first, size):
        inner = pl.ds(first, size)

        @pl.loop(0, n_tiles)
        def _(i):
            cols = lanes(i * tile, tile)
            h[:, cols] += mm(src[:, inner], weight[rows_at(i * tile, tile, 16), inner], NT)

    def context_back():
        @pl.loop(0, width // tile)
        def _(i):
            d = mm(df[...], ow[rows_at(i * tile, tile, 16), :], NT)
            cx[:, lanes(i * tile, tile)] = d.astype(bf16)

    def attend_back(s):
        key = pl.ds(s * SEG_LEN, SEG_LEN)
        factor = (LANES // 2) ** (-0.5)

        @pl.loop(0, pairs, unroll=True)
        def _(j):
            a = at[rows_at((s * pairs + j) * 2 * SEG_LEN, 2 * SEG_LEN, 16), :]
            q_cols = lanes(j * LANES, LANES)
            k_cols = lanes(width + j * LANES, LANES)
            v_cols = lanes(2 * width + j * LANES, LANES)
            qs = jnp.concatenate(lane_halves(pk[key, q_cols]), axis=0)
            ks = jnp.concatenate(lane_halves(pk[key, k_cols]), axis=0)
            ds_in = jnp.concatenate(lane_halves(cx[key, q_cols]), axis=0)
            da = mm(ds_in, pk[key, v_cols], NT)
            af = a.astype(f32)
            ds = (af * (da - jnp.sum(af * da, axis=-1, keepdims=True))).astype(bf16)
            dv = mm(a, ds_in, TN)
            both = jnp.concatenate([ds[:SEG_LEN], ds[SEG_LEN:]], axis=1)
            dq = mm(both, ks, NN) * factor
            dk = mm(ds, qs, TN) * factor
            pk[key, q_cols] = dq.astype(bf16)
            pk[key, k_cols] = dk.astype(bf16)
            pk[key, v_cols] = dv.astype(bf16)

    def result():
        @pl.loop(0, rows // block_rows, unroll=2)
        def _(i):
            key = rows_at(i * block_rows, block_rows, 16)
            gt_ref[key, :] = h[key, :].astype(bf16)

    def smalls():
        dws[:, :LANES] = small[...].T.astype(bf16)
        dws[:, LANES:] = jnp.zeros((dws.shape[0], LANES), bf16)

    need(0)
    params()
    for i in range(3):
        need(1 + i)
        project(i * n_tiles, n_tiles)
    for s in range(segs):
        attend(s)
        comm.upto("drain", 4 + s)
    branch()
    for i in range(per):
        need(4 + per + i)
        feed_in(i * n_tiles, n_tiles)
        if i:
            feed_back(i - 1)
    wo_start()
    need(4 + 2 * per)
    feed_back(per - 1)
    leaders()
    cross()
    comm.finish()
    for i in range(n_seg + 2):
        pair(i).wait_send()
    patch()
    sum_step = lambda: scatter_step(sums, jobs)
    norm_leaders()
    factors[1].plane()
    factors[2].plane()
    factors[0].last()
    for i in range(per):
        active_back(i)
        outer(bw, tr, g, i * width, width)
        sum_step()
        if i == 0:
            factors[3].line()
            factors[1].last()
        if i == 1:
            factors[2].last()
            factors[3].plane()
        if i == 2:
            factors[3].last()
    turn(tr, nl)
    add_back(sl, iw, 0, 2 * width)
    add_back(sl, iw, 2 * width, hidden - 2 * width)
    outer(iw, tr, sl, 0, width)
    sum_step()
    norm_back(z1, r1_ref, 0, df, 0)
    outer(iw, tr, sl, width, width)
    sum_step()
    smalls()
    turn(tr2, cx)
    context_back()
    attend_back(0)
    for i in range(2, per - 1):
        outer(iw, tr, sl, i * width, width)
        sum_step()
    attend_back(1)
    outer(iw, tr, sl, (per - 1) * width, width)
    sum_step()
    attend_back(2)
    outer(ow, tr2, df, 0, width)
    sum_step()
    attend_back(3)
    sum_step()
    turn(tr2, x_ref)
    for at_col, size in tail_units(width):
        add_back(pk, qw, at_col, size)
        outer(qw, tr2, pk, at_col, size)
        sum_step()
    result()
    for unit in factors:
        unit.drain()
    factor_grads()
    sums.finish()
    for unit in factors:
        unit.finish()
    for i in range(4):
        swap(i).wait_send()
    wait_leads()


def layer(wq, wo, wi, wb, gain, bias, pos, docs, x, cot):
    wrows = 16 * ROWS
    rows, width = x.shape
    segs = rows // SEG_LEN
    leads = docs.shape[1]
    hidden = wi.shape[2]
    own = ROWS // 2
    cross_width = 3 * width
    total = 2 * LANES + 3 * width + width + 2 * hidden + 4 * cross_width + width
    parts = 5 + 2 * hidden // width + 2
    n_units = parts - 2 + 3
    vm = pl.BlockSpec(memory_space=VM)
    arr = jax.ShapeDtypeStruct
    DMA = pltpu.SemaphoreType.DMA
    att_rows = segs * HEADS * SEG_LEN
    wide = lambda v, kind=bf16: VM((rows, v), kind)
    weight = lambda v: VM((wrows, v), bf16)
    widths = [width] * (2 * (hidden // width) + 1) + [256] + [size for _, size in tail_units(width)]
    bufs = []
    for i, w in enumerate(widths):
        bufs += scatter_buffers(w, i % 2 == 0)
    small_units = len([w for w in widths if w == 256])
    return pl.pallas_call(
        layer_kernel,
        out_shape=[
            arr((rows, width), bf16),
            arr((rows, width), bf16),
            arr((2, own, 3 * width), f32),
            arr((2, own, width), f32),
            arr((2, own, hidden), f32),
            arr((2, own, hidden), f32),
            arr((own, 256), f32),
        ],
        in_specs=[vm] * 10,
        out_specs=[vm] * 7,
        scratch_shapes=[
            weight(2 * LANES), weight(width), weight(3 * width), weight(hidden), weight(hidden),
            weight(cross_width), VM((wrows // 4, width), bf16),
            wide(3 * width), VM((att_rows, SEG_LEN), bf16), wide(width), wide(width, f32), wide(width),
            wide(hidden), wide(hidden), wide(width), wide(width),
            wide(LANES, f32), wide(LANES, f32), VM((24, width), f32),
            VM((32, total), bf16), VM((32, total), bf16), VM((ROWS, 4 * cross_width + width), bf16),
            VM((LANES, LANES), f32),
            VM((2, 2, 2 * width), f32), VM((8, 2, 2 * width), f32), VM((leads, 2 * width), f32),
            VM((4, 4, leads, width), bf16), VM((8, 2, width), f32), VM((leads, 3 * width // 4), f32),
            VM((2, 2, width), f32), VM((2, 2, width), f32), VM((8, 2, width), f32), VM((8, 2, width), f32),
            VM((leads, 4 * width), bf16), VM((leads, 4 * width), bf16),
            VM((8, width), f32),
            wide(width), VM((width, rows), bf16), VM((width, rows), bf16), weight(256),
            VM((LANES, width), f32), VM((32 * leads, 4 * width), bf16), VM((width // 4, width), f32),
            VM((PAIR_SLOTS, wrows, width // 2), bf16), weight((width - 256) // 2),
            VM((small_units, wrows, LANES), bf16),
            DMA((n_units, 11)), DMA((n_units, 11)), DMA((parts,)), DMA((parts,)),
            DMA((5,)), DMA((5,)), DMA,
            DMA((8,)), DMA((8,)), DMA((4, 3)), DMA((4, 4)), DMA, DMA, DMA, DMA((8,)), DMA((8,)),
            DMA((4, 11)), DMA((4, 11)), DMA((4,)), DMA((4,)),
            DMA((len(widths), 12)), DMA((len(widths), 12)), pltpu.SemaphoreType.REGULAR((PAIR_SLOTS,)),
        ]
        + bufs,
        compiler_params=pltpu.CompilerParams(
            collective_id=0, has_side_effects=True, vmem_limit_bytes=63 * MIB
        ),
    )(wq, wo, wi, wb, gain, bias, pos, docs, x, cot)


def matmul(left, right, form):
    return jnp.einsum(form, left, right, preferred_element_type=jnp.float32)


def norm_forward(summed, gains, biases):
    average = jnp.mean(summed, axis=-1, keepdims=True)
    centred = summed - average
    variance = jnp.mean(centred * centred, axis=-1, keepdims=True)
    inverse = lax.rsqrt(variance + epsilon)
    scaled = centred * inverse
    return (scaled * gains + biases, scaled, inverse)


def norm_backward(grad_result, scaled, inverse, gains):
    grad_scaled = grad_result * gains
    first_mean = jnp.mean(grad_scaled, axis=-1, keepdims=True)
    second_mean = jnp.mean(grad_scaled * scaled, axis=-1, keepdims=True)
    grad_sum = inverse * (grad_scaled - first_mean - scaled * second_mean)
    return (grad_sum, jnp.sum(grad_result * scaled, axis=(0, 1)), jnp.sum(grad_result, axis=(0, 1)))


def split_heads(packed):
    groups, length, model_width = packed.shape
    return packed.reshape(groups, length, HEADS, model_width // HEADS)


def join_heads(split_part):
    groups, length, heads_count, head_size = split_part.shape
    return split_part.reshape(groups, length, heads_count * head_size)


def attend_forward(query_part, key_part, value_part, allowed):
    head_size = query_part.shape[-1]
    scores = matmul(query_part, key_part, "glhe,gmhe->ghlm") * head_size ** (-0.5)
    scores = jnp.where(allowed[:, None], scores, -1e30)
    row_max = jnp.max(scores, axis=-1, keepdims=True)
    exp_terms = jnp.exp(scores - row_max)
    row_total = jnp.sum(exp_terms, axis=-1, keepdims=True)
    attention = exp_terms / row_total
    context = matmul(attention.astype(jnp.bfloat16), value_part, "ghlm,gmhe->glhe")
    return (join_heads(context).astype(jnp.bfloat16), row_max + jnp.log(row_total))


def attend_backward(query_part, key_part, value_part, allowed, log_total, grad_context):
    head_size = query_part.shape[-1]
    factor = head_size ** (-0.5)
    scores = matmul(query_part, key_part, "glhe,gmhe->ghlm") * factor
    scores = jnp.where(allowed[:, None], scores, -1e30)
    attention = jnp.exp(scores - log_total)
    grad_attention = matmul(grad_context, value_part, "glhe,gmhe->ghlm")
    grad_value = matmul(attention.astype(jnp.bfloat16), grad_context, "ghlm,glhe->gmhe")
    inner = jnp.sum(attention * grad_attention, axis=-1, keepdims=True)
    grad_scores = (attention * (grad_attention - inner)).astype(jnp.bfloat16)
    grad_query = matmul(grad_scores, key_part, "ghlm,gmhe->glhe") * factor
    grad_key = matmul(grad_scores, query_part, "ghlm,glhe->gmhe") * factor
    return (join_heads(grad_query), join_heads(grad_key), join_heads(grad_value))


def segment_attend(packed):
    groups, length, total_width = packed.shape
    model_width = total_width // 3
    allowed = jnp.ones((groups, length, length), dtype=jnp.bool_)
    context, log_total = attend_forward(
        split_heads(packed[..., :model_width]),
        split_heads(packed[..., model_width : 2 * model_width]),
        split_heads(packed[..., 2 * model_width :]),
        allowed,
    )
    return (context, log_total)


def segment_attend_back(packed, log_total, grad_context):
    groups, length, total_width = packed.shape
    model_width = total_width // 3
    allowed = jnp.ones((groups, length, length), dtype=jnp.bool_)
    grad_query, grad_key, grad_value = attend_backward(
        split_heads(packed[..., :model_width]),
        split_heads(packed[..., model_width : 2 * model_width]),
        split_heads(packed[..., 2 * model_width :]),
        allowed,
        log_total,
        split_heads(grad_context),
    )
    return jnp.concatenate([grad_query, grad_key, grad_value], axis=-1)


def cross_attend(packed, allowed):
    model_width = packed.shape[-1] // 3
    remote = lax.all_gather(packed[..., model_width:], "fsdp", axis=1, tiled=True)
    context, log_total = attend_forward(
        split_heads(packed[..., :model_width]),
        split_heads(remote[..., :model_width]),
        split_heads(remote[..., model_width:]),
        allowed,
    )
    return (context, (remote, log_total))


def cross_attend_back(packed, saved, grad_context, allowed):
    remote, log_total = saved
    model_width = packed.shape[-1] // 3
    grad_query, grad_key, grad_value = attend_backward(
        split_heads(packed[..., :model_width]),
        split_heads(remote[..., :model_width]),
        split_heads(remote[..., model_width:]),
        allowed,
        log_total,
        split_heads(grad_context),
    )
    shared = jnp.concatenate([grad_key, grad_value], axis=-1)
    own_part = lax.psum_scatter(
        shared.astype(jnp.bfloat16), "fsdp", scatter_dimension=1, tiled=True
    ).astype(jnp.float32)
    return jnp.concatenate([grad_query, own_part], axis=-1)


def block_forward(states, weights, attend):
    w_qkv, w_out, w_in, w_back, gains, biases = weights
    gains = gains.astype(jnp.float32)
    biases = biases.astype(jnp.float32)
    states_low = states.astype(jnp.bfloat16)
    packed = matmul(states_low, w_qkv, "gld,de->gle").astype(jnp.bfloat16)
    context, saved = attend(packed)
    branch = matmul(context, w_out, "gld,de->gle")
    normed, scaled_one, inverse_one = norm_forward(states + branch, gains[0], biases[0])
    normed_low = normed.astype(jnp.bfloat16)
    hidden = matmul(normed_low, w_in, "gld,df->glf")
    active_low = jax.nn.gelu(hidden, approximate=False).astype(jnp.bfloat16)
    feed_out = matmul(active_low, w_back, "glf,fd->gld")
    result, scaled_two, inverse_two = norm_forward(normed + feed_out, gains[1], biases[1])
    kept = (
        states_low,
        packed,
        context,
        saved,
        scaled_one,
        inverse_one,
        normed_low,
        hidden,
        active_low,
        scaled_two,
        inverse_two,
    )
    return (result, kept)


def block_backward(grad_result, kept, weights, attend_back):
    w_qkv, w_out, w_in, w_back, gains, biases = weights
    gains = gains.astype(jnp.float32)
    (
        states_low,
        packed,
        context,
        saved,
        scaled_one,
        inverse_one,
        normed_low,
        hidden,
        active_low,
        scaled_two,
        inverse_two,
    ) = kept
    grad_sum_two, gain_two, bias_two = norm_backward(grad_result, scaled_two, inverse_two, gains[1])
    grad_feed = grad_sum_two.astype(jnp.bfloat16)
    grad_active = matmul(grad_feed, w_back, "gld,fd->glf")
    cumulative = 0.5 * (1.0 + lax.erf(hidden * root_half))
    slope = cumulative + hidden * inv_root_tau * jnp.exp(-0.5 * hidden * hidden)
    grad_hidden = (grad_active * slope).astype(jnp.bfloat16)
    grad_normed = grad_sum_two + matmul(grad_hidden, w_in, "glf,df->gld")
    grad_sum_one, gain_one, bias_one = norm_backward(grad_normed, scaled_one, inverse_one, gains[0])
    grad_branch = grad_sum_one.astype(jnp.bfloat16)
    grad_context = matmul(grad_branch, w_out, "gle,de->gld").astype(jnp.bfloat16)
    grad_packed = attend_back(packed, saved, grad_context).astype(jnp.bfloat16)
    grad_states = grad_sum_one + matmul(grad_packed, w_qkv, "gle,de->gld")
    factors = (
        states_low,
        grad_packed,
        context,
        grad_branch,
        normed_low,
        grad_hidden,
        grad_feed,
        active_low,
    )
    smalls = (jnp.stack([gain_one, gain_two]), jnp.stack([bias_one, bias_two]))
    return (grad_states, factors, smalls)


def weight_terms(factors):
    (
        states_low,
        grad_packed,
        context,
        grad_branch,
        normed_low,
        grad_hidden,
        grad_feed,
        active_low,
    ) = factors
    term_qkv = matmul(states_low, grad_packed, "gld,gle->de")
    term_out = matmul(context, grad_branch, "gld,gle->de")
    term_in = matmul(normed_low, grad_hidden, "gld,glf->df")
    term_back = matmul(grad_feed, active_low, "gld,glf->df")
    return jnp.concatenate([term_qkv, term_out, term_in, term_back], axis=1)


def gather_segment(w_qkv, w_out, w_in, w_back, norm_gain, norm_bias):
    return (
        lax.all_gather(w_qkv[0], ("dp", "fsdp"), axis=0, tiled=True),
        lax.all_gather(w_out[0], ("dp", "fsdp"), axis=0, tiled=True),
        lax.all_gather(w_in[0], ("dp", "fsdp"), axis=0, tiled=True),
        lax.all_gather(w_back[0], ("dp", "fsdp"), axis=1, tiled=True),
        lax.all_gather(norm_gain[0], ("dp", "fsdp"), axis=1, tiled=True),
        lax.all_gather(norm_bias[0], ("dp", "fsdp"), axis=1, tiled=True),
    )


def gather_cross(pos_embed, w_qkv, w_out, w_in, w_back, norm_gain, norm_bias):
    gathered = (
        lax.all_gather(w_qkv[1], ("dp", "fsdp"), axis=0, tiled=True),
        lax.all_gather(w_out[1], ("dp", "fsdp"), axis=0, tiled=True),
        lax.all_gather(w_in[1], ("dp", "fsdp"), axis=0, tiled=True),
        lax.all_gather(w_back[1], ("dp", "fsdp"), axis=1, tiled=True),
        lax.all_gather(norm_gain[1], ("dp", "fsdp"), axis=1, tiled=True),
        lax.all_gather(norm_bias[1], ("dp", "fsdp"), axis=1, tiled=True),
        lax.all_gather(pos_embed, ("dp", "fsdp"), axis=1, tiled=True),
    )
    return (gathered[:6], gathered[6])


def layer_forward(tokens, doc_ids, seg_weights, cross_weights, pos_full):
    rows, local_len, model_width = tokens.shape
    seg_count = local_len // SEG_LEN
    segments = tokens.reshape(rows * seg_count, SEG_LEN, model_width).astype(jnp.float32)
    seg_out, seg_kept = block_forward(segments, seg_weights, segment_attend)
    start = lax.axis_index("fsdp") * seg_count
    pos_local = lax.dynamic_slice_in_dim(pos_full, start, seg_count, 0).astype(jnp.float32)
    leaders = seg_out[:, 0, :].reshape(rows, seg_count, model_width) + pos_local
    own_docs = lax.dynamic_slice_in_dim(doc_ids, start, seg_count, 1)
    allowed = own_docs[:, :, None] == doc_ids[:, None, :]
    cross_out, cross_kept = block_forward(
        leaders, cross_weights, partial(cross_attend, allowed=allowed)
    )
    joined = jnp.concatenate(
        [cross_out.reshape(rows * seg_count, 1, model_width), seg_out[:, 1:, :]], axis=1
    )
    output = joined.reshape(rows, local_len, model_width).astype(jnp.bfloat16)
    return (output, (seg_kept, cross_kept, allowed))


def layer_backward(cotangent, doc_ids, kept, seg_weights, cross_weights):
    seg_kept, cross_kept, allowed = kept
    rows, local_len, model_width = cotangent.shape
    seg_count = local_len // SEG_LEN
    grad_all = cotangent.reshape(rows * seg_count, SEG_LEN, model_width).astype(jnp.float32)
    grad_cross = grad_all[:, 0, :].reshape(rows, seg_count, model_width)
    grad_leaders, cross_factors, cross_smalls = block_backward(
        grad_cross, cross_kept, cross_weights, partial(cross_attend_back, allowed=allowed)
    )
    start = lax.axis_index("fsdp") * seg_count
    empty_pos = jnp.zeros((doc_ids.shape[1], model_width), jnp.float32)
    grad_pos = lax.dynamic_update_slice_in_dim(empty_pos, jnp.sum(grad_leaders, axis=0), start, 0)
    grad_seg = jnp.concatenate(
        [grad_leaders.reshape(rows * seg_count, 1, model_width), grad_all[:, 1:, :]], axis=1
    )
    grad_states, seg_factors, seg_smalls = block_backward(
        grad_seg, seg_kept, seg_weights, segment_attend_back
    )
    grad_tokens = grad_states.reshape(rows, local_len, model_width).astype(jnp.bfloat16)
    return (grad_tokens, seg_factors, cross_factors, seg_smalls, cross_smalls, grad_pos)


def body(tokens, doc_ids, pos_embed, w_qkv, w_out, w_in, w_back, norm_gain, norm_bias, cotangent):
    seg_weights = gather_segment(w_qkv, w_out, w_in, w_back, norm_gain, norm_bias)
    cross_weights, pos_full = gather_cross(
        pos_embed, w_qkv, w_out, w_in, w_back, norm_gain, norm_bias
    )
    output, kept = layer_forward(tokens, doc_ids, seg_weights, cross_weights, pos_full)
    grad_tokens, seg_factors, cross_factors, seg_smalls, cross_smalls, grad_pos = layer_backward(
        cotangent, doc_ids, kept, seg_weights, cross_weights
    )
    model_width = tokens.shape[2]
    hidden_width = w_in.shape[2]
    seg_term = lax.psum_scatter(
        weight_terms(seg_factors), ("dp", "fsdp"), scatter_dimension=0, tiled=True
    )
    cross_term = lax.psum_scatter(
        weight_terms(cross_factors), ("dp", "fsdp"), scatter_dimension=0, tiled=True
    )
    stacked = jnp.stack([seg_term, cross_term])
    grad_qkv = stacked[:, :, : 3 * model_width]
    grad_out = stacked[:, :, 3 * model_width : 4 * model_width]
    grad_in = stacked[:, :, 4 * model_width : 4 * model_width + hidden_width]
    grad_back = jnp.transpose(stacked[:, :, 4 * model_width + hidden_width :], (0, 2, 1))
    gain_all = jnp.stack([seg_smalls[0], cross_smalls[0]])
    bias_all = jnp.stack([seg_smalls[1], cross_smalls[1]])
    grad_gain, grad_bias, pos_shard = (
        lax.psum_scatter(gain_all, ("dp", "fsdp"), scatter_dimension=2, tiled=True),
        lax.psum_scatter(bias_all, ("dp", "fsdp"), scatter_dimension=2, tiled=True),
        lax.psum_scatter(grad_pos, ("dp", "fsdp"), scatter_dimension=1, tiled=True),
    )
    return (
        output,
        grad_tokens,
        pos_shard,
        grad_qkv,
        grad_out,
        grad_in,
        grad_back,
        grad_gain,
        grad_bias,
    )


def write_kernel(n, *refs):
    sources, smalls = refs[:n], refs[n]
    targets, pos_ref, gain_ref, bias_ref, sems = refs[n + 1 : 2 * n + 1], *refs[2 * n + 1 :]
    copies = [pltpu.make_async_copy(sources[i], targets[i], sems.at[i]) for i in range(n)]
    for copy in copies:
        copy.start()
    rows = smalls[:, :LANES].T[:, : smalls.shape[0]]
    pos_ref[...] = rows[8 : 8 + pos_ref.shape[0]]
    for b in range(2):
        gain_ref[b] = rows[4 * b : 4 * b + 2]
        bias_ref[b] = rows[4 * b + 2 : 4 * b + 4]
    for copy in copies:
        copy.wait()


def write_results(arrays, smalls, positions):
    n = len(arrays)
    own = smalls.shape[0]
    hbm, vm = pl.BlockSpec(memory_space=pl.ANY), pl.BlockSpec(memory_space=VM)
    like = [jax.ShapeDtypeStruct(v.shape, v.dtype) for v in arrays]
    shapes = [(positions, own), (2, 2, own), (2, 2, own)]
    return pl.pallas_call(
        partial(write_kernel, n),
        out_shape=like + [jax.ShapeDtypeStruct(v, f32) for v in shapes],
        in_specs=[vm] * (n + 1),
        out_specs=[hbm] * n + [vm] * 3,
        scratch_shapes=[pltpu.SemaphoreType.DMA((n,))],
    )(*arrays, smalls)


def fast_body(tokens, doc_ids, pos_embed, w_qkv, w_out, w_in, w_back, norm_gain, norm_bias, cotangent):
    nrows, local_len, width = tokens.shape
    rows = nrows * local_len
    x = tokens.reshape(rows, width)
    cot = cotangent.reshape(rows, width)
    output, grad_tokens, g_qkv, g_out, g_in, g_back, t_small = layer(
        w_qkv, w_out, w_in, jnp.swapaxes(w_back, 1, 2), norm_gain, norm_bias, pos_embed, doc_ids, x, cot
    )
    output, grad_tokens, g_qkv, g_out, g_in, g_back, grad_pos, grad_gain, grad_bias = write_results(
        (output, grad_tokens, g_qkv, g_out, g_in, g_back), t_small, doc_ids.shape[1]
    )
    return (
        output.reshape(tokens.shape),
        grad_tokens.reshape(tokens.shape),
        grad_pos,
        g_qkv,
        g_out,
        g_in,
        jnp.swapaxes(g_back, 1, 2),
        grad_gain,
        grad_bias,
    )


def solution(mesh):
    fast = dict(mesh.shape) == {"dp": 4, "fsdp": 8}
    return jax.shard_map(
        fast_body if fast else body,
        mesh=mesh,
        in_specs=(
            P("dp", "fsdp", None),
            P("dp", None),
            P(None, ("dp", "fsdp")),
            P(None, ("dp", "fsdp"), None),
            P(None, ("dp", "fsdp"), None),
            P(None, ("dp", "fsdp"), None),
            P(None, None, ("dp", "fsdp")),
            P(None, None, ("dp", "fsdp")),
            P(None, None, ("dp", "fsdp")),
            P("dp", "fsdp", None),
        ),
        out_specs=(
            P("dp", "fsdp", None),
            P("dp", "fsdp", None),
            P(None, ("dp", "fsdp")),
            P(None, ("dp", "fsdp"), None),
            P(None, ("dp", "fsdp"), None),
            P(None, ("dp", "fsdp"), None),
            P(None, None, ("dp", "fsdp")),
            P(None, None, ("dp", "fsdp")),
            P(None, None, ("dp", "fsdp")),
        ),
        check_vma=False,
    )
```

```python
from functools import partial

import jax
import jax.numpy as jnp
from jax import lax
from jax.experimental import pallas as pl
from jax.experimental.pallas import tpu as pltpu
from jax.sharding import PartitionSpec as P

HEADS = 12
SEG_LEN = 128


epsilon = 1e-05
root_half = 0.7071067811865476
inv_root_tau = 0.3989422804014327

bf16 = jnp.bfloat16
f32 = jnp.float32
MESH = pl.DeviceIdType.MESH
VM = pltpu.VMEM
MIB = 1024 * 1024
ROWS = 48
LANES = 128


class Place:
    def __init__(self):
        self.dp = lax.axis_index("dp")
        self.fsdp = lax.axis_index("fsdp")
        self.y, self.x = self.dp // 2, self.dp % 2
        self.z, self.core = self.fsdp // 2, self.fsdp % 2

    def at(self, dp, z, core):
        return (dp, z * 2 + core)

    @property
    def sib(self):
        return (self.dp, self.z * 2 + 1 - self.core)

    @property
    def xdp(self):
        return self.y * 2 + 1 - self.x

    @property
    def ydp(self):
        return (1 - self.y) * 2 + self.x

    @property
    def xnbr(self):
        return (self.xdp, self.fsdp)

    @property
    def ynbr(self):
        return (self.ydp, self.fsdp)


def greet(devices, meanwhile):
    barrier = pltpu.get_barrier_semaphore()
    for device in devices:
        pl.semaphore_signal(barrier, inc=1, device_id=device, device_id_type=MESH)
    meanwhile()
    pl.semaphore_wait(barrier, len(devices))


def remote(src, dst, send, recv, device):
    return pltpu.make_async_remote_copy(
        src_ref=src, dst_ref=dst, send_sem=send, recv_sem=recv, device_id=device, device_id_type=MESH
    )


def lanes(start, size):
    if isinstance(start, int):
        return pl.ds(start, size)
    return pl.ds(pl.multiple_of(start, LANES), size)


def rows_at(start, size, unit):
    return pl.ds(pl.multiple_of(start, unit), size)


class Gather:
    def __init__(self, place, out, off, width, source, index, sems, height2, wide_a=True):
        self.p, self.out, self.off, self.source = place, out, off, source
        self.m, self.sems, self.h2 = index, sems, height2
        self.half = width // 2
        tiles = self.half // LANES
        self.a = ((tiles + 1) // 2 if wide_a else max(tiles // 2, 1)) * LANES
        self.b = self.half - self.a
        self.sent = []
        self.far = (1 - place.y) * 2 + 1 - place.x

    def cols(self, core, part="AB"):
        at, size = {"A": (0, self.a), "B": (self.a, self.b), "AB": (0, self.half)}[part]
        return lanes(self.off + core * self.half + at, size)

    def block(self, z, core):
        return self.out.at[rows_at((self.p.dp * 4 + z) * self.h2, self.h2, 16), self.cols(core)]

    def group(self, dp, core, part="AB"):
        return self.out.at[rows_at(dp * 4 * self.h2, self.h2 * 4, 16), self.cols(core, part)]

    def go(self, src, dst, slot, device):
        copy = remote(src, dst, self.sems[0].at[self.m, slot], self.sems[1].at[self.m, slot], device)
        copy.start()
        self.sent.append(copy)

    def hand(self, ref, slot):
        self.go(ref, ref, slot, self.p.sib)

    def arrived(self, dst, slot):
        remote(dst, dst, self.sems[0].at[self.m, slot], self.sems[1].at[self.m, slot], self.p.sib).wait_recv()

    def own(self):
        p = self.p
        for d in (1, 3, 2):
            z = (p.z + d) % 4
            self.go(self.source(z), self.block(p.z, p.core), d - 1, p.at(p.dp, z, p.core))

    def line(self):
        p = self.p
        for d in (1, 3, 2):
            self.arrived(self.block((p.z + 4 - d) % 4, p.core), d - 1)
        mine = self.group(p.dp, p.core)
        self.go(mine, mine, 3, p.xnbr)
        self.go(mine, mine, 4, p.ynbr)
        self.hand(mine, 7)

    def plane(self):
        p = self.p
        over_x, over_y = self.group(p.xdp, p.core), self.group(p.ydp, p.core)
        self.arrived(over_x, 3)
        part = self.group(p.xdp, p.core, "A")
        self.go(part, part, 5, p.ynbr)
        self.arrived(over_y, 4)
        if self.b:
            part = self.group(p.ydp, p.core, "B")
            self.go(part, part, 6, p.xnbr)
        self.hand(over_x, 8)
        self.hand(over_y, 9)

    def last(self):
        p = self.p
        self.arrived(self.group(self.far, p.core, "A"), 5)
        if self.b:
            self.arrived(self.group(self.far, p.core, "B"), 6)
        self.hand(self.group(self.far, p.core), 10)

    def drain(self):
        p = self.p
        for slot, dp in ((7, p.dp), (8, p.xdp), (9, p.ydp), (10, self.far)):
            self.arrived(self.group(dp, 1 - p.core), slot)

    def finish(self):
        for copy in self.sent:
            copy.wait_send()


class Staged:
    def __init__(self, units, order):
        self.units, self.order, self.at = units, order, 0

    def step(self, count=1):
        for name, i in self.order[self.at : self.at + count]:
            getattr(self.units[i], name)()
        self.at += count

    def upto(self, name, i):
        spot = self.order.index((name, i)) + 1
        if spot > self.at:
            self.step(spot - self.at)

    def finish(self):
        self.step(len(self.order) - self.at)
        for unit in self.units:
            unit.finish()


def staggered(count, lags, first=0):
    order = []
    for t in range(min(lags.values()), count + max(lags.values())):
        for name, lag in lags.items():
            if 0 <= t - lag < count and (t >= 0 or lag < 0):
                order.append((name, t - lag + first))
    return order


def gather_peers(p):
    peers = [p.sib, p.xnbr, p.ynbr]
    for d in (1, 2, 3):
        peers.append(p.at(p.dp, (p.z + d) % 4, p.core))
    return peers


def everyone(p):
    return [
        (lax.rem(p.dp + i, 4), lax.rem(p.fsdp + j, 8)) for i in range(4) for j in range(8) if i or j
    ]


NEG = -1e30


def mm(a, b, dims):
    return lax.dot_general(a, b, (dims, ((), ())), preferred_element_type=f32)


NN = ((1,), (0,))
NT = ((1,), (1,))
TN = ((0,), (0,))


def norm_rows(summed, gain, bias):
    centred = summed - jnp.mean(summed, axis=-1, keepdims=True)
    variance = jnp.mean(centred * centred, axis=-1, keepdims=True)
    inverse = lax.rsqrt(variance + epsilon)
    scaled = centred * inverse
    return scaled * gain + bias, scaled, inverse


def norm_rows_back(grad, scaled, inverse, gain):
    g = grad * gain
    first = jnp.mean(g, axis=-1, keepdims=True)
    second = jnp.mean(g * scaled, axis=-1, keepdims=True)
    return inverse * (g - first - scaled * second)


def gelu_parts(u):
    cumulative = 0.5 * (1.0 + lax.erf(u * root_half))
    return cumulative, cumulative + u * inv_root_tau * jnp.exp(-0.5 * u * u)


def lane_halves(v):
    low = lax.broadcasted_iota(jnp.int32, v.shape, 1) < LANES // 2
    zero = jnp.zeros_like(v)
    return jnp.where(low, v, zero), jnp.where(low, zero, v)


FORWARD_LAGS = {"own": -3, "line": 0, "plane": 1, "last": 2, "drain": 3}


def forward_order(n_seg, n_cross):
    n = n_seg + n_cross
    order = staggered(n, FORWARD_LAGS)
    stop = order.index(("line", n_seg))
    head, rest = order[:stop], order[stop:]
    head += [s for s in rest if s[0] == "own"]
    done = set(head)
    tail = [("plane", n_seg - 1), ("line", n_seg), ("line", n_seg + 1)]
    for u in range(n_seg - 3, n_seg):
        tail += [("last", u), ("drain", u)]
    tail += [("plane", n_seg), ("line", n_seg + 2)]
    for u in range(n_seg, n):
        tail += [("last", u), ("plane", u + 1), ("drain", u)]
    return head + [s for s in tail if s not in done and s[1] < n]


class Scatter:
    def __init__(self, place, grad, off, width, out, index, sems, bufs, wide_a=True):
        self.p, self.grad, self.off, self.out, self.m = place, grad, off, out, index
        self.send, self.recv = sems
        self.pair, self.r1a, self.r1b, self.rx, self.ry, self.r3, self.give = bufs
        self.half = width // 2
        self.a = split_half(width, wide_a)
        self.b = self.half - self.a
        self.sent = []
        self.free, self.waits, self.frees = None, False, False
        p = place
        self.far = (1 - p.y) * 2 + 1 - p.x
        self.groups = (self.far, p.xdp, p.ydp, p.dp)

    def go(self, src, dst, slot, device):
        copy = remote(src, dst, self.send.at[self.m, slot], self.recv.at[self.m, slot], device)
        copy.start()
        self.sent.append(copy)

    def arrived(self, dst, slot):
        remote(dst, dst, self.send.at[self.m, slot], self.recv.at[self.m, slot], self.p.sib).wait_recv()

    def cols(self, part="AB", core=None):
        at, size = {"A": (0, self.a), "B": (self.a, self.b), "AB": (0, self.half)}[part]
        core = self.p.core if core is None else core
        return lanes(self.off + core * self.half + at, size)

    def group(self, dp):
        return rows_at(dp * 4 * ROWS, 4 * ROWS, 16)

    def side(self, dp, part="AB"):
        return self.grad.at[self.group(dp), self.cols(part)]

    def start(self):
        p = self.p
        if self.waits:
            pl.semaphore_wait(self.free, 1)
        for i, dp in enumerate(self.groups):
            theirs = self.grad.at[self.group(dp), self.cols("AB", 1 - p.core)]
            self.go(theirs, self.pair.at[self.group(dp)], i, p.sib)

    def add(self, dp, part, other, other_row=0):
        @pl.loop(0, 4)
        def _(i):
            key = (rows_at(dp * 4 * ROWS + i * ROWS, ROWS, 16), self.cols(part))
            self.grad[key] = self.grad[key] + other[rows_at(other_row + i * ROWS, ROWS, 16), :]

    def one(self):
        p = self.p
        for i, dp in enumerate(self.groups):
            self.arrived(self.pair.at[self.group(dp)], i)
            self.add(dp, "AB", self.pair, dp * 4 * ROWS)
            if i == 0:
                self.go(self.side(dp, "A"), self.r1a, 4, p.ynbr)
                if self.b:
                    self.go(self.side(dp, "B"), self.r1b, 5, p.xnbr)
        if self.frees:
            pl.semaphore_signal(self.free, inc=1, device_id=p.sib, device_id_type=MESH)

    def two(self):
        p = self.p
        self.arrived(self.r1a, 4)
        self.add(p.xdp, "A", self.r1a)
        self.go(self.side(p.xdp), self.rx, 6, p.xnbr)
        if self.b:
            self.arrived(self.r1b, 5)
            self.add(p.ydp, "B", self.r1b)
        self.go(self.side(p.ydp), self.ry, 7, p.ynbr)

    def three(self):
        p = self.p
        self.arrived(self.rx, 6)
        self.arrived(self.ry, 7)

        @pl.loop(0, 4)
        def _(i):
            key = (rows_at(p.dp * 4 * ROWS + i * ROWS, ROWS, 16), self.cols())
            own = rows_at(i * ROWS, ROWS, 16)
            self.grad[key] = self.grad[key] + (self.rx[own, :] + self.ry[own, :])

        for d in (1, 3, 2):
            z = (p.z + d) % 4
            src = self.grad.at[rows_at((p.dp * 4 + z) * ROWS, ROWS, 16), self.cols()]
            self.go(src, self.r3.at[d - 1], 7 + d, p.at(p.dp, z, p.core))

    def four(self):
        p = self.p
        for d in (1, 3, 2):
            self.arrived(self.r3.at[d - 1], 7 + d)
        rows = rows_at((p.dp * 4 + p.z) * ROWS, ROWS, 16)
        total = self.grad[rows, self.cols()].astype(f32)
        for d in range(3):
            total = total + self.r3[d].astype(f32)
        upper, lower = total[: ROWS // 2], total[ROWS // 2 :]
        first = p.core == 0
        self.give[...] = jnp.where(first, lower, upper)
        self.out[:, self.cols()] = jnp.where(first, upper, lower)
        self.go(self.give, self.out.at[:, self.cols()], 11, p.sib)

    def five(self):
        self.arrived(self.out.at[:, self.cols("AB", 1 - self.p.core)], 11)

    def finish(self):
        for copy in self.sent:
            copy.wait_send()


def split_half(width, wide_a):
    tiles = width // 2 // LANES
    return ((tiles + 1) // 2 if wide_a else max(tiles // 2, 1)) * LANES


def scatter_buffers(width, wide_a):
    half = width // 2
    a = split_half(width, wide_a)
    b = half - a
    return [
        VM((4 * ROWS, a), bf16),
        VM((4 * ROWS if b else 16, max(b, LANES)), bf16),
        VM((4 * ROWS, half), bf16),
        VM((4 * ROWS, half), bf16),
        VM((3, ROWS, half), bf16),
        VM((ROWS // 2, half), f32),
    ]


SCATTER_LAGS = {"start": 0, "one": 1, "two": 2, "three": 4, "four": 7, "five": 9}
PAIR_SLOTS = 4


def tail_units(width):
    return [(0, width), (width, width), (2 * width, width - 256), (3 * width - 256, 256)]


def scatter_step(sums, jobs):
    begun = len([s for s in sums.order[: sums.at] if s[0] == "start"])
    follow = [i for i, s in enumerate(sums.order) if s == ("start", begun + 1)]
    if begun < len(jobs):
        sums.step((follow[0] if follow else sums.order.index(("start", begun)) + 1) - sums.at)


def layer_kernel(*refs):
    wq_ref, wo_ref, wi_ref, wb_ref, gain_ref, bias_ref, pos_ref, docs_ref, x_hbm, cot_hbm = refs[:10]
    y_ref, gt_ref, gq_ref, go_ref, gi_ref, gb_ref, gs_ref = refs[10:17]
    (
        sw, ow, qw, iw, bw, cw, cwo,
        pk, at, cx, h, nl, g, sl, z1, z2, r1_ref, r2_ref, par_ref,
        x_ref, cot_ref, in_sem, own_buf, sib_buf, block, square,
        lead_out, gbuf, lead, xbuf, ybuf, dpack, home_y, home_dx, dbuf, dland, fac, fac_sib, csmall,
        df, tr, tr2, dws, small, full, tmp, ring, pair_wide, pair_small,
        s_send, s_recv, pair_send, pair_recv, wo_send, wo_recv, local,
        g_send, g_recv, x_send, x_recv, h_send, h_recv, lead_sem, d_send, d_recv,
        f_send, f_recv, swap_send, swap_recv, rs_send, rs_recv, free,
    ) = refs[17:89]
    bufs = refs[89:]
    p = Place()
    inputs = [
        pltpu.make_async_copy(x_hbm, x_ref, in_sem.at[0]),
        pltpu.make_async_copy(cot_hbm, cot_ref, in_sem.at[1]),
    ]
    for copy in inputs:
        copy.start()
    rows, width = x_ref.shape
    segs = rows // SEG_LEN
    hidden = iw.shape[1]
    pairs = width // LANES
    slab = width // 4
    cross_width = cw.shape[1]
    half_rows = ROWS // 2
    key_own = rows_at((p.dp * 4 + p.z) * ROWS, ROWS, 16)

    sizes = [sw.shape[1]] + [width] * (3 + 1 + 2 * (hidden // width)) + [4 * cross_width, width]
    starts = [sum(sizes[:i]) for i in range(len(sizes))]
    n_seg = len(sizes) - 2
    part_cross, part_wo = n_seg, n_seg + 1

    def put(start, value):
        zero = jnp.zeros((own_buf.shape[0] - half_rows, value.shape[1]), f32)
        full = jnp.concatenate([value.astype(f32), zero], axis=0).astype(bf16)
        own_buf[:, pl.ds(start, value.shape[1])] = full

    def pair(i):
        cols = pl.ds(starts[i], sizes[i])
        return remote(
            own_buf.at[:, cols], sib_buf.at[:, cols], pair_send.at[i], pair_recv.at[i], p.sib
        )

    def stage(i):
        spot = starts[i]
        per = hidden // width
        if i == 0:
            own = gain_ref.shape[2]
            square[...] = jnp.zeros_like(square)
            for b in range(2):
                square[4 * b : 4 * b + 2, :own] = gain_ref[b].astype(f32)
                square[4 * b + 2 : 4 * b + 4, :own] = bias_ref[b].astype(f32)
            square[8 : 8 + pos_ref.shape[0], :own] = pos_ref[...].astype(f32)
            turned = square[...].T[:half_rows]
            put(spot, jnp.concatenate([turned, jnp.zeros_like(turned)], axis=1))
        elif i < 4:
            put(spot, wq_ref[0, :, (i - 1) * width : i * width])
        elif i == 4:
            put(spot, wo_ref[0])
        elif i < 5 + per:
            put(spot, wi_ref[0, :, (i - 5) * width : (i - 4) * width])
        elif i < 5 + 2 * per:
            put(spot, wb_ref[0, :, (i - 5 - per) * width : (i - 4 - per) * width])
        elif i == part_cross:
            for z in range(4):
                heads = [wq_ref[1, :, j * width + z * slab : j * width + (z + 1) * slab] for j in range(3)]
                heads.append(heads[2])
                put(spot, jnp.concatenate([v.astype(f32) for v in heads], axis=1).astype(bf16))
                put(spot + width, wi_ref[1, :, z * width : (z + 1) * width])
                put(spot + 2 * width, wb_ref[1, :, z * width : (z + 1) * width])
                spot += cross_width
        else:
            put(spot, wo_ref[1])

    def joined(start, size):
        cols = lanes(start, size)
        first = p.core == 0
        mine = own_buf[:, cols].astype(f32)[:half_rows]
        theirs = sib_buf[:, cols].astype(f32)[:half_rows]
        both = [jnp.where(first, mine, theirs), jnp.where(first, theirs, mine)]
        return jnp.concatenate(both, axis=0).astype(bf16)

    ahead = 4

    def begin(i):
        if i < n_seg + 2:
            stage(i)
            pair(i).start()

    greet(everyone(p), lambda: [stage(i) for i in range(ahead)])
    for i in range(ahead):
        pair(i).start()

    sems = (s_send, s_recv)
    dests = [(sw, 0)] + [(qw, i * width) for i in range(3)] + [(ow, 0)]
    dests += [(iw, i * width) for i in range(hidden // width)]
    dests += [(bw, i * width) for i in range(hidden // width)]

    class SegUnit(Gather):
        def __init__(self, i):
            dst, off = dests[i]
            mine = lambda z: dst.at[key_own, self.cols(p.core)]
            super().__init__(p, dst, off, sizes[i], mine, i, sems, ROWS, i % 2 == 0)
            self.i = i

        def own(self):
            pair(self.i).wait_recv()
            self.out[key_own, self.cols(p.core)] = joined(
                starts[self.i] + p.core * self.half, self.half
            )
            super().own()
            begin(self.i + ahead)

    class CrossUnit(Gather):
        def __init__(self, i):
            start = i * width
            self.i = i

            def mine(z):
                spot = z * cross_width + start + p.core * self.half
                return block.at[:, lanes(spot, self.half)]

            super().__init__(p, cw, start, width, mine, n_seg + i, sems, ROWS, i % 2 == 0)

        def own(self):
            if self.i == 0:
                pair(part_cross).wait_recv()

                @pl.loop(0, 4 * cross_width // width)
                def _(k):
                    block[:, lanes(k * width, width)] = joined(starts[part_cross] + k * width, width)

            spot = p.z * cross_width + self.i * width + p.core * self.half
            self.out[key_own, self.cols(p.core)] = block[:, lanes(spot, self.half)]
            super().own()

    units = [SegUnit(i) for i in range(n_seg)] + [CrossUnit(i) for i in range(cross_width // width)]
    n_cross = len(units) - n_seg
    comm = Staged(units, forward_order(n_seg, n_cross))

    def need(i):
        comm.upto("drain", i)

    def pump():
        comm.step(5)

    half_wo = width // 2
    wo_block = block.at[:, pl.ds(4 * cross_width, width)]
    wo_src = block.at[:, lanes(4 * cross_width + p.core * half_wo, half_wo)]
    wo_dst = cwo.at[rows_at(p.z * ROWS, ROWS, 16), lanes(p.core * half_wo, half_wo)]

    def wo_copy(i):
        return remote(wo_src, wo_dst, wo_send.at[i], wo_recv.at[p.z], p.at(i, p.dp, p.core))

    def wo_start():
        pair(part_wo).wait_recv()
        wo_block[...] = joined(starts[part_wo], width)
        for i in range(4):
            here = jnp.logical_and(p.dp == i, p.dp == p.z)

            @pl.when(jnp.logical_not(here))
            def _():
                wo_copy(i).start()

            @pl.when(here)
            def _():
                mine = pltpu.make_async_copy(wo_src, wo_dst, local)
                mine.start()
                mine.wait()

    wo_mine = cwo.at[:, lanes(p.core * half_wo, half_wo)]
    wo_theirs = cwo.at[:, lanes((1 - p.core) * half_wo, half_wo)]
    wo_hand = remote(wo_mine, wo_mine, wo_send.at[4], wo_recv.at[4], p.sib)

    def wo_middle():
        for i in range(4):
            piece = cwo.at[pl.ds(i * ROWS, ROWS), lanes(p.core * half_wo, half_wo)]

            @pl.when(jnp.logical_not(jnp.logical_and(p.z == p.dp, p.z == i)))
            def _():
                remote(piece, piece, wo_send.at[i], wo_recv.at[i], p.sib).wait_recv()

        wo_hand.start()

    def wo_finish():
        remote(wo_theirs, wo_theirs, wo_send.at[4], wo_recv.at[4], p.sib).wait_recv()
        wo_hand.wait_send()
        for i in range(4):

            @pl.when(jnp.logical_not(jnp.logical_and(p.dp == i, p.dp == p.z)))
            def _():
                wo_copy(i).wait_send()

    tile = 256

    def params():
        par_ref[...] = sw[...].astype(f32).T[: par_ref.shape[0]]

    def project(first, count):
        @pl.loop(first, first + count)
        def _(i):
            cols = lanes(i * tile, tile)
            pk[:, cols] = mm(x_ref[...], qw[:, cols], NN).astype(bf16)

    def attend(s):
        key = pl.ds(s * SEG_LEN, SEG_LEN)

        @pl.loop(0, pairs, unroll=True)
        def _(j):
            q2 = pk[key, lanes(j * LANES, LANES)]
            k2 = pk[key, lanes(width + j * LANES, LANES)]
            v2 = pk[key, lanes(2 * width + j * LANES, LANES)]
            scores = mm(jnp.concatenate(lane_halves(q2), axis=0), k2, NT) * (LANES // 2) ** (-0.5)
            top = jnp.max(scores, axis=-1, keepdims=True)
            terms = jnp.exp(scores - top)
            a = (terms / jnp.sum(terms, axis=-1, keepdims=True)).astype(bf16)
            at[rows_at((s * pairs + j) * 2 * SEG_LEN, 2 * SEG_LEN, 16), :] = a
            both = jnp.concatenate([a[:SEG_LEN], a[SEG_LEN:]], axis=1)
            c2 = mm(both, jnp.concatenate(lane_halves(v2), axis=0), NN)
            cx[key, lanes(j * LANES, LANES)] = c2.astype(bf16)

    block_rows = 64

    def branch():
        @pl.loop(0, width // tile)
        def _(i):
            cols = lanes(i * tile, tile)
            h[:, cols] = x_ref[:, cols].astype(f32) + mm(cx[...], ow[:, cols], NN)

        @pl.loop(0, rows // block_rows, unroll=2)
        def _(i):
            key = rows_at(i * block_rows, block_rows, 16)
            normed, scaled, inverse = norm_rows(h[key, :], par_ref[0:1, :], par_ref[2:3, :])
            h[key, :] = normed
            nl[key, :] = normed.astype(bf16)
            z1[key, :] = scaled.astype(bf16)
            r1_ref[key, :] = jnp.broadcast_to(inverse, (block_rows, LANES))

    def feed_in(first, count):
        @pl.loop(first, first + count)
        def _(i):
            cols = lanes(i * tile, tile)
            u = mm(nl[...], iw[:, cols], NN)
            phi, slope = gelu_parts(u)
            g[:, cols] = (u * phi).astype(bf16)
            sl[:, cols] = slope.astype(bf16)

    def feed_back(part):
        inner = pl.ds(part * width, width)

        @pl.loop(0, width // tile)
        def _(i):
            cols = lanes(i * tile, tile)
            h[:, cols] += mm(g[:, inner], bw[rows_at(i * tile, tile, 16), inner], NT)

    def finish_block():
        @pl.loop(0, rows // block_rows, unroll=2)
        def _(i):
            key = rows_at(i * block_rows, block_rows, 16)
            result, scaled, inverse = norm_rows(h[key, :], par_ref[1:2, :], par_ref[3:4, :])
            h[key, :] = result
            y_ref[key, :] = result.astype(bf16)
            z2[key, :] = scaled.astype(bf16)
            r2_ref[key, :] = jnp.broadcast_to(inverse, (block_rows, LANES))

    def leaders():
        first = [h[s * SEG_LEN : s * SEG_LEN + 1, :] for s in range(segs)]
        result = norm_rows(jnp.concatenate(first, axis=0), par_ref[1:2, :], par_ref[3:4, :])[0]
        for s in range(segs):
            pos = par_ref[pl.ds(8 + p.fsdp * 2 + s % 2, 1), :]
            lead_out[s // 2, s % 2 : s % 2 + 1, :width] = result[s : s + 1] + pos
            lead_out[s // 2, s % 2 : s % 2 + 1, width:] = cot_ref[s * SEG_LEN : s * SEG_LEN + 16, :].astype(f32)[:1]

    def lead_copy(z, j):
        i = 2 * z + j
        return remote(lead_out.at[j], gbuf.at[p.fsdp], g_send.at[i], g_recv.at[p.fsdp], (p.dp, i))


    leads = fac.shape[0]
    lead2 = 2 * leads
    key_f = rows_at((p.dp * 4 + p.z) * lead2, lead2, 16)

    def swap(i):
        cols = pl.ds(i * width, width)
        return remote(fac.at[:, cols], fac_sib.at[:, cols], swap_send.at[i], swap_recv.at[i], p.sib)

    def give_factor(i, value):
        fac[:, i * width : (i + 1) * width] = value
        swap(i).start()

    class Factor(Gather):
        def __init__(self, i):
            mine = lambda z: full.at[key_f, self.cols(p.core)]
            super().__init__(p, full, i * width, width, mine, i, (f_send, f_recv), lead2, i % 2 == 0)
            self.i = i

        def own(self):
            swap(self.i).wait_recv()
            base = (p.dp * 4 + p.z) * lead2
            cols = lanes(self.i * width + p.core * (width // 2), width // 2)
            full[rows_at(base + p.core * leads, leads, 16), cols] = fac[:, cols]
            full[rows_at(base + (1 - p.core) * leads, leads, 16), cols] = fac_sib[:, cols]
            super().own()

    factors = [Factor(i) for i in range(4)]

    def factor_grads():
        def rows_of(z, at_col, size):
            return jnp.concatenate(
                [full[rows_at((i * 4 + z) * lead2, lead2, 16), pl.ds(at_col, size)] for i in range(4)],
                axis=0,
            )

        base = 2 * width
        own = rows_at(p.fsdp * (ROWS // 2), ROWS // 2, 8)
        xl = rows_of(p.dp, base, slab)
        nlf = rows_of(p.dp, base + slab, slab)
        dff = rows_of(p.dp, base + 2 * slab, slab)
        ctx = rows_of(p.dp, base + 3 * slab, slab)
        for z in range(4):
            tmp[:, :width] = mm(dff, rows_of(z, 0, width), TN)
            gb_ref[1, :, z * width : (z + 1) * width] = tmp[own, :width]
            tmp[:, :width] = mm(nlf, rows_of(z, width, width), TN)
            gi_ref[1, :, z * width : (z + 1) * width] = tmp[own, :width]
            tmp[:, : 3 * slab] = mm(xl, rows_of(z, 3 * width, 3 * slab), TN)
            got = tmp[own, : 3 * slab]
            for j in range(3):
                spot = j * width + z * slab
                gq_ref[1, :, spot : spot + slab] = got[:, j * slab : (j + 1) * slab]
            tmp[:, :slab] = mm(ctx, rows_of(z, 3 * width + 3 * slab, slab), TN)
            go_ref[1, :, z * slab : (z + 1) * slab] = tmp[own, :slab]


    n_tiles = width // tile
    head = width // HEADS
    heads = HEADS // 4

    def cross():
        for d in range(4):
            z = (p.z + d) % 4
            for j in range(2):
                if d:
                    lead_copy(z, j).start()
                else:

                    @pl.when(p.core != j)
                    def _():
                        lead_copy(z, j).start()

                    @pl.when(p.core == j)
                    def _():
                        mine = pltpu.make_async_copy(lead_out.at[j], gbuf.at[p.fsdp], lead_sem)
                        mine.start()
                        mine.wait()

        comm.upto("plane", n_seg)
        comm.upto("line", n_seg + 2)
        finish_block()
        need(n_seg)
        wo_middle()
        for d in range(1, 8):
            i = lax.rem(p.fsdp + d, 8)
            remote(gbuf.at[i], gbuf.at[i], g_send.at[i], g_recv.at[i], p.sib).wait_recv()
        for i in range(8):
            lead[2 * i : 2 * i + 2, :] = gbuf[i]
        states = lead[:, :width]
        cot_rows = lead[:, width:]

        def sum_z(e, partial_sum, between):
            xbuf[e, p.z] = partial_sum.astype(bf16)
            copies = []
            for d in (1, 3, 2):
                z = (p.z + d) % 4
                copy = remote(
                    xbuf.at[e, p.z], xbuf.at[e, p.z], x_send.at[e, d - 1], x_recv.at[e, p.z],
                    p.at(p.dp, z, p.core),
                )
                copy.start()
                copies.append(copy)
            between()
            for d in (1, 3, 2):
                z = (p.z + d) % 4
                piece = xbuf.at[e, z]
                remote(piece, piece, x_send.at[e, d - 1], x_recv.at[e, z], p.sib).wait_recv()
            for copy in copies:
                copy.wait_send()
            return sum(xbuf[e, z].astype(f32) for z in range(4))

        gain0, gain1 = par_ref[4:5, :], par_ref[5:6, :]
        bias0, bias1 = par_ref[6:7, :], par_ref[7:8, :]
        in_cols, back_cols = pl.ds(width, width), pl.ds(2 * width, width)
        qkv_cols = pl.ds(0, 3 * slab)
        factor = head ** (-0.5)
        docs = docs_ref[...].astype(f32)
        number = docs.shape[1]
        square[:number, :number] = jnp.broadcast_to(
            jnp.where(p.core == 0, docs[0:1], docs[1:2]), (number, number)
        )
        allowed = square[:number, :number] == square[...].T[:number, :number]

        def part(full):
            pieces = [full[:, i * slab : (i + 1) * slab] for i in range(4)]
            out = pieces[0]
            for i in range(1, 4):
                out = jnp.where(p.z == i, pieces[i], out)
            return out.astype(bf16)

        xl = states.astype(bf16)
        packed = mm(xl, cw[:, qkv_cols], NN).astype(bf16)
        q = [packed[:, i * head : (i + 1) * head] for i in range(heads)]
        k = [packed[:, slab + i * head : slab + (i + 1) * head] for i in range(heads)]
        v = [packed[:, 2 * slab + i * head : 2 * slab + (i + 1) * head] for i in range(heads)]
        att, context = [], []
        for i in range(heads):
            scores = jnp.where(allowed, mm(q[i], k[i], NT) * factor, NEG)
            top = jnp.max(scores, axis=-1, keepdims=True)
            terms = jnp.exp(scores - top)
            a = terms / jnp.sum(terms, axis=-1, keepdims=True)
            att.append(a)
            context.append(mm(a.astype(bf16), v[i], NN))
        context = jnp.concatenate(context, axis=1).astype(bf16)
        wo_finish()
        branch = sum_z(0, mm(context, cwo[...], NN), norm_two)
        normed, z_one, r_one = norm_rows(states + branch, gain0, bias0)
        nl = normed.astype(bf16)
        need(n_seg + 1)
        hidden = mm(nl, cw[:, in_cols], NN)
        phi, slope = gelu_parts(hidden)
        active = (hidden * phi).astype(bf16)
        give_factor(0, active)
        need(n_seg + 2)

        def during_one():
            factors[0].own()

        feed = sum_z(1, mm(active, cw[:, back_cols], NT), during_one)
        result, z_two, r_two = norm_rows(normed + feed, gain1, bias1)
        d_two = norm_rows_back(cot_rows, z_two, r_two, gain1)
        df = d_two.astype(bf16)
        du = (mm(df, cw[:, back_cols], NN) * slope).astype(bf16)
        give_factor(1, du)
        give_factor(2, jnp.concatenate([part(states), part(normed), part(d_two), context], axis=1))

        for i in range(8):
            ybuf[i] = result[2 * i : 2 * i + 2]
        home = remote(ybuf.at[2 * p.z + 1 - p.core], home_y.at[p.core], h_send, h_recv, p.sib)

        def during_two():
            home.start()
            home_y[p.core] = ybuf[2 * p.z + p.core]
            factors[0].line()
            factors[1].own()

        d_normed = d_two + sum_z(2, mm(du, cw[:, in_cols], NT), during_two)
        d_one = norm_rows_back(d_normed, z_one, r_one, gain0)
        db = d_one.astype(bf16)
        dc = mm(db, cwo[...], NT).astype(bf16)
        for i in range(heads):
            a = att[i]
            dci = dc[:, i * head : (i + 1) * head]
            da = mm(dci, v[i], NT)
            dv = mm(a.astype(bf16), dci, TN)
            ds = (a * (da - jnp.sum(a * da, axis=-1, keepdims=True))).astype(bf16)
            dq = mm(ds, k[i], NN) * factor
            dk = mm(ds, q[i], TN) * factor
            for j, piece in enumerate((dq, dk, dv)):
                dpack[:, j * slab + i * head : j * slab + (i + 1) * head] = piece
        dp = dpack[...].astype(bf16)
        give_factor(3, jnp.concatenate([dp, part(d_one)], axis=1))

        def during_three():
            factors[0].plane()
            factors[2].own()
            factors[1].line()

        partial_dx = mm(dp, cw[:, qkv_cols], NT)
        for i in range(8):
            mine = jnp.where(p.z == i // 2, 1.0, 0.0) * d_one[2 * i : 2 * i + 2]
            dbuf[i] = partial_dx[2 * i : 2 * i + 2] + mine
        sent = []
        for d in range(1, 8):
            i = lax.rem(p.fsdp + d, 8)
            copy = remote(dbuf.at[i], dland.at[p.fsdp], d_send.at[d], d_recv.at[p.fsdp], (p.dp, i))
            copy.start()
            sent.append(copy)
        during_three()
        dland[p.fsdp] = dbuf[p.fsdp]
        for d in range(1, 8):
            i = lax.rem(p.fsdp + d, 8)
            remote(dland.at[i], dland.at[i], d_send.at[d], d_recv.at[i], p.sib).wait_recv()
        for j in range(2):
            home_dx[j] = (dland[j] + dland[2 + j]) + (dland[4 + j] + dland[6 + j])
        for copy in sent:
            copy.wait_send()
        once = jnp.where(p.z == 0, 1.0, 0.0)
        sums_of = [d_normed * z_one, cot_rows * z_two, d_normed, cot_rows]
        csmall[...] = jnp.zeros_like(csmall)
        for i, s in enumerate(sums_of):
            csmall[i : i + 1, :] = once * jnp.sum(s, axis=0, keepdims=True)
        theirs = home_y.at[1 - p.core]
        remote(theirs, theirs, h_send, h_recv, p.sib).wait_recv()
        home.wait_send()

    def wait_leads():
        for d in range(4):
            z = (p.z + d) % 4
            for j in range(2):
                if d:
                    lead_copy(z, j).wait_send()
                else:

                    @pl.when(p.core != j)
                    def _():
                        lead_copy(z, j).wait_send()


    def patch():
        for s in range(segs):
            spot = pl.ds(s * SEG_LEN, 16)
            old = y_ref[spot, :].astype(f32)
            new = jnp.broadcast_to(home_y[s // 2, s % 2 : s % 2 + 1, :], old.shape)
            top = lax.broadcasted_iota(jnp.int32, old.shape, 0) == 0
            y_ref[spot, :] = jnp.where(top, new, old).astype(bf16)
    per = hidden // width
    parts = [(bw, i * width, width, gb_ref.at[0]) for i in range(per)]
    parts += [(iw, i * width, width, gi_ref.at[0]) for i in range(per)]
    parts += [(ow, 0, width, go_ref.at[0]), (dws, 0, dws.shape[1], gs_ref)]
    parts += [(qw, at_col, size, gq_ref.at[0]) for at_col, size in tail_units(width)]
    jobs, shared = [], []
    for i, (grad, off, size, dst) in enumerate(parts):
        job_bufs = list(bufs[6 * i : 6 * i + 6])
        if size == width:
            slot = len(shared) % PAIR_SLOTS
            job = Scatter(p, grad, off, size, dst, i, (rs_send, rs_recv), [ring.at[slot]] + job_bufs, i % 2 == 0)
            job.free = free.at[slot]
            if len(shared) >= PAIR_SLOTS:
                job.waits = True
                shared[len(shared) - PAIR_SLOTS].frees = True
            shared.append(job)
        else:
            own_pair = pair_wide if size > 256 else pair_small.at[len([j for j in jobs if j.half == LANES])]
            job = Scatter(p, grad, off, size, dst, i, (rs_send, rs_recv), [own_pair] + job_bufs, i % 2 == 0)
        jobs.append(job)
    sums = Staged(jobs, staggered(len(jobs), SCATTER_LAGS))


    def norm_back(z_ref, r_ref, gain_row, low_ref, sums):
        def step(i, acc):
            key = rows_at(i * block_rows, block_rows, 16)
            dy = h[key, :]
            z = z_ref[key, :].astype(f32)
            r = jnp.concatenate([r_ref[key, :]] * (width // LANES), axis=1)
            e = dy * par_ref[gain_row : gain_row + 1, :]
            first = jnp.mean(e, axis=-1, keepdims=True)
            second = jnp.mean(e * z, axis=-1, keepdims=True)
            d = r * (e - first - z * second)
            h[key, :] = d
            low_ref[key, :] = d.astype(bf16)
            fold = lambda v: jnp.sum(v.reshape(block_rows // 8, 8, width), axis=0)
            return acc[0] + fold(dy * z), acc[1] + fold(dy)

        zero = jnp.zeros((8, width), f32)
        gain, bias = lax.fori_loop(0, rows // block_rows, step, (zero, zero), unroll=2)
        small[sums : sums + 1, :] = jnp.sum(gain, axis=0, keepdims=True)
        small[sums + 2 : sums + 3, :] = jnp.sum(bias, axis=0, keepdims=True)

    def turn(tr, ref):
        @pl.loop(0, width // tile)
        def _(i):
            tr[rows_at(i * tile, tile, 16), :] = ref[:, lanes(i * tile, tile)].T

    def outer(dst, tr, src, first, size):
        @pl.loop(first // tile, (first + size) // tile)
        def _(i):
            cols = lanes(i * tile, tile)
            dst[:, cols] = mm(tr[...], src[:, cols], NN).astype(bf16)

    def norm_two():
        @pl.loop(0, rows // block_rows)
        def _(i):
            key = rows_at(i * block_rows, block_rows, 16)
            h[key, :] = cot_ref[key, :].astype(f32)

        for s in range(segs):
            h[s * SEG_LEN : s * SEG_LEN + 1, :] = jnp.zeros((1, width), f32)
        small[...] = jnp.zeros_like(small)
        norm_back(z2, r2_ref, 1, df, 1)

    def norm_leaders():
        pick = lambda take: jnp.concatenate([take(s * SEG_LEN) for s in range(segs)], axis=0)
        dy = jnp.concatenate([home_dx[s // 2, s % 2 : s % 2 + 1, :] for s in range(segs)], axis=0)
        z = pick(lambda row: z2[row : row + 16, :].astype(f32)[:1])
        r = pick(lambda row: jnp.concatenate([r2_ref[row : row + 1, :]] * (width // LANES), axis=1))
        d = norm_rows_back(dy, z, r, par_ref[1:2, :])
        for s in range(segs):
            h[s * SEG_LEN : s * SEG_LEN + 1, :] = d[s : s + 1]
            spot = pl.ds(s * SEG_LEN, 16)
            old = df[spot, :].astype(f32)
            top = lax.broadcasted_iota(jnp.int32, old.shape, 0) == 0
            df[spot, :] = jnp.where(top, jnp.broadcast_to(d[s : s + 1], old.shape), old).astype(bf16)
        small[1:2, :] += jnp.sum(dy * z, axis=0, keepdims=True)
        small[3:4, :] += jnp.sum(dy, axis=0, keepdims=True)
        small[4:8, :] = csmall[0:4, :]
        for s in range(2):
            row = home_dx[0, s : s + 1, :] + home_dx[1, s : s + 1, :]
            small[pl.ds(8 + p.fsdp * 2 + s, 1), :] = row
        turn(tr, df)

    def active_back(part):
        @pl.loop(part * n_tiles, (part + 1) * n_tiles)
        def _(i):
            cols = lanes(i * tile, tile)
            d = mm(df[...], bw[:, cols], NN) * sl[:, cols].astype(f32)
            sl[:, cols] = d.astype(bf16)

    def add_back(src, weight, first, size):
        inner = pl.ds(first, size)

        @pl.loop(0, n_tiles)
        def _(i):
            cols = lanes(i * tile, tile)
            h[:, cols] += mm(src[:, inner], weight[rows_at(i * tile, tile, 16), inner], NT)

    def context_back():
        @pl.loop(0, width // tile)
        def _(i):
            d = mm(df[...], ow[rows_at(i * tile, tile, 16), :], NT)
            cx[:, lanes(i * tile, tile)] = d.astype(bf16)

    def attend_back(s):
        key = pl.ds(s * SEG_LEN, SEG_LEN)
        factor = (LANES // 2) ** (-0.5)

        @pl.loop(0, pairs, unroll=True)
        def _(j):
            a = at[rows_at((s * pairs + j) * 2 * SEG_LEN, 2 * SEG_LEN, 16), :]
            q_cols = lanes(j * LANES, LANES)
            k_cols = lanes(width + j * LANES, LANES)
            v_cols = lanes(2 * width + j * LANES, LANES)
            qs = jnp.concatenate(lane_halves(pk[key, q_cols]), axis=0)
            ks = jnp.concatenate(lane_halves(pk[key, k_cols]), axis=0)
            ds_in = jnp.concatenate(lane_halves(cx[key, q_cols]), axis=0)
            da = mm(ds_in, pk[key, v_cols], NT)
            af = a.astype(f32)
            ds = (af * (da - jnp.sum(af * da, axis=-1, keepdims=True))).astype(bf16)
            dv = mm(a, ds_in, TN)
            both = jnp.concatenate([ds[:SEG_LEN], ds[SEG_LEN:]], axis=1)
            dq = mm(both, ks, NN) * factor
            dk = mm(ds, qs, TN) * factor
            pk[key, q_cols] = dq.astype(bf16)
            pk[key, k_cols] = dk.astype(bf16)
            pk[key, v_cols] = dv.astype(bf16)

    def result():
        @pl.loop(0, rows // block_rows, unroll=2)
        def _(i):
            key = rows_at(i * block_rows, block_rows, 16)
            gt_ref[key, :] = h[key, :].astype(bf16)

    def smalls():
        dws[:, :LANES] = small[...].T.astype(bf16)
        dws[:, LANES:] = jnp.zeros((dws.shape[0], LANES), bf16)

    need(0)
    params()
    for copy in inputs:
        copy.wait()
    for i in range(3):
        need(1 + i)
        project(i * n_tiles, n_tiles)
    for s in range(segs):
        attend(s)
        comm.upto("drain", 4 + s)
    branch()
    for i in range(per):
        need(4 + per + i)
        feed_in(i * n_tiles, n_tiles)
        if i:
            feed_back(i - 1)
    wo_start()
    need(4 + 2 * per)
    feed_back(per - 1)
    leaders()
    cross()
    comm.finish()
    for i in range(n_seg + 2):
        pair(i).wait_send()
    patch()
    sum_step = lambda: scatter_step(sums, jobs)
    factors[3].own()
    norm_leaders()
    factors[2].line()
    factors[1].plane()
    factors[0].last()
    for i in range(per):
        active_back(i)
        outer(bw, tr, g, i * width, width)
        sum_step()
        if i == 0:
            factors[3].line()
            factors[2].plane()
            factors[1].last()
        if i == 1:
            factors[3].plane()
            factors[2].last()
        if i == 2:
            factors[3].last()
    turn(tr, nl)
    add_back(sl, iw, 0, 2 * width)
    add_back(sl, iw, 2 * width, hidden - 2 * width)
    outer(iw, tr, sl, 0, width)
    sum_step()
    norm_back(z1, r1_ref, 0, df, 0)
    outer(iw, tr, sl, width, width)
    sum_step()
    smalls()
    turn(tr2, cx)
    context_back()
    attend_back(0)
    for i in range(2, per - 1):
        outer(iw, tr, sl, i * width, width)
        sum_step()
    attend_back(1)
    outer(iw, tr, sl, (per - 1) * width, width)
    sum_step()
    attend_back(2)
    outer(ow, tr2, df, 0, width)
    sum_step()
    attend_back(3)
    sum_step()
    turn(tr2, x_ref)
    for at_col, size in tail_units(width):
        add_back(pk, qw, at_col, size)
        outer(qw, tr2, pk, at_col, size)
        sum_step()
    result()
    for unit in factors:
        unit.drain()
    factor_grads()
    sums.finish()
    for unit in factors:
        unit.finish()
    for i in range(4):
        swap(i).wait_send()
    wait_leads()


def layer(wq, wo, wi, wb, gain, bias, pos, docs, x, cot):
    wrows = 16 * ROWS
    rows, width = x.shape
    segs = rows // SEG_LEN
    leads = docs.shape[1]
    hidden = wi.shape[2]
    own = ROWS // 2
    cross_width = 3 * width
    total = 2 * LANES + 3 * width + width + 2 * hidden + 4 * cross_width + width
    parts = 5 + 2 * hidden // width + 2
    n_units = parts - 2 + 3
    vm = pl.BlockSpec(memory_space=VM)
    arr = jax.ShapeDtypeStruct
    DMA = pltpu.SemaphoreType.DMA
    att_rows = segs * HEADS * SEG_LEN
    wide = lambda v, kind=bf16: VM((rows, v), kind)
    weight = lambda v: VM((wrows, v), bf16)
    widths = [width] * (2 * (hidden // width) + 1) + [256] + [size for _, size in tail_units(width)]
    bufs = []
    for i, w in enumerate(widths):
        bufs += scatter_buffers(w, i % 2 == 0)
    small_units = len([w for w in widths if w == 256])
    return pl.pallas_call(
        layer_kernel,
        out_shape=[
            arr((rows, width), bf16),
            arr((rows, width), bf16),
            arr((2, own, 3 * width), f32),
            arr((2, own, width), f32),
            arr((2, own, hidden), f32),
            arr((2, own, hidden), f32),
            arr((own, 256), f32),
        ],
        in_specs=[vm] * 8 + [pl.BlockSpec(memory_space=pl.ANY)] * 2,
        out_specs=[vm] * 7,
        scratch_shapes=[
            weight(2 * LANES), weight(width), weight(3 * width), weight(hidden), weight(hidden),
            weight(cross_width), VM((wrows // 4, width), bf16),
            wide(3 * width), VM((att_rows, SEG_LEN), bf16), wide(width), wide(width, f32), wide(width),
            wide(hidden), wide(hidden), wide(width), wide(width),
            wide(LANES, f32), wide(LANES, f32), VM((24, width), f32),
            wide(width), wide(width), DMA((2,)),
            VM((32, total), bf16), VM((32, total), bf16), VM((ROWS, 4 * cross_width + width), bf16),
            VM((LANES, LANES), f32),
            VM((2, 2, 2 * width), f32), VM((8, 2, 2 * width), f32), VM((leads, 2 * width), f32),
            VM((4, 4, leads, width), bf16), VM((8, 2, width), f32), VM((leads, 3 * width // 4), f32),
            VM((2, 2, width), f32), VM((2, 2, width), f32), VM((8, 2, width), f32), VM((8, 2, width), f32),
            VM((leads, 4 * width), bf16), VM((leads, 4 * width), bf16),
            VM((8, width), f32),
            wide(width), VM((width, rows), bf16), VM((width, rows), bf16), weight(256),
            VM((LANES, width), f32), VM((32 * leads, 4 * width), bf16), VM((width // 4, width), f32),
            VM((PAIR_SLOTS, wrows, width // 2), bf16), weight((width - 256) // 2),
            VM((small_units, wrows, LANES), bf16),
            DMA((n_units, 11)), DMA((n_units, 11)), DMA((parts,)), DMA((parts,)),
            DMA((5,)), DMA((5,)), DMA,
            DMA((8,)), DMA((8,)), DMA((4, 3)), DMA((4, 4)), DMA, DMA, DMA, DMA((8,)), DMA((8,)),
            DMA((4, 11)), DMA((4, 11)), DMA((4,)), DMA((4,)),
            DMA((len(widths), 12)), DMA((len(widths), 12)), pltpu.SemaphoreType.REGULAR((PAIR_SLOTS,)),
        ]
        + bufs,
        compiler_params=pltpu.CompilerParams(
            collective_id=0, has_side_effects=True, vmem_limit_bytes=63 * MIB
        ),
    )(wq, wo, wi, wb, gain, bias, pos, docs, x, cot)


def matmul(left, right, form):
    return jnp.einsum(form, left, right, preferred_element_type=jnp.float32)


def norm_forward(summed, gains, biases):
    average = jnp.mean(summed, axis=-1, keepdims=True)
    centred = summed - average
    variance = jnp.mean(centred * centred, axis=-1, keepdims=True)
    inverse = lax.rsqrt(variance + epsilon)
    scaled = centred * inverse
    return (scaled * gains + biases, scaled, inverse)


def norm_backward(grad_result, scaled, inverse, gains):
    grad_scaled = grad_result * gains
    first_mean = jnp.mean(grad_scaled, axis=-1, keepdims=True)
    second_mean = jnp.mean(grad_scaled * scaled, axis=-1, keepdims=True)
    grad_sum = inverse * (grad_scaled - first_mean - scaled * second_mean)
    return (grad_sum, jnp.sum(grad_result * scaled, axis=(0, 1)), jnp.sum(grad_result, axis=(0, 1)))


def split_heads(packed):
    groups, length, model_width = packed.shape
    return packed.reshape(groups, length, HEADS, model_width // HEADS)


def join_heads(split_part):
    groups, length, heads_count, head_size = split_part.shape
    return split_part.reshape(groups, length, heads_count * head_size)


def attend_forward(query_part, key_part, value_part, allowed):
    head_size = query_part.shape[-1]
    scores = matmul(query_part, key_part, "glhe,gmhe->ghlm") * head_size ** (-0.5)
    scores = jnp.where(allowed[:, None], scores, -1e30)
    row_max = jnp.max(scores, axis=-1, keepdims=True)
    exp_terms = jnp.exp(scores - row_max)
    row_total = jnp.sum(exp_terms, axis=-1, keepdims=True)
    attention = exp_terms / row_total
    context = matmul(attention.astype(jnp.bfloat16), value_part, "ghlm,gmhe->glhe")
    return (join_heads(context).astype(jnp.bfloat16), row_max + jnp.log(row_total))


def attend_backward(query_part, key_part, value_part, allowed, log_total, grad_context):
    head_size = query_part.shape[-1]
    factor = head_size ** (-0.5)
    scores = matmul(query_part, key_part, "glhe,gmhe->ghlm") * factor
    scores = jnp.where(allowed[:, None], scores, -1e30)
    attention = jnp.exp(scores - log_total)
    grad_attention = matmul(grad_context, value_part, "glhe,gmhe->ghlm")
    grad_value = matmul(attention.astype(jnp.bfloat16), grad_context, "ghlm,glhe->gmhe")
    inner = jnp.sum(attention * grad_attention, axis=-1, keepdims=True)
    grad_scores = (attention * (grad_attention - inner)).astype(jnp.bfloat16)
    grad_query = matmul(grad_scores, key_part, "ghlm,gmhe->glhe") * factor
    grad_key = matmul(grad_scores, query_part, "ghlm,glhe->gmhe") * factor
    return (join_heads(grad_query), join_heads(grad_key), join_heads(grad_value))


def segment_attend(packed):
    groups, length, total_width = packed.shape
    model_width = total_width // 3
    allowed = jnp.ones((groups, length, length), dtype=jnp.bool_)
    context, log_total = attend_forward(
        split_heads(packed[..., :model_width]),
        split_heads(packed[..., model_width : 2 * model_width]),
        split_heads(packed[..., 2 * model_width :]),
        allowed,
    )
    return (context, log_total)


def segment_attend_back(packed, log_total, grad_context):
    groups, length, total_width = packed.shape
    model_width = total_width // 3
    allowed = jnp.ones((groups, length, length), dtype=jnp.bool_)
    grad_query, grad_key, grad_value = attend_backward(
        split_heads(packed[..., :model_width]),
        split_heads(packed[..., model_width : 2 * model_width]),
        split_heads(packed[..., 2 * model_width :]),
        allowed,
        log_total,
        split_heads(grad_context),
    )
    return jnp.concatenate([grad_query, grad_key, grad_value], axis=-1)


def cross_attend(packed, allowed):
    model_width = packed.shape[-1] // 3
    remote = lax.all_gather(packed[..., model_width:], "fsdp", axis=1, tiled=True)
    context, log_total = attend_forward(
        split_heads(packed[..., :model_width]),
        split_heads(remote[..., :model_width]),
        split_heads(remote[..., model_width:]),
        allowed,
    )
    return (context, (remote, log_total))


def cross_attend_back(packed, saved, grad_context, allowed):
    remote, log_total = saved
    model_width = packed.shape[-1] // 3
    grad_query, grad_key, grad_value = attend_backward(
        split_heads(packed[..., :model_width]),
        split_heads(remote[..., :model_width]),
        split_heads(remote[..., model_width:]),
        allowed,
        log_total,
        split_heads(grad_context),
    )
    shared = jnp.concatenate([grad_key, grad_value], axis=-1)
    own_part = lax.psum_scatter(
        shared.astype(jnp.bfloat16), "fsdp", scatter_dimension=1, tiled=True
    ).astype(jnp.float32)
    return jnp.concatenate([grad_query, own_part], axis=-1)


def block_forward(states, weights, attend):
    w_qkv, w_out, w_in, w_back, gains, biases = weights
    gains = gains.astype(jnp.float32)
    biases = biases.astype(jnp.float32)
    states_low = states.astype(jnp.bfloat16)
    packed = matmul(states_low, w_qkv, "gld,de->gle").astype(jnp.bfloat16)
    context, saved = attend(packed)
    branch = matmul(context, w_out, "gld,de->gle")
    normed, scaled_one, inverse_one = norm_forward(states + branch, gains[0], biases[0])
    normed_low = normed.astype(jnp.bfloat16)
    hidden = matmul(normed_low, w_in, "gld,df->glf")
    active_low = jax.nn.gelu(hidden, approximate=False).astype(jnp.bfloat16)
    feed_out = matmul(active_low, w_back, "glf,fd->gld")
    result, scaled_two, inverse_two = norm_forward(normed + feed_out, gains[1], biases[1])
    kept = (
        states_low,
        packed,
        context,
        saved,
        scaled_one,
        inverse_one,
        normed_low,
        hidden,
        active_low,
        scaled_two,
        inverse_two,
    )
    return (result, kept)


def block_backward(grad_result, kept, weights, attend_back):
    w_qkv, w_out, w_in, w_back, gains, biases = weights
    gains = gains.astype(jnp.float32)
    (
        states_low,
        packed,
        context,
        saved,
        scaled_one,
        inverse_one,
        normed_low,
        hidden,
        active_low,
        scaled_two,
        inverse_two,
    ) = kept
    grad_sum_two, gain_two, bias_two = norm_backward(grad_result, scaled_two, inverse_two, gains[1])
    grad_feed = grad_sum_two.astype(jnp.bfloat16)
    grad_active = matmul(grad_feed, w_back, "gld,fd->glf")
    cumulative = 0.5 * (1.0 + lax.erf(hidden * root_half))
    slope = cumulative + hidden * inv_root_tau * jnp.exp(-0.5 * hidden * hidden)
    grad_hidden = (grad_active * slope).astype(jnp.bfloat16)
    grad_normed = grad_sum_two + matmul(grad_hidden, w_in, "glf,df->gld")
    grad_sum_one, gain_one, bias_one = norm_backward(grad_normed, scaled_one, inverse_one, gains[0])
    grad_branch = grad_sum_one.astype(jnp.bfloat16)
    grad_context = matmul(grad_branch, w_out, "gle,de->gld").astype(jnp.bfloat16)
    grad_packed = attend_back(packed, saved, grad_context).astype(jnp.bfloat16)
    grad_states = grad_sum_one + matmul(grad_packed, w_qkv, "gle,de->gld")
    factors = (
        states_low,
        grad_packed,
        context,
        grad_branch,
        normed_low,
        grad_hidden,
        grad_feed,
        active_low,
    )
    smalls = (jnp.stack([gain_one, gain_two]), jnp.stack([bias_one, bias_two]))
    return (grad_states, factors, smalls)


def weight_terms(factors):
    (
        states_low,
        grad_packed,
        context,
        grad_branch,
        normed_low,
        grad_hidden,
        grad_feed,
        active_low,
    ) = factors
    term_qkv = matmul(states_low, grad_packed, "gld,gle->de")
    term_out = matmul(context, grad_branch, "gld,gle->de")
    term_in = matmul(normed_low, grad_hidden, "gld,glf->df")
    term_back = matmul(grad_feed, active_low, "gld,glf->df")
    return jnp.concatenate([term_qkv, term_out, term_in, term_back], axis=1)


def gather_segment(w_qkv, w_out, w_in, w_back, norm_gain, norm_bias):
    return (
        lax.all_gather(w_qkv[0], ("dp", "fsdp"), axis=0, tiled=True),
        lax.all_gather(w_out[0], ("dp", "fsdp"), axis=0, tiled=True),
        lax.all_gather(w_in[0], ("dp", "fsdp"), axis=0, tiled=True),
        lax.all_gather(w_back[0], ("dp", "fsdp"), axis=1, tiled=True),
        lax.all_gather(norm_gain[0], ("dp", "fsdp"), axis=1, tiled=True),
        lax.all_gather(norm_bias[0], ("dp", "fsdp"), axis=1, tiled=True),
    )


def gather_cross(pos_embed, w_qkv, w_out, w_in, w_back, norm_gain, norm_bias):
    gathered = (
        lax.all_gather(w_qkv[1], ("dp", "fsdp"), axis=0, tiled=True),
        lax.all_gather(w_out[1], ("dp", "fsdp"), axis=0, tiled=True),
        lax.all_gather(w_in[1], ("dp", "fsdp"), axis=0, tiled=True),
        lax.all_gather(w_back[1], ("dp", "fsdp"), axis=1, tiled=True),
        lax.all_gather(norm_gain[1], ("dp", "fsdp"), axis=1, tiled=True),
        lax.all_gather(norm_bias[1], ("dp", "fsdp"), axis=1, tiled=True),
        lax.all_gather(pos_embed, ("dp", "fsdp"), axis=1, tiled=True),
    )
    return (gathered[:6], gathered[6])


def layer_forward(tokens, doc_ids, seg_weights, cross_weights, pos_full):
    rows, local_len, model_width = tokens.shape
    seg_count = local_len // SEG_LEN
    segments = tokens.reshape(rows * seg_count, SEG_LEN, model_width).astype(jnp.float32)
    seg_out, seg_kept = block_forward(segments, seg_weights, segment_attend)
    start = lax.axis_index("fsdp") * seg_count
    pos_local = lax.dynamic_slice_in_dim(pos_full, start, seg_count, 0).astype(jnp.float32)
    leaders = seg_out[:, 0, :].reshape(rows, seg_count, model_width) + pos_local
    own_docs = lax.dynamic_slice_in_dim(doc_ids, start, seg_count, 1)
    allowed = own_docs[:, :, None] == doc_ids[:, None, :]
    cross_out, cross_kept = block_forward(
        leaders, cross_weights, partial(cross_attend, allowed=allowed)
    )
    joined = jnp.concatenate(
        [cross_out.reshape(rows * seg_count, 1, model_width), seg_out[:, 1:, :]], axis=1
    )
    output = joined.reshape(rows, local_len, model_width).astype(jnp.bfloat16)
    return (output, (seg_kept, cross_kept, allowed))


def layer_backward(cotangent, doc_ids, kept, seg_weights, cross_weights):
    seg_kept, cross_kept, allowed = kept
    rows, local_len, model_width = cotangent.shape
    seg_count = local_len // SEG_LEN
    grad_all = cotangent.reshape(rows * seg_count, SEG_LEN, model_width).astype(jnp.float32)
    grad_cross = grad_all[:, 0, :].reshape(rows, seg_count, model_width)
    grad_leaders, cross_factors, cross_smalls = block_backward(
        grad_cross, cross_kept, cross_weights, partial(cross_attend_back, allowed=allowed)
    )
    start = lax.axis_index("fsdp") * seg_count
    empty_pos = jnp.zeros((doc_ids.shape[1], model_width), jnp.float32)
    grad_pos = lax.dynamic_update_slice_in_dim(empty_pos, jnp.sum(grad_leaders, axis=0), start, 0)
    grad_seg = jnp.concatenate(
        [grad_leaders.reshape(rows * seg_count, 1, model_width), grad_all[:, 1:, :]], axis=1
    )
    grad_states, seg_factors, seg_smalls = block_backward(
        grad_seg, seg_kept, seg_weights, segment_attend_back
    )
    grad_tokens = grad_states.reshape(rows, local_len, model_width).astype(jnp.bfloat16)
    return (grad_tokens, seg_factors, cross_factors, seg_smalls, cross_smalls, grad_pos)


def body(tokens, doc_ids, pos_embed, w_qkv, w_out, w_in, w_back, norm_gain, norm_bias, cotangent):
    seg_weights = gather_segment(w_qkv, w_out, w_in, w_back, norm_gain, norm_bias)
    cross_weights, pos_full = gather_cross(
        pos_embed, w_qkv, w_out, w_in, w_back, norm_gain, norm_bias
    )
    output, kept = layer_forward(tokens, doc_ids, seg_weights, cross_weights, pos_full)
    grad_tokens, seg_factors, cross_factors, seg_smalls, cross_smalls, grad_pos = layer_backward(
        cotangent, doc_ids, kept, seg_weights, cross_weights
    )
    model_width = tokens.shape[2]
    hidden_width = w_in.shape[2]
    seg_term = lax.psum_scatter(
        weight_terms(seg_factors), ("dp", "fsdp"), scatter_dimension=0, tiled=True
    )
    cross_term = lax.psum_scatter(
        weight_terms(cross_factors), ("dp", "fsdp"), scatter_dimension=0, tiled=True
    )
    stacked = jnp.stack([seg_term, cross_term])
    grad_qkv = stacked[:, :, : 3 * model_width]
    grad_out = stacked[:, :, 3 * model_width : 4 * model_width]
    grad_in = stacked[:, :, 4 * model_width : 4 * model_width + hidden_width]
    grad_back = jnp.transpose(stacked[:, :, 4 * model_width + hidden_width :], (0, 2, 1))
    gain_all = jnp.stack([seg_smalls[0], cross_smalls[0]])
    bias_all = jnp.stack([seg_smalls[1], cross_smalls[1]])
    grad_gain, grad_bias, pos_shard = (
        lax.psum_scatter(gain_all, ("dp", "fsdp"), scatter_dimension=2, tiled=True),
        lax.psum_scatter(bias_all, ("dp", "fsdp"), scatter_dimension=2, tiled=True),
        lax.psum_scatter(grad_pos, ("dp", "fsdp"), scatter_dimension=1, tiled=True),
    )
    return (
        output,
        grad_tokens,
        pos_shard,
        grad_qkv,
        grad_out,
        grad_in,
        grad_back,
        grad_gain,
        grad_bias,
    )


def write_kernel(n, *refs):
    sources, smalls = refs[:n], refs[n]
    targets, pos_ref, gain_ref, bias_ref = refs[n + 1 : 2 * n + 1], *refs[2 * n + 1 : 2 * n + 4]
    bufs, sems = refs[2 * n + 4 : 3 * n + 4], refs[3 * n + 4]
    loads = [pltpu.make_async_copy(sources[i], bufs[i], sems.at[0, i]) for i in range(n)]
    copies = [pltpu.make_async_copy(bufs[i], targets[i], sems.at[1, i]) for i in range(n)]
    for load in loads:
        load.start()
    for load, copy in zip(loads, copies):
        load.wait()
        copy.start()
    rows = smalls[:, :LANES].T[:, : smalls.shape[0]]
    pos_ref[...] = rows[8 : 8 + pos_ref.shape[0]]
    for b in range(2):
        gain_ref[b] = rows[4 * b : 4 * b + 2]
        bias_ref[b] = rows[4 * b + 2 : 4 * b + 4]
    for copy in copies:
        copy.wait()


def write_results(arrays, smalls, positions):
    n = len(arrays)
    own = smalls.shape[0]
    hbm, vm = pl.BlockSpec(memory_space=pl.ANY), pl.BlockSpec(memory_space=VM)
    like = [jax.ShapeDtypeStruct(v.shape, v.dtype) for v in arrays]
    shapes = [(positions, own), (2, 2, own), (2, 2, own)]
    return pl.pallas_call(
        partial(write_kernel, n),
        out_shape=like + [jax.ShapeDtypeStruct(v, f32) for v in shapes],
        in_specs=[hbm] * n + [vm],
        out_specs=[hbm] * n + [vm] * 3,
        scratch_shapes=[VM(v.shape, v.dtype) for v in arrays] + [pltpu.SemaphoreType.DMA((2, n))],
    )(*arrays, smalls)


def fast_body(tokens, doc_ids, pos_embed, w_qkv, w_out, w_in, w_back, norm_gain, norm_bias, cotangent):
    nrows, local_len, width = tokens.shape
    rows = nrows * local_len
    x = tokens.reshape(rows, width)
    cot = cotangent.reshape(rows, width)
    output, grad_tokens, g_qkv, g_out, g_in, g_back, t_small = layer(
        w_qkv, w_out, w_in, jnp.swapaxes(w_back, 1, 2), norm_gain, norm_bias, pos_embed, doc_ids, x, cot
    )
    output, grad_tokens, g_qkv, g_out, g_in, g_back, grad_pos, grad_gain, grad_bias = write_results(
        (output, grad_tokens, g_qkv, g_out, g_in, g_back), t_small, doc_ids.shape[1]
    )
    return (
        output.reshape(tokens.shape),
        grad_tokens.reshape(tokens.shape),
        grad_pos,
        g_qkv,
        g_out,
        g_in,
        jnp.swapaxes(g_back, 1, 2),
        grad_gain,
        grad_bias,
    )


def solution(mesh):
    fast = dict(mesh.shape) == {"dp": 4, "fsdp": 8}
    return jax.shard_map(
        fast_body if fast else body,
        mesh=mesh,
        in_specs=(
            P("dp", "fsdp", None),
            P("dp", None),
            P(None, ("dp", "fsdp")),
            P(None, ("dp", "fsdp"), None),
            P(None, ("dp", "fsdp"), None),
            P(None, ("dp", "fsdp"), None),
            P(None, None, ("dp", "fsdp")),
            P(None, None, ("dp", "fsdp")),
            P(None, None, ("dp", "fsdp")),
            P("dp", "fsdp", None),
        ),
        out_specs=(
            P("dp", "fsdp", None),
            P("dp", "fsdp", None),
            P(None, ("dp", "fsdp")),
            P(None, ("dp", "fsdp"), None),
            P(None, ("dp", "fsdp"), None),
            P(None, ("dp", "fsdp"), None),
            P(None, None, ("dp", "fsdp")),
            P(None, None, ("dp", "fsdp")),
            P(None, None, ("dp", "fsdp")),
        ),
        check_vma=False,
    )
```

```python
from functools import partial

import jax
import jax.numpy as jnp
from jax import lax
from jax.experimental import pallas as pl
from jax.experimental.pallas import tpu as pltpu
from jax.sharding import PartitionSpec as P

HEADS = 12
SEG_LEN = 128


epsilon = 1e-05
root_half = 0.7071067811865476
inv_root_tau = 0.3989422804014327

bf16 = jnp.bfloat16
f32 = jnp.float32
MESH = pl.DeviceIdType.MESH
VM = pltpu.VMEM
MIB = 1024 * 1024
ROWS = 48
LANES = 128


class Place:
    def __init__(self):
        self.dp = lax.axis_index("dp")
        self.fsdp = lax.axis_index("fsdp")
        self.y, self.x = self.dp // 2, self.dp % 2
        self.z, self.core = self.fsdp // 2, self.fsdp % 2

    def at(self, dp, z, core):
        return (dp, z * 2 + core)

    @property
    def sib(self):
        return (self.dp, self.z * 2 + 1 - self.core)

    @property
    def xdp(self):
        return self.y * 2 + 1 - self.x

    @property
    def ydp(self):
        return (1 - self.y) * 2 + self.x

    @property
    def xnbr(self):
        return (self.xdp, self.fsdp)

    @property
    def ynbr(self):
        return (self.ydp, self.fsdp)


def greet(devices, meanwhile):
    barrier = pltpu.get_barrier_semaphore()
    for device in devices:
        pl.semaphore_signal(barrier, inc=1, device_id=device, device_id_type=MESH)
    meanwhile()
    pl.semaphore_wait(barrier, len(devices))


def remote(src, dst, send, recv, device):
    return pltpu.make_async_remote_copy(
        src_ref=src, dst_ref=dst, send_sem=send, recv_sem=recv, device_id=device, device_id_type=MESH
    )


def lanes(start, size):
    if isinstance(start, int):
        return pl.ds(start, size)
    return pl.ds(pl.multiple_of(start, LANES), size)


def rows_at(start, size, unit):
    return pl.ds(pl.multiple_of(start, unit), size)


class Gather:
    def __init__(self, place, out, off, width, source, index, sems, height2, wide_a=True):
        self.p, self.out, self.off, self.source = place, out, off, source
        self.m, self.sems, self.h2 = index, sems, height2
        self.half = width // 2
        tiles = self.half // LANES
        self.a = ((tiles + 1) // 2 if wide_a else max(tiles // 2, 1)) * LANES
        self.b = self.half - self.a
        self.sent = []
        self.far = (1 - place.y) * 2 + 1 - place.x

    def cols(self, core, part="AB"):
        at, size = {"A": (0, self.a), "B": (self.a, self.b), "AB": (0, self.half)}[part]
        return lanes(self.off + core * self.half + at, size)

    def block(self, z, core):
        return self.out.at[rows_at((self.p.dp * 4 + z) * self.h2, self.h2, 16), self.cols(core)]

    def group(self, dp, core, part="AB"):
        return self.out.at[rows_at(dp * 4 * self.h2, self.h2 * 4, 16), self.cols(core, part)]

    def go(self, src, dst, slot, device):
        copy = remote(src, dst, self.sems[0].at[self.m, slot], self.sems[1].at[self.m, slot], device)
        copy.start()
        self.sent.append(copy)

    def hand(self, ref, slot):
        self.go(ref, ref, slot, self.p.sib)

    def arrived(self, dst, slot):
        remote(dst, dst, self.sems[0].at[self.m, slot], self.sems[1].at[self.m, slot], self.p.sib).wait_recv()

    def own(self):
        p = self.p
        for d in (1, 3, 2):
            z = (p.z + d) % 4
            self.go(self.source(z), self.block(p.z, p.core), d - 1, p.at(p.dp, z, p.core))

    def line(self):
        p = self.p
        for d in (1, 3, 2):
            self.arrived(self.block((p.z + 4 - d) % 4, p.core), d - 1)
        mine = self.group(p.dp, p.core)
        self.go(mine, mine, 3, p.xnbr)
        self.go(mine, mine, 4, p.ynbr)
        self.hand(mine, 7)

    def plane(self):
        p = self.p
        over_x, over_y = self.group(p.xdp, p.core), self.group(p.ydp, p.core)
        self.arrived(over_x, 3)
        part = self.group(p.xdp, p.core, "A")
        self.go(part, part, 5, p.ynbr)
        self.arrived(over_y, 4)
        if self.b:
            part = self.group(p.ydp, p.core, "B")
            self.go(part, part, 6, p.xnbr)
        self.hand(over_x, 8)
        self.hand(over_y, 9)

    def last(self):
        p = self.p
        self.arrived(self.group(self.far, p.core, "A"), 5)
        if self.b:
            self.arrived(self.group(self.far, p.core, "B"), 6)
        self.hand(self.group(self.far, p.core), 10)

    def drain(self):
        p = self.p
        for slot, dp in ((7, p.dp), (8, p.xdp), (9, p.ydp), (10, self.far)):
            self.arrived(self.group(dp, 1 - p.core), slot)

    def finish(self):
        for copy in self.sent:
            copy.wait_send()


class Staged:
    def __init__(self, units, order):
        self.units, self.order, self.at = units, order, 0

    def step(self, count=1):
        for name, i in self.order[self.at : self.at + count]:
            getattr(self.units[i], name)()
        self.at += count

    def upto(self, name, i):
        spot = self.order.index((name, i)) + 1
        if spot > self.at:
            self.step(spot - self.at)

    def finish(self):
        self.step(len(self.order) - self.at)
        for unit in self.units:
            unit.finish()


def staggered(count, lags, first=0):
    order = []
    for t in range(min(lags.values()), count + max(lags.values())):
        for name, lag in lags.items():
            if 0 <= t - lag < count and (t >= 0 or lag < 0):
                order.append((name, t - lag + first))
    return order


def gather_peers(p):
    peers = [p.sib, p.xnbr, p.ynbr]
    for d in (1, 2, 3):
        peers.append(p.at(p.dp, (p.z + d) % 4, p.core))
    return peers


def everyone(p):
    return [
        (lax.rem(p.dp + i, 4), lax.rem(p.fsdp + j, 8)) for i in range(4) for j in range(8) if i or j
    ]


NEG = -1e30


def mm(a, b, dims):
    return lax.dot_general(a, b, (dims, ((), ())), preferred_element_type=f32)


NN = ((1,), (0,))
NT = ((1,), (1,))
TN = ((0,), (0,))


def norm_rows(summed, gain, bias):
    centred = summed - jnp.mean(summed, axis=-1, keepdims=True)
    variance = jnp.mean(centred * centred, axis=-1, keepdims=True)
    inverse = lax.rsqrt(variance + epsilon)
    scaled = centred * inverse
    return scaled * gain + bias, scaled, inverse


def norm_rows_back(grad, scaled, inverse, gain):
    g = grad * gain
    first = jnp.mean(g, axis=-1, keepdims=True)
    second = jnp.mean(g * scaled, axis=-1, keepdims=True)
    return inverse * (g - first - scaled * second)


def gelu_parts(u):
    cumulative = 0.5 * (1.0 + lax.erf(u * root_half))
    return cumulative, cumulative + u * inv_root_tau * jnp.exp(-0.5 * u * u)


def lane_halves(v):
    low = lax.broadcasted_iota(jnp.int32, v.shape, 1) < LANES // 2
    zero = jnp.zeros_like(v)
    return jnp.where(low, v, zero), jnp.where(low, zero, v)


FORWARD_LAGS = {"own": -3, "line": 0, "plane": 1, "last": 2, "drain": 3}


def forward_order(n_seg, n_cross):
    n = n_seg + n_cross
    order = staggered(n, FORWARD_LAGS)
    stop = order.index(("line", n_seg))
    head, rest = order[:stop], order[stop:]
    head += [s for s in rest if s[0] == "own"]
    done = set(head)
    tail = [("plane", n_seg - 1), ("line", n_seg), ("line", n_seg + 1)]
    for u in range(n_seg - 3, n_seg):
        tail += [("last", u), ("drain", u)]
    tail += [("plane", n_seg), ("line", n_seg + 2)]
    for u in range(n_seg, n):
        tail += [("last", u), ("plane", u + 1), ("drain", u)]
    return head + [s for s in tail if s not in done and s[1] < n]


class Scatter:
    def __init__(self, place, grad, off, width, out, index, sems, bufs, wide_a=True):
        self.p, self.grad, self.off, self.out, self.m = place, grad, off, out, index
        self.send, self.recv = sems
        self.pair, self.r1a, self.r1b, self.rx, self.ry, self.r3, self.give = bufs
        self.half = width // 2
        self.a = split_half(width, wide_a)
        self.b = self.half - self.a
        self.sent = []
        self.free, self.waits, self.frees = None, False, False
        p = place
        self.far = (1 - p.y) * 2 + 1 - p.x
        self.groups = (self.far, p.xdp, p.ydp, p.dp)

    def go(self, src, dst, slot, device):
        copy = remote(src, dst, self.send.at[self.m, slot], self.recv.at[self.m, slot], device)
        copy.start()
        self.sent.append(copy)

    def arrived(self, dst, slot):
        remote(dst, dst, self.send.at[self.m, slot], self.recv.at[self.m, slot], self.p.sib).wait_recv()

    def cols(self, part="AB", core=None):
        at, size = {"A": (0, self.a), "B": (self.a, self.b), "AB": (0, self.half)}[part]
        core = self.p.core if core is None else core
        return lanes(self.off + core * self.half + at, size)

    def group(self, dp):
        return rows_at(dp * 4 * ROWS, 4 * ROWS, 16)

    def side(self, dp, part="AB"):
        return self.grad.at[self.group(dp), self.cols(part)]

    def start(self):
        p = self.p
        if self.waits:
            pl.semaphore_wait(self.free, 1)
        for i, dp in enumerate(self.groups):
            theirs = self.grad.at[self.group(dp), self.cols("AB", 1 - p.core)]
            self.go(theirs, self.pair.at[self.group(dp)], i, p.sib)

    def add(self, dp, part, other, other_row=0):
        @pl.loop(0, 4)
        def _(i):
            key = (rows_at(dp * 4 * ROWS + i * ROWS, ROWS, 16), self.cols(part))
            self.grad[key] = self.grad[key] + other[rows_at(other_row + i * ROWS, ROWS, 16), :]

    def one(self):
        p = self.p
        for i, dp in enumerate(self.groups):
            self.arrived(self.pair.at[self.group(dp)], i)
            self.add(dp, "AB", self.pair, dp * 4 * ROWS)
            if i == 0:
                self.go(self.side(dp, "A"), self.r1a, 4, p.ynbr)
                if self.b:
                    self.go(self.side(dp, "B"), self.r1b, 5, p.xnbr)
        if self.frees:
            pl.semaphore_signal(self.free, inc=1, device_id=p.sib, device_id_type=MESH)

    def two(self):
        p = self.p
        self.arrived(self.r1a, 4)
        self.add(p.xdp, "A", self.r1a)
        self.go(self.side(p.xdp), self.rx, 6, p.xnbr)
        if self.b:
            self.arrived(self.r1b, 5)
            self.add(p.ydp, "B", self.r1b)
        self.go(self.side(p.ydp), self.ry, 7, p.ynbr)

    def three(self):
        p = self.p
        self.arrived(self.rx, 6)
        self.arrived(self.ry, 7)

        @pl.loop(0, 4)
        def _(i):
            key = (rows_at(p.dp * 4 * ROWS + i * ROWS, ROWS, 16), self.cols())
            own = rows_at(i * ROWS, ROWS, 16)
            self.grad[key] = self.grad[key] + (self.rx[own, :] + self.ry[own, :])

        for d in (1, 3, 2):
            z = (p.z + d) % 4
            src = self.grad.at[rows_at((p.dp * 4 + z) * ROWS, ROWS, 16), self.cols()]
            self.go(src, self.r3.at[d - 1], 7 + d, p.at(p.dp, z, p.core))

    def four(self):
        p = self.p
        for d in (1, 3, 2):
            self.arrived(self.r3.at[d - 1], 7 + d)
        rows = rows_at((p.dp * 4 + p.z) * ROWS, ROWS, 16)
        total = self.grad[rows, self.cols()].astype(f32)
        for d in range(3):
            total = total + self.r3[d].astype(f32)
        upper, lower = total[: ROWS // 2], total[ROWS // 2 :]
        first = p.core == 0
        self.give[...] = jnp.where(first, lower, upper)
        self.out[:, self.cols()] = jnp.where(first, upper, lower)
        self.go(self.give, self.out.at[:, self.cols()], 11, p.sib)

    def five(self):
        self.arrived(self.out.at[:, self.cols("AB", 1 - self.p.core)], 11)

    def finish(self):
        for copy in self.sent:
            copy.wait_send()


def split_half(width, wide_a):
    tiles = width // 2 // LANES
    return ((tiles + 1) // 2 if wide_a else max(tiles // 2, 1)) * LANES


def scatter_buffers(width, wide_a):
    half = width // 2
    a = split_half(width, wide_a)
    b = half - a
    return [
        VM((4 * ROWS, a), bf16),
        VM((4 * ROWS if b else 16, max(b, LANES)), bf16),
        VM((4 * ROWS, half), bf16),
        VM((4 * ROWS, half), bf16),
        VM((3, ROWS, half), bf16),
        VM((ROWS // 2, half), f32),
    ]


SCATTER_LAGS = {"start": 0, "one": 1, "two": 2, "three": 4, "four": 7, "five": 9}
PAIR_SLOTS = 4


def tail_units(width):
    return [(0, width), (width, width), (2 * width, width - 256), (3 * width - 256, 256)]


def scatter_step(sums, jobs):
    begun = len([s for s in sums.order[: sums.at] if s[0] == "start"])
    follow = [i for i, s in enumerate(sums.order) if s == ("start", begun + 1)]
    if begun < len(jobs):
        sums.step((follow[0] if follow else sums.order.index(("start", begun)) + 1) - sums.at)


def layer_kernel(*refs):
    wq_ref, wo_ref, wi_ref, wb_ref, gain_ref, bias_ref, pos_ref, docs_ref, x_hbm, cot_hbm = refs[:10]
    y_ref, gt_ref, gq_ref, go_ref, gi_ref, gb_ref, gs_ref = refs[10:17]
    (
        sw, ow, qw, iw, bw, cw, cwo,
        pk, at, cx, h, nl, g, sl, z1, z2, r1_ref, r2_ref, par_ref,
        x_ref, cot_ref, in_sem, own_buf, sib_buf, block, square,
        lead_out, gbuf, lead, xbuf, ybuf, dpack, home_y, home_dx, dbuf, dland, fac, fac_sib, csmall,
        df, tr, tr2, dws, small, full, tmp, ring, pair_wide, pair_small,
        s_send, s_recv, pair_send, pair_recv, wo_send, wo_recv, local,
        g_send, g_recv, x_send, x_recv, h_send, h_recv, lead_sem, d_send, d_recv,
        f_send, f_recv, swap_send, swap_recv, rs_send, rs_recv, free,
    ) = refs[17:89]
    bufs = refs[89:]
    p = Place()
    inputs = [
        pltpu.make_async_copy(x_hbm, x_ref, in_sem.at[0]),
        pltpu.make_async_copy(cot_hbm, cot_ref, in_sem.at[1]),
    ]
    for copy in inputs:
        copy.start()
    rows, width = x_ref.shape
    segs = rows // SEG_LEN
    hidden = iw.shape[1]
    pairs = width // LANES
    slab = width // 4
    cross_width = cw.shape[1]
    half_rows = ROWS // 2
    key_own = rows_at((p.dp * 4 + p.z) * ROWS, ROWS, 16)

    sizes = [sw.shape[1]] + [width] * (3 + 1 + 2 * (hidden // width)) + [4 * cross_width, width]
    starts = [sum(sizes[:i]) for i in range(len(sizes))]
    n_seg = len(sizes) - 2
    part_cross, part_wo = n_seg, n_seg + 1

    def put(start, value):
        zero = jnp.zeros((own_buf.shape[0] - half_rows, value.shape[1]), f32)
        full = jnp.concatenate([value.astype(f32), zero], axis=0).astype(bf16)
        own_buf[:, pl.ds(start, value.shape[1])] = full

    def pair(i):
        cols = pl.ds(starts[i], sizes[i])
        return remote(
            own_buf.at[:, cols], sib_buf.at[:, cols], pair_send.at[i], pair_recv.at[i], p.sib
        )

    def stage(i):
        spot = starts[i]
        per = hidden // width
        if i == 0:
            own = gain_ref.shape[2]
            square[...] = jnp.zeros_like(square)
            for b in range(2):
                square[4 * b : 4 * b + 2, :own] = gain_ref[b].astype(f32)
                square[4 * b + 2 : 4 * b + 4, :own] = bias_ref[b].astype(f32)
            square[8 : 8 + pos_ref.shape[0], :own] = pos_ref[...].astype(f32)
            turned = square[...].T[:half_rows]
            put(spot, jnp.concatenate([turned, jnp.zeros_like(turned)], axis=1))
        elif i < 4:
            put(spot, wq_ref[0, :, (i - 1) * width : i * width])
        elif i == 4:
            put(spot, wo_ref[0])
        elif i < 5 + per:
            put(spot, wi_ref[0, :, (i - 5) * width : (i - 4) * width])
        elif i < 5 + 2 * per:
            put(spot, wb_ref[0, :, (i - 5 - per) * width : (i - 4 - per) * width])
        elif i == part_cross:
            for z in range(4):
                heads = [wq_ref[1, :, j * width + z * slab : j * width + (z + 1) * slab] for j in range(3)]
                heads.append(heads[2])
                put(spot, jnp.concatenate([v.astype(f32) for v in heads], axis=1).astype(bf16))
                put(spot + width, wi_ref[1, :, z * width : (z + 1) * width])
                put(spot + 2 * width, wb_ref[1, :, z * width : (z + 1) * width])
                spot += cross_width
        else:
            put(spot, wo_ref[1])

    def joined(start, size):
        cols = lanes(start, size)
        first = p.core == 0
        mine = own_buf[:, cols].astype(f32)[:half_rows]
        theirs = sib_buf[:, cols].astype(f32)[:half_rows]
        both = [jnp.where(first, mine, theirs), jnp.where(first, theirs, mine)]
        return jnp.concatenate(both, axis=0).astype(bf16)

    ahead = 4

    def begin(i):
        if i < n_seg + 2:
            stage(i)
            pair(i).start()

    greet(everyone(p), lambda: [stage(i) for i in range(ahead)])
    for i in range(ahead):
        pair(i).start()

    sems = (s_send, s_recv)
    dests = [(sw, 0)] + [(qw, i * width) for i in range(3)] + [(ow, 0)]
    dests += [(iw, i * width) for i in range(hidden // width)]
    dests += [(bw, i * width) for i in range(hidden // width)]

    class SegUnit(Gather):
        def __init__(self, i):
            dst, off = dests[i]
            mine = lambda z: dst.at[key_own, self.cols(p.core)]
            super().__init__(p, dst, off, sizes[i], mine, i, sems, ROWS, i % 2 == 0)
            self.i = i

        def own(self):
            pair(self.i).wait_recv()
            self.out[key_own, self.cols(p.core)] = joined(
                starts[self.i] + p.core * self.half, self.half
            )
            super().own()
            begin(self.i + ahead)

    class CrossUnit(Gather):
        def __init__(self, i):
            start = i * width
            self.i = i

            def mine(z):
                spot = z * cross_width + start + p.core * self.half
                return block.at[:, lanes(spot, self.half)]

            super().__init__(p, cw, start, width, mine, n_seg + i, sems, ROWS, i % 2 == 0)

        def own(self):
            if self.i == 0:
                pair(part_cross).wait_recv()

                @pl.loop(0, 4 * cross_width // width)
                def _(k):
                    block[:, lanes(k * width, width)] = joined(starts[part_cross] + k * width, width)

            spot = p.z * cross_width + self.i * width + p.core * self.half
            self.out[key_own, self.cols(p.core)] = block[:, lanes(spot, self.half)]
            super().own()

    units = [SegUnit(i) for i in range(n_seg)] + [CrossUnit(i) for i in range(cross_width // width)]
    n_cross = len(units) - n_seg
    comm = Staged(units, forward_order(n_seg, n_cross))

    def need(i):
        comm.upto("drain", i)

    def pump():
        comm.step(5)

    half_wo = width // 2
    wo_block = block.at[:, pl.ds(4 * cross_width, width)]
    wo_src = block.at[:, lanes(4 * cross_width + p.core * half_wo, half_wo)]
    wo_dst = cwo.at[rows_at(p.z * ROWS, ROWS, 16), lanes(p.core * half_wo, half_wo)]

    def wo_copy(i):
        return remote(wo_src, wo_dst, wo_send.at[i], wo_recv.at[p.z], p.at(i, p.dp, p.core))

    def wo_start():
        pair(part_wo).wait_recv()
        wo_block[...] = joined(starts[part_wo], width)
        for i in range(4):
            here = jnp.logical_and(p.dp == i, p.dp == p.z)

            @pl.when(jnp.logical_not(here))
            def _():
                wo_copy(i).start()

            @pl.when(here)
            def _():
                mine = pltpu.make_async_copy(wo_src, wo_dst, local)
                mine.start()
                mine.wait()

    wo_mine = cwo.at[:, lanes(p.core * half_wo, half_wo)]
    wo_theirs = cwo.at[:, lanes((1 - p.core) * half_wo, half_wo)]
    wo_hand = remote(wo_mine, wo_mine, wo_send.at[4], wo_recv.at[4], p.sib)

    def wo_middle():
        for i in range(4):
            piece = cwo.at[pl.ds(i * ROWS, ROWS), lanes(p.core * half_wo, half_wo)]

            @pl.when(jnp.logical_not(jnp.logical_and(p.z == p.dp, p.z == i)))
            def _():
                remote(piece, piece, wo_send.at[i], wo_recv.at[i], p.sib).wait_recv()

        wo_hand.start()

    def wo_finish():
        remote(wo_theirs, wo_theirs, wo_send.at[4], wo_recv.at[4], p.sib).wait_recv()
        wo_hand.wait_send()
        for i in range(4):

            @pl.when(jnp.logical_not(jnp.logical_and(p.dp == i, p.dp == p.z)))
            def _():
                wo_copy(i).wait_send()

    tile = 256

    def params():
        par_ref[...] = sw[...].astype(f32).T[: par_ref.shape[0]]

    def project(first, count):
        @pl.loop(first, first + count)
        def _(i):
            cols = lanes(i * tile, tile)
            pk[:, cols] = mm(x_ref[...], qw[:, cols], NN).astype(bf16)

    def attend(s):
        key = pl.ds(s * SEG_LEN, SEG_LEN)

        @pl.loop(0, pairs, unroll=True)
        def _(j):
            q2 = pk[key, lanes(j * LANES, LANES)]
            k2 = pk[key, lanes(width + j * LANES, LANES)]
            v2 = pk[key, lanes(2 * width + j * LANES, LANES)]
            scores = mm(jnp.concatenate(lane_halves(q2), axis=0), k2, NT) * (LANES // 2) ** (-0.5)
            top = jnp.max(scores, axis=-1, keepdims=True)
            terms = jnp.exp(scores - top)
            a = (terms / jnp.sum(terms, axis=-1, keepdims=True)).astype(bf16)
            at[rows_at((s * pairs + j) * 2 * SEG_LEN, 2 * SEG_LEN, 16), :] = a
            both = jnp.concatenate([a[:SEG_LEN], a[SEG_LEN:]], axis=1)
            c2 = mm(both, jnp.concatenate(lane_halves(v2), axis=0), NN)
            cx[key, lanes(j * LANES, LANES)] = c2.astype(bf16)

    block_rows = 64

    def branch():
        @pl.loop(0, width // tile)
        def _(i):
            cols = lanes(i * tile, tile)
            h[:, cols] = x_ref[:, cols].astype(f32) + mm(cx[...], ow[:, cols], NN)

        @pl.loop(0, rows // block_rows, unroll=2)
        def _(i):
            key = rows_at(i * block_rows, block_rows, 16)
            normed, scaled, inverse = norm_rows(h[key, :], par_ref[0:1, :], par_ref[2:3, :])
            h[key, :] = normed
            nl[key, :] = normed.astype(bf16)
            z1[key, :] = scaled.astype(bf16)
            r1_ref[key, :] = jnp.broadcast_to(inverse, (block_rows, LANES))

    def feed_in(first, count):
        @pl.loop(first, first + count)
        def _(i):
            cols = lanes(i * tile, tile)
            u = mm(nl[...], iw[:, cols], NN)
            phi, slope = gelu_parts(u)
            g[:, cols] = (u * phi).astype(bf16)
            sl[:, cols] = slope.astype(bf16)

    def feed_back(part):
        inner = pl.ds(part * width, width)

        @pl.loop(0, width // tile)
        def _(i):
            cols = lanes(i * tile, tile)
            h[:, cols] += mm(g[:, inner], bw[rows_at(i * tile, tile, 16), inner], NT)

    def finish_block():
        @pl.loop(0, rows // block_rows, unroll=2)
        def _(i):
            key = rows_at(i * block_rows, block_rows, 16)
            result, scaled, inverse = norm_rows(h[key, :], par_ref[1:2, :], par_ref[3:4, :])
            h[key, :] = result
            y_ref[key, :] = result.astype(bf16)
            z2[key, :] = scaled.astype(bf16)
            r2_ref[key, :] = jnp.broadcast_to(inverse, (block_rows, LANES))

    def leaders():
        first = [h[s * SEG_LEN : s * SEG_LEN + 1, :] for s in range(segs)]
        result = norm_rows(jnp.concatenate(first, axis=0), par_ref[1:2, :], par_ref[3:4, :])[0]
        for s in range(segs):
            pos = par_ref[pl.ds(8 + p.fsdp * 2 + s % 2, 1), :]
            lead_out[s // 2, s % 2 : s % 2 + 1, :width] = result[s : s + 1] + pos
            lead_out[s // 2, s % 2 : s % 2 + 1, width:] = cot_ref[s * SEG_LEN : s * SEG_LEN + 16, :].astype(f32)[:1]

    def lead_copy(z, j):
        i = 2 * z + j
        return remote(lead_out.at[j], gbuf.at[p.fsdp], g_send.at[i], g_recv.at[p.fsdp], (p.dp, i))


    leads = fac.shape[0]
    lead2 = 2 * leads
    key_f = rows_at((p.dp * 4 + p.z) * lead2, lead2, 16)

    def swap(i):
        cols = pl.ds(i * width, width)
        return remote(fac.at[:, cols], fac_sib.at[:, cols], swap_send.at[i], swap_recv.at[i], p.sib)

    def give_factor(i, value):
        fac[:, i * width : (i + 1) * width] = value
        swap(i).start()

    class Factor(Gather):
        def __init__(self, i):
            mine = lambda z: full.at[key_f, self.cols(p.core)]
            super().__init__(p, full, i * width, width, mine, i, (f_send, f_recv), lead2, i % 2 == 0)
            self.i = i

        def own(self):
            swap(self.i).wait_recv()
            base = (p.dp * 4 + p.z) * lead2
            cols = lanes(self.i * width + p.core * (width // 2), width // 2)
            full[rows_at(base + p.core * leads, leads, 16), cols] = fac[:, cols]
            full[rows_at(base + (1 - p.core) * leads, leads, 16), cols] = fac_sib[:, cols]
            super().own()

    factors = [Factor(i) for i in range(4)]

    def factor_grads():
        def rows_of(z, at_col, size):
            return jnp.concatenate(
                [full[rows_at((i * 4 + z) * lead2, lead2, 16), pl.ds(at_col, size)] for i in range(4)],
                axis=0,
            )

        base = 2 * width
        own = rows_at(p.fsdp * (ROWS // 2), ROWS // 2, 8)
        xl = rows_of(p.dp, base, slab)
        nlf = rows_of(p.dp, base + slab, slab)
        dff = rows_of(p.dp, base + 2 * slab, slab)
        ctx = rows_of(p.dp, base + 3 * slab, slab)
        for z in range(4):
            tmp[:, :width] = mm(dff, rows_of(z, 0, width), TN)
            gb_ref[1, :, z * width : (z + 1) * width] = tmp[own, :width]
            tmp[:, :width] = mm(nlf, rows_of(z, width, width), TN)
            gi_ref[1, :, z * width : (z + 1) * width] = tmp[own, :width]
            tmp[:, : 3 * slab] = mm(xl, rows_of(z, 3 * width, 3 * slab), TN)
            got = tmp[own, : 3 * slab]
            for j in range(3):
                spot = j * width + z * slab
                gq_ref[1, :, spot : spot + slab] = got[:, j * slab : (j + 1) * slab]
            tmp[:, :slab] = mm(ctx, rows_of(z, 3 * width + 3 * slab, slab), TN)
            go_ref[1, :, z * slab : (z + 1) * slab] = tmp[own, :slab]


    n_tiles = width // tile
    head = width // HEADS
    heads = HEADS // 4

    def cross():
        for d in range(4):
            z = (p.z + d) % 4
            for j in range(2):
                if d:
                    lead_copy(z, j).start()
                else:

                    @pl.when(p.core != j)
                    def _():
                        lead_copy(z, j).start()

                    @pl.when(p.core == j)
                    def _():
                        mine = pltpu.make_async_copy(lead_out.at[j], gbuf.at[p.fsdp], lead_sem)
                        mine.start()
                        mine.wait()

        comm.upto("plane", n_seg)
        comm.upto("line", n_seg + 2)
        finish_block()
        need(n_seg)
        wo_middle()
        for d in range(1, 8):
            i = lax.rem(p.fsdp + d, 8)
            remote(gbuf.at[i], gbuf.at[i], g_send.at[i], g_recv.at[i], p.sib).wait_recv()
        for i in range(8):
            lead[2 * i : 2 * i + 2, :] = gbuf[i]
        states = lead[:, :width]
        cot_rows = lead[:, width:]

        def sum_z(e, partial_sum, between):
            xbuf[e, p.z] = partial_sum.astype(bf16)
            copies = []
            for d in (1, 3, 2):
                z = (p.z + d) % 4
                copy = remote(
                    xbuf.at[e, p.z], xbuf.at[e, p.z], x_send.at[e, d - 1], x_recv.at[e, p.z],
                    p.at(p.dp, z, p.core),
                )
                copy.start()
                copies.append(copy)
            between()
            for d in (1, 3, 2):
                z = (p.z + d) % 4
                piece = xbuf.at[e, z]
                remote(piece, piece, x_send.at[e, d - 1], x_recv.at[e, z], p.sib).wait_recv()
            for copy in copies:
                copy.wait_send()
            return sum(xbuf[e, z].astype(f32) for z in range(4))

        gain0, gain1 = par_ref[4:5, :], par_ref[5:6, :]
        bias0, bias1 = par_ref[6:7, :], par_ref[7:8, :]
        in_cols, back_cols = pl.ds(width, width), pl.ds(2 * width, width)
        qkv_cols = pl.ds(0, 3 * slab)
        factor = head ** (-0.5)
        docs = docs_ref[...].astype(f32)
        number = docs.shape[1]
        square[:number, :number] = jnp.broadcast_to(
            jnp.where(p.core == 0, docs[0:1], docs[1:2]), (number, number)
        )
        allowed = square[:number, :number] == square[...].T[:number, :number]

        def part(full):
            pieces = [full[:, i * slab : (i + 1) * slab] for i in range(4)]
            out = pieces[0]
            for i in range(1, 4):
                out = jnp.where(p.z == i, pieces[i], out)
            return out.astype(bf16)

        xl = states.astype(bf16)
        packed = mm(xl, cw[:, qkv_cols], NN).astype(bf16)
        q = [packed[:, i * head : (i + 1) * head] for i in range(heads)]
        k = [packed[:, slab + i * head : slab + (i + 1) * head] for i in range(heads)]
        v = [packed[:, 2 * slab + i * head : 2 * slab + (i + 1) * head] for i in range(heads)]
        att, context = [], []
        for i in range(heads):
            scores = jnp.where(allowed, mm(q[i], k[i], NT) * factor, NEG)
            top = jnp.max(scores, axis=-1, keepdims=True)
            terms = jnp.exp(scores - top)
            a = terms / jnp.sum(terms, axis=-1, keepdims=True)
            att.append(a)
            context.append(mm(a.astype(bf16), v[i], NN))
        context = jnp.concatenate(context, axis=1).astype(bf16)
        wo_finish()
        branch = sum_z(0, mm(context, cwo[...], NN), norm_two)
        normed, z_one, r_one = norm_rows(states + branch, gain0, bias0)
        nl = normed.astype(bf16)
        need(n_seg + 1)
        hidden = mm(nl, cw[:, in_cols], NN)
        phi, slope = gelu_parts(hidden)
        active = (hidden * phi).astype(bf16)
        give_factor(0, active)
        need(n_seg + 2)

        def during_one():
            factors[0].own()

        feed = sum_z(1, mm(active, cw[:, back_cols], NT), during_one)
        result, z_two, r_two = norm_rows(normed + feed, gain1, bias1)
        d_two = norm_rows_back(cot_rows, z_two, r_two, gain1)
        df = d_two.astype(bf16)
        du = (mm(df, cw[:, back_cols], NN) * slope).astype(bf16)
        give_factor(1, du)
        give_factor(2, jnp.concatenate([part(states), part(normed), part(d_two), context], axis=1))

        for i in range(8):
            ybuf[i] = result[2 * i : 2 * i + 2]
        home = remote(ybuf.at[2 * p.z + 1 - p.core], home_y.at[p.core], h_send, h_recv, p.sib)

        def during_two():
            home.start()
            home_y[p.core] = ybuf[2 * p.z + p.core]
            factors[0].line()
            factors[1].own()

        d_normed = d_two + sum_z(2, mm(du, cw[:, in_cols], NT), during_two)
        d_one = norm_rows_back(d_normed, z_one, r_one, gain0)
        db = d_one.astype(bf16)
        dc = mm(db, cwo[...], NT).astype(bf16)
        for i in range(heads):
            a = att[i]
            dci = dc[:, i * head : (i + 1) * head]
            da = mm(dci, v[i], NT)
            dv = mm(a.astype(bf16), dci, TN)
            ds = (a * (da - jnp.sum(a * da, axis=-1, keepdims=True))).astype(bf16)
            dq = mm(ds, k[i], NN) * factor
            dk = mm(ds, q[i], TN) * factor
            for j, piece in enumerate((dq, dk, dv)):
                dpack[:, j * slab + i * head : j * slab + (i + 1) * head] = piece
        dp = dpack[...].astype(bf16)
        give_factor(3, jnp.concatenate([dp, part(d_one)], axis=1))

        def during_three():
            factors[0].plane()
            factors[2].own()
            factors[1].line()

        partial_dx = mm(dp, cw[:, qkv_cols], NT)
        for i in range(8):
            mine = jnp.where(p.z == i // 2, 1.0, 0.0) * d_one[2 * i : 2 * i + 2]
            dbuf[i] = partial_dx[2 * i : 2 * i + 2] + mine
        sent = []
        for d in range(1, 8):
            i = lax.rem(p.fsdp + d, 8)
            copy = remote(dbuf.at[i], dland.at[p.fsdp], d_send.at[d], d_recv.at[p.fsdp], (p.dp, i))
            copy.start()
            sent.append(copy)
        during_three()
        dland[p.fsdp] = dbuf[p.fsdp]
        for d in range(1, 8):
            i = lax.rem(p.fsdp + d, 8)
            remote(dland.at[i], dland.at[i], d_send.at[d], d_recv.at[i], p.sib).wait_recv()
        for j in range(2):
            home_dx[j] = (dland[j] + dland[2 + j]) + (dland[4 + j] + dland[6 + j])
        for copy in sent:
            copy.wait_send()
        once = jnp.where(p.z == 0, 1.0, 0.0)
        sums_of = [d_normed * z_one, cot_rows * z_two, d_normed, cot_rows]
        csmall[...] = jnp.zeros_like(csmall)
        for i, s in enumerate(sums_of):
            csmall[i : i + 1, :] = once * jnp.sum(s, axis=0, keepdims=True)
        theirs = home_y.at[1 - p.core]
        remote(theirs, theirs, h_send, h_recv, p.sib).wait_recv()
        home.wait_send()

    def wait_leads():
        for d in range(4):
            z = (p.z + d) % 4
            for j in range(2):
                if d:
                    lead_copy(z, j).wait_send()
                else:

                    @pl.when(p.core != j)
                    def _():
                        lead_copy(z, j).wait_send()


    def patch():
        for s in range(segs):
            spot = pl.ds(s * SEG_LEN, 16)
            old = y_ref[spot, :].astype(f32)
            new = jnp.broadcast_to(home_y[s // 2, s % 2 : s % 2 + 1, :], old.shape)
            top = lax.broadcasted_iota(jnp.int32, old.shape, 0) == 0
            y_ref[spot, :] = jnp.where(top, new, old).astype(bf16)
    per = hidden // width
    parts = [(bw, i * width, width, gb_ref.at[0]) for i in range(per)]
    parts += [(iw, i * width, width, gi_ref.at[0]) for i in range(per)]
    parts += [(ow, 0, width, go_ref.at[0]), (dws, 0, dws.shape[1], gs_ref)]
    parts += [(qw, at_col, size, gq_ref.at[0]) for at_col, size in tail_units(width)]
    jobs, shared = [], []
    for i, (grad, off, size, dst) in enumerate(parts):
        job_bufs = list(bufs[6 * i : 6 * i + 6])
        if size == width:
            slot = len(shared) % PAIR_SLOTS
            job = Scatter(p, grad, off, size, dst, i, (rs_send, rs_recv), [ring.at[slot]] + job_bufs, i % 2 == 0)
            job.free = free.at[slot]
            if len(shared) >= PAIR_SLOTS:
                job.waits = True
                shared[len(shared) - PAIR_SLOTS].frees = True
            shared.append(job)
        else:
            own_pair = pair_wide if size > 256 else pair_small.at[len([j for j in jobs if j.half == LANES])]
            job = Scatter(p, grad, off, size, dst, i, (rs_send, rs_recv), [own_pair] + job_bufs, i % 2 == 0)
        jobs.append(job)
    sums = Staged(jobs, staggered(len(jobs), SCATTER_LAGS))


    def norm_back(z_ref, r_ref, gain_row, low_ref, sums):
        def step(i, acc):
            key = rows_at(i * block_rows, block_rows, 16)
            dy = h[key, :]
            z = z_ref[key, :].astype(f32)
            r = jnp.concatenate([r_ref[key, :]] * (width // LANES), axis=1)
            e = dy * par_ref[gain_row : gain_row + 1, :]
            first = jnp.mean(e, axis=-1, keepdims=True)
            second = jnp.mean(e * z, axis=-1, keepdims=True)
            d = r * (e - first - z * second)
            h[key, :] = d
            low_ref[key, :] = d.astype(bf16)
            fold = lambda v: jnp.sum(v.reshape(block_rows // 8, 8, width), axis=0)
            return acc[0] + fold(dy * z), acc[1] + fold(dy)

        zero = jnp.zeros((8, width), f32)
        gain, bias = lax.fori_loop(0, rows // block_rows, step, (zero, zero), unroll=2)
        small[sums : sums + 1, :] = jnp.sum(gain, axis=0, keepdims=True)
        small[sums + 2 : sums + 3, :] = jnp.sum(bias, axis=0, keepdims=True)

    def turn(tr, ref):
        @pl.loop(0, width // tile)
        def _(i):
            tr[rows_at(i * tile, tile, 16), :] = ref[:, lanes(i * tile, tile)].T

    def outer(dst, tr, src, first, size):
        @pl.loop(first // tile, (first + size) // tile)
        def _(i):
            cols = lanes(i * tile, tile)
            dst[:, cols] = mm(tr[...], src[:, cols], NN).astype(bf16)

    def norm_two():
        @pl.loop(0, rows // block_rows)
        def _(i):
            key = rows_at(i * block_rows, block_rows, 16)
            h[key, :] = cot_ref[key, :].astype(f32)

        for s in range(segs):
            h[s * SEG_LEN : s * SEG_LEN + 1, :] = jnp.zeros((1, width), f32)
        small[...] = jnp.zeros_like(small)
        norm_back(z2, r2_ref, 1, df, 1)

    def norm_leaders():
        pick = lambda take: jnp.concatenate([take(s * SEG_LEN) for s in range(segs)], axis=0)
        dy = jnp.concatenate([home_dx[s // 2, s % 2 : s % 2 + 1, :] for s in range(segs)], axis=0)
        z = pick(lambda row: z2[row : row + 16, :].astype(f32)[:1])
        r = pick(lambda row: jnp.concatenate([r2_ref[row : row + 1, :]] * (width // LANES), axis=1))
        d = norm_rows_back(dy, z, r, par_ref[1:2, :])
        for s in range(segs):
            h[s * SEG_LEN : s * SEG_LEN + 1, :] = d[s : s + 1]
            spot = pl.ds(s * SEG_LEN, 16)
            old = df[spot, :].astype(f32)
            top = lax.broadcasted_iota(jnp.int32, old.shape, 0) == 0
            df[spot, :] = jnp.where(top, jnp.broadcast_to(d[s : s + 1], old.shape), old).astype(bf16)
        small[1:2, :] += jnp.sum(dy * z, axis=0, keepdims=True)
        small[3:4, :] += jnp.sum(dy, axis=0, keepdims=True)
        small[4:8, :] = csmall[0:4, :]
        for s in range(2):
            row = home_dx[0, s : s + 1, :] + home_dx[1, s : s + 1, :]
            small[pl.ds(8 + p.fsdp * 2 + s, 1), :] = row
        turn(tr, df)

    def active_back(part):
        @pl.loop(part * n_tiles, (part + 1) * n_tiles)
        def _(i):
            cols = lanes(i * tile, tile)
            d = mm(df[...], bw[:, cols], NN) * sl[:, cols].astype(f32)
            sl[:, cols] = d.astype(bf16)

    def add_back(src, weight, first, size):
        inner = pl.ds(first, size)

        @pl.loop(0, n_tiles)
        def _(i):
            cols = lanes(i * tile, tile)
            h[:, cols] += mm(src[:, inner], weight[rows_at(i * tile, tile, 16), inner], NT)

    def context_back():
        @pl.loop(0, width // tile)
        def _(i):
            d = mm(df[...], ow[rows_at(i * tile, tile, 16), :], NT)
            cx[:, lanes(i * tile, tile)] = d.astype(bf16)

    def attend_back(s):
        key = pl.ds(s * SEG_LEN, SEG_LEN)
        factor = (LANES // 2) ** (-0.5)

        @pl.loop(0, pairs, unroll=True)
        def _(j):
            a = at[rows_at((s * pairs + j) * 2 * SEG_LEN, 2 * SEG_LEN, 16), :]
            q_cols = lanes(j * LANES, LANES)
            k_cols = lanes(width + j * LANES, LANES)
            v_cols = lanes(2 * width + j * LANES, LANES)
            qs = jnp.concatenate(lane_halves(pk[key, q_cols]), axis=0)
            ks = jnp.concatenate(lane_halves(pk[key, k_cols]), axis=0)
            ds_in = jnp.concatenate(lane_halves(cx[key, q_cols]), axis=0)
            da = mm(ds_in, pk[key, v_cols], NT)
            af = a.astype(f32)
            inner = jnp.sum(af * da, axis=-1, keepdims=True) / jnp.sum(af, axis=-1, keepdims=True)
            ds = (af * (da - inner)).astype(bf16)
            dv = mm(a, ds_in, TN)
            both = jnp.concatenate([ds[:SEG_LEN], ds[SEG_LEN:]], axis=1)
            dq = mm(both, ks, NN) * factor
            dk = mm(ds, qs, TN) * factor
            pk[key, q_cols] = dq.astype(bf16)
            pk[key, k_cols] = dk.astype(bf16)
            pk[key, v_cols] = dv.astype(bf16)

    def result():
        @pl.loop(0, rows // block_rows, unroll=2)
        def _(i):
            key = rows_at(i * block_rows, block_rows, 16)
            gt_ref[key, :] = h[key, :].astype(bf16)

    def smalls():
        dws[:, :LANES] = small[...].T.astype(bf16)
        dws[:, LANES:] = jnp.zeros((dws.shape[0], LANES), bf16)

    need(0)
    params()
    for copy in inputs:
        copy.wait()
    for i in range(3):
        need(1 + i)
        project(i * n_tiles, n_tiles)
    for s in range(segs):
        attend(s)
        comm.upto("drain", 4 + s)
    branch()
    for i in range(per):
        need(4 + per + i)
        feed_in(i * n_tiles, n_tiles)
        if i:
            feed_back(i - 1)
    wo_start()
    need(4 + 2 * per)
    feed_back(per - 1)
    leaders()
    cross()
    comm.finish()
    for i in range(n_seg + 2):
        pair(i).wait_send()
    patch()
    sum_step = lambda: scatter_step(sums, jobs)
    factors[3].own()
    norm_leaders()
    factors[2].line()
    factors[1].plane()
    factors[0].last()
    for i in range(per):
        active_back(i)
        outer(bw, tr, g, i * width, width)
        sum_step()
        if i == 0:
            factors[3].line()
            factors[2].plane()
            factors[1].last()
        if i == 1:
            factors[3].plane()
            factors[2].last()
        if i == 2:
            factors[3].last()
    turn(tr, nl)
    add_back(sl, iw, 0, 2 * width)
    add_back(sl, iw, 2 * width, hidden - 2 * width)
    outer(iw, tr, sl, 0, width)
    sum_step()
    norm_back(z1, r1_ref, 0, df, 0)
    outer(iw, tr, sl, width, width)
    sum_step()
    smalls()
    turn(tr2, cx)
    context_back()
    attend_back(0)
    for i in range(2, per - 1):
        outer(iw, tr, sl, i * width, width)
        sum_step()
    attend_back(1)
    outer(iw, tr, sl, (per - 1) * width, width)
    sum_step()
    attend_back(2)
    outer(ow, tr2, df, 0, width)
    sum_step()
    attend_back(3)
    sum_step()
    turn(tr2, x_ref)
    for at_col, size in tail_units(width):
        add_back(pk, qw, at_col, size)
        outer(qw, tr2, pk, at_col, size)
        sum_step()
    result()
    for unit in factors:
        unit.drain()
    factor_grads()
    sums.finish()
    for unit in factors:
        unit.finish()
    for i in range(4):
        swap(i).wait_send()
    wait_leads()


def layer(wq, wo, wi, wb, gain, bias, pos, docs, x, cot):
    wrows = 16 * ROWS
    rows, width = x.shape
    segs = rows // SEG_LEN
    leads = docs.shape[1]
    hidden = wi.shape[2]
    own = ROWS // 2
    cross_width = 3 * width
    total = 2 * LANES + 3 * width + width + 2 * hidden + 4 * cross_width + width
    parts = 5 + 2 * hidden // width + 2
    n_units = parts - 2 + 3
    vm = pl.BlockSpec(memory_space=VM)
    arr = jax.ShapeDtypeStruct
    DMA = pltpu.SemaphoreType.DMA
    att_rows = segs * HEADS * SEG_LEN
    wide = lambda v, kind=bf16: VM((rows, v), kind)
    weight = lambda v: VM((wrows, v), bf16)
    widths = [width] * (2 * (hidden // width) + 1) + [256] + [size for _, size in tail_units(width)]
    bufs = []
    for i, w in enumerate(widths):
        bufs += scatter_buffers(w, i % 2 == 0)
    small_units = len([w for w in widths if w == 256])
    return pl.pallas_call(
        layer_kernel,
        out_shape=[
            arr((rows, width), bf16),
            arr((rows, width), bf16),
            arr((2, own, 3 * width), f32),
            arr((2, own, width), f32),
            arr((2, own, hidden), f32),
            arr((2, own, hidden), f32),
            arr((own, 256), f32),
        ],
        in_specs=[vm] * 8 + [pl.BlockSpec(memory_space=pl.ANY)] * 2,
        out_specs=[vm] * 7,
        scratch_shapes=[
            weight(2 * LANES), weight(width), weight(3 * width), weight(hidden), weight(hidden),
            weight(cross_width), VM((wrows // 4, width), bf16),
            wide(3 * width), VM((att_rows, SEG_LEN), bf16), wide(width), wide(width, f32), wide(width),
            wide(hidden), wide(hidden), wide(width), wide(width),
            wide(LANES, f32), wide(LANES, f32), VM((24, width), f32),
            wide(width), wide(width), DMA((2,)),
            VM((32, total), bf16), VM((32, total), bf16), VM((ROWS, 4 * cross_width + width), bf16),
            VM((LANES, LANES), f32),
            VM((2, 2, 2 * width), f32), VM((8, 2, 2 * width), f32), VM((leads, 2 * width), f32),
            VM((4, 4, leads, width), bf16), VM((8, 2, width), f32), VM((leads, 3 * width // 4), f32),
            VM((2, 2, width), f32), VM((2, 2, width), f32), VM((8, 2, width), f32), VM((8, 2, width), f32),
            VM((leads, 4 * width), bf16), VM((leads, 4 * width), bf16),
            VM((8, width), f32),
            wide(width), VM((width, rows), bf16), VM((width, rows), bf16), weight(256),
            VM((LANES, width), f32), VM((32 * leads, 4 * width), bf16), VM((width // 4, width), f32),
            VM((PAIR_SLOTS, wrows, width // 2), bf16), weight((width - 256) // 2),
            VM((small_units, wrows, LANES), bf16),
            DMA((n_units, 11)), DMA((n_units, 11)), DMA((parts,)), DMA((parts,)),
            DMA((5,)), DMA((5,)), DMA,
            DMA((8,)), DMA((8,)), DMA((4, 3)), DMA((4, 4)), DMA, DMA, DMA, DMA((8,)), DMA((8,)),
            DMA((4, 11)), DMA((4, 11)), DMA((4,)), DMA((4,)),
            DMA((len(widths), 12)), DMA((len(widths), 12)), pltpu.SemaphoreType.REGULAR((PAIR_SLOTS,)),
        ]
        + bufs,
        compiler_params=pltpu.CompilerParams(
            collective_id=0, has_side_effects=True, vmem_limit_bytes=63 * MIB
        ),
    )(wq, wo, wi, wb, gain, bias, pos, docs, x, cot)


def matmul(left, right, form):
    return jnp.einsum(form, left, right, preferred_element_type=jnp.float32)


def norm_forward(summed, gains, biases):
    average = jnp.mean(summed, axis=-1, keepdims=True)
    centred = summed - average
    variance = jnp.mean(centred * centred, axis=-1, keepdims=True)
    inverse = lax.rsqrt(variance + epsilon)
    scaled = centred * inverse
    return (scaled * gains + biases, scaled, inverse)


def norm_backward(grad_result, scaled, inverse, gains):
    grad_scaled = grad_result * gains
    first_mean = jnp.mean(grad_scaled, axis=-1, keepdims=True)
    second_mean = jnp.mean(grad_scaled * scaled, axis=-1, keepdims=True)
    grad_sum = inverse * (grad_scaled - first_mean - scaled * second_mean)
    return (grad_sum, jnp.sum(grad_result * scaled, axis=(0, 1)), jnp.sum(grad_result, axis=(0, 1)))


def split_heads(packed):
    groups, length, model_width = packed.shape
    return packed.reshape(groups, length, HEADS, model_width // HEADS)


def join_heads(split_part):
    groups, length, heads_count, head_size = split_part.shape
    return split_part.reshape(groups, length, heads_count * head_size)


def attend_forward(query_part, key_part, value_part, allowed):
    head_size = query_part.shape[-1]
    scores = matmul(query_part, key_part, "glhe,gmhe->ghlm") * head_size ** (-0.5)
    scores = jnp.where(allowed[:, None], scores, -1e30)
    row_max = jnp.max(scores, axis=-1, keepdims=True)
    exp_terms = jnp.exp(scores - row_max)
    row_total = jnp.sum(exp_terms, axis=-1, keepdims=True)
    attention = exp_terms / row_total
    context = matmul(attention.astype(jnp.bfloat16), value_part, "ghlm,gmhe->glhe")
    return (join_heads(context).astype(jnp.bfloat16), row_max + jnp.log(row_total))


def attend_backward(query_part, key_part, value_part, allowed, log_total, grad_context):
    head_size = query_part.shape[-1]
    factor = head_size ** (-0.5)
    scores = matmul(query_part, key_part, "glhe,gmhe->ghlm") * factor
    scores = jnp.where(allowed[:, None], scores, -1e30)
    attention = jnp.exp(scores - log_total)
    grad_attention = matmul(grad_context, value_part, "glhe,gmhe->ghlm")
    grad_value = matmul(attention.astype(jnp.bfloat16), grad_context, "ghlm,glhe->gmhe")
    inner = jnp.sum(attention * grad_attention, axis=-1, keepdims=True)
    grad_scores = (attention * (grad_attention - inner)).astype(jnp.bfloat16)
    grad_query = matmul(grad_scores, key_part, "ghlm,gmhe->glhe") * factor
    grad_key = matmul(grad_scores, query_part, "ghlm,glhe->gmhe") * factor
    return (join_heads(grad_query), join_heads(grad_key), join_heads(grad_value))


def segment_attend(packed):
    groups, length, total_width = packed.shape
    model_width = total_width // 3
    allowed = jnp.ones((groups, length, length), dtype=jnp.bool_)
    context, log_total = attend_forward(
        split_heads(packed[..., :model_width]),
        split_heads(packed[..., model_width : 2 * model_width]),
        split_heads(packed[..., 2 * model_width :]),
        allowed,
    )
    return (context, log_total)


def segment_attend_back(packed, log_total, grad_context):
    groups, length, total_width = packed.shape
    model_width = total_width // 3
    allowed = jnp.ones((groups, length, length), dtype=jnp.bool_)
    grad_query, grad_key, grad_value = attend_backward(
        split_heads(packed[..., :model_width]),
        split_heads(packed[..., model_width : 2 * model_width]),
        split_heads(packed[..., 2 * model_width :]),
        allowed,
        log_total,
        split_heads(grad_context),
    )
    return jnp.concatenate([grad_query, grad_key, grad_value], axis=-1)


def cross_attend(packed, allowed):
    model_width = packed.shape[-1] // 3
    remote = lax.all_gather(packed[..., model_width:], "fsdp", axis=1, tiled=True)
    context, log_total = attend_forward(
        split_heads(packed[..., :model_width]),
        split_heads(remote[..., :model_width]),
        split_heads(remote[..., model_width:]),
        allowed,
    )
    return (context, (remote, log_total))


def cross_attend_back(packed, saved, grad_context, allowed):
    remote, log_total = saved
    model_width = packed.shape[-1] // 3
    grad_query, grad_key, grad_value = attend_backward(
        split_heads(packed[..., :model_width]),
        split_heads(remote[..., :model_width]),
        split_heads(remote[..., model_width:]),
        allowed,
        log_total,
        split_heads(grad_context),
    )
    shared = jnp.concatenate([grad_key, grad_value], axis=-1)
    own_part = lax.psum_scatter(
        shared.astype(jnp.bfloat16), "fsdp", scatter_dimension=1, tiled=True
    ).astype(jnp.float32)
    return jnp.concatenate([grad_query, own_part], axis=-1)


def block_forward(states, weights, attend):
    w_qkv, w_out, w_in, w_back, gains, biases = weights
    gains = gains.astype(jnp.float32)
    biases = biases.astype(jnp.float32)
    states_low = states.astype(jnp.bfloat16)
    packed = matmul(states_low, w_qkv, "gld,de->gle").astype(jnp.bfloat16)
    context, saved = attend(packed)
    branch = matmul(context, w_out, "gld,de->gle")
    normed, scaled_one, inverse_one = norm_forward(states + branch, gains[0], biases[0])
    normed_low = normed.astype(jnp.bfloat16)
    hidden = matmul(normed_low, w_in, "gld,df->glf")
    active_low = jax.nn.gelu(hidden, approximate=False).astype(jnp.bfloat16)
    feed_out = matmul(active_low, w_back, "glf,fd->gld")
    result, scaled_two, inverse_two = norm_forward(normed + feed_out, gains[1], biases[1])
    kept = (
        states_low,
        packed,
        context,
        saved,
        scaled_one,
        inverse_one,
        normed_low,
        hidden,
        active_low,
        scaled_two,
        inverse_two,
    )
    return (result, kept)


def block_backward(grad_result, kept, weights, attend_back):
    w_qkv, w_out, w_in, w_back, gains, biases = weights
    gains = gains.astype(jnp.float32)
    (
        states_low,
        packed,
        context,
        saved,
        scaled_one,
        inverse_one,
        normed_low,
        hidden,
        active_low,
        scaled_two,
        inverse_two,
    ) = kept
    grad_sum_two, gain_two, bias_two = norm_backward(grad_result, scaled_two, inverse_two, gains[1])
    grad_feed = grad_sum_two.astype(jnp.bfloat16)
    grad_active = matmul(grad_feed, w_back, "gld,fd->glf")
    cumulative = 0.5 * (1.0 + lax.erf(hidden * root_half))
    slope = cumulative + hidden * inv_root_tau * jnp.exp(-0.5 * hidden * hidden)
    grad_hidden = (grad_active * slope).astype(jnp.bfloat16)
    grad_normed = grad_sum_two + matmul(grad_hidden, w_in, "glf,df->gld")
    grad_sum_one, gain_one, bias_one = norm_backward(grad_normed, scaled_one, inverse_one, gains[0])
    grad_branch = grad_sum_one.astype(jnp.bfloat16)
    grad_context = matmul(grad_branch, w_out, "gle,de->gld").astype(jnp.bfloat16)
    grad_packed = attend_back(packed, saved, grad_context).astype(jnp.bfloat16)
    grad_states = grad_sum_one + matmul(grad_packed, w_qkv, "gle,de->gld")
    factors = (
        states_low,
        grad_packed,
        context,
        grad_branch,
        normed_low,
        grad_hidden,
        grad_feed,
        active_low,
    )
    smalls = (jnp.stack([gain_one, gain_two]), jnp.stack([bias_one, bias_two]))
    return (grad_states, factors, smalls)


def weight_terms(factors):
    (
        states_low,
        grad_packed,
        context,
        grad_branch,
        normed_low,
        grad_hidden,
        grad_feed,
        active_low,
    ) = factors
    term_qkv = matmul(states_low, grad_packed, "gld,gle->de")
    term_out = matmul(context, grad_branch, "gld,gle->de")
    term_in = matmul(normed_low, grad_hidden, "gld,glf->df")
    term_back = matmul(grad_feed, active_low, "gld,glf->df")
    return jnp.concatenate([term_qkv, term_out, term_in, term_back], axis=1)


def gather_segment(w_qkv, w_out, w_in, w_back, norm_gain, norm_bias):
    return (
        lax.all_gather(w_qkv[0], ("dp", "fsdp"), axis=0, tiled=True),
        lax.all_gather(w_out[0], ("dp", "fsdp"), axis=0, tiled=True),
        lax.all_gather(w_in[0], ("dp", "fsdp"), axis=0, tiled=True),
        lax.all_gather(w_back[0], ("dp", "fsdp"), axis=1, tiled=True),
        lax.all_gather(norm_gain[0], ("dp", "fsdp"), axis=1, tiled=True),
        lax.all_gather(norm_bias[0], ("dp", "fsdp"), axis=1, tiled=True),
    )


def gather_cross(pos_embed, w_qkv, w_out, w_in, w_back, norm_gain, norm_bias):
    gathered = (
        lax.all_gather(w_qkv[1], ("dp", "fsdp"), axis=0, tiled=True),
        lax.all_gather(w_out[1], ("dp", "fsdp"), axis=0, tiled=True),
        lax.all_gather(w_in[1], ("dp", "fsdp"), axis=0, tiled=True),
        lax.all_gather(w_back[1], ("dp", "fsdp"), axis=1, tiled=True),
        lax.all_gather(norm_gain[1], ("dp", "fsdp"), axis=1, tiled=True),
        lax.all_gather(norm_bias[1], ("dp", "fsdp"), axis=1, tiled=True),
        lax.all_gather(pos_embed, ("dp", "fsdp"), axis=1, tiled=True),
    )
    return (gathered[:6], gathered[6])


def layer_forward(tokens, doc_ids, seg_weights, cross_weights, pos_full):
    rows, local_len, model_width = tokens.shape
    seg_count = local_len // SEG_LEN
    segments = tokens.reshape(rows * seg_count, SEG_LEN, model_width).astype(jnp.float32)
    seg_out, seg_kept = block_forward(segments, seg_weights, segment_attend)
    start = lax.axis_index("fsdp") * seg_count
    pos_local = lax.dynamic_slice_in_dim(pos_full, start, seg_count, 0).astype(jnp.float32)
    leaders = seg_out[:, 0, :].reshape(rows, seg_count, model_width) + pos_local
    own_docs = lax.dynamic_slice_in_dim(doc_ids, start, seg_count, 1)
    allowed = own_docs[:, :, None] == doc_ids[:, None, :]
    cross_out, cross_kept = block_forward(
        leaders, cross_weights, partial(cross_attend, allowed=allowed)
    )
    joined = jnp.concatenate(
        [cross_out.reshape(rows * seg_count, 1, model_width), seg_out[:, 1:, :]], axis=1
    )
    output = joined.reshape(rows, local_len, model_width).astype(jnp.bfloat16)
    return (output, (seg_kept, cross_kept, allowed))


def layer_backward(cotangent, doc_ids, kept, seg_weights, cross_weights):
    seg_kept, cross_kept, allowed = kept
    rows, local_len, model_width = cotangent.shape
    seg_count = local_len // SEG_LEN
    grad_all = cotangent.reshape(rows * seg_count, SEG_LEN, model_width).astype(jnp.float32)
    grad_cross = grad_all[:, 0, :].reshape(rows, seg_count, model_width)
    grad_leaders, cross_factors, cross_smalls = block_backward(
        grad_cross, cross_kept, cross_weights, partial(cross_attend_back, allowed=allowed)
    )
    start = lax.axis_index("fsdp") * seg_count
    empty_pos = jnp.zeros((doc_ids.shape[1], model_width), jnp.float32)
    grad_pos = lax.dynamic_update_slice_in_dim(empty_pos, jnp.sum(grad_leaders, axis=0), start, 0)
    grad_seg = jnp.concatenate(
        [grad_leaders.reshape(rows * seg_count, 1, model_width), grad_all[:, 1:, :]], axis=1
    )
    grad_states, seg_factors, seg_smalls = block_backward(
        grad_seg, seg_kept, seg_weights, segment_attend_back
    )
    grad_tokens = grad_states.reshape(rows, local_len, model_width).astype(jnp.bfloat16)
    return (grad_tokens, seg_factors, cross_factors, seg_smalls, cross_smalls, grad_pos)


def body(tokens, doc_ids, pos_embed, w_qkv, w_out, w_in, w_back, norm_gain, norm_bias, cotangent):
    seg_weights = gather_segment(w_qkv, w_out, w_in, w_back, norm_gain, norm_bias)
    cross_weights, pos_full = gather_cross(
        pos_embed, w_qkv, w_out, w_in, w_back, norm_gain, norm_bias
    )
    output, kept = layer_forward(tokens, doc_ids, seg_weights, cross_weights, pos_full)
    grad_tokens, seg_factors, cross_factors, seg_smalls, cross_smalls, grad_pos = layer_backward(
        cotangent, doc_ids, kept, seg_weights, cross_weights
    )
    model_width = tokens.shape[2]
    hidden_width = w_in.shape[2]
    seg_term = lax.psum_scatter(
        weight_terms(seg_factors), ("dp", "fsdp"), scatter_dimension=0, tiled=True
    )
    cross_term = lax.psum_scatter(
        weight_terms(cross_factors), ("dp", "fsdp"), scatter_dimension=0, tiled=True
    )
    stacked = jnp.stack([seg_term, cross_term])
    grad_qkv = stacked[:, :, : 3 * model_width]
    grad_out = stacked[:, :, 3 * model_width : 4 * model_width]
    grad_in = stacked[:, :, 4 * model_width : 4 * model_width + hidden_width]
    grad_back = jnp.transpose(stacked[:, :, 4 * model_width + hidden_width :], (0, 2, 1))
    gain_all = jnp.stack([seg_smalls[0], cross_smalls[0]])
    bias_all = jnp.stack([seg_smalls[1], cross_smalls[1]])
    grad_gain, grad_bias, pos_shard = (
        lax.psum_scatter(gain_all, ("dp", "fsdp"), scatter_dimension=2, tiled=True),
        lax.psum_scatter(bias_all, ("dp", "fsdp"), scatter_dimension=2, tiled=True),
        lax.psum_scatter(grad_pos, ("dp", "fsdp"), scatter_dimension=1, tiled=True),
    )
    return (
        output,
        grad_tokens,
        pos_shard,
        grad_qkv,
        grad_out,
        grad_in,
        grad_back,
        grad_gain,
        grad_bias,
    )


def write_kernel(n, *refs):
    sources, smalls = refs[:n], refs[n]
    targets, pos_ref, gain_ref, bias_ref = refs[n + 1 : 2 * n + 1], *refs[2 * n + 1 : 2 * n + 4]
    bufs, sems = refs[2 * n + 4 : 3 * n + 4], refs[3 * n + 4]
    loads = [pltpu.make_async_copy(sources[i], bufs[i], sems.at[0, i]) for i in range(n)]
    copies = [pltpu.make_async_copy(bufs[i], targets[i], sems.at[1, i]) for i in range(n)]
    for load in loads:
        load.start()
    for load, copy in zip(loads, copies):
        load.wait()
        copy.start()
    rows = smalls[:, :LANES].T[:, : smalls.shape[0]]
    pos_ref[...] = rows[8 : 8 + pos_ref.shape[0]]
    for b in range(2):
        gain_ref[b] = rows[4 * b : 4 * b + 2]
        bias_ref[b] = rows[4 * b + 2 : 4 * b + 4]
    for copy in copies:
        copy.wait()


def write_results(arrays, smalls, positions):
    n = len(arrays)
    own = smalls.shape[0]
    hbm, vm = pl.BlockSpec(memory_space=pl.ANY), pl.BlockSpec(memory_space=VM)
    like = [jax.ShapeDtypeStruct(v.shape, v.dtype) for v in arrays]
    shapes = [(positions, own), (2, 2, own), (2, 2, own)]
    return pl.pallas_call(
        partial(write_kernel, n),
        out_shape=like + [jax.ShapeDtypeStruct(v, f32) for v in shapes],
        in_specs=[hbm] * n + [vm],
        out_specs=[hbm] * n + [vm] * 3,
        scratch_shapes=[VM(v.shape, v.dtype) for v in arrays] + [pltpu.SemaphoreType.DMA((2, n))],
    )(*arrays, smalls)


def fast_body(tokens, doc_ids, pos_embed, w_qkv, w_out, w_in, w_back, norm_gain, norm_bias, cotangent):
    nrows, local_len, width = tokens.shape
    rows = nrows * local_len
    x = tokens.reshape(rows, width)
    cot = cotangent.reshape(rows, width)
    output, grad_tokens, g_qkv, g_out, g_in, g_back, t_small = layer(
        w_qkv, w_out, w_in, jnp.swapaxes(w_back, 1, 2), norm_gain, norm_bias, pos_embed, doc_ids, x, cot
    )
    output, grad_tokens, g_qkv, g_out, g_in, g_back, grad_pos, grad_gain, grad_bias = write_results(
        (output, grad_tokens, g_qkv, g_out, g_in, g_back), t_small, doc_ids.shape[1]
    )
    return (
        output.reshape(tokens.shape),
        grad_tokens.reshape(tokens.shape),
        grad_pos,
        g_qkv,
        g_out,
        g_in,
        jnp.swapaxes(g_back, 1, 2),
        grad_gain,
        grad_bias,
    )


def solution(mesh):
    fast = dict(mesh.shape) == {"dp": 4, "fsdp": 8}
    return jax.shard_map(
        fast_body if fast else body,
        mesh=mesh,
        in_specs=(
            P("dp", "fsdp", None),
            P("dp", None),
            P(None, ("dp", "fsdp")),
            P(None, ("dp", "fsdp"), None),
            P(None, ("dp", "fsdp"), None),
            P(None, ("dp", "fsdp"), None),
            P(None, None, ("dp", "fsdp")),
            P(None, None, ("dp", "fsdp")),
            P(None, None, ("dp", "fsdp")),
            P("dp", "fsdp", None),
        ),
        out_specs=(
            P("dp", "fsdp", None),
            P("dp", "fsdp", None),
            P(None, ("dp", "fsdp")),
            P(None, ("dp", "fsdp"), None),
            P(None, ("dp", "fsdp"), None),
            P(None, ("dp", "fsdp"), None),
            P(None, None, ("dp", "fsdp")),
            P(None, None, ("dp", "fsdp")),
            P(None, None, ("dp", "fsdp")),
        ),
        check_vma=False,
    )
```
